32 devices in a mesh: dp: 2 (over x), head: 1, row: 16 (over z, y, core).
Axes of the slice: x: 2, y: 2, z: 4, core: 2. Of those that a mesh axis runs over, the one named last changes fastest.
Arguments:
- pair_act: bfloat16 [256, 128, 128], P(('dp', 'row')), parts along dimension 0, may hold values from -12 to 12
- chain_id: int32 [256], P('dp'), parts along dimension 0, may hold values from 0 to 3, never falling along the last dimension, each value on 1 to 64 neighbouring positions
- residue_mask: int32 [256], P('dp'), parts along dimension 0, may hold values 0 or 1
- norm_gain: float32 [128], replicated, may hold values from 0.5 to 1.5
- w_proj: bfloat16 [128, 4, 128], P(None, 'head'), may hold values from -1.25 to 1.25
- w_bias: bfloat16 [128, 4], P(None, 'head'), may hold values from -0.9 to 0.9
- chain_bias: float32 [2, 4], P(None, 'head'), may hold values from -2 to 2
- w_out: bfloat16 [4, 32, 128], P('head'), may hold values from -0.5 to 0.5
- w_dist: bfloat16 [128, 64], replicated, may hold values from -0.5 to 0.5
- dist_bias: float32 [64], replicated, may hold values from -3 to 3
Outputs:
- new_pair: bfloat16 [256, 128, 128], P(('dp', 'row')), parts along dimension 0
- distogram: bfloat16 [256, 128, 64], P(('dp', 'row')), parts along dimension 0
The draws below stay inside these ranges and needn't reach their ends.
There are 2 independent parts, one for each index of `dp`. The reference program is written for one: setup_inputs(seed, part) draws one part's arguments, and reference() takes and returns one part's arrays. A program takes and returns all parts, laid end to end along the dimension named above; an argument that names none is the same for every part. Nothing has to cross between parts.
Inputs may be any that keep to these rules, and one draw needn't show every extreme that they name: `chain_id`: chain ids never fall along the residues; no chain has more than half of the 128 residues.
All inputs are finite; a program needn't handle non-finite values.
Results may differ from the reference program's by a relative error of at most 0.013.
Values may be sent and summed in bfloat16 or wider, within the bound.
No kernel may reach another device: no remote copies, remote signals or barrier semaphores. Data moves between devices by JAX's collectives and lax.ppermute only.
A program may use at most 64 MiB of HBM per device.

```python
import math
import jax
import jax.numpy as jnp
import numpy as np
from jax import lax

PAIR = 128
HEADS = 4
HEAD_DIM = 32
BINS = 64
N_RES = 128
N_HEAD = 1


def draw_pair_act(key, part):
    key = jax.random.fold_in(key, 5)
    first_key = jax.random.fold_in(key, 0)
    base = jax.random.normal(first_key, (N_RES, N_RES, PAIR), jnp.float32)
    return jnp.clip(base, -12.0, 12.0).astype(jnp.bfloat16)


def projection_block(key, spread):
    first_key, second_key = jax.random.split(key, 2)
    score_cols = jax.random.normal(first_key, (PAIR, HEADS, 2 * HEAD_DIM), jnp.float32) * (spread * PAIR ** (-0.5))
    other_cols = jax.random.normal(second_key, (PAIR, HEADS, 2 * HEAD_DIM), jnp.float32) * PAIR ** (-0.5)
    joined = jnp.concatenate([score_cols, other_cols], -1)
    return jnp.clip(joined, -1.25, 1.25).astype(jnp.bfloat16)


def draw_w_proj(key, part):
    key = jax.random.fold_in(key, 9)
    return projection_block(key, 2.83)


def draw_w_bias(key, part):
    key = jax.random.fold_in(key, 7)
    return jnp.clip(0.25 * jax.random.normal(key, (PAIR, HEADS), jnp.float32), -0.9, 0.9).astype(jnp.bfloat16)


def set_ends(array, rng, smallest, largest):
    extent = array.shape
    spot = [jax.random.randint(jax.random.fold_in(rng, axis), (), 0, extent[axis]) for axis in range(len(extent))]
    array = array.at[tuple(spot)].set(smallest)
    longest = extent.index(max(extent))
    spot[longest] = (spot[longest] + 1) % extent[longest]
    return array.at[tuple(spot)].set(largest)


def split_up(number_of, total, reach, slope):
    weights = [(1 << 20) // math.isqrt(rank ** slope) + 1 for rank in range(2, number_of + 1)]
    surplus, counts = total - reach - (number_of - 1), [1] * (number_of - 1)
    while surplus > 0:
        free = [i for i in range(number_of - 1) if counts[i] < reach]
        mass, left = sum([weights[i] for i in free]), surplus
        for i in free:
            addition = min(reach - counts[i], max(1, left * weights[i] // mass), surplus)
            counts[i] = counts[i] + addition
            surplus = surplus - addition
    return np.array([reach] + counts)


def ragged_sizes(stream_key, count, total, reach, lean):
    if count == 2:
        one = jax.random.randint(stream_key, (), max(1, total - reach), min(reach, total - 1) + 1)
        return jnp.stack([one, total - one])
    lengths = jnp.asarray(split_up(count, total, reach, lean), jnp.int32)
    couples = (count - 1) // 2
    giver, taker = lengths[1:1 + 2 * couples:2], lengths[2:2 + 2 * couples:2]
    margin = jnp.minimum(giver - 1, reach - taker)
    passed = jax.random.randint(jax.random.fold_in(stream_key, 1), (couples,), 0, 1 << 20) % (margin + 1)
    lengths = lengths.at[1:1 + 2 * couples:2].set(giver - passed).at[2:2 + 2 * couples:2].set(taker + passed)
    return lengths[jax.random.permutation(jax.random.fold_in(stream_key, 2), count)]


def gaussian(key, dims, width, reach, dtype=jnp.bfloat16):
    entries = width * jax.random.normal(key, dims, jnp.float32)
    return jnp.clip(entries, min=-reach, max=reach).astype(dtype)


def setup_inputs(seed: int = 0, part: int = 0) -> dict:
    seeds = jax.random.split(jax.random.key(seed), 11)
    own_keys = jax.random.split(jax.random.fold_in(seeds[10], part), 11)
    return {
        "pair_act": draw_pair_act(jax.random.fold_in(jax.random.fold_in(seeds[10], part), 71), part),
        "chain_id": jnp.searchsorted(jnp.cumsum(ragged_sizes(own_keys[1], 4, N_RES, N_RES // 2, 1)), jnp.arange(N_RES), side="right").astype(jnp.int32),
        "residue_mask": set_ends((jax.random.randint(own_keys[2], (N_RES,), 0, 8) < 7).astype(jnp.int32), jax.random.fold_in(own_keys[2], 1), 0, 1),
        "norm_gain": jnp.clip(1.0 + 0.1 * jax.random.normal(seeds[3], (PAIR,), jnp.float32), 0.5, 1.5),
        "w_proj": draw_w_proj(jax.random.fold_in(seeds[10], 71), part),
        "w_bias": draw_w_bias(jax.random.fold_in(seeds[10], 71), part),
        "chain_bias": jnp.clip(jax.random.uniform(seeds[6], (2, HEADS), jnp.float32, -2.0, 2.0), -2.0, 2.0),
        "w_out": gaussian(seeds[7], (HEADS, HEAD_DIM, PAIR), (HEADS * HEAD_DIM) ** -0.5, 0.5),
        "w_dist": gaussian(seeds[8], (PAIR, BINS), PAIR ** -0.5, 0.5),
        "dist_bias": gaussian(seeds[9], (BINS,), 0.5, 3.0, jnp.float32),
    }


def normalize(values, gain_vec):
    values = values.astype(jnp.float32)
    center_val = lax.optimization_barrier(jnp.mean(values, -1, keepdims=True))
    centered = values - center_val
    variance = lax.optimization_barrier(jnp.mean(centered * centered, -1, keepdims=True))
    return centered * lax.rsqrt(variance + 1e-05) * gain_vec

def reference(pair_act, chain_id, residue_mask, norm_gain, w_proj, w_bias, chain_bias, w_out, w_dist, dist_bias):
    pair_float = pair_act.astype(jnp.float32)
    normed = normalize(pair_float, norm_gain).astype(jnp.bfloat16)
    bias_kih = jnp.dot(normed, w_bias, preferred_element_type=jnp.float32).astype(jnp.bfloat16)
    bias_full = jnp.transpose(bias_kih, (2, 1, 0)).astype(jnp.float32)
    same_chain = chain_id[:, None] == chain_id[None, :]
    chain_term = jnp.where(same_chain[None], chain_bias[1][:, None, None], chain_bias[0][:, None, None])
    mask_term = (residue_mask.astype(jnp.float32) - 1.0) * 1000000000.0
    group_heads = HEADS // N_HEAD
    flat_w = w_proj.reshape(PAIR, HEADS * 4 * HEAD_DIM)
    out_groups = w_out.reshape(N_HEAD, group_heads, HEAD_DIM, PAIR).astype(jnp.float32)
    scaling = HEAD_DIM ** (-0.5)

    def column_step(column):
        projected = jnp.dot(column, flat_w, preferred_element_type=jnp.float32).astype(jnp.bfloat16)
        projected = projected.reshape(N_RES, HEADS, 4 * HEAD_DIM).astype(jnp.float32)
        queries = projected[..., :HEAD_DIM]
        keys_part = projected[..., HEAD_DIM:2 * HEAD_DIM]
        values_part = projected[..., 2 * HEAD_DIM:3 * HEAD_DIM]
        gate_part = projected[..., 3 * HEAD_DIM:]
        scores = jnp.einsum('ihd,khd->hik', queries, keys_part) * scaling
        scores = scores + bias_full + chain_term + mask_term[None, None, :]
        row_max = lax.optimization_barrier(jnp.max(scores, -1, keepdims=True))
        weights = jnp.exp(scores - row_max)
        softmax_w = (weights / lax.optimization_barrier(jnp.sum(weights, -1, keepdims=True))).astype(jnp.bfloat16)
        attended = jnp.einsum('hik,khd->ihd', softmax_w.astype(jnp.float32), values_part)
        gated = (jax.nn.sigmoid(gate_part) * attended).astype(jnp.bfloat16)
        grouped = gated.reshape(N_RES, N_HEAD, group_heads, HEAD_DIM).astype(jnp.float32)
        partials = jnp.einsum('ighd,ghdc->gic', grouped, out_groups).astype(jnp.bfloat16)
        partials = lax.optimization_barrier(partials)
        return lax.optimization_barrier(jnp.sum(partials.astype(jnp.float32), 0))
    columns_in = jnp.transpose(normed, (1, 0, 2))
    update = lax.map(column_step, columns_in)
    new_pair = (pair_float + jnp.transpose(update, (1, 0, 2))).astype(jnp.bfloat16)
    logits = (jnp.dot(new_pair, w_dist, preferred_element_type=jnp.float32) + dist_bias).astype(jnp.bfloat16)
    logits_float = logits.astype(jnp.float32)
    distogram = (logits_float + jnp.transpose(logits_float, (1, 0, 2))).astype(jnp.bfloat16)
    return (new_pair, distogram)
```

```python
import functools

import jax
import jax.numpy as jnp
from jax import lax
from jax.experimental import pallas as pl
from jax.experimental.pallas import tpu as pltpu
from jax.sharding import PartitionSpec as P

LANES = 128
F32 = jnp.float32
BF16 = jnp.bfloat16


def dot_nt(a, b):
    return lax.dot_general(a, b, (((1,), (1,)), ((), ())), preferred_element_type=F32)


def dot_tn(a, b):
    return lax.dot_general(a, b, (((0,), (0,)), ((), ())), preferred_element_type=F32)


def dot_nn(a, b):
    return jnp.dot(a, b, preferred_element_type=F32)


def layer_norm(values, gain):
    center = jnp.mean(values, -1, keepdims=True)
    centered = values - center
    variance = jnp.mean(centered * centered, -1, keepdims=True)
    return (centered * lax.rsqrt(variance + 1e-05) * gain).astype(BF16)


def swap_matrix(rows):
    size = 2 * rows * rows
    out = lax.broadcasted_iota(jnp.int32, (size, size), 0)
    col = lax.broadcasted_iota(jnp.int32, (size, size), 1)
    b, rest = out // (2 * rows), out % (2 * rows)
    wanted = (rest // rows) * (rows * rows) + (rest % rows) * rows + b
    return jnp.where(col == wanted, 1.0, 0.0).astype(BF16)


def pack_kernel(x_ref, gain_ref, wb_ref, out_ref):
    rows, n, chan = x_ref.shape
    peers = n // rows
    tiles = n // LANES
    wb = wb_ref[...]
    owner = lax.broadcasted_iota(jnp.int32, wb.shape, 0) % rows
    gain = gain_ref[...]
    bias = jnp.zeros((wb.shape[0], n), F32)
    for pair in range(rows // 2):
        both = []
        for k in (2 * pair, 2 * pair + 1):
            x = x_ref[k].astype(F32)
            both.append(x.reshape(peers, rows, chan))
            bias = bias + dot_nt(jnp.where(owner == k, wb, jnp.zeros_like(wb)), layer_norm(x, gain))
        out_ref[:, 2 * rows * pair : 2 * rows * (pair + 1), :] = jnp.concatenate(both, 1).astype(BF16)
    bias = bias.astype(BF16)
    base, step = rows * rows, wb.shape[0]
    for t in range(tiles):
        block = bias[:, t * LANES : (t + 1) * LANES]
        for d in range(peers):
            out_ref[d, base + t * step : base + (t + 1) * step, :] = block


def attend_kernel(
    heads, fused,
    recv_ref, chain_ref, mask_ref, gain_ref, cb_ref, w_ref, wo_ref, wd_ref, db_ref,
    out_ref, second_ref, x_s, n_s, bias_s,
):
    peers = recv_ref.shape[0]
    rows, n, chan = x_s.shape
    tiles = n // LANES
    dim = w_ref.shape[0] // (4 * heads)
    width = heads * dim
    base, step = rows * rows, heads * rows
    gain = gain_ref[...]
    swap = swap_matrix(rows)
    group = 2 * rows

    def unpack(pair):
        at = pl.ds(pl.multiple_of(pair * group, group), group)
        both = recv_ref[pl.ds(2 * pair, 2)]
        x = dot_nn(swap, both[:, :base, :].reshape(2 * base, chan))
        normed = layer_norm(x, gain)
        x_s[:, at, :] = x.astype(BF16).reshape(rows, group, chan)
        n_s[:, at, :] = normed.reshape(rows, group, chan)
        extra = both[:, base:, :].astype(F32)
        for t in range(tiles):
            for h in range(heads):
                start = t * step + h * rows
                bias_s[h, at, t * LANES : (t + 1) * LANES] = extra[:, start : start + rows, :].reshape(
                    group, LANES
                )

    if tiles == 1:
        for pair in range(peers // 2):
            unpack(pair)
    else:
        pl.loop(0, peers // 2)(unpack)

    def column_of(row):
        return jnp.transpose(jnp.broadcast_to(row, (LANES, LANES)))

    for kt in range(tiles):
        ks = slice(kt * LANES, (kt + 1) * LANES)
        chain_k = column_of(chain_ref[:, ks].astype(F32))
        mask_k = (column_of(mask_ref[:, ks].astype(F32)) - 1.0) * 1000000000.0
        for it in range(tiles):
            cs = slice(it * LANES, (it + 1) * LANES)
            same = chain_k == chain_ref[:, cs].astype(F32)
            for h in range(heads):
                term = jnp.where(same, cb_ref[1, h], cb_ref[0, h]) + mask_k
                bias_s[h, ks, cs] = bias_s[h, ks, cs] + term

    scaling = dim ** (-0.5)
    w_q, w_k = w_ref[:width], w_ref[width : 2 * width]
    w_v, w_g = w_ref[2 * width : 3 * width], w_ref[3 * width :]
    w_out = wo_ref[...]
    w_dist = wd_ref[...]
    d_bias = db_ref[...]
    head_of = lax.broadcasted_iota(jnp.int32, (width, LANES), 0) // dim

    def column(j):
        normed = n_s[j]
        q = dot_nt(w_q, normed)
        k = dot_nt(normed, w_k).astype(BF16)
        v = dot_nt(w_v, normed).astype(BF16)
        gate = jax.nn.sigmoid(dot_nt(w_g, normed).astype(BF16).astype(F32))
        updates = []
        for t in range(tiles):
            cs = slice(t * LANES, (t + 1) * LANES)
            q_t = q[:, cs]
            spread = jnp.concatenate(
                [jnp.where(head_of == h, q_t, 0.0).astype(BF16) for h in range(heads)], 1
            )
            scores = dot_nn(k, spread)
            gated = []
            for h in range(heads):
                s = scores[:, h * LANES : (h + 1) * LANES] * scaling + bias_s[h, :, cs]
                e = jnp.exp(s - jnp.max(s, 0, keepdims=True))
                total = jnp.sum(e, 0, keepdims=True)
                mine = slice(h * dim, (h + 1) * dim)
                o = dot_nn(v[mine], e.astype(BF16)) * (1.0 / total)
                gated.append((gate[mine, cs] * o).astype(BF16))
            updates.append(dot_tn(jnp.concatenate(gated, 0), w_out).astype(BF16))
        return jnp.concatenate(updates, 0)

    def column_pair(jp):
        both = []
        for side in range(2):
            j = 2 * jp + side
            update = column(j)
            if not fused:
                out_ref[j] = update
                second_ref[j] = x_s[j]
                continue
            new = (x_s[j].astype(F32) + update.astype(F32)).astype(BF16)
            second_ref[j] = (dot_nt(w_dist, new) + d_bias).astype(BF16)
            both.append(new.astype(F32).reshape(peers, rows, chan))
        if fused:
            at = pl.ds(pl.multiple_of(jp * group, group), group)
            out_ref[:, at, :] = jnp.concatenate(both, 1).astype(BF16)

    if tiles == 1:
        for jp in range(rows // 2):
            column_pair(jp)
    else:
        pl.loop(0, rows // 2)(column_pair)


def finish_kernel(recv_ref, mirror_ref, wd_ref, db_ref, new_ref, dist_ref):
    peers, _, chan = recv_ref.shape
    rows = new_ref.shape[0]
    group = 2 * rows
    swap = swap_matrix(rows)

    def unpack(pair):
        at = pl.ds(pl.multiple_of(pair * group, group), group)
        both = recv_ref[pl.ds(2 * pair, 2)].reshape(2 * rows * rows, chan)
        new_ref[:, at, :] = dot_nn(swap, both).astype(BF16).reshape(rows, group, chan)

    for pair in range(peers // 2):
        unpack(pair)
    w_dist = wd_ref[...]
    d_bias = db_ref[...]
    for i in range(rows):
        logits = (dot_nt(w_dist, new_ref[i]) + d_bias).astype(BF16)
        dist_ref[i] = (logits.astype(F32) + mirror_ref[i].astype(F32)).astype(BF16)


def call(kernel, outs, args, scratch=(), smem=()):
    specs = [pl.BlockSpec(memory_space=pltpu.SMEM if i in smem else pltpu.VMEM) for i in range(len(args))]
    return pl.pallas_call(
        kernel,
        out_shape=[jax.ShapeDtypeStruct(s, d) for s, d in outs],
        in_specs=specs,
        out_specs=[pl.BlockSpec(memory_space=pltpu.VMEM)] * len(outs),
        scratch_shapes=list(scratch),
        compiler_params=pltpu.CompilerParams(vmem_limit_bytes=48 * 1024 * 1024),
    )(*args)


def shards(
    pair_act, chain_id, residue_mask, norm_gain, w_proj, w_bias, chain_bias, w_out, w_dist, dist_bias,
):
    rows, n, chan = pair_act.shape
    peers = n // rows
    heads, dim = w_out.shape[0], w_out.shape[1]
    bins = w_dist.shape[1]
    tiles = n // LANES
    fused = lax.axis_size("head") == 1
    gain = norm_gain[None, :]
    length = rows * rows + tiles * heads * rows

    wb_rows = jnp.repeat(w_bias.T, rows, axis=0)
    (packed,) = call(pack_kernel, [((peers, length, chan), BF16)], [pair_act, gain, wb_rows])
    received = lax.all_to_all(packed, "row", split_axis=0, concat_axis=0, tiled=True)

    w_types = w_proj.reshape(chan, heads, 4, dim).transpose(2, 1, 3, 0).reshape(4 * heads * dim, chan)
    wd_t = w_dist.T
    db_col = jnp.broadcast_to(dist_bias[:, None], (bins, n))
    if fused:
        outs = [((peers, rows * rows, chan), BF16), ((rows, bins, n), BF16)]
    else:
        outs = [((rows, n, chan), BF16), ((rows, n, chan), BF16)]
    first, second = call(
        functools.partial(attend_kernel, heads, fused),
        outs,
        [
            received, chain_id[None, :], residue_mask[None, :], gain, chain_bias,
            w_types, w_out.reshape(heads * dim, chan), wd_t, db_col,
        ],
        scratch=[
            pltpu.VMEM((rows, n, chan), BF16),
            pltpu.VMEM((rows, n, chan), BF16),
            pltpu.VMEM((heads, n, n), F32),
        ],
        smem=(4,),
    )
    if fused:
        to_rows, mirror = first, second
    else:
        update = lax.psum(first, "head").astype(F32)
        new = (second.astype(F32) + update).astype(BF16)
        logits = jnp.einsum("cb,jic->jbi", w_dist, new, preferred_element_type=F32)
        mirror = (logits + dist_bias[None, :, None]).astype(BF16)
        to_rows = new.reshape(rows, peers, rows, chan).transpose(1, 0, 2, 3).reshape(peers, rows * rows, chan)
    arrived = lax.all_to_all(to_rows, "row", split_axis=0, concat_axis=0, tiled=True)
    new_rows, dist = call(
        finish_kernel,
        [((rows, n, chan), BF16), ((rows, bins, n), BF16)],
        [arrived, mirror, wd_t, db_col],
    )
    return new_rows, dist.transpose(0, 2, 1)


def solution(mesh):
    in_specs = (
        P(("dp", "row"), None, None),
        P("dp"),
        P("dp"),
        P(),
        P(None, "head", None),
        P(None, "head"),
        P(None, "head"),
        P("head", None, None),
        P(),
        P(),
    )
    out_specs = (P(("dp", "row"), None, None), P(("dp", "row"), None, None))
    return jax.shard_map(shards, mesh=mesh, in_specs=in_specs, out_specs=out_specs, check_vma=False)
```

```python
import functools

import jax
import jax.numpy as jnp
from jax import lax
from jax.experimental import pallas as pl
from jax.experimental.pallas import tpu as pltpu
from jax.sharding import PartitionSpec as P

LANES = 128
F32 = jnp.float32
BF16 = jnp.bfloat16


def dot_nt(a, b):
    return lax.dot_general(a, b, (((1,), (1,)), ((), ())), preferred_element_type=F32)


def dot_tn(a, b):
    return lax.dot_general(a, b, (((0,), (0,)), ((), ())), preferred_element_type=F32)


def dot_nn(a, b):
    return jnp.dot(a, b, preferred_element_type=F32)


def layer_norm(values, gain):
    center = jnp.mean(values, -1, keepdims=True)
    centered = values - center
    variance = jnp.mean(centered * centered, -1, keepdims=True)
    return (centered * lax.rsqrt(variance + 1e-05) * gain).astype(BF16)


def swap_matrix(rows, flip):
    size = 2 * rows * rows
    out = lax.broadcasted_iota(jnp.int32, (size, size), 0)
    col = lax.broadcasted_iota(jnp.int32, (size, size), 1)
    b, rest = out // (2 * rows), out % (2 * rows)
    wanted = ((rest // rows) ^ flip) * (rows * rows) + (rest % rows) * rows + b
    return jnp.where(col == wanted, 1.0, 0.0).astype(BF16)


def pack_kernel(peers, x_hbm, gain_hbm, wb_hbm, *refs):
    outs, (x_ref, gain_ref, wb_ref, wide, sems) = refs[:peers], refs[peers:]
    rows, n, chan = x_ref.shape
    tiles = n // LANES
    me = lax.axis_index("row")
    copies = [pltpu.make_async_copy(x_hbm.at[k], x_ref.at[k], sems.at[k]) for k in range(rows)]
    copies.append(pltpu.make_async_copy(gain_hbm, gain_ref, sems.at[rows]))
    copies.append(pltpu.make_async_copy(wb_hbm, wb_ref, sems.at[rows + 1]))
    for copy in copies[rows:] + copies[:rows]:
        copy.start()
    for copy in copies[rows:]:
        copy.wait()
    wb = wb_ref[...]
    owner = lax.broadcasted_iota(jnp.int32, wb.shape, 0) % rows
    gain = gain_ref[...]
    bias = jnp.zeros((wb.shape[0], n), F32)
    for k in range(rows):
        copies[k].wait()
        x = x_ref[k].astype(F32)
        wide[k] = x
        bias = bias + dot_nt(jnp.where(owner == k, wb, jnp.zeros_like(wb)), layer_norm(x, gain))
    bias = bias.astype(BF16)
    base, step = rows * rows, wb.shape[0]
    for s in range(peers):
        at = pl.ds(pl.multiple_of((me ^ s) * rows, rows), rows)
        outs[s][:base] = wide[:, at, :].reshape(base, chan).astype(BF16)
        for t in range(tiles):
            outs[s][base + t * step : base + (t + 1) * step] = bias[:, t * LANES : (t + 1) * LANES]


def prepare_kernel(heads, chain_ref, mask_ref, cb_ref, w_ref, db_ref, term_ref, wt_ref, dbc_ref):
    n = chain_ref.shape[1]
    tiles = n // LANES
    chan = w_ref.shape[0]
    dim = w_ref.shape[2] // 4
    width = heads * dim

    def column_of(row):
        return jnp.transpose(jnp.broadcast_to(row, (LANES, LANES)))

    for kt in range(tiles):
        ks = slice(kt * LANES, (kt + 1) * LANES)
        chain_k = column_of(chain_ref[:, ks].astype(F32))
        mask_k = (column_of(mask_ref[:, ks].astype(F32)) - 1.0) * 1000000000.0
        for it in range(tiles):
            cs = slice(it * LANES, (it + 1) * LANES)
            same = chain_k == chain_ref[:, cs].astype(F32)
            for h in range(heads):
                term_ref[h, ks, cs] = jnp.where(same, cb_ref[1, h], cb_ref[0, h]) + mask_k
    for h in range(heads):
        turned = jnp.transpose(w_ref[:, h, :].astype(F32)).astype(BF16)
        for kind in range(4):
            start = kind * width + h * dim
            wt_ref[start : start + dim] = turned[kind * dim : (kind + 1) * dim]
    bins = dbc_ref.shape[0]
    db_rows = jnp.broadcast_to(jnp.concatenate([db_ref[...], db_ref[...]], 1)[:, :LANES], (LANES, LANES))
    dbc_ref[...] = jnp.transpose(db_rows)[:bins]


def attend_kernel(heads, fused, peers, *refs):
    recv, refs = refs[:peers], refs[peers:]
    (term_ref, gain_ref, w_ref, wo_ref, wd_ref, db_ref), refs = refs[:6], refs[6:]
    if fused:
        outs, (second_ref, x_s, n_s, bias_s, new_s) = refs[:peers], refs[peers:]
    else:
        out_ref, second_ref, x_s, n_s, bias_s = refs
    rows, n, chan = x_s.shape
    tiles = n // LANES
    dim = w_ref.shape[0] // (4 * heads)
    width = heads * dim
    base, step = rows * rows, heads * rows
    gain = gain_ref[...]
    me = lax.axis_index("row")
    swap = swap_matrix(rows, me & 1)
    group = 2 * rows

    for s in range(0, peers, 2):
        at = pl.ds(pl.multiple_of(((me ^ s) // 2) * group, group), group)
        both = jnp.concatenate([recv[s][:base], recv[s + 1][:base]], 0)
        x = dot_nn(swap, both)
        x_s[:, at, :] = x.astype(BF16).reshape(rows, group, chan)
        n_s[:, at, :] = layer_norm(x, gain).reshape(rows, group, chan)
    for s in range(peers):
        extra = recv[s][base:].astype(F32)
        at = pl.ds(pl.multiple_of((me ^ s) * rows, rows), rows)
        for t in range(tiles):
            cs = slice(t * LANES, (t + 1) * LANES)
            for h in range(heads):
                start = t * step + h * rows
                bias_s[h, at, cs] = extra[start : start + rows] + term_ref[h, at, cs]

    scaling = dim ** (-0.5)
    w_q, w_k = w_ref[:width], w_ref[width : 2 * width]
    w_v, w_g = w_ref[2 * width : 3 * width], w_ref[3 * width :]
    w_out = wo_ref[...]
    w_dist = wd_ref[...]
    d_bias = db_ref[:, :1]
    head_of = lax.broadcasted_iota(jnp.int32, (width, LANES), 0) // dim

    def column(j):
        normed = n_s[j]
        q = dot_nt(w_q, normed)
        k = dot_nt(normed, w_k).astype(BF16)
        v = dot_nt(w_v, normed).astype(BF16)
        gate = jax.nn.sigmoid(dot_nt(w_g, normed).astype(BF16).astype(F32))
        updates = []
        for t in range(tiles):
            cs = slice(t * LANES, (t + 1) * LANES)
            q_t = q[:, cs]
            spread = jnp.concatenate(
                [jnp.where(head_of == h, q_t, 0.0).astype(BF16) for h in range(heads)], 1
            )
            scores = dot_nn(k, spread)
            gated = []
            for h in range(heads):
                s = scores[:, h * LANES : (h + 1) * LANES] * scaling + bias_s[h, :, cs]
                e = jnp.exp(s - jnp.max(s, 0, keepdims=True))
                total = jnp.sum(e, 0, keepdims=True)
                mine = slice(h * dim, (h + 1) * dim)
                o = dot_nn(v[mine], e.astype(BF16)) * (1.0 / total)
                gated.append((gate[mine, cs] * o).astype(BF16))
            updates.append(dot_tn(jnp.concatenate(gated, 0), w_out).astype(BF16))
        update = jnp.concatenate(updates, 0)
        if not fused:
            out_ref[j] = update
            second_ref[j] = x_s[j]
            return
        new = (x_s[j].astype(F32) + update.astype(F32)).astype(BF16)
        second_ref[j] = (dot_nt(w_dist, new) + d_bias).astype(BF16)
        new_s[j] = new.astype(F32)

    if tiles == 1:
        for j in range(rows):
            column(j)
    else:
        pl.loop(0, rows)(column)
    if fused:
        for s in range(peers):
            at = pl.ds(pl.multiple_of((me ^ s) * rows, rows), rows)
            outs[s][...] = new_s[:, at, :].reshape(base, chan).astype(BF16)


def finish_kernel(peers, *refs):
    recv, (mirror_ref, wd_ref, db_ref, new_ref, dist_ref) = refs[:peers], refs[peers:]
    rows, n, chan = new_ref.shape
    group = 2 * rows
    me = lax.axis_index("row")
    swap = swap_matrix(rows, me & 1)
    for s in range(0, peers, 2):
        at = pl.ds(pl.multiple_of(((me ^ s) // 2) * group, group), group)
        both = jnp.concatenate([recv[s][...], recv[s + 1][...]], 0)
        new_ref[:, at, :] = dot_nn(swap, both).astype(BF16).reshape(rows, group, chan)
    w_dist = wd_ref[...]
    d_bias = db_ref[:, :1]
    for i in range(rows):
        logits = (dot_nt(w_dist, new_ref[i]) + d_bias).astype(BF16)
        dist_ref[i] = (logits.astype(F32) + mirror_ref[i].astype(F32)).astype(BF16)


def call(kernel, outs, args, scratch=(), smem=(), hbm=(), flops=0):
    spaces = [pltpu.SMEM if i in smem else pltpu.HBM if i in hbm else pltpu.VMEM for i in range(len(args))]
    return pl.pallas_call(
        kernel,
        out_shape=[jax.ShapeDtypeStruct(s, d) for s, d in outs],
        in_specs=[pl.BlockSpec(memory_space=space) for space in spaces],
        out_specs=[pl.BlockSpec(memory_space=pltpu.VMEM)] * len(outs),
        scratch_shapes=list(scratch),
        compiler_params=pltpu.CompilerParams(vmem_limit_bytes=48 * 1024 * 1024),
    )(*args)


def exchange(messages):
    peers = len(messages)
    return [messages[0]] + [
        lax.ppermute(messages[s], "row", [(i, i ^ s) for i in range(peers)]) for s in range(1, peers)
    ]


def shards(
    pair_act, chain_id, residue_mask, norm_gain, w_proj, w_bias, chain_bias, w_out, w_dist, dist_bias,
):
    rows, n, chan = pair_act.shape
    peers = n // rows
    heads, dim = w_out.shape[0], w_out.shape[1]
    bins = w_dist.shape[1]
    tiles = n // LANES
    fused = lax.axis_size("head") == 1
    gain = norm_gain[None, :]
    base = rows * rows
    length = base + tiles * heads * rows

    wb_rows = jnp.repeat(w_bias.T, rows, axis=0)
    packed = call(
        functools.partial(pack_kernel, peers),
        [((length, chan), BF16)] * peers,
        [pair_act, gain, wb_rows],
        scratch=[
            pltpu.VMEM(pair_act.shape, BF16),
            pltpu.VMEM(gain.shape, F32),
            pltpu.VMEM(wb_rows.shape, BF16),
            pltpu.VMEM(pair_act.shape, F32),
            pltpu.SemaphoreType.DMA((rows + 2,)),
        ],
        hbm=(0, 1, 2),
    )
    received = exchange(packed)
    term, w_types, db_col = call(
        functools.partial(prepare_kernel, heads),
        [((heads, n, n), F32), ((4 * heads * dim, chan), BF16), ((bins, LANES), F32)],
        [chain_id[None, :], residue_mask[None, :], chain_bias, w_proj, dist_bias[None, :]],
        smem=(2,),
    )
    wd_t = w_dist.T
    if fused:
        outs = [((base, chan), BF16)] * peers + [((rows, bins, n), BF16)]
    else:
        outs = [((rows, n, chan), BF16), ((rows, n, chan), BF16)]
    scratch = [
        pltpu.VMEM((rows, n, chan), BF16),
        pltpu.VMEM((rows, n, chan), BF16),
        pltpu.VMEM((heads, n, n), F32),
    ]
    if fused:
        scratch.append(pltpu.VMEM((rows, n, chan), F32))
    result = call(
        functools.partial(attend_kernel, heads, fused, peers),
        outs,
        [*received, term, gain, w_types, w_out.reshape(heads * dim, chan), wd_t, db_col],
        scratch=scratch,
    )
    if fused:
        to_rows, mirror = result[:peers], result[peers]
    else:
        update = lax.psum(result[0], "head").astype(F32)
        new = (result[1].astype(F32) + update).astype(BF16)
        logits = jnp.einsum("cb,jic->jbi", w_dist, new, preferred_element_type=F32)
        mirror = (logits + dist_bias[None, :, None]).astype(BF16)
        blocks = new.reshape(rows, peers, rows, chan).transpose(1, 0, 2, 3).reshape(peers, base, chan)
        me = lax.axis_index("row")
        to_rows = [lax.dynamic_index_in_dim(blocks, me ^ s, 0, keepdims=False) for s in range(peers)]
    arrived = exchange(to_rows)
    new_rows, dist = call(
        functools.partial(finish_kernel, peers),
        [((rows, n, chan), BF16), ((rows, bins, n), BF16)],
        [*arrived, mirror, wd_t, db_col],
    )
    return new_rows, dist.transpose(0, 2, 1)


def solution(mesh):
    in_specs = (
        P(("dp", "row"), None, None),
        P("dp"),
        P("dp"),
        P(),
        P(None, "head", None),
        P(None, "head"),
        P(None, "head"),
        P("head", None, None),
        P(),
        P(),
    )
    out_specs = (P(("dp", "row"), None, None), P(("dp", "row"), None, None))
    return jax.shard_map(shards, mesh=mesh, in_specs=in_specs, out_specs=out_specs, check_vma=False)
```

```python
import functools

import jax
import jax.numpy as jnp
from jax import lax
from jax.experimental import pallas as pl
from jax.experimental.pallas import tpu as pltpu
from jax.sharding import PartitionSpec as P

LANES = 128
F32 = jnp.float32
BF16 = jnp.bfloat16


def dot_nt(a, b):
    return lax.dot_general(a, b, (((1,), (1,)), ((), ())), preferred_element_type=F32)


def dot_tn(a, b):
    return lax.dot_general(a, b, (((0,), (0,)), ((), ())), preferred_element_type=F32)


def dot_nn(a, b):
    return jnp.dot(a, b, preferred_element_type=F32)


def centring(chan):
    row = lax.broadcasted_iota(jnp.int32, (chan, chan), 0)
    col = lax.broadcasted_iota(jnp.int32, (chan, chan), 1)
    return (jnp.where(row == col, 1.0, 0.0) - 1.0 / chan).astype(BF16)


def layer_norm(values, centre, gain):
    centered = dot_nn(values, centre)
    variance = jnp.mean(centered * centered, -1, keepdims=True)
    return (centered * lax.rsqrt(variance + 1e-05) * gain).astype(BF16)


def swap_matrix(rows):
    size = 2 * rows * rows
    out = lax.broadcasted_iota(jnp.int32, (size, size), 0)
    col = lax.broadcasted_iota(jnp.int32, (size, size), 1)
    b, rest = out // (2 * rows), out % (2 * rows)
    wanted = (rest // rows) * (rows * rows) + (rest % rows) * rows + b
    return jnp.where(col == wanted, 1.0, 0.0).astype(BF16)


def pack_kernel(x_ref, out_ref):
    rows, n, chan = x_ref.shape
    peers = n // rows
    for pair in range(rows // 2):
        both = [x_ref[k].astype(F32).reshape(peers, rows, chan) for k in (2 * pair, 2 * pair + 1)]
        out_ref[:, 2 * rows * pair : 2 * rows * (pair + 1), :] = jnp.concatenate(both, 1).astype(BF16)


def bias_kernel(x_ref, gain_ref, wb_ref, out_ref):
    rows, n, chan = x_ref.shape
    wb = wb_ref[...]
    owner = lax.broadcasted_iota(jnp.int32, wb.shape, 0) % rows
    gain = gain_ref[...]
    centre = centring(chan)
    bias = jnp.zeros((wb.shape[0], n), F32)
    for k in range(rows):
        mine = jnp.where(owner == k, wb, jnp.zeros_like(wb))
        bias = bias + dot_nt(mine, layer_norm(x_ref[k], centre, gain))
    bias = bias.astype(BF16)
    step = wb.shape[0]
    for t in range(n // LANES):
        out_ref[0, t * step : (t + 1) * step] = bias[:, t * LANES : (t + 1) * LANES]


def prepare_kernel(heads, chain_ref, mask_ref, cb_ref, w_ref, db_ref, term_ref, wt_ref, dbc_ref):
    n = chain_ref.shape[1]
    tiles = n // LANES
    chan = w_ref.shape[0]
    dim = w_ref.shape[2] // 4
    width = heads * dim

    def column_of(row):
        return jnp.transpose(jnp.broadcast_to(row, (LANES, LANES)))

    for kt in range(tiles):
        ks = slice(kt * LANES, (kt + 1) * LANES)
        chain_k = column_of(chain_ref[:, ks].astype(F32))
        mask_k = (column_of(mask_ref[:, ks].astype(F32)) - 1.0) * 1000000000.0
        for it in range(tiles):
            cs = slice(it * LANES, (it + 1) * LANES)
            same = chain_k == chain_ref[:, cs].astype(F32)
            for h in range(heads):
                term_ref[h, ks, cs] = jnp.where(same, cb_ref[1, h], cb_ref[0, h]) + mask_k
    for h in range(heads):
        turned = jnp.transpose(w_ref[:, h, :].astype(F32)).astype(BF16)
        for place, kind in enumerate((0, 2, 3, 1)):
            start = place * width + h * dim
            wt_ref[start : start + dim] = turned[kind * dim : (kind + 1) * dim]
    bins = dbc_ref.shape[0]
    db_rows = jnp.broadcast_to(jnp.concatenate([db_ref[...], db_ref[...]], 1)[:, :LANES], (LANES, LANES))
    dbc_ref[...] = jnp.transpose(db_rows)[:bins]


def attend_kernel(
    heads, fused,
    recv_ref, here_ref, there_ref, term_ref, gain_ref, w_ref, wo_ref, wd_ref, db_ref,
    out_ref, second_ref, x_s, n_s, bias_s, spread_s, k_s, v_s, g_s,
):
    peers = recv_ref.shape[0]
    rows, n, chan = x_s.shape
    tiles = n // LANES
    dim = w_ref.shape[0] // (4 * heads)
    width = heads * dim
    step = heads * rows
    gain = gain_ref[...]
    swap = swap_matrix(rows)
    centre = centring(chan)
    group = 2 * rows
    me = lax.axis_index("row")

    for pair in range(peers // 2):
        at = slice(pair * group, (pair + 1) * group)
        both = recv_ref[2 * pair : 2 * pair + 2].reshape(2 * rows * rows, chan)
        x = dot_nn(swap, both).astype(BF16)
        x_s[:, at, :] = x.reshape(rows, group, chan)
        n_s[:, at, :] = layer_norm(x, centre, gain).reshape(rows, group, chan)

    w_qvg, w_k = w_ref[: 3 * width], w_ref[3 * width :]
    zero = jnp.zeros((dim, LANES), BF16)

    def project(j):
        normed = n_s[j]
        qvg = dot_nt(w_qvg, normed).astype(BF16)
        k_s[j] = dot_nt(normed, w_k).astype(BF16)
        v_s[j] = qvg[width : 2 * width]
        g_s[j] = jax.nn.sigmoid(qvg[2 * width :].astype(F32))
        for t in range(tiles):
            for h in range(heads):
                for other in range(heads):
                    block = qvg[h * dim : (h + 1) * dim, t * LANES : (t + 1) * LANES] if h == other else zero
                    spread_s[j, t, other * dim : (other + 1) * dim, h * LANES : (h + 1) * LANES] = block

    if tiles == 1:
        for j in range(rows):
            project(j)
    else:
        pl.loop(0, rows)(project)

    for half, ref in enumerate((here_ref, there_ref)):
        count = peers // 2
        for b in range(count):
            offset = half
            for bit in range(count.bit_length() - 1):
                offset += (count >> bit) * ((b >> bit) & 1)
            extra = ref[b].astype(F32)
            at = pl.ds(pl.multiple_of((me ^ offset) * rows, rows), rows)
            for t in range(tiles):
                cs = slice(t * LANES, (t + 1) * LANES)
                for h in range(heads):
                    start = t * step + h * rows
                    bias_s[h, at, cs] = extra[start : start + rows] + term_ref[h, at, cs]

    scaling = dim ** (-0.5)
    w_out = wo_ref[...]
    w_dist = wd_ref[...]
    d_bias = db_ref[:, :1]

    def score(j, t):
        return dot_nn(k_s[j], spread_s[j, t])

    def attend(j, t, scores):
        cs = slice(t * LANES, (t + 1) * LANES)
        gated = []
        for first in range(0, heads, 2):
            weights, scales = [], []
            for h in (first, first + 1):
                s = scores[:, h * LANES : (h + 1) * LANES] * scaling + bias_s[h, :, cs]
                e = jnp.exp(s - jnp.max(s, 0, keepdims=True))
                scales.append(1.0 / jnp.sum(e, 0, keepdims=True))
                weights.append(e.astype(BF16))
            o = dot_nn(v_s[j, first * dim : (first + 2) * dim, :], jnp.concatenate(weights, 1))
            for side in range(2):
                h = first + side
                part = o[side * dim : (side + 1) * dim, side * LANES : (side + 1) * LANES]
                gated.append((g_s[j, h * dim : (h + 1) * dim, cs] * (part * scales[side])).astype(BF16))
        return dot_tn(jnp.concatenate(gated, 0), w_out).astype(BF16)

    def residual(j, update):
        new = (x_s[j].astype(F32) + update.astype(F32)).astype(BF16)
        second_ref[j] = (dot_nt(w_dist, new) + d_bias).astype(BF16)
        return new.astype(F32).reshape(peers, rows, chan)

    if not fused:

        @pl.loop(0, rows)
        def _(j):
            for t in range(tiles):
                out_ref[j, t * LANES : (t + 1) * LANES] = attend(j, t, score(j, t))
            second_ref[j] = x_s[j]

        return

    both = []
    scores = score(0, 0)
    for j in range(rows):
        later = score(j + 1, 0) if j + 1 < rows and tiles == 1 else None
        updates = [attend(j, 0, scores)]
        for t in range(1, tiles):
            updates.append(attend(j, t, score(j, t)))
        both.append(residual(j, jnp.concatenate(updates, 0)))
        scores = later if tiles == 1 or j + 1 == rows else score(j + 1, 0)
        if j % 2:
            out_ref[:, (j - 1) * rows : (j + 1) * rows, :] = jnp.concatenate(both, 1).astype(BF16)
            both = []


def finish_kernel(recv_ref, mirror_ref, wd_ref, db_ref, new_ref, dist_ref):
    peers, _, chan = recv_ref.shape
    rows = new_ref.shape[0]
    group = 2 * rows
    swap = swap_matrix(rows)

    def unpack(pair):
        at = pl.ds(pl.multiple_of(pair * group, group), group)
        both = recv_ref[pl.ds(2 * pair, 2)].reshape(2 * rows * rows, chan)
        new_ref[:, at, :] = dot_nn(swap, both).astype(BF16).reshape(rows, group, chan)

    for pair in range(peers // 2):
        unpack(pair)
    w_dist = wd_ref[...]
    d_bias = db_ref[:, :1]
    for i in range(rows):
        logits = (dot_nt(w_dist, new_ref[i]) + d_bias).astype(BF16)
        dist_ref[i] = (logits.astype(F32) + mirror_ref[i].astype(F32)).astype(BF16)


def call(kernel, outs, args, scratch=(), smem=(), limit=48):
    specs = [pl.BlockSpec(memory_space=pltpu.SMEM if i in smem else pltpu.VMEM) for i in range(len(args))]
    return pl.pallas_call(
        kernel,
        out_shape=[jax.ShapeDtypeStruct(s, d) for s, d in outs],
        in_specs=specs,
        out_specs=[pl.BlockSpec(memory_space=pltpu.VMEM)] * len(outs),
        scratch_shapes=list(scratch),
        compiler_params=pltpu.CompilerParams(vmem_limit_bytes=limit * 1024 * 1024),
    )(*args)


def all_to_all(blocks):
    return lax.all_to_all(blocks, "row", split_axis=0, concat_axis=0, tiled=True)


def gather_halves(block, peers):
    held = block
    bit = peers // 2
    while True:
        other = lax.ppermute(held, "row", [(i, i ^ bit) for i in range(peers)])
        if bit == 1:
            return held, other
        held = jnp.concatenate([held, other], 0)
        bit //= 2


def shards(
    pair_act, chain_id, residue_mask, norm_gain, w_proj, w_bias, chain_bias, w_out, w_dist, dist_bias,
):
    rows, n, chan = pair_act.shape
    peers = n // rows
    heads, dim = w_out.shape[0], w_out.shape[1]
    bins = w_dist.shape[1]
    tiles = n // LANES
    fused = lax.axis_size("head") == 1
    gain = norm_gain[None, :]
    base = rows * rows

    (packed,) = call(pack_kernel, [((peers, base, chan), BF16)], [pair_act], limit=60)
    received = all_to_all(packed)
    pair_act, _ = lax.optimization_barrier((pair_act, packed))
    wb_rows = jnp.repeat(w_bias.T, rows, axis=0)
    (bias,) = call(bias_kernel, [((1, tiles * heads * rows, LANES), BF16)], [pair_act, gain, wb_rows])
    here, there = gather_halves(bias, peers)
    term, w_types, db_col = call(
        functools.partial(prepare_kernel, heads),
        [((heads, n, n), F32), ((4 * heads * dim, chan), BF16), ((bins, LANES), F32)],
        [chain_id[None, :], residue_mask[None, :], chain_bias, w_proj, dist_bias[None, :]],
        smem=(2,),
    )
    wd_t = w_dist.T
    if fused:
        outs = [((peers, base, chan), BF16), ((rows, bins, n), BF16)]
    else:
        outs = [((rows, n, chan), BF16), ((rows, n, chan), BF16)]
    first, second = call(
        functools.partial(attend_kernel, heads, fused),
        outs,
        [received, here, there, term, gain, w_types, w_out.reshape(heads * dim, chan), wd_t, db_col],
        scratch=[
            pltpu.VMEM((rows, n, chan), BF16),
            pltpu.VMEM((rows, n, chan), BF16),
            pltpu.VMEM((heads, n, n), F32),
            pltpu.VMEM((rows, tiles, heads * dim, heads * LANES), BF16),
            pltpu.VMEM((rows, n, heads * dim), BF16),
            pltpu.VMEM((rows, heads * dim, n), BF16),
            pltpu.VMEM((rows, heads * dim, n), F32),
        ],
    )
    if fused:
        to_rows, mirror = first, second
    else:
        update = lax.psum(first, "head").astype(F32)
        new = (second.astype(F32) + update).astype(BF16)
        logits = jnp.einsum("cb,jic->jbi", w_dist, new, preferred_element_type=F32)
        mirror = (logits + dist_bias[None, :, None]).astype(BF16)
        to_rows = new.reshape(rows, peers, rows, chan).transpose(1, 0, 2, 3).reshape(peers, base, chan)
    arrived = all_to_all(to_rows)
    new_rows, dist = call(
        finish_kernel,
        [((rows, n, chan), BF16), ((rows, bins, n), BF16)],
        [arrived, mirror, wd_t, db_col],
    )
    return new_rows, dist.transpose(0, 2, 1)


def solution(mesh):
    in_specs = (
        P(("dp", "row"), None, None),
        P("dp"),
        P("dp"),
        P(),
        P(None, "head", None),
        P(None, "head"),
        P(None, "head"),
        P("head", None, None),
        P(),
        P(),
    )
    out_specs = (P(("dp", "row"), None, None), P(("dp", "row"), None, None))
    return jax.shard_map(shards, mesh=mesh, in_specs=in_specs, out_specs=out_specs, check_vma=False)
```

```python
import functools

import jax
import jax.numpy as jnp
from jax import lax
from jax.experimental import pallas as pl
from jax.experimental.pallas import tpu as pltpu
from jax.sharding import PartitionSpec as P

LANES = 128
F32 = jnp.float32
BF16 = jnp.bfloat16


def dot_nt(a, b):
    return lax.dot_general(a, b, (((1,), (1,)), ((), ())), preferred_element_type=F32)


def dot_tn(a, b):
    return lax.dot_general(a, b, (((0,), (0,)), ((), ())), preferred_element_type=F32)


def dot_nn(a, b):
    return jnp.dot(a, b, preferred_element_type=F32)


def centring(chan):
    row = lax.broadcasted_iota(jnp.int32, (chan, chan), 0)
    col = lax.broadcasted_iota(jnp.int32, (chan, chan), 1)
    return (jnp.where(row == col, 1.0, 0.0) - 1.0 / chan).astype(BF16)


def layer_norm(values, centre, gain):
    centered = dot_nn(values, centre)
    variance = jnp.mean(centered * centered, -1, keepdims=True)
    return (centered * lax.rsqrt(variance + 1e-05) * gain).astype(BF16)


def swap_matrix(rows, flip):
    size = 2 * rows * rows
    out = lax.broadcasted_iota(jnp.int32, (size, size), 0)
    col = lax.broadcasted_iota(jnp.int32, (size, size), 1)
    b, rest = out // (2 * rows), out % (2 * rows)
    wanted = ((rest // rows) ^ flip) * (rows * rows) + (rest % rows) * rows + b
    return jnp.where(col == wanted, 1.0, 0.0).astype(BF16)


def pack_kernel(x_hbm, keep_ref, send_ref, x_ref, sems):
    rows, n, chan = x_ref.shape
    chips = n // (2 * rows)
    core = lax.axis_index("row") % 2
    copies = [pltpu.make_async_copy(x_hbm.at[k], x_ref.at[k], sems.at[k]) for k in range(rows)]
    for copy in copies:
        copy.start()
    for pair in range(rows // 2):
        own, away = [], []
        for k in (2 * pair, 2 * pair + 1):
            copies[k].wait()
            x = x_ref[k].astype(F32).reshape(chips, 2, rows, chan)
            own.append(jnp.where(core == 0, x[:, 0], x[:, 1]))
            away.append(jnp.where(core == 0, x[:, 1], x[:, 0]))
        at = slice(2 * rows * pair, 2 * rows * (pair + 1))
        keep_ref[:, at, :] = jnp.concatenate(own, 1).astype(BF16)
        send_ref[:, at, :] = jnp.concatenate(away, 1).astype(BF16)


def bias_kernel(x_ref, gain_ref, wb_ref, out_ref):
    rows, n, chan = x_ref.shape
    wb = wb_ref[...]
    owner = lax.broadcasted_iota(jnp.int32, wb.shape, 0) % rows
    gain = gain_ref[...]
    centre = centring(chan)
    bias = jnp.zeros((wb.shape[0], n), F32)
    for k in range(rows):
        mine = jnp.where(owner == k, wb, jnp.zeros_like(wb))
        bias = bias + dot_nt(mine, layer_norm(x_ref[k], centre, gain))
    bias = bias.astype(BF16)
    step = wb.shape[0]
    for t in range(n // LANES):
        for chip in range(out_ref.shape[0]):
            out_ref[chip, t * step : (t + 1) * step] = bias[:, t * LANES : (t + 1) * LANES]


def prepare_kernel(heads, chain_ref, mask_ref, cb_ref, w_ref, db_ref, term_ref, wt_ref, dbc_ref):
    n = chain_ref.shape[1]
    tiles = n // LANES
    chan = w_ref.shape[0]
    dim = w_ref.shape[2] // 4
    width = heads * dim

    def column_of(row):
        return jnp.transpose(jnp.broadcast_to(row, (LANES, LANES)))

    for kt in range(tiles):
        ks = slice(kt * LANES, (kt + 1) * LANES)
        chain_k = column_of(chain_ref[:, ks].astype(F32))
        mask_k = (column_of(mask_ref[:, ks].astype(F32)) - 1.0) * 1000000000.0
        for it in range(tiles):
            cs = slice(it * LANES, (it + 1) * LANES)
            same = chain_k == chain_ref[:, cs].astype(F32)
            for h in range(heads):
                term_ref[h, ks, cs] = jnp.where(same, cb_ref[1, h], cb_ref[0, h]) + mask_k
    for h in range(heads):
        turned = jnp.transpose(w_ref[:, h, :].astype(F32)).astype(BF16)
        for place, kind in enumerate((0, 2, 3, 1)):
            start = place * width + h * dim
            wt_ref[start : start + dim] = turned[kind * dim : (kind + 1) * dim]
    bins = dbc_ref.shape[0]
    db_rows = jnp.broadcast_to(jnp.concatenate([db_ref[...], db_ref[...]], 1)[:, :LANES], (LANES, LANES))
    dbc_ref[...] = jnp.transpose(db_rows)[:bins]


def project_kernel(heads, recv_ref, gain_ref, w_ref, x_s, spread_s, k_s, v_s, g_s, n_s):
    chips = recv_ref.shape[0]
    rows, n, chan = x_s.shape
    tiles = n // LANES
    dim = w_ref.shape[0] // (4 * heads)
    width = heads * dim
    base = rows * rows
    gain = gain_ref[...]
    swap = swap_matrix(rows, lax.axis_index("row") % 2)
    centre = centring(chan)
    group = 2 * rows

    for chip in range(chips):
        at = slice(chip * group, (chip + 1) * group)
        x = dot_nn(swap, recv_ref[chip, : 2 * base]).astype(BF16)
        x_s[:, at, :] = x.reshape(rows, group, chan)
        n_s[:, at, :] = layer_norm(x, centre, gain).reshape(rows, group, chan)

    w_qvg, w_k = w_ref[: 3 * width], w_ref[3 * width :]
    zero = jnp.zeros((dim, LANES), BF16)

    def project(j):
        normed = n_s[j]
        qvg = dot_nt(w_qvg, normed).astype(BF16)
        k_s[j] = dot_nt(normed, w_k).astype(BF16)
        v_s[j] = qvg[width : 2 * width]
        g_s[j] = jax.nn.sigmoid(qvg[2 * width :].astype(F32))
        for t in range(tiles):
            for h in range(heads):
                for other in range(heads):
                    block = qvg[h * dim : (h + 1) * dim, t * LANES : (t + 1) * LANES] if h == other else zero
                    spread_s[j, t, other * dim : (other + 1) * dim, h * LANES : (h + 1) * LANES] = block

    if tiles == 1:
        for j in range(rows):
            project(j)
    else:
        pl.loop(0, rows)(project)


def attend_kernel(
    heads, fused,
    recv_ref, other_ref, term_ref, wo_ref, wd_ref, db_ref, x_s, spread_s, k_s, v_s, g_s,
    out_ref, *refs,
):
    if fused:
        away_ref, second_ref, bias_s = refs
    else:
        (bias_s,) = refs
    chips = recv_ref.shape[0]
    rows, n, chan = x_s.shape
    tiles = n // LANES
    dim = wo_ref.shape[0] // heads
    step = heads * rows
    base = rows * rows
    core = lax.axis_index("row") % 2

    for chip in range(chips):
        for block, owner in ((recv_ref[chip, 2 * base :], core), (other_ref[chip], 1 - core)):
            extra = block.astype(F32)
            at = pl.ds(pl.multiple_of((2 * chip + owner) * rows, rows), rows)
            for t in range(tiles):
                cs = slice(t * LANES, (t + 1) * LANES)
                for h in range(heads):
                    start = t * step + h * rows
                    bias_s[h, at, cs] = extra[start : start + rows] + term_ref[h, at, cs]

    scaling = dim ** (-0.5)
    w_out = wo_ref[...]
    w_dist = wd_ref[...]
    d_bias = db_ref[:, :1]

    def score(j, t):
        return dot_nn(k_s[j], spread_s[j, t])

    def attend(j, t, scores):
        cs = slice(t * LANES, (t + 1) * LANES)
        gated = []
        for first in range(0, heads, 2):
            weights, scales = [], []
            for h in (first, first + 1):
                s = scores[:, h * LANES : (h + 1) * LANES] * scaling + bias_s[h, :, cs]
                e = jnp.exp(s - jnp.max(s, 0, keepdims=True))
                scales.append(1.0 / jnp.sum(e, 0, keepdims=True))
                weights.append(e.astype(BF16))
            o = dot_nn(v_s[j, first * dim : (first + 2) * dim, :], jnp.concatenate(weights, 1))
            for side in range(2):
                h = first + side
                part = o[side * dim : (side + 1) * dim, side * LANES : (side + 1) * LANES]
                gated.append((g_s[j, h * dim : (h + 1) * dim, cs] * (part * scales[side])).astype(BF16))
        return dot_tn(jnp.concatenate(gated, 0), w_out).astype(BF16)

    def residual(j, update):
        new = (x_s[j].astype(F32) + update.astype(F32)).astype(BF16)
        second_ref[j] = (dot_nt(w_dist, new) + d_bias).astype(BF16)
        return new.astype(F32).reshape(chips, 2, rows, chan)

    if not fused:

        @pl.loop(0, rows)
        def _(j):
            for t in range(tiles):
                out_ref[j, t * LANES : (t + 1) * LANES] = attend(j, t, score(j, t))

        return

    own, away = [], []
    scores = score(0, 0)
    for j in range(rows):
        later = score(j + 1, 0) if j + 1 < rows and tiles == 1 else None
        updates = [attend(j, 0, scores)]
        for t in range(1, tiles):
            updates.append(attend(j, t, score(j, t)))
        new = residual(j, jnp.concatenate(updates, 0))
        own.append(jnp.where(core == 0, new[:, 0], new[:, 1]))
        away.append(jnp.where(core == 0, new[:, 1], new[:, 0]))
        scores = later if tiles == 1 or j + 1 == rows else score(j + 1, 0)
        if j % 2:
            at = slice((j - 1) * rows, (j + 1) * rows)
            out_ref[:, at, :] = jnp.concatenate(own, 1).astype(BF16)
            away_ref[:, at, :] = jnp.concatenate(away, 1).astype(BF16)
            own, away = [], []


def finish_kernel(recv_ref, mirror_ref, wd_ref, db_ref, new_ref, dist_ref):
    chips, _, chan = recv_ref.shape
    rows = new_ref.shape[0]
    group = 2 * rows
    swap = swap_matrix(rows, lax.axis_index("row") % 2)
    for chip in range(chips):
        at = slice(chip * group, (chip + 1) * group)
        new_ref[:, at, :] = dot_nn(swap, recv_ref[chip]).astype(BF16).reshape(rows, group, chan)
    w_dist = wd_ref[...]
    d_bias = db_ref[:, :1]
    for i in range(rows):
        logits = (dot_nt(w_dist, new_ref[i]) + d_bias).astype(BF16)
        dist_ref[i] = (logits.astype(F32) + mirror_ref[i].astype(F32)).astype(BF16)


def call(kernel, outs, args, scratch=(), smem=(), hbm=(), limit=48):
    spaces = [pltpu.SMEM if i in smem else pl.ANY if i in hbm else pltpu.VMEM for i in range(len(args))]
    return pl.pallas_call(
        kernel,
        out_shape=[jax.ShapeDtypeStruct(s, d) for s, d in outs],
        in_specs=[pl.BlockSpec(memory_space=space) for space in spaces],
        out_specs=[pl.BlockSpec(memory_space=pltpu.VMEM)] * len(outs),
        scratch_shapes=list(scratch),
        compiler_params=pltpu.CompilerParams(vmem_limit_bytes=limit * 1024 * 1024),
    )(*args)


def swap_cores(values):
    peers = lax.axis_size("row")
    return lax.ppermute(values, "row", [(i, i ^ 1) for i in range(peers)])


def all_to_all(blocks):
    peers = lax.axis_size("row")
    groups = [list(range(core, peers, 2)) for core in range(2)]
    return lax.all_to_all(blocks, "row", split_axis=0, concat_axis=0, tiled=True, axis_index_groups=groups)


def shards(
    pair_act, chain_id, residue_mask, norm_gain, w_proj, w_bias, chain_bias, w_out, w_dist, dist_bias,
):
    rows, n, chan = pair_act.shape
    chips = n // (2 * rows)
    heads, dim = w_out.shape[0], w_out.shape[1]
    bins = w_dist.shape[1]
    tiles = n // LANES
    width = heads * dim
    fused = lax.axis_size("head") == 1
    gain = norm_gain[None, :]
    base = rows * rows
    extra = tiles * heads * rows

    keep, send = call(
        pack_kernel,
        [((chips, base, chan), BF16)] * 2,
        [pair_act],
        scratch=[pltpu.VMEM(pair_act.shape, BF16), pltpu.SemaphoreType.DMA((rows,))],
        hbm=(0,),
        limit=60,
    )
    swapped = swap_cores(send)
    wb_rows = jnp.repeat(w_bias.T, rows, axis=0)
    late_pair, _ = lax.optimization_barrier((pair_act, keep))
    (bias,) = call(bias_kernel, [((chips, extra, LANES), BF16)], [late_pair, gain, wb_rows])
    received = all_to_all(jnp.concatenate([keep, swapped, bias], 1))
    other_bias = swap_cores(received[:, 2 * base :])
    term, w_types, db_col = call(
        functools.partial(prepare_kernel, heads),
        [((heads, n, n), F32), ((4 * width, chan), BF16), ((bins, LANES), F32)],
        [chain_id[None, :], residue_mask[None, :], chain_bias, w_proj, dist_bias[None, :]],
        smem=(2,),
    )
    wd_t = w_dist.T
    x_cols, spread, keys, values, gates = call(
        functools.partial(project_kernel, heads),
        [
            ((rows, n, chan), BF16),
            ((rows, tiles, width, heads * LANES), BF16),
            ((rows, n, width), BF16),
            ((rows, width, n), BF16),
            ((rows, width, n), F32),
        ],
        [received, gain, w_types],
        scratch=[pltpu.VMEM((rows, n, chan), BF16)],
    )
    if fused:
        outs = [((chips, base, chan), BF16)] * 2 + [((rows, bins, n), BF16)]
    else:
        outs = [((rows, n, chan), BF16)]
    result = call(
        functools.partial(attend_kernel, heads, fused),
        outs,
        [
            received, other_bias, term, w_out.reshape(width, chan), wd_t, db_col,
            x_cols, spread, keys, values, gates,
        ],
        scratch=[pltpu.VMEM((heads, n, n), F32)],
    )
    if fused:
        keep, send, mirror = result
    else:
        update = lax.psum(result[0], "head").astype(F32)
        new = (x_cols.astype(F32) + update).astype(BF16)
        logits = jnp.einsum("cb,jic->jbi", w_dist, new, preferred_element_type=F32)
        mirror = (logits + dist_bias[None, :, None]).astype(BF16)
        blocks = new.reshape(rows, chips, 2, rows, chan).transpose(2, 1, 0, 3, 4).reshape(2, chips, base, chan)
        core = lax.axis_index("row") % 2
        keep, send = jnp.where(core == 0, blocks[0], blocks[1]), jnp.where(core == 0, blocks[1], blocks[0])
    arrived = all_to_all(jnp.concatenate([keep, swap_cores(send)], 1))
    new_rows, dist = call(
        finish_kernel,
        [((rows, n, chan), BF16), ((rows, bins, n), BF16)],
        [arrived, mirror, wd_t, db_col],
    )
    return new_rows, dist.transpose(0, 2, 1)


def solution(mesh):
    in_specs = (
        P(("dp", "row"), None, None),
        P("dp"),
        P("dp"),
        P(),
        P(None, "head", None),
        P(None, "head"),
        P(None, "head"),
        P("head", None, None),
        P(),
        P(),
    )
    out_specs = (P(("dp", "row"), None, None), P(("dp", "row"), None, None))
    return jax.shard_map(shards, mesh=mesh, in_specs=in_specs, out_specs=out_specs, check_vma=False)
```

```python
import functools

import jax
import jax.numpy as jnp
from jax import lax
from jax.experimental import pallas as pl
from jax.experimental.pallas import tpu as pltpu
from jax.sharding import PartitionSpec as P

LANES = 128
F32 = jnp.float32
BF16 = jnp.bfloat16


def dot_nt(a, b):
    return lax.dot_general(a, b, (((1,), (1,)), ((), ())), preferred_element_type=F32)


def dot_tn(a, b):
    return lax.dot_general(a, b, (((0,), (0,)), ((), ())), preferred_element_type=F32)


def dot_nn(a, b):
    return jnp.dot(a, b, preferred_element_type=F32)


def centring(chan):
    row = lax.broadcasted_iota(jnp.int32, (chan, chan), 0)
    col = lax.broadcasted_iota(jnp.int32, (chan, chan), 1)
    return (jnp.where(row == col, 1.0, 0.0) - 1.0 / chan).astype(BF16)


def layer_norm(values, centre, gain):
    centered = dot_nn(values, centre)
    variance = jnp.mean(centered * centered, -1, keepdims=True)
    return (centered * lax.rsqrt(variance + 1e-05) * gain).astype(BF16)


def swap_matrix(rows):
    size = 2 * rows * rows
    out = lax.broadcasted_iota(jnp.int32, (size, size), 0)
    col = lax.broadcasted_iota(jnp.int32, (size, size), 1)
    b, rest = out // (2 * rows), out % (2 * rows)
    wanted = (rest // rows) * (rows * rows) + (rest % rows) * rows + b
    return jnp.where(col == wanted, 1.0, 0.0).astype(BF16)


def pack_kernel(x_hbm, gain_hbm, wb_hbm, out_hbm, x_ref, gain_ref, wb_ref, out_ref, sems, out_sems):
    rows, n, chan = x_ref.shape
    peers = n // rows
    heads = wb_ref.shape[0]
    half = heads * rows // 2
    base = rows * rows
    fetch_gain = pltpu.make_async_copy(gain_hbm, gain_ref, sems.at[rows])
    fetch_wb = pltpu.make_async_copy(wb_hbm, wb_ref, sems.at[rows + 1])
    fetches = [pltpu.make_async_copy(x_hbm.at[k], x_ref.at[k], sems.at[k]) for k in range(rows)]
    for copy in (fetch_gain, fetch_wb, *fetches):
        copy.start()
    stores = []

    def store(first, count):
        at = pl.ds(first, count)
        copy = pltpu.make_async_copy(out_ref.at[:, at, :], out_hbm.at[:, at, :], out_sems.at[len(stores)])
        copy.start()
        stores.append(copy)

    centre = centring(chan)
    fetch_gain.wait()
    fetch_wb.wait()
    gain = gain_ref[...]
    wb = wb_ref[...].astype(F32)
    wb = jnp.concatenate([jnp.broadcast_to(wb[h : h + 1], (rows, chan)) for h in range(heads)], 0)
    owner = lax.broadcasted_iota(jnp.int32, wb.shape, 0) % rows
    bias = jnp.zeros((wb.shape[0], n), F32)
    for pair in range(rows // 2):
        both = []
        for k in (2 * pair, 2 * pair + 1):
            fetches[k].wait()
            x = x_ref[k]
            both.append(x.astype(F32).reshape(peers, rows, chan))
            mine = jnp.where(owner == k, wb, 0.0).astype(BF16)
            bias = bias + dot_nt(mine, layer_norm(x, centre, gain))
        out_ref[:, 2 * rows * pair : 2 * rows * (pair + 1), :] = jnp.concatenate(both, 1).astype(BF16)
        store(2 * rows * pair, 2 * rows)
    bias = bias.astype(BF16)
    for t in range(n // LANES):
        block = bias[:, t * LANES : (t + 1) * LANES]
        for d in range(peers):
            part = block[(d % 2) * half : (d % 2 + 1) * half]
            out_ref[d, base + t * half : base + (t + 1) * half] = part
    store(base, (n // LANES) * half)
    for copy in stores:
        copy.wait()


def prepare_kernel(
    heads,
    chain_ref, mask_ref, cb_ref, w_ref, db_ref, gain_ref, wo_ref, wd_ref,
    term_ref, wt_ref, dbc_ref, gain_out, wo_out, wd_out,
):
    gain_out[...] = gain_ref[...]
    wo_out[...] = wo_ref[...]
    wd_out[...] = wd_ref[...]
    n = chain_ref.shape[1]
    tiles = n // LANES
    chan = w_ref.shape[0]
    dim = w_ref.shape[2] // 4
    width = heads * dim

    def column_of(row):
        return jnp.transpose(jnp.broadcast_to(row, (LANES, LANES)))

    for kt in range(tiles):
        ks = slice(kt * LANES, (kt + 1) * LANES)
        chain_k = column_of(chain_ref[:, ks].astype(F32))
        mask_k = (column_of(mask_ref[:, ks].astype(F32)) - 1.0) * 1000000000.0
        for it in range(tiles):
            cs = slice(it * LANES, (it + 1) * LANES)
            same = chain_k == chain_ref[:, cs].astype(F32)
            for h in range(heads):
                term_ref[h, ks, cs] = jnp.where(same, cb_ref[1, h], cb_ref[0, h]) + mask_k
    for h in range(heads):
        turned = jnp.transpose(w_ref[:, h, :].astype(F32)).astype(BF16)
        for place, kind in enumerate((0, 2, 3, 1)):
            start = place * width + h * dim
            wt_ref[start : start + dim] = turned[kind * dim : (kind + 1) * dim]
    bins = dbc_ref.shape[0]
    db_rows = jnp.broadcast_to(jnp.concatenate([db_ref[...], db_ref[...]], 1)[:, :LANES], (LANES, LANES))
    dbc_ref[...] = jnp.transpose(db_rows)[:bins]


def project_kernel(heads, recv_ref, gain_ref, w_ref, x_s, spread_s, k_s, v_s, g_s, n_s):
    peers = recv_ref.shape[0]
    rows, n, chan = x_s.shape
    tiles = n // LANES
    dim = w_ref.shape[0] // (4 * heads)
    width = heads * dim
    base = rows * rows
    gain = gain_ref[...]
    swap = swap_matrix(rows)
    centre = centring(chan)
    group = 2 * rows

    for pair in range(peers // 2):
        at = slice(pair * group, (pair + 1) * group)
        both = jnp.concatenate([recv_ref[2 * pair, :base], recv_ref[2 * pair + 1, :base]], 0)
        x = dot_nn(swap, both).astype(BF16)
        x_s[:, at, :] = x.reshape(rows, group, chan)
        n_s[:, at, :] = layer_norm(x, centre, gain).reshape(rows, group, chan)

    w_qvg, w_k = w_ref[: 3 * width], w_ref[3 * width :]
    zero = jnp.zeros((dim, LANES), BF16)

    def project(j):
        normed = n_s[j]
        qvg = dot_nt(w_qvg, normed).astype(BF16)
        k_s[j] = dot_nt(normed, w_k).astype(BF16)
        v_s[j] = qvg[width : 2 * width]
        g_s[j] = jax.nn.sigmoid(qvg[2 * width :].astype(F32))
        for t in range(tiles):
            for h in range(heads):
                for other in range(heads):
                    block = qvg[h * dim : (h + 1) * dim, t * LANES : (t + 1) * LANES] if h == other else zero
                    spread_s[j, t, other * dim : (other + 1) * dim, h * LANES : (h + 1) * LANES] = block

    if tiles == 1:
        for j in range(rows):
            project(j)
    else:
        pl.loop(0, rows)(project)


def attend_kernel(
    heads, fused,
    recv_ref, other_ref, term_ref, wo_ref, wd_ref, db_ref, x_s, spread_s, k_s, v_s, g_s,
    out_ref, *refs,
):
    if fused:
        second_ref, bias_s = refs
    else:
        (bias_s,) = refs
    peers = recv_ref.shape[0]
    rows, n, chan = x_s.shape
    tiles = n // LANES
    dim = wo_ref.shape[0] // heads
    half = heads // 2
    base = rows * rows
    core = lax.axis_index("row") % 2

    for s in range(peers):
        at = slice(s * rows, (s + 1) * rows)
        for block, owner in ((recv_ref[s, base:], core), (other_ref[s], 1 - core)):
            extra = block.astype(F32)
            for t in range(tiles):
                cs = slice(t * LANES, (t + 1) * LANES)
                for h in range(half):
                    start = (t * half + h) * rows
                    head = owner * half + h
                    bias_s[head, at, cs] = extra[start : start + rows] + term_ref[head, at, cs]

    scaling = dim ** (-0.5)
    w_out = wo_ref[...]
    w_dist = wd_ref[...]
    d_bias = db_ref[:, :1]

    def score(j, t):
        return dot_nn(k_s[j], spread_s[j, t])

    def attend(j, t, scores):
        cs = slice(t * LANES, (t + 1) * LANES)
        gated = []
        for first in range(0, heads, 2):
            weights, scales = [], []
            for h in (first, first + 1):
                s = scores[:, h * LANES : (h + 1) * LANES] * scaling + bias_s[h, :, cs]
                e = jnp.exp(s - jnp.max(s, 0, keepdims=True))
                scales.append(1.0 / jnp.sum(e, 0, keepdims=True))
                weights.append(e.astype(BF16))
            o = dot_nn(v_s[j, first * dim : (first + 2) * dim, :], jnp.concatenate(weights, 1))
            for side in range(2):
                h = first + side
                part = o[side * dim : (side + 1) * dim, side * LANES : (side + 1) * LANES]
                gated.append((g_s[j, h * dim : (h + 1) * dim, cs] * (part * scales[side])).astype(BF16))
        return dot_tn(jnp.concatenate(gated, 0), w_out).astype(BF16)

    def residual(j, update):
        new = (x_s[j].astype(F32) + update.astype(F32)).astype(BF16)
        second_ref[j] = (dot_nt(w_dist, new) + d_bias).astype(BF16)
        return new.astype(F32).reshape(peers, rows, chan)

    if not fused:

        @pl.loop(0, rows)
        def _(j):
            for t in range(tiles):
                out_ref[j, t * LANES : (t + 1) * LANES] = attend(j, t, score(j, t))

        return

    both = []
    scores = score(0, 0)
    for j in range(rows):
        later = score(j + 1, 0) if j + 1 < rows and tiles == 1 else None
        updates = [attend(j, 0, scores)]
        for t in range(1, tiles):
            updates.append(attend(j, t, score(j, t)))
        both.append(residual(j, jnp.concatenate(updates, 0)))
        scores = later if tiles == 1 or j + 1 == rows else score(j + 1, 0)
        if j % 2:
            out_ref[:, (j - 1) * rows : (j + 1) * rows, :] = jnp.concatenate(both, 1).astype(BF16)
            both = []


def finish_kernel(recv_ref, mirror_ref, wd_ref, db_ref, new_hbm, dist_hbm, new_ref, dist_ref, sems):
    peers, _, chan = recv_ref.shape
    rows = new_ref.shape[0]
    group = 2 * rows
    swap = swap_matrix(rows)
    for pair in range(peers // 2):
        at = slice(pair * group, (pair + 1) * group)
        both = recv_ref[2 * pair : 2 * pair + 2].reshape(2 * rows * rows, chan)
        new_ref[:, at, :] = dot_nn(swap, both).astype(BF16).reshape(rows, group, chan)
    copies = [pltpu.make_async_copy(new_ref, new_hbm, sems.at[0])]
    copies[0].start()
    w_dist = wd_ref[...]
    d_bias = db_ref[:, :1]
    for i in range(rows):
        logits = (dot_nt(w_dist, new_ref[i]) + d_bias).astype(BF16)
        dist_ref[i] = (logits.astype(F32) + mirror_ref[i].astype(F32)).astype(BF16)
        if i % 2:
            at = pl.ds(i - 1, 2)
            copies.append(pltpu.make_async_copy(dist_ref.at[at], dist_hbm.at[at], sems.at[1 + i // 2]))
            copies[-1].start()
    for copy in copies:
        copy.wait()


def call(kernel, outs, args, scratch=(), smem=(), hbm=(), hbm_outs=False, limit=48):
    spaces = [pltpu.SMEM if i in smem else pl.ANY if i in hbm else pltpu.VMEM for i in range(len(args))]
    return pl.pallas_call(
        kernel,
        out_shape=[jax.ShapeDtypeStruct(s, d) for s, d in outs],
        in_specs=[pl.BlockSpec(memory_space=space) for space in spaces],
        out_specs=[pl.BlockSpec(memory_space=pl.ANY if hbm_outs else pltpu.VMEM)] * len(outs),
        scratch_shapes=list(scratch),
        compiler_params=pltpu.CompilerParams(vmem_limit_bytes=limit * 1024 * 1024),
    )(*args)


def swap_cores(values):
    peers = lax.axis_size("row")
    return lax.ppermute(values, "row", [(i, i ^ 1) for i in range(peers)])


def all_to_all(blocks):
    return lax.all_to_all(blocks, "row", split_axis=0, concat_axis=0, tiled=True)


def shards(
    pair_act, chain_id, residue_mask, norm_gain, w_proj, w_bias, chain_bias, w_out, w_dist, dist_bias,
):
    rows, n, chan = pair_act.shape
    peers = n // rows
    heads, dim = w_out.shape[0], w_out.shape[1]
    bins = w_dist.shape[1]
    tiles = n // LANES
    width = heads * dim
    fused = lax.axis_size("head") == 1
    gain = norm_gain[None, :]
    base = rows * rows
    length = base + tiles * heads * rows // 2

    (packed,) = call(
        pack_kernel,
        [((peers, length, chan), BF16)],
        [pair_act, gain, w_bias.T],
        scratch=[
            pltpu.VMEM(pair_act.shape, BF16),
            pltpu.VMEM(gain.shape, F32),
            pltpu.VMEM((heads, chan), BF16),
            pltpu.VMEM((peers, length, chan), BF16),
            pltpu.SemaphoreType.DMA((rows + 2,)),
            pltpu.SemaphoreType.DMA((rows // 2 + 1,)),
        ],
        hbm=(0, 1, 2),
        hbm_outs=True,
        limit=60,
    )
    received = all_to_all(packed)
    term, w_types, db_col, gain, w_out, wd_t = call(
        functools.partial(prepare_kernel, heads),
        [
            ((heads, n, n), F32), ((4 * width, chan), BF16), ((bins, LANES), F32),
            ((1, chan), F32), ((width, chan), BF16), ((bins, chan), BF16),
        ],
        [
            chain_id[None, :], residue_mask[None, :], chain_bias, w_proj, dist_bias[None, :],
            gain, w_out.reshape(width, chan), w_dist.T,
        ],
        smem=(2,),
    )
    other_bias = swap_cores(received[:, base:])
    x_cols, spread, keys, values, gates = call(
        functools.partial(project_kernel, heads),
        [
            ((rows, n, chan), BF16),
            ((rows, tiles, width, heads * LANES), BF16),
            ((rows, n, width), BF16),
            ((rows, width, n), BF16),
            ((rows, width, n), F32),
        ],
        [received, gain, w_types],
        scratch=[pltpu.VMEM((rows, n, chan), BF16)],
    )
    if fused:
        outs = [((peers, base, chan), BF16), ((rows, bins, n), BF16)]
    else:
        outs = [((rows, n, chan), BF16)]
    result = call(
        functools.partial(attend_kernel, heads, fused),
        outs,
        [received, other_bias, term, w_out, wd_t, db_col, x_cols, spread, keys, values, gates],
        scratch=[pltpu.VMEM((heads, n, n), F32)],
    )
    if fused:
        to_rows, mirror = result
    else:
        update = lax.psum(result[0], "head").astype(F32)
        new = (x_cols.astype(F32) + update).astype(BF16)
        logits = jnp.einsum("cb,jic->jbi", w_dist, new, preferred_element_type=F32)
        mirror = (logits + dist_bias[None, :, None]).astype(BF16)
        to_rows = new.reshape(rows, peers, rows, chan).transpose(1, 0, 2, 3).reshape(peers, base, chan)
    arrived = all_to_all(to_rows)
    new_rows, dist = call(
        finish_kernel,
        [((rows, n, chan), BF16), ((rows, bins, n), BF16)],
        [arrived, mirror, wd_t, db_col],
        scratch=[
            pltpu.VMEM((rows, n, chan), BF16),
            pltpu.VMEM((rows, bins, n), BF16),
            pltpu.SemaphoreType.DMA((1 + rows // 2,)),
        ],
        hbm_outs=True,
    )
    return new_rows, dist.transpose(0, 2, 1)


def solution(mesh):
    in_specs = (
        P(("dp", "row"), None, None),
        P("dp"),
        P("dp"),
        P(),
        P(None, "head", None),
        P(None, "head"),
        P(None, "head"),
        P("head", None, None),
        P(),
        P(),
    )
    out_specs = (P(("dp", "row"), None, None), P(("dp", "row"), None, None))
    return jax.shard_map(shards, mesh=mesh, in_specs=in_specs, out_specs=out_specs, check_vma=False)
```

```python
import functools

import jax
import jax.numpy as jnp
from jax import lax
from jax.experimental import pallas as pl
from jax.experimental.pallas import tpu as pltpu
from jax.sharding import PartitionSpec as P

LANES = 128
F32 = jnp.float32
BF16 = jnp.bfloat16


def dot_nt(a, b):
    return lax.dot_general(a, b, (((1,), (1,)), ((), ())), preferred_element_type=F32)


def dot_tn(a, b):
    return lax.dot_general(a, b, (((0,), (0,)), ((), ())), preferred_element_type=F32)


def dot_nn(a, b):
    return jnp.dot(a, b, preferred_element_type=F32)


def centring(chan):
    row = lax.broadcasted_iota(jnp.int32, (chan, chan), 0)
    col = lax.broadcasted_iota(jnp.int32, (chan, chan), 1)
    return (jnp.where(row == col, 1.0, 0.0) - 1.0 / chan).astype(BF16)


def layer_norm(values, centre, gain):
    centered = dot_nn(values, centre)
    variance = jnp.mean(centered * centered, -1, keepdims=True)
    return (centered * lax.rsqrt(variance + 1e-05) * gain).astype(BF16)


def swap_matrix(rows):
    size = 2 * rows * rows
    out = lax.broadcasted_iota(jnp.int32, (size, size), 0)
    col = lax.broadcasted_iota(jnp.int32, (size, size), 1)
    b, rest = out // (2 * rows), out % (2 * rows)
    wanted = (rest // rows) * (rows * rows) + (rest % rows) * rows + b
    return jnp.where(col == wanted, 1.0, 0.0).astype(BF16)


def pack_kernel(x_hbm, gain_hbm, wb_hbm, out_hbm, x_ref, gain_ref, wb_ref, out_ref, sems, out_sems):
    rows, n, chan = x_ref.shape
    peers = n // rows
    heads = wb_ref.shape[0]
    half = heads * rows // 2
    base = rows * rows
    fetch_gain = pltpu.make_async_copy(gain_hbm, gain_ref, sems.at[rows])
    fetch_wb = pltpu.make_async_copy(wb_hbm, wb_ref, sems.at[rows + 1])
    fetches = [pltpu.make_async_copy(x_hbm.at[k], x_ref.at[k], sems.at[k]) for k in range(rows)]
    for copy in (fetch_gain, fetch_wb, *fetches):
        copy.start()
    stores = []

    def store(first, count):
        at = pl.ds(first, count)
        copy = pltpu.make_async_copy(out_ref.at[:, at, :], out_hbm.at[:, at, :], out_sems.at[len(stores)])
        copy.start()
        stores.append(copy)

    for copy in (fetch_gain, fetch_wb, *fetches):
        copy.wait()
    for pair in range(rows // 2):
        both = [x_ref[k].astype(F32).reshape(peers, rows, chan) for k in (2 * pair, 2 * pair + 1)]
        out_ref[:, 2 * rows * pair : 2 * rows * (pair + 1), :] = jnp.concatenate(both, 1).astype(BF16)
    store(0, base)
    centre = centring(chan)
    gain = gain_ref[...]
    wb = wb_ref[...].astype(F32)
    wb = jnp.concatenate([jnp.broadcast_to(wb[h : h + 1], (rows, chan)) for h in range(heads)], 0)
    owner = lax.broadcasted_iota(jnp.int32, wb.shape, 0) % rows
    bias = jnp.zeros((wb.shape[0], n), F32)
    for k in range(rows):
        mine = jnp.where(owner == k, wb, 0.0).astype(BF16)
        bias = bias + dot_nt(mine, layer_norm(x_ref[k], centre, gain))
    bias = bias.astype(BF16)
    for t in range(n // LANES):
        block = bias[:, t * LANES : (t + 1) * LANES]
        for d in range(peers):
            part = block[(d % 2) * half : (d % 2 + 1) * half]
            out_ref[d, base + t * half : base + (t + 1) * half] = part
    store(base, (n // LANES) * half)
    for copy in stores:
        copy.wait()


def prepare_kernel(
    heads,
    chain_ref, mask_ref, cb_ref, w_ref, db_ref, gain_ref, wo_ref, wd_ref,
    term_ref, wt_ref, dbc_ref, gain_out, wo_out, wd_out,
):
    gain_out[...] = gain_ref[...]
    wo_out[...] = wo_ref[...]
    wd_out[...] = wd_ref[...]
    n = chain_ref.shape[1]
    tiles = n // LANES
    chan = w_ref.shape[0]
    dim = w_ref.shape[2] // 4
    width = heads * dim

    def column_of(row):
        return jnp.transpose(jnp.broadcast_to(row, (LANES, LANES)))

    for kt in range(tiles):
        ks = slice(kt * LANES, (kt + 1) * LANES)
        chain_k = column_of(chain_ref[:, ks].astype(F32))
        mask_k = (column_of(mask_ref[:, ks].astype(F32)) - 1.0) * 1000000000.0
        for it in range(tiles):
            cs = slice(it * LANES, (it + 1) * LANES)
            same = chain_k == chain_ref[:, cs].astype(F32)
            for h in range(heads):
                term_ref[h, ks, cs] = jnp.where(same, cb_ref[1, h], cb_ref[0, h]) + mask_k
    for h in range(heads):
        turned = jnp.transpose(w_ref[:, h, :].astype(F32)).astype(BF16)
        for place, kind in enumerate((0, 2, 3, 1)):
            start = place * width + h * dim
            wt_ref[start : start + dim] = turned[kind * dim : (kind + 1) * dim]
    bins = dbc_ref.shape[0]
    db_rows = jnp.broadcast_to(jnp.concatenate([db_ref[...], db_ref[...]], 1)[:, :LANES], (LANES, LANES))
    dbc_ref[...] = jnp.transpose(db_rows)[:bins]


def project_kernel(heads, recv_ref, gain_ref, w_ref, x_s, spread_s, k_s, v_s, g_s, n_s):
    peers = recv_ref.shape[0]
    rows, n, chan = x_s.shape
    tiles = n // LANES
    dim = w_ref.shape[0] // (4 * heads)
    width = heads * dim
    base = rows * rows
    gain = gain_ref[...]
    swap = swap_matrix(rows)
    centre = centring(chan)
    group = 2 * rows

    for pair in range(peers // 2):
        at = slice(pair * group, (pair + 1) * group)
        both = jnp.concatenate([recv_ref[2 * pair, :base], recv_ref[2 * pair + 1, :base]], 0)
        x = dot_nn(swap, both).astype(BF16)
        x_s[:, at, :] = x.reshape(rows, group, chan)
        n_s[:, at, :] = layer_norm(x, centre, gain).reshape(rows, group, chan)

    w_qvg, w_k = w_ref[: 3 * width], w_ref[3 * width :]
    zero = jnp.zeros((dim, LANES), BF16)

    def project(j):
        normed = n_s[j]
        qvg = dot_nt(w_qvg, normed).astype(BF16)
        k_s[j] = dot_nt(normed, w_k).astype(BF16)
        v_s[j] = qvg[width : 2 * width]
        g_s[j] = jax.nn.sigmoid(qvg[2 * width :].astype(F32))
        for t in range(tiles):
            for h in range(heads):
                for other in range(heads):
                    block = qvg[h * dim : (h + 1) * dim, t * LANES : (t + 1) * LANES] if h == other else zero
                    spread_s[j, t, other * dim : (other + 1) * dim, h * LANES : (h + 1) * LANES] = block

    if tiles == 1:
        for j in range(rows):
            project(j)
    else:
        pl.loop(0, rows)(project)


def attend_kernel(
    heads, fused,
    recv_ref, other_ref, term_ref, wo_ref, wd_ref, db_ref, x_s, spread_s, k_s, v_s, g_s,
    out_ref, *refs,
):
    if fused:
        second_ref, bias_s = refs
    else:
        (bias_s,) = refs
    peers = recv_ref.shape[0]
    rows, n, chan = x_s.shape
    tiles = n // LANES
    dim = wo_ref.shape[0] // heads
    half = heads // 2
    base = rows * rows
    core = lax.axis_index("row") % 2

    for s in range(peers):
        at = slice(s * rows, (s + 1) * rows)
        for block, owner in ((recv_ref[s, base:], core), (other_ref[s], 1 - core)):
            extra = block.astype(F32)
            for t in range(tiles):
                cs = slice(t * LANES, (t + 1) * LANES)
                for h in range(half):
                    start = (t * half + h) * rows
                    head = owner * half + h
                    bias_s[head, at, cs] = extra[start : start + rows] + term_ref[head, at, cs]

    scaling = dim ** (-0.5)
    w_out = wo_ref[...]
    w_dist = wd_ref[...]
    d_bias = db_ref[:, :1]

    def score(j, t):
        return dot_nn(k_s[j], spread_s[j, t])

    def attend(j, t, scores):
        cs = slice(t * LANES, (t + 1) * LANES)
        gated = []
        for first in range(0, heads, 2):
            weights, scales = [], []
            for h in (first, first + 1):
                s = scores[:, h * LANES : (h + 1) * LANES] * scaling + bias_s[h, :, cs]
                e = jnp.exp(s - jnp.max(s, 0, keepdims=True))
                scales.append(1.0 / jnp.sum(e, 0, keepdims=True))
                weights.append(e.astype(BF16))
            o = dot_nn(v_s[j, first * dim : (first + 2) * dim, :], jnp.concatenate(weights, 1))
            for side in range(2):
                h = first + side
                part = o[side * dim : (side + 1) * dim, side * LANES : (side + 1) * LANES]
                gated.append((g_s[j, h * dim : (h + 1) * dim, cs] * (part * scales[side])).astype(BF16))
        return dot_tn(jnp.concatenate(gated, 0), w_out).astype(BF16)

    def residual(j, update):
        new = (x_s[j].astype(F32) + update.astype(F32)).astype(BF16)
        second_ref[j] = (dot_nt(w_dist, new) + d_bias).astype(BF16)
        return new.astype(F32).reshape(peers, rows, chan)

    if not fused:

        @pl.loop(0, rows)
        def _(j):
            for t in range(tiles):
                out_ref[j, t * LANES : (t + 1) * LANES] = attend(j, t, score(j, t))

        return

    both = []
    scores = score(0, 0)
    for j in range(rows):
        later = score(j + 1, 0) if j + 1 < rows and tiles == 1 else None
        updates = [attend(j, 0, scores)]
        for t in range(1, tiles):
            updates.append(attend(j, t, score(j, t)))
        both.append(residual(j, jnp.concatenate(updates, 0)))
        scores = later if tiles == 1 or j + 1 == rows else score(j + 1, 0)
        if j % 2:
            out_ref[:, (j - 1) * rows : (j + 1) * rows, :] = jnp.concatenate(both, 1).astype(BF16)
            both = []


def finish_kernel(recv_ref, mirror_ref, wd_ref, db_ref, new_hbm, dist_hbm, new_ref, dist_ref, sems):
    peers, _, chan = recv_ref.shape
    rows = new_ref.shape[0]
    group = 2 * rows
    swap = swap_matrix(rows)
    for pair in range(peers // 2):
        at = slice(pair * group, (pair + 1) * group)
        both = recv_ref[2 * pair : 2 * pair + 2].reshape(2 * rows * rows, chan)
        new_ref[:, at, :] = dot_nn(swap, both).astype(BF16).reshape(rows, group, chan)
    copies = [pltpu.make_async_copy(new_ref, new_hbm, sems.at[0])]
    copies[0].start()
    w_dist = wd_ref[...]
    d_bias = db_ref[:, :1]
    for i in range(rows):
        logits = (dot_nt(w_dist, new_ref[i]) + d_bias).astype(BF16)
        dist_ref[i] = (logits.astype(F32) + mirror_ref[i].astype(F32)).astype(BF16)
        if i % 2:
            at = pl.ds(i - 1, 2)
            copies.append(pltpu.make_async_copy(dist_ref.at[at], dist_hbm.at[at], sems.at[1 + i // 2]))
            copies[-1].start()
    for copy in copies:
        copy.wait()


def call(kernel, outs, args, scratch=(), smem=(), hbm=(), hbm_outs=False, limit=48):
    spaces = [pltpu.SMEM if i in smem else pl.ANY if i in hbm else pltpu.VMEM for i in range(len(args))]
    return pl.pallas_call(
        kernel,
        out_shape=[jax.ShapeDtypeStruct(s, d) for s, d in outs],
        in_specs=[pl.BlockSpec(memory_space=space) for space in spaces],
        out_specs=[pl.BlockSpec(memory_space=pl.ANY if hbm_outs else pltpu.VMEM)] * len(outs),
        scratch_shapes=list(scratch),
        compiler_params=pltpu.CompilerParams(vmem_limit_bytes=limit * 1024 * 1024),
    )(*args)


def swap_cores(values):
    peers = lax.axis_size("row")
    return lax.ppermute(values, "row", [(i, i ^ 1) for i in range(peers)])


def all_to_all(blocks):
    return lax.all_to_all(blocks, "row", split_axis=0, concat_axis=0, tiled=True)


def shards(
    pair_act, chain_id, residue_mask, norm_gain, w_proj, w_bias, chain_bias, w_out, w_dist, dist_bias,
):
    rows, n, chan = pair_act.shape
    peers = n // rows
    heads, dim = w_out.shape[0], w_out.shape[1]
    bins = w_dist.shape[1]
    tiles = n // LANES
    width = heads * dim
    fused = lax.axis_size("head") == 1
    gain = norm_gain[None, :]
    base = rows * rows
    length = base + tiles * heads * rows // 2

    (packed,) = call(
        pack_kernel,
        [((peers, length, chan), BF16)],
        [pair_act, gain, w_bias.T],
        scratch=[
            pltpu.VMEM(pair_act.shape, BF16),
            pltpu.VMEM(gain.shape, F32),
            pltpu.VMEM((heads, chan), BF16),
            pltpu.VMEM((peers, length, chan), BF16),
            pltpu.SemaphoreType.DMA((rows + 2,)),
            pltpu.SemaphoreType.DMA((2,)),
        ],
        hbm=(0, 1, 2),
        hbm_outs=True,
        limit=60,
    )
    received = all_to_all(packed)
    term, w_types, db_col, gain, w_out, wd_t = call(
        functools.partial(prepare_kernel, heads),
        [
            ((heads, n, n), F32), ((4 * width, chan), BF16), ((bins, LANES), F32),
            ((1, chan), F32), ((width, chan), BF16), ((bins, chan), BF16),
        ],
        [
            chain_id[None, :], residue_mask[None, :], chain_bias, w_proj, dist_bias[None, :],
            gain, w_out.reshape(width, chan), w_dist.T,
        ],
        smem=(2,),
    )
    received, term, w_types, db_col, gain, w_out, wd_t = lax.optimization_barrier(
        (received, term, w_types, db_col, gain, w_out, wd_t)
    )
    other_bias = swap_cores(received[:, base:])
    x_cols, spread, keys, values, gates = call(
        functools.partial(project_kernel, heads),
        [
            ((rows, n, chan), BF16),
            ((rows, tiles, width, heads * LANES), BF16),
            ((rows, n, width), BF16),
            ((rows, width, n), BF16),
            ((rows, width, n), F32),
        ],
        [received, gain, w_types],
        scratch=[pltpu.VMEM((rows, n, chan), BF16)],
    )
    if fused:
        outs = [((peers, base, chan), BF16), ((rows, bins, n), BF16)]
    else:
        outs = [((rows, n, chan), BF16)]
    result = call(
        functools.partial(attend_kernel, heads, fused),
        outs,
        [received, other_bias, term, w_out, wd_t, db_col, x_cols, spread, keys, values, gates],
        scratch=[pltpu.VMEM((heads, n, n), F32)],
    )
    if fused:
        to_rows, mirror = result
    else:
        update = lax.psum(result[0], "head").astype(F32)
        new = (x_cols.astype(F32) + update).astype(BF16)
        logits = jnp.einsum("cb,jic->jbi", w_dist, new, preferred_element_type=F32)
        mirror = (logits + dist_bias[None, :, None]).astype(BF16)
        to_rows = new.reshape(rows, peers, rows, chan).transpose(1, 0, 2, 3).reshape(peers, base, chan)
    arrived = all_to_all(to_rows)
    new_rows, dist = call(
        finish_kernel,
        [((rows, n, chan), BF16), ((rows, bins, n), BF16)],
        [arrived, mirror, wd_t, db_col],
        scratch=[
            pltpu.VMEM((rows, n, chan), BF16),
            pltpu.VMEM((rows, bins, n), BF16),
            pltpu.SemaphoreType.DMA((1 + rows // 2,)),
        ],
        hbm_outs=True,
    )
    return new_rows, dist.transpose(0, 2, 1)


def solution(mesh):
    in_specs = (
        P(("dp", "row"), None, None),
        P("dp"),
        P("dp"),
        P(),
        P(None, "head", None),
        P(None, "head"),
        P(None, "head"),
        P("head", None, None),
        P(),
        P(),
    )
    out_specs = (P(("dp", "row"), None, None), P(("dp", "row"), None, None))
    return jax.shard_map(shards, mesh=mesh, in_specs=in_specs, out_specs=out_specs, check_vma=False)
```

```python
import functools

import jax
import jax.numpy as jnp
from jax import lax
from jax.experimental import pallas as pl
from jax.experimental.pallas import tpu as pltpu
from jax.sharding import PartitionSpec as P

LANES = 128
NEAR = 4
F32 = jnp.float32
BF16 = jnp.bfloat16


def dot_nt(a, b):
    return lax.dot_general(a, b, (((1,), (1,)), ((), ())), preferred_element_type=F32)


def dot_tn(a, b):
    return lax.dot_general(a, b, (((0,), (0,)), ((), ())), preferred_element_type=F32)


def dot_nn(a, b):
    return jnp.dot(a, b, preferred_element_type=F32)


def centring(chan):
    row = lax.broadcasted_iota(jnp.int32, (chan, chan), 0)
    col = lax.broadcasted_iota(jnp.int32, (chan, chan), 1)
    return (jnp.where(row == col, 1.0, 0.0) - 1.0 / chan).astype(BF16)


def layer_norm(values, centre, gain):
    centered = dot_nn(values, centre)
    variance = jnp.mean(centered * centered, -1, keepdims=True)
    return (centered * lax.rsqrt(variance + 1e-05) * gain).astype(BF16)


def swap_matrix(rows, flip=0):
    size = 2 * rows * rows
    out = lax.broadcasted_iota(jnp.int32, (size, size), 0)
    col = lax.broadcasted_iota(jnp.int32, (size, size), 1)
    b, rest = out // (2 * rows), out % (2 * rows)
    wanted = ((rest // rows) ^ flip) * (rows * rows) + (rest % rows) * rows + b
    return jnp.where(col == wanted, 1.0, 0.0).astype(BF16)


def pack_kernel(x_hbm, gain_hbm, wb_hbm, out_hbm, x_ref, gain_ref, wb_ref, out_ref, sems, out_sems):
    rows, n, chan = x_ref.shape
    peers = n // rows
    heads = wb_ref.shape[0]
    half = heads * rows // 2
    base = rows * rows
    fetch_gain = pltpu.make_async_copy(gain_hbm, gain_ref, sems.at[rows])
    fetch_wb = pltpu.make_async_copy(wb_hbm, wb_ref, sems.at[rows + 1])
    fetches = [pltpu.make_async_copy(x_hbm.at[k], x_ref.at[k], sems.at[k]) for k in range(rows)]
    for copy in (fetch_gain, fetch_wb, *fetches):
        copy.start()
    stores = []

    def store(first, count):
        at = pl.ds(first, count)
        copy = pltpu.make_async_copy(out_ref.at[:, at, :], out_hbm.at[:, at, :], out_sems.at[len(stores)])
        copy.start()
        stores.append(copy)

    for copy in (fetch_gain, fetch_wb, *fetches):
        copy.wait()
    for pair in range(rows // 2):
        both = [x_ref[k].astype(F32).reshape(peers, rows, chan) for k in (2 * pair, 2 * pair + 1)]
        out_ref[:, 2 * rows * pair : 2 * rows * (pair + 1), :] = jnp.concatenate(both, 1).astype(BF16)
    store(0, base)
    centre = centring(chan)
    gain = gain_ref[...]
    wb = wb_ref[...].astype(F32)
    wb = jnp.concatenate([jnp.broadcast_to(wb[h : h + 1], (rows, chan)) for h in range(heads)], 0)
    owner = lax.broadcasted_iota(jnp.int32, wb.shape, 0) % rows
    bias = jnp.zeros((wb.shape[0], n), F32)
    for k in range(rows):
        mine = jnp.where(owner == k, wb, 0.0).astype(BF16)
        bias = bias + dot_nt(mine, layer_norm(x_ref[k], centre, gain))
    bias = bias.astype(BF16)
    for t in range(n // LANES):
        block = bias[:, t * LANES : (t + 1) * LANES]
        for d in range(peers):
            part = block[(d % 2) * half : (d % 2 + 1) * half]
            out_ref[d, base + t * half : base + (t + 1) * half] = part
    store(base, (n // LANES) * half)
    for copy in stores:
        copy.wait()


def prepare_kernel(
    heads,
    chain_ref, mask_ref, cb_ref, w_ref, db_ref, gain_ref, wo_ref, wd_ref,
    term_ref, wt_ref, dbc_ref, gain_out, wo_out, wd_out,
):
    gain_out[...] = gain_ref[...]
    wo_out[...] = wo_ref[...]
    wd_out[...] = wd_ref[...]
    n = chain_ref.shape[1]
    tiles = n // LANES
    chan = w_ref.shape[0]
    dim = w_ref.shape[2] // 4
    width = heads * dim

    def column_of(row):
        return jnp.transpose(jnp.broadcast_to(row, (LANES, LANES)))

    for kt in range(tiles):
        ks = slice(kt * LANES, (kt + 1) * LANES)
        chain_k = column_of(chain_ref[:, ks].astype(F32))
        mask_k = (column_of(mask_ref[:, ks].astype(F32)) - 1.0) * 1000000000.0
        for it in range(tiles):
            cs = slice(it * LANES, (it + 1) * LANES)
            same = chain_k == chain_ref[:, cs].astype(F32)
            for h in range(heads):
                term_ref[h, ks, cs] = jnp.where(same, cb_ref[1, h], cb_ref[0, h]) + mask_k
    for h in range(heads):
        turned = jnp.transpose(w_ref[:, h, :].astype(F32)).astype(BF16)
        for place, kind in enumerate((0, 2, 3, 1)):
            start = place * width + h * dim
            wt_ref[start : start + dim] = turned[kind * dim : (kind + 1) * dim]
    bins = dbc_ref.shape[0]
    db_rows = jnp.broadcast_to(jnp.concatenate([db_ref[...], db_ref[...]], 1)[:, :LANES], (LANES, LANES))
    dbc_ref[...] = jnp.transpose(db_rows)[:bins]


def project_kernel(heads, recv_ref, gain_ref, w_ref, x_s, spread_s, k_s, v_s, g_s, n_s):
    peers = recv_ref.shape[0]
    rows, n, chan = x_s.shape
    tiles = n // LANES
    dim = w_ref.shape[0] // (4 * heads)
    width = heads * dim
    base = rows * rows
    gain = gain_ref[...]
    swap = swap_matrix(rows)
    centre = centring(chan)
    group = 2 * rows

    for pair in range(peers // 2):
        at = slice(pair * group, (pair + 1) * group)
        both = jnp.concatenate([recv_ref[2 * pair, :base], recv_ref[2 * pair + 1, :base]], 0)
        x = dot_nn(swap, both).astype(BF16)
        x_s[:, at, :] = x.reshape(rows, group, chan)
        n_s[:, at, :] = layer_norm(x, centre, gain).reshape(rows, group, chan)

    w_qvg, w_k = w_ref[: 3 * width], w_ref[3 * width :]
    zero = jnp.zeros((dim, LANES), BF16)

    def project(j):
        normed = n_s[j]
        qvg = dot_nt(w_qvg, normed).astype(BF16)
        k_s[j] = dot_nt(normed, w_k).astype(BF16)
        v_s[j] = qvg[width : 2 * width]
        g_s[j] = jax.nn.sigmoid(qvg[2 * width :].astype(F32))
        for t in range(tiles):
            for h in range(heads):
                for other in range(heads):
                    block = qvg[h * dim : (h + 1) * dim, t * LANES : (t + 1) * LANES] if h == other else zero
                    spread_s[j, t, other * dim : (other + 1) * dim, h * LANES : (h + 1) * LANES] = block

    if tiles == 1:
        for j in range(rows):
            project(j)
    else:
        pl.loop(0, rows)(project)


def attend_kernel(
    heads, fused,
    recv_ref, other_ref, term_ref, wo_ref, wd_ref, db_ref, x_s, spread_s, k_s, v_s, g_s,
    out_ref, *refs,
):
    if fused:
        second_ref, bias_s = refs
    else:
        (bias_s,) = refs
    peers = recv_ref.shape[0]
    rows, n, chan = x_s.shape
    tiles = n // LANES
    dim = wo_ref.shape[0] // heads
    half = heads // 2
    base = rows * rows
    me = lax.axis_index("row")
    core = me % 2

    for s in range(peers):
        at = slice(s * rows, (s + 1) * rows)
        for block, owner in ((recv_ref[s, base:], core), (other_ref[s], 1 - core)):
            extra = block.astype(F32)
            for t in range(tiles):
                cs = slice(t * LANES, (t + 1) * LANES)
                for h in range(half):
                    start = (t * half + h) * rows
                    head = owner * half + h
                    bias_s[head, at, cs] = extra[start : start + rows] + term_ref[head, at, cs]

    scaling = dim ** (-0.5)
    w_out = wo_ref[...]
    w_dist = wd_ref[...]
    d_bias = db_ref[:, :1]

    def score(j, t):
        return dot_nn(k_s[j], spread_s[j, t])

    def attend(j, t, scores):
        cs = slice(t * LANES, (t + 1) * LANES)
        gated = []
        for first in range(0, heads, 2):
            weights, scales = [], []
            for h in (first, first + 1):
                s = scores[:, h * LANES : (h + 1) * LANES] * scaling + bias_s[h, :, cs]
                e = jnp.exp(s - jnp.max(s, 0, keepdims=True))
                scales.append(1.0 / jnp.sum(e, 0, keepdims=True))
                weights.append(e.astype(BF16))
            o = dot_nn(v_s[j, first * dim : (first + 2) * dim, :], jnp.concatenate(weights, 1))
            for side in range(2):
                h = first + side
                part = o[side * dim : (side + 1) * dim, side * LANES : (side + 1) * LANES]
                gated.append((g_s[j, h * dim : (h + 1) * dim, cs] * (part * scales[side])).astype(BF16))
        return dot_tn(jnp.concatenate(gated, 0), w_out).astype(BF16)

    def residual(j, update):
        new = (x_s[j].astype(F32) + update.astype(F32)).astype(BF16)
        second_ref[j] = (dot_nt(w_dist, new) + d_bias).astype(BF16)
        return new.astype(F32).reshape(peers, rows, chan)

    if not fused:

        @pl.loop(0, rows)
        def _(j):
            for t in range(tiles):
                out_ref[j, t * LANES : (t + 1) * LANES] = attend(j, t, score(j, t))

        return

    both = []
    scores = score(0, 0)
    for j in range(rows):
        later = score(j + 1, 0) if j + 1 < rows and tiles == 1 else None
        updates = [attend(j, 0, scores)]
        for t in range(1, tiles):
            updates.append(attend(j, t, score(j, t)))
        both.append(residual(j, jnp.concatenate(updates, 0)))
        scores = later if tiles == 1 or j + 1 == rows else score(j + 1, 0)
        if j % 2:
            joined = jnp.concatenate(both, 1).astype(BF16)
            for d in range(peers):
                out_ref[me ^ d, (j - 1) * rows : (j + 1) * rows, :] = joined[d]
            both = []


def finish_kernel(near, *refs):
    recv, (mirror_ref, wd_ref, db_ref, new_hbm, dist_hbm, new_ref, dist_ref, sems) = refs[:near], refs[near:]
    far, _, chan = recv[0].shape
    rows = new_ref.shape[0]
    group = 2 * rows
    me = lax.axis_index("row")
    swap = swap_matrix(rows, me % 2)
    for m in range(far):
        for c in range(0, near, 2):
            at = pl.ds(pl.multiple_of((me ^ (near * m + c)) // 2 * group, group), group)
            both = jnp.concatenate([recv[c][m], recv[c + 1][m]], 0)
            new_ref[:, at, :] = dot_nn(swap, both).astype(BF16).reshape(rows, group, chan)
    copies = [pltpu.make_async_copy(new_ref, new_hbm, sems.at[0])]
    copies[0].start()
    w_dist = wd_ref[...]
    d_bias = db_ref[:, :1]
    for i in range(rows):
        logits = (dot_nt(w_dist, new_ref[i]) + d_bias).astype(BF16)
        dist_ref[i] = (logits.astype(F32) + mirror_ref[i].astype(F32)).astype(BF16)
        if i % 2:
            at = pl.ds(i - 1, 2)
            copies.append(pltpu.make_async_copy(dist_ref.at[at], dist_hbm.at[at], sems.at[1 + i // 2]))
            copies[-1].start()
    for copy in copies:
        copy.wait()


def call(kernel, outs, args, scratch=(), smem=(), hbm=(), hbm_outs=False, limit=48):
    spaces = [pltpu.SMEM if i in smem else pl.ANY if i in hbm else pltpu.VMEM for i in range(len(args))]
    return pl.pallas_call(
        kernel,
        out_shape=[jax.ShapeDtypeStruct(s, d) for s, d in outs],
        in_specs=[pl.BlockSpec(memory_space=space) for space in spaces],
        out_specs=[pl.BlockSpec(memory_space=pl.ANY if hbm_outs else pltpu.VMEM)] * len(outs),
        scratch_shapes=list(scratch),
        compiler_params=pltpu.CompilerParams(vmem_limit_bytes=limit * 1024 * 1024),
    )(*args)


def swap_cores(values):
    peers = lax.axis_size("row")
    return lax.ppermute(values, "row", [(i, i ^ 1) for i in range(peers)])


def exchange(blocks, near):
    peers = blocks.shape[0]
    far = peers // near

    def send(values, offset):
        return lax.ppermute(values, "row", [(i, i ^ offset) for i in range(peers)]) if offset else values

    parts = [send(blocks[near * m : near * (m + 1)], near * m) for m in range(far)]
    return [send(jnp.stack([part[c] for part in parts]), c) for c in range(near)]


def all_to_all(blocks):
    return lax.all_to_all(blocks, "row", split_axis=0, concat_axis=0, tiled=True)


def shards(
    pair_act, chain_id, residue_mask, norm_gain, w_proj, w_bias, chain_bias, w_out, w_dist, dist_bias,
):
    rows, n, chan = pair_act.shape
    peers = n // rows
    heads, dim = w_out.shape[0], w_out.shape[1]
    bins = w_dist.shape[1]
    tiles = n // LANES
    width = heads * dim
    fused = lax.axis_size("head") == 1
    gain = norm_gain[None, :]
    base = rows * rows
    length = base + tiles * heads * rows // 2

    (packed,) = call(
        pack_kernel,
        [((peers, length, chan), BF16)],
        [pair_act, gain, w_bias.T],
        scratch=[
            pltpu.VMEM(pair_act.shape, BF16),
            pltpu.VMEM(gain.shape, F32),
            pltpu.VMEM((heads, chan), BF16),
            pltpu.VMEM((peers, length, chan), BF16),
            pltpu.SemaphoreType.DMA((rows + 2,)),
            pltpu.SemaphoreType.DMA((2,)),
        ],
        hbm=(0, 1, 2),
        hbm_outs=True,
        limit=60,
    )
    received = all_to_all(packed)
    term, w_types, db_col, gain, w_out, wd_t = call(
        functools.partial(prepare_kernel, heads),
        [
            ((heads, n, n), F32), ((4 * width, chan), BF16), ((bins, LANES), F32),
            ((1, chan), F32), ((width, chan), BF16), ((bins, chan), BF16),
        ],
        [
            chain_id[None, :], residue_mask[None, :], chain_bias, w_proj, dist_bias[None, :],
            gain, w_out.reshape(width, chan), w_dist.T,
        ],
        smem=(2,),
    )
    received, term, w_types, db_col, gain, w_out, wd_t = lax.optimization_barrier(
        (received, term, w_types, db_col, gain, w_out, wd_t)
    )
    other_bias = swap_cores(received[:, base:])
    x_cols, spread, keys, values, gates = call(
        functools.partial(project_kernel, heads),
        [
            ((rows, n, chan), BF16),
            ((rows, tiles, width, heads * LANES), BF16),
            ((rows, n, width), BF16),
            ((rows, width, n), BF16),
            ((rows, width, n), F32),
        ],
        [received, gain, w_types],
        scratch=[pltpu.VMEM((rows, n, chan), BF16)],
    )
    if fused:
        outs = [((peers, base, chan), BF16), ((rows, bins, n), BF16)]
    else:
        outs = [((rows, n, chan), BF16)]
    result = call(
        functools.partial(attend_kernel, heads, fused),
        outs,
        [received, other_bias, term, w_out, wd_t, db_col, x_cols, spread, keys, values, gates],
        scratch=[pltpu.VMEM((heads, n, n), F32)],
    )
    if fused:
        to_rows, mirror = result
    else:
        update = lax.psum(result[0], "head").astype(F32)
        new = (x_cols.astype(F32) + update).astype(BF16)
        logits = jnp.einsum("cb,jic->jbi", w_dist, new, preferred_element_type=F32)
        mirror = (logits + dist_bias[None, :, None]).astype(BF16)
        to_rows = new.reshape(rows, peers, rows, chan).transpose(1, 0, 2, 3).reshape(peers, base, chan)
        to_rows = to_rows[jnp.arange(peers) ^ lax.axis_index("row")]
    arrived = exchange(to_rows, NEAR)
    new_rows, dist = call(
        functools.partial(finish_kernel, NEAR),
        [((rows, n, chan), BF16), ((rows, bins, n), BF16)],
        [*arrived, mirror, wd_t, db_col],
        scratch=[
            pltpu.VMEM((rows, n, chan), BF16),
            pltpu.VMEM((rows, bins, n), BF16),
            pltpu.SemaphoreType.DMA((1 + rows // 2,)),
        ],
        hbm_outs=True,
    )
    return new_rows, dist.transpose(0, 2, 1)


def solution(mesh):
    in_specs = (
        P(("dp", "row"), None, None),
        P("dp"),
        P("dp"),
        P(),
        P(None, "head", None),
        P(None, "head"),
        P(None, "head"),
        P("head", None, None),
        P(),
        P(),
    )
    out_specs = (P(("dp", "row"), None, None), P(("dp", "row"), None, None))
    return jax.shard_map(shards, mesh=mesh, in_specs=in_specs, out_specs=out_specs, check_vma=False)
```

```python
import functools

import jax
import jax.numpy as jnp
from jax import lax
from jax.experimental import pallas as pl
from jax.experimental.pallas import tpu as pltpu
from jax.sharding import PartitionSpec as P

LANES = 128
F32 = jnp.float32
BF16 = jnp.bfloat16
LOG2E = 1.4426950408889634


def dot_nt(a, b):
    return lax.dot_general(a, b, (((1,), (1,)), ((), ())), preferred_element_type=F32)


def dot_tn(a, b):
    return lax.dot_general(a, b, (((0,), (0,)), ((), ())), preferred_element_type=F32)


def dot_nn(a, b):
    return jnp.dot(a, b, preferred_element_type=F32)


def centring(chan):
    row = lax.broadcasted_iota(jnp.int32, (chan, chan), 0)
    col = lax.broadcasted_iota(jnp.int32, (chan, chan), 1)
    return (jnp.where(row == col, 1.0, 0.0) - 1.0 / chan).astype(BF16)


def layer_norm(values, centre, gain):
    centered = dot_nn(values, centre)
    variance = jnp.mean(centered * centered, -1, keepdims=True)
    return (centered * lax.rsqrt(variance + 1e-05) * gain).astype(BF16)


def swap_matrix(rows):
    size = 2 * rows * rows
    out = lax.broadcasted_iota(jnp.int32, (size, size), 0)
    col = lax.broadcasted_iota(jnp.int32, (size, size), 1)
    b, rest = out // (2 * rows), out % (2 * rows)
    wanted = (rest // rows) * (rows * rows) + (rest % rows) * rows + b
    return jnp.where(col == wanted, 1.0, 0.0).astype(BF16)


def pack_kernel(x_hbm, gain_hbm, wb_hbm, out_hbm, x_ref, gain_ref, wb_ref, n_ref, out_ref, sems, out_sems):
    rows, n, chan = x_ref.shape
    peers = n // rows
    heads = wb_ref.shape[0]
    half = heads * rows // 2
    base = rows * rows
    fetch_gain = pltpu.make_async_copy(gain_hbm, gain_ref, sems.at[rows])
    fetch_wb = pltpu.make_async_copy(wb_hbm, wb_ref, sems.at[rows + 1])
    fetches = [pltpu.make_async_copy(x_hbm.at[k], x_ref.at[k], sems.at[k]) for k in range(rows)]
    for copy in (fetch_gain, fetch_wb, *fetches):
        copy.start()
    stores = []

    def store(first, count):
        at = pl.ds(first, count)
        copy = pltpu.make_async_copy(out_ref.at[:, at, :], out_hbm.at[:, at, :], out_sems.at[len(stores)])
        copy.start()
        stores.append(copy)

    for copy in (fetch_gain, fetch_wb, *fetches):
        copy.wait()
    for pair in range(rows // 2):
        both = [x_ref[k].astype(F32).reshape(peers, rows, chan) for k in (2 * pair, 2 * pair + 1)]
        out_ref[:, 2 * rows * pair : 2 * rows * (pair + 1), :] = jnp.concatenate(both, 1).astype(BF16)
    store(0, base)
    centre = centring(chan)
    gain = gain_ref[...]
    wb = wb_ref[...].astype(F32)
    wb = jnp.concatenate([jnp.broadcast_to(wb[h : h + 1], (rows, chan)) for h in range(heads)], 0)
    owner = lax.broadcasted_iota(jnp.int32, wb.shape, 0) % rows
    bias = jnp.zeros((wb.shape[0], n), F32)
    for k in range(rows):
        n_ref[k] = layer_norm(x_ref[k], centre, gain)
    for k in range(rows):
        mine = jnp.where(owner == k, wb, 0.0).astype(BF16)
        bias = bias + dot_nt(mine, n_ref[k])
    bias = bias.astype(BF16)
    for t in range(n // LANES):
        block = bias[:, t * LANES : (t + 1) * LANES]
        for d in range(peers):
            part = block[(d % 2) * half : (d % 2 + 1) * half]
            out_ref[d, base + t * half : base + (t + 1) * half] = part
    store(base, (n // LANES) * half)
    for copy in stores:
        copy.wait()


def prepare_kernel(
    heads,
    chain_ref, mask_ref, cb_ref, w_ref, db_ref, gain_ref, wo_ref, wd_ref,
    term_ref, wt_ref, dbc_ref, gain_out, wo_out, wd_out,
):
    gain_out[...] = gain_ref[...]
    wo_out[...] = wo_ref[...]
    wd_out[...] = wd_ref[...]
    n = chain_ref.shape[1]
    tiles = n // LANES
    chan = w_ref.shape[0]
    dim = w_ref.shape[2] // 4
    width = heads * dim

    def column_of(row):
        return jnp.transpose(jnp.broadcast_to(row, (LANES, LANES)))

    for kt in range(tiles):
        ks = slice(kt * LANES, (kt + 1) * LANES)
        chain_k = column_of(chain_ref[:, ks].astype(F32))
        mask_k = (column_of(mask_ref[:, ks].astype(F32)) - 1.0) * 1000000000.0
        for it in range(tiles):
            cs = slice(it * LANES, (it + 1) * LANES)
            same = chain_k == chain_ref[:, cs].astype(F32)
            for h in range(heads):
                term_ref[h, ks, cs] = (jnp.where(same, cb_ref[1, h], cb_ref[0, h]) + mask_k) * LOG2E
    for h in range(heads):
        turned = jnp.transpose(w_ref[:, h, :].astype(F32)).astype(BF16)
        for place, kind in enumerate((0, 2, 3, 1)):
            start = place * width + h * dim
            wt_ref[start : start + dim] = turned[kind * dim : (kind + 1) * dim]
    bins = dbc_ref.shape[0]
    db_rows = jnp.broadcast_to(jnp.concatenate([db_ref[...], db_ref[...]], 1)[:, :LANES], (LANES, LANES))
    dbc_ref[...] = jnp.transpose(db_rows)[:bins]


def project_kernel(heads, recv_ref, gain_ref, w_ref, x_s, spread_s, k_s, v_s, g_s, n_s):
    peers = recv_ref.shape[0]
    rows, n, chan = x_s.shape
    tiles = n // LANES
    dim = w_ref.shape[0] // (4 * heads)
    width = heads * dim
    base = rows * rows
    gain = gain_ref[...]
    swap = swap_matrix(rows)
    centre = centring(chan)
    group = 2 * rows

    for pair in range(peers // 2):
        at = slice(pair * group, (pair + 1) * group)
        both = jnp.concatenate([recv_ref[2 * pair, :base], recv_ref[2 * pair + 1, :base]], 0)
        x = dot_nn(swap, both).astype(BF16)
        x_s[:, at, :] = x.reshape(rows, group, chan)
        n_s[:, at, :] = layer_norm(x, centre, gain).reshape(rows, group, chan)

    w_qvg, w_k = w_ref[: 3 * width], w_ref[3 * width :]
    zero = jnp.zeros((dim, LANES), BF16)

    def project(j):
        normed = n_s[j]
        qvg = dot_nt(w_qvg, normed).astype(BF16)
        k_s[j] = dot_nt(normed, w_k).astype(BF16)
        v_s[j] = qvg[width : 2 * width]
        g_s[j] = jax.nn.sigmoid(qvg[2 * width :].astype(F32))
        for t in range(tiles):
            for h in range(heads):
                for other in range(heads):
                    block = qvg[h * dim : (h + 1) * dim, t * LANES : (t + 1) * LANES] if h == other else zero
                    spread_s[j, t, other * dim : (other + 1) * dim, h * LANES : (h + 1) * LANES] = block

    if tiles == 1:
        for j in range(rows):
            project(j)
    else:
        pl.loop(0, rows)(project)


def attend_kernel(
    heads, fused,
    recv_ref, other_ref, term_ref, wo_ref, wd_ref, db_ref, x_s, spread_s, k_s, v_s, g_s,
    out_ref, *refs,
):
    if fused:
        second_ref, bias_s, inv_s, e_s, gated_s, new_s = refs
    else:
        bias_s, inv_s, e_s, gated_s = refs
    peers = recv_ref.shape[0]
    rows, n, chan = x_s.shape
    tiles = n // LANES
    dim = wo_ref.shape[0] // heads
    half = heads // 2
    base = rows * rows
    core = lax.axis_index("row") % 2

    for s in range(peers):
        at = slice(s * rows, (s + 1) * rows)
        for block, owner in ((recv_ref[s, base:], core), (other_ref[s], 1 - core)):
            extra = block.astype(F32) * LOG2E
            for t in range(tiles):
                cs = slice(t * LANES, (t + 1) * LANES)
                for h in range(half):
                    start = (t * half + h) * rows
                    head = owner * half + h
                    bias_s[head, at, cs] = extra[start : start + rows] + term_ref[head, at, cs]

    scaling = dim ** (-0.5) * LOG2E
    w_out = wo_ref[...]

    def soften(j, t):
        cs = slice(t * LANES, (t + 1) * LANES)
        scores = dot_nn(k_s[j], spread_s[j, t])
        for h in range(heads):
            s = scores[:, h * LANES : (h + 1) * LANES] * scaling + bias_s[h, :, cs]
            e = jnp.exp2(s - jnp.max(s, 0, keepdims=True))
            inv_s[j, t, h : h + 1] = 1.0 / jnp.sum(e, 0, keepdims=True)
            e_s[j, t, :, h * LANES : (h + 1) * LANES] = e.astype(BF16)

    def combine(j, t):
        cs = slice(t * LANES, (t + 1) * LANES)
        for first in range(0, heads, 2):
            o = dot_nn(v_s[j, first * dim : (first + 2) * dim], e_s[j, t, :, first * LANES : (first + 2) * LANES])
            for side in range(2):
                h = first + side
                part = o[side * dim : (side + 1) * dim, side * LANES : (side + 1) * LANES]
                mine = slice(h * dim, (h + 1) * dim)
                gated_s[j, mine, cs] = (g_s[j, mine, cs] * (part * inv_s[j, t, h : h + 1])).astype(BF16)

    if not fused:

        @pl.loop(0, rows)
        def _(j):
            for t in range(tiles):
                soften(j, t)
                combine(j, t)
            out_ref[j] = dot_tn(gated_s[j], w_out).astype(BF16)

        return

    for stage in (soften, combine):
        for j in range(rows):
            for t in range(tiles):
                stage(j, t)
    for j in range(rows):
        update = dot_tn(gated_s[j], w_out).astype(BF16)
        new_s[j] = (x_s[j].astype(F32) + update.astype(F32)).astype(BF16)
    for j in range(0, rows, 2):
        both = [new_s[j + side].astype(F32).reshape(peers, rows, chan) for side in range(2)]
        out_ref[:, j * rows : (j + 2) * rows, :] = jnp.concatenate(both, 1).astype(BF16)
    logits_of(new_s, wd_ref[...], db_ref[:, :1], second_ref)


def logits_of(new_ref, w_dist, d_bias, out_ref):
    rows, n, chan = new_ref.shape
    logits = dot_nt(w_dist, new_ref[...].reshape(rows * n, chan)) + d_bias
    for j in range(rows):
        out_ref[j] = logits[:, j * n : (j + 1) * n].astype(BF16)


def finish_kernel(recv_ref, mirror_ref, wd_ref, db_ref, new_hbm, dist_hbm, new_ref, dist_ref, sems):
    peers, _, chan = recv_ref.shape
    rows = new_ref.shape[0]
    group = 2 * rows
    swap = swap_matrix(rows)
    for pair in range(peers // 2):
        at = slice(pair * group, (pair + 1) * group)
        both = recv_ref[2 * pair : 2 * pair + 2].reshape(2 * rows * rows, chan)
        new_ref[:, at, :] = dot_nn(swap, both).astype(BF16).reshape(rows, group, chan)
    copies = [pltpu.make_async_copy(new_ref, new_hbm, sems.at[0])]
    copies[0].start()
    logits_of(new_ref, wd_ref[...], db_ref[:, :1], dist_ref)
    for i in range(rows):
        dist_ref[i] = (dist_ref[i].astype(F32) + mirror_ref[i].astype(F32)).astype(BF16)
        if i % 2:
            at = pl.ds(i - 1, 2)
            copies.append(pltpu.make_async_copy(dist_ref.at[at], dist_hbm.at[at], sems.at[1 + i // 2]))
            copies[-1].start()
    for copy in copies:
        copy.wait()


def call(kernel, outs, args, scratch=(), smem=(), hbm=(), hbm_outs=False, limit=48):
    spaces = [pltpu.SMEM if i in smem else pl.ANY if i in hbm else pltpu.VMEM for i in range(len(args))]
    return pl.pallas_call(
        kernel,
        out_shape=[jax.ShapeDtypeStruct(s, d) for s, d in outs],
        in_specs=[pl.BlockSpec(memory_space=space) for space in spaces],
        out_specs=[pl.BlockSpec(memory_space=pl.ANY if hbm_outs else pltpu.VMEM)] * len(outs),
        scratch_shapes=list(scratch),
        compiler_params=pltpu.CompilerParams(vmem_limit_bytes=limit * 1024 * 1024),
    )(*args)


def swap_cores(values):
    peers = lax.axis_size("row")
    return lax.ppermute(values, "row", [(i, i ^ 1) for i in range(peers)])


def all_to_all(blocks):
    return lax.all_to_all(blocks, "row", split_axis=0, concat_axis=0, tiled=True)


def shards(
    pair_act, chain_id, residue_mask, norm_gain, w_proj, w_bias, chain_bias, w_out, w_dist, dist_bias,
):
    rows, n, chan = pair_act.shape
    peers = n // rows
    heads, dim = w_out.shape[0], w_out.shape[1]
    bins = w_dist.shape[1]
    tiles = n // LANES
    width = heads * dim
    fused = lax.axis_size("head") == 1
    gain = norm_gain[None, :]
    base = rows * rows
    length = base + tiles * heads * rows // 2

    (packed,) = call(
        pack_kernel,
        [((peers, length, chan), BF16)],
        [pair_act, gain, w_bias.T],
        scratch=[
            pltpu.VMEM(pair_act.shape, BF16),
            pltpu.VMEM(gain.shape, F32),
            pltpu.VMEM((heads, chan), BF16),
            pltpu.VMEM(pair_act.shape, BF16),
            pltpu.VMEM((peers, length, chan), BF16),
            pltpu.SemaphoreType.DMA((rows + 2,)),
            pltpu.SemaphoreType.DMA((2,)),
        ],
        hbm=(0, 1, 2),
        hbm_outs=True,
        limit=60,
    )
    received = all_to_all(packed)
    term, w_types, db_col, gain, w_out, wd_t = call(
        functools.partial(prepare_kernel, heads),
        [
            ((heads, n, n), F32), ((4 * width, chan), BF16), ((bins, LANES), F32),
            ((1, chan), F32), ((width, chan), BF16), ((bins, chan), BF16),
        ],
        [
            chain_id[None, :], residue_mask[None, :], chain_bias, w_proj, dist_bias[None, :],
            gain, w_out.reshape(width, chan), w_dist.T,
        ],
        smem=(2,),
    )
    received, term, w_types, db_col, gain, w_out, wd_t = lax.optimization_barrier(
        (received, term, w_types, db_col, gain, w_out, wd_t)
    )
    other_bias = swap_cores(received[:, base:])
    x_cols, spread, keys, values, gates = call(
        functools.partial(project_kernel, heads),
        [
            ((rows, n, chan), BF16),
            ((rows, tiles, width, heads * LANES), BF16),
            ((rows, n, width), BF16),
            ((rows, width, n), BF16),
            ((rows, width, n), F32),
        ],
        [received, gain, w_types],
        scratch=[pltpu.VMEM((rows, n, chan), BF16)],
    )
    if fused:
        outs = [((peers, base, chan), BF16), ((rows, bins, n), BF16)]
    else:
        outs = [((rows, n, chan), BF16)]
    result = call(
        functools.partial(attend_kernel, heads, fused),
        outs,
        [received, other_bias, term, w_out, wd_t, db_col, x_cols, spread, keys, values, gates],
        scratch=[
            pltpu.VMEM((heads, n, n), F32),
            pltpu.VMEM((rows, tiles, heads, LANES), F32),
            pltpu.VMEM((rows, tiles, n, heads * LANES), BF16),
            pltpu.VMEM((rows, width, n), BF16),
        ]
        + [pltpu.VMEM((rows, n, chan), BF16)] * fused,
    )
    if fused:
        to_rows, mirror = result
    else:
        update = lax.psum(result[0], "head").astype(F32)
        new = (x_cols.astype(F32) + update).astype(BF16)
        logits = jnp.einsum("cb,jic->jbi", w_dist, new, preferred_element_type=F32)
        mirror = (logits + dist_bias[None, :, None]).astype(BF16)
        to_rows = new.reshape(rows, peers, rows, chan).transpose(1, 0, 2, 3).reshape(peers, base, chan)
    arrived = all_to_all(to_rows)
    new_rows, dist = call(
        finish_kernel,
        [((rows, n, chan), BF16), ((rows, bins, n), BF16)],
        [arrived, mirror, wd_t, db_col],
        scratch=[
            pltpu.VMEM((rows, n, chan), BF16),
            pltpu.VMEM((rows, bins, n), BF16),
            pltpu.SemaphoreType.DMA((1 + rows // 2,)),
        ],
        hbm_outs=True,
    )
    return new_rows, dist.transpose(0, 2, 1)


def solution(mesh):
    in_specs = (
        P(("dp", "row"), None, None),
        P("dp"),
        P("dp"),
        P(),
        P(None, "head", None),
        P(None, "head"),
        P(None, "head"),
        P("head", None, None),
        P(),
        P(),
    )
    out_specs = (P(("dp", "row"), None, None), P(("dp", "row"), None, None))
    return jax.shard_map(shards, mesh=mesh, in_specs=in_specs, out_specs=out_specs, check_vma=False)
```

```python
import functools

import jax
import jax.numpy as jnp
from jax import lax
from jax.experimental import pallas as pl
from jax.experimental.pallas import tpu as pltpu
from jax.sharding import PartitionSpec as P

LANES = 128
F32 = jnp.float32
BF16 = jnp.bfloat16
LOG2E = 1.4426950408889634


def dot_nt(a, b):
    return lax.dot_general(a, b, (((1,), (1,)), ((), ())), preferred_element_type=F32)


def dot_tn(a, b):
    return lax.dot_general(a, b, (((0,), (0,)), ((), ())), preferred_element_type=F32)


def dot_nn(a, b):
    return jnp.dot(a, b, preferred_element_type=F32)


def centring(chan):
    row = lax.broadcasted_iota(jnp.int32, (2 * chan, 2 * chan), 0)
    col = lax.broadcasted_iota(jnp.int32, (2 * chan, 2 * chan), 1)
    inside = (row // chan) == (col // chan)
    return (jnp.where(row == col, 1.0, 0.0) - jnp.where(inside, 1.0 / chan, 0.0)).astype(BF16)


def layer_norm(values, centre, gain):
    chan = gain.shape[1]
    centered = dot_nn(values, centre)
    halves = []
    for part in (centered[:, :chan], centered[:, chan:]):
        variance = jnp.mean(part * part, -1, keepdims=True)
        halves.append((part * lax.rsqrt(variance + 1e-05) * gain).astype(BF16))
    return halves


def swap_matrix(rows):
    size = 2 * rows * rows
    out = lax.broadcasted_iota(jnp.int32, (size, size), 0)
    col = lax.broadcasted_iota(jnp.int32, (size, size), 1)
    b, rest = out // (2 * rows), out % (2 * rows)
    wanted = (rest // rows) * (rows * rows) + (rest % rows) * rows + b
    return jnp.where(col == wanted, 1.0, 0.0).astype(BF16)


def pack_kernel(x_hbm, gain_hbm, wb_hbm, out_hbm, x_ref, gain_ref, wb_ref, n_ref, out_ref, sems, out_sems):
    rows, n, chan = x_ref.shape
    peers = n // rows
    heads = wb_ref.shape[0]
    half = heads * rows // 2
    base = rows * rows
    fetch_gain = pltpu.make_async_copy(gain_hbm, gain_ref, sems.at[rows])
    fetch_wb = pltpu.make_async_copy(wb_hbm, wb_ref, sems.at[rows + 1])
    fetches = [pltpu.make_async_copy(x_hbm.at[k], x_ref.at[k], sems.at[k]) for k in range(rows)]
    for copy in (fetch_gain, fetch_wb, *fetches):
        copy.start()
    stores = []

    def store(first, count):
        at = pl.ds(first, count)
        copy = pltpu.make_async_copy(out_ref.at[:, at, :], out_hbm.at[:, at, :], out_sems.at[len(stores)])
        copy.start()
        stores.append(copy)

    for copy in (fetch_gain, fetch_wb, *fetches):
        copy.wait()
    for pair in range(rows // 2):
        both = [x_ref[k].astype(F32).reshape(peers, rows, chan) for k in (2 * pair, 2 * pair + 1)]
        out_ref[:, 2 * rows * pair : 2 * rows * (pair + 1), :] = jnp.concatenate(both, 1).astype(BF16)
    store(0, base)
    centre = centring(chan)
    gain = gain_ref[...]
    wb = wb_ref[...].astype(F32)
    wb = jnp.concatenate([jnp.broadcast_to(wb[h : h + 1], (rows, chan)) for h in range(heads)], 0)
    owner = lax.broadcasted_iota(jnp.int32, wb.shape, 0) % rows
    bias = jnp.zeros((wb.shape[0], n), F32)
    for pair in range(rows // 2):
        two = jnp.concatenate([x_ref[2 * pair], x_ref[2 * pair + 1]], 1)
        n_ref[pair] = jnp.concatenate(layer_norm(two, centre, gain), 1)
    for pair in range(rows // 2):
        mine = [jnp.where(owner == k, wb, 0.0).astype(BF16) for k in (2 * pair, 2 * pair + 1)]
        bias = bias + dot_nt(jnp.concatenate(mine, 1), n_ref[pair])
    bias = bias.astype(BF16)
    for t in range(n // LANES):
        block = bias[:, t * LANES : (t + 1) * LANES]
        for d in range(peers):
            part = block[(d % 2) * half : (d % 2 + 1) * half]
            out_ref[d, base + t * half : base + (t + 1) * half] = part
    store(base, (n // LANES) * half)
    for copy in stores:
        copy.wait()


def prepare_kernel(
    heads,
    chain_ref, mask_ref, cb_ref, w_ref, db_ref, gain_ref, wo_ref, wd_ref,
    term_ref, wt_ref, wk_out, dbc_ref, gain_out, wo_out, wd_out,
):
    gain_out[...] = gain_ref[...]
    chan = w_ref.shape[0]
    width = wo_ref.shape[0]
    wk_out[...] = jnp.zeros_like(wk_out)
    wo_out[...] = jnp.zeros_like(wo_out)
    for side in range(2):
        wo_out[side * width : (side + 1) * width, side * chan : (side + 1) * chan] = wo_ref[...]
    wd_out[...] = wd_ref[...]
    n = chain_ref.shape[1]
    tiles = n // LANES
    dim = w_ref.shape[2] // 4

    def column_of(row):
        return jnp.transpose(jnp.broadcast_to(row, (LANES, LANES)))

    for kt in range(tiles):
        ks = slice(kt * LANES, (kt + 1) * LANES)
        chain_k = column_of(chain_ref[:, ks].astype(F32))
        mask_k = (column_of(mask_ref[:, ks].astype(F32)) - 1.0) * 1000000000.0
        for it in range(tiles):
            cs = slice(it * LANES, (it + 1) * LANES)
            same = chain_k == chain_ref[:, cs].astype(F32)
            for h in range(heads):
                term_ref[h, ks, cs] = (jnp.where(same, cb_ref[1, h], cb_ref[0, h]) + mask_k) * LOG2E
    for h in range(heads):
        turned = jnp.transpose(w_ref[:, h, :].astype(F32)).astype(BF16)
        for place, kind in enumerate((0, 2, 3)):
            start = place * width + h * dim
            wt_ref[start : start + dim] = turned[kind * dim : (kind + 1) * dim]
        for side in range(2):
            start = side * width + h * dim
            wk_out[start : start + dim, side * chan : (side + 1) * chan] = turned[dim : 2 * dim]
    bins = dbc_ref.shape[0]
    db_rows = jnp.broadcast_to(jnp.concatenate([db_ref[...], db_ref[...]], 1)[:, :LANES], (LANES, LANES))
    dbc_ref[...] = jnp.transpose(db_rows)[:bins]


def permuted(blocks, swap):
    left, right = jnp.concatenate(blocks[:2], 0), jnp.concatenate(blocks[2:], 0)
    return dot_nn(swap, jnp.concatenate([left, right], 1)).astype(BF16)


def project_kernel(heads, recv_ref, gain_ref, w_ref, wk_ref, x_s, spread_s, k_s, v_s, g_s, n_s):
    peers = recv_ref.shape[0]
    rows, n, chan = x_s.shape
    tiles = n // LANES
    dim = w_ref.shape[0] // (3 * heads)
    width = heads * dim
    base = rows * rows
    gain = gain_ref[...]
    swap = swap_matrix(rows)
    centre = centring(chan)
    group = 2 * rows
    w_k = wk_ref[...]

    for quad in range(peers // 4):
        x = permuted([recv_ref[4 * quad + s, :base] for s in range(4)], swap)
        normed = layer_norm(x, centre, gain)
        keys = dot_nt(jnp.concatenate(normed, 1), w_k).astype(BF16)
        for side in range(2):
            at = slice((2 * quad + side) * group, (2 * quad + side + 1) * group)
            x_s[:, at, :] = x[:, side * chan : (side + 1) * chan].reshape(rows, group, chan)
            n_s[:, at, :] = normed[side].reshape(rows, group, chan)
            k_s[:, at, :] = keys[:, side * width : (side + 1) * width].reshape(rows, group, width)

    w_qvg = w_ref[...]
    zero = jnp.zeros((dim, LANES), BF16)

    def project(pair):
        both = dot_nt(w_qvg, n_s[pl.ds(2 * pair, 2)].reshape(2 * n, chan)).astype(BF16)
        for side in range(2):
            j = 2 * pair + side
            qvg = both[:, side * n : (side + 1) * n]
            v_s[j] = qvg[width : 2 * width]
            g_s[j] = jax.nn.sigmoid(qvg[2 * width :].astype(F32))
            for t in range(tiles):
                for h in range(heads):
                    for other in range(heads):
                        block = qvg[h * dim : (h + 1) * dim, t * LANES : (t + 1) * LANES] if h == other else zero
                        spread_s[j, t, other * dim : (other + 1) * dim, h * LANES : (h + 1) * LANES] = block

    if tiles == 1:
        for pair in range(rows // 2):
            project(pair)
    else:
        pl.loop(0, rows // 2)(project)


def attend_kernel(
    heads, fused,
    recv_ref, other_ref, term_ref, wo_ref, wd_ref, db_ref, x_s, spread_s, k_s, v_s, g_s,
    out_ref, *refs,
):
    if fused:
        second_ref, bias_s, inv_s, e_s, gated_s, new_s = refs
    else:
        bias_s, inv_s, e_s, gated_s = refs
    peers = recv_ref.shape[0]
    rows, n, chan = x_s.shape
    tiles = n // LANES
    dim = wo_ref.shape[0] // (2 * heads)
    half = heads // 2
    base = rows * rows
    core = lax.axis_index("row") % 2

    for s in range(peers):
        at = slice(s * rows, (s + 1) * rows)
        for block, owner in ((recv_ref[s, base:], core), (other_ref[s], 1 - core)):
            extra = block.astype(F32) * LOG2E
            for t in range(tiles):
                cs = slice(t * LANES, (t + 1) * LANES)
                for h in range(half):
                    start = (t * half + h) * rows
                    head = owner * half + h
                    bias_s[head, at, cs] = extra[start : start + rows] + term_ref[head, at, cs]

    scaling = dim ** (-0.5) * LOG2E
    w_out = wo_ref[...]

    def soften(j, t):
        cs = slice(t * LANES, (t + 1) * LANES)
        scores = dot_nn(k_s[j], spread_s[j, t])
        for h in range(heads):
            s = scores[:, h * LANES : (h + 1) * LANES] * scaling + bias_s[h, :, cs]
            e = jnp.exp2(s - jnp.max(s, 0, keepdims=True))
            inv_s[j, t, h : h + 1] = 1.0 / jnp.sum(e, 0, keepdims=True)
            e_s[j, t, :, h * LANES : (h + 1) * LANES] = e.astype(BF16)

    def combine(j, t):
        cs = slice(t * LANES, (t + 1) * LANES)
        for first in range(0, heads, 2):
            o = dot_nn(v_s[j, first * dim : (first + 2) * dim], e_s[j, t, :, first * LANES : (first + 2) * LANES])
            for side in range(2):
                h = first + side
                part = o[side * dim : (side + 1) * dim, side * LANES : (side + 1) * LANES]
                mine = slice(h * dim, (h + 1) * dim)
                gated_s[j, mine, cs] = (g_s[j, mine, cs] * (part * inv_s[j, t, h : h + 1])).astype(BF16)

    def updated(pair):
        both = gated_s[pl.ds(2 * pair, 2)].reshape(2 * heads * dim, n)
        return dot_tn(both, w_out).astype(BF16)

    if not fused:

        @pl.loop(0, rows // 2)
        def _(pair):
            for j in (2 * pair, 2 * pair + 1):
                for t in range(tiles):
                    soften(j, t)
                    combine(j, t)
            update = updated(pair)
            for side in range(2):
                out_ref[2 * pair + side] = update[:, side * chan : (side + 1) * chan]

        return

    for stage in (soften, combine):
        for j in range(rows):
            for t in range(tiles):
                stage(j, t)
    for j in range(0, rows, 2):
        update = updated(j // 2).astype(F32)
        both = []
        for side in range(2):
            new = (x_s[j + side].astype(F32) + update[:, side * chan : (side + 1) * chan]).astype(BF16)
            new_s[j + side] = new
            both.append(new.astype(F32).reshape(peers, rows, chan))
        out_ref[:, j * rows : (j + 2) * rows, :] = jnp.concatenate(both, 1).astype(BF16)
    logits_of(new_s, wd_ref[...], db_ref[:, :1], second_ref)


def logits_of(new_ref, w_dist, d_bias, out_ref):
    rows, n, chan = new_ref.shape
    logits = dot_nt(w_dist, new_ref[...].reshape(rows * n, chan)) + d_bias
    for j in range(rows):
        out_ref[j] = logits[:, j * n : (j + 1) * n].astype(BF16)


def finish_kernel(recv_ref, mirror_ref, wd_ref, db_ref, new_hbm, dist_hbm, new_ref, dist_ref, sems):
    peers, _, chan = recv_ref.shape
    rows = new_ref.shape[0]
    group = 2 * rows
    swap = swap_matrix(rows)
    for quad in range(peers // 4):
        new = permuted([recv_ref[4 * quad + s] for s in range(4)], swap)
        for side in range(2):
            at = slice((2 * quad + side) * group, (2 * quad + side + 1) * group)
            new_ref[:, at, :] = new[:, side * chan : (side + 1) * chan].reshape(rows, group, chan)
    copies = [pltpu.make_async_copy(new_ref, new_hbm, sems.at[0])]
    copies[0].start()
    logits_of(new_ref, wd_ref[...], db_ref[:, :1], dist_ref)
    for i in range(rows):
        dist_ref[i] = (dist_ref[i].astype(F32) + mirror_ref[i].astype(F32)).astype(BF16)
        if i % 2:
            at = pl.ds(i - 1, 2)
            copies.append(pltpu.make_async_copy(dist_ref.at[at], dist_hbm.at[at], sems.at[1 + i // 2]))
            copies[-1].start()
    for copy in copies:
        copy.wait()


def call(kernel, outs, args, scratch=(), smem=(), hbm=(), hbm_outs=False, limit=48):
    spaces = [pltpu.SMEM if i in smem else pl.ANY if i in hbm else pltpu.VMEM for i in range(len(args))]
    return pl.pallas_call(
        kernel,
        out_shape=[jax.ShapeDtypeStruct(s, d) for s, d in outs],
        in_specs=[pl.BlockSpec(memory_space=space) for space in spaces],
        out_specs=[pl.BlockSpec(memory_space=pl.ANY if hbm_outs else pltpu.VMEM)] * len(outs),
        scratch_shapes=list(scratch),
        compiler_params=pltpu.CompilerParams(vmem_limit_bytes=limit * 1024 * 1024),
    )(*args)


def swap_cores(values):
    peers = lax.axis_size("row")
    return lax.ppermute(values, "row", [(i, i ^ 1) for i in range(peers)])


def all_to_all(blocks):
    return lax.all_to_all(blocks, "row", split_axis=0, concat_axis=0, tiled=True)


def shards(
    pair_act, chain_id, residue_mask, norm_gain, w_proj, w_bias, chain_bias, w_out, w_dist, dist_bias,
):
    rows, n, chan = pair_act.shape
    peers = n // rows
    heads, dim = w_out.shape[0], w_out.shape[1]
    bins = w_dist.shape[1]
    tiles = n // LANES
    width = heads * dim
    fused = lax.axis_size("head") == 1
    gain = norm_gain[None, :]
    base = rows * rows
    length = base + tiles * heads * rows // 2

    (packed,) = call(
        pack_kernel,
        [((peers, length, chan), BF16)],
        [pair_act, gain, w_bias.T],
        scratch=[
            pltpu.VMEM(pair_act.shape, BF16),
            pltpu.VMEM(gain.shape, F32),
            pltpu.VMEM((heads, chan), BF16),
            pltpu.VMEM((rows // 2, n, 2 * chan), BF16),
            pltpu.VMEM((peers, length, chan), BF16),
            pltpu.SemaphoreType.DMA((rows + 2,)),
            pltpu.SemaphoreType.DMA((2,)),
        ],
        hbm=(0, 1, 2),
        hbm_outs=True,
        limit=60,
    )
    received = all_to_all(packed)
    term, w_types, w_keys, db_col, gain, w_out, wd_t = call(
        functools.partial(prepare_kernel, heads),
        [
            ((heads, n, n), F32), ((3 * width, chan), BF16), ((2 * width, 2 * chan), BF16), ((bins, LANES), F32),
            ((1, chan), F32), ((2 * width, 2 * chan), BF16), ((bins, chan), BF16),
        ],
        [
            chain_id[None, :], residue_mask[None, :], chain_bias, w_proj, dist_bias[None, :],
            gain, w_out.reshape(width, chan), w_dist.T,
        ],
        smem=(2,),
    )
    received, term, w_types, w_keys, db_col, gain, w_out, wd_t = lax.optimization_barrier(
        (received, term, w_types, w_keys, db_col, gain, w_out, wd_t)
    )
    other_bias = swap_cores(received[:, base:])
    x_cols, spread, keys, values, gates = call(
        functools.partial(project_kernel, heads),
        [
            ((rows, n, chan), BF16),
            ((rows, tiles, width, heads * LANES), BF16),
            ((rows, n, width), BF16),
            ((rows, width, n), BF16),
            ((rows, width, n), F32),
        ],
        [received, gain, w_types, w_keys],
        scratch=[pltpu.VMEM((rows, n, chan), BF16)],
    )
    if fused:
        outs = [((peers, base, chan), BF16), ((rows, bins, n), BF16)]
    else:
        outs = [((rows, n, chan), BF16)]
    result = call(
        functools.partial(attend_kernel, heads, fused),
        outs,
        [received, other_bias, term, w_out, wd_t, db_col, x_cols, spread, keys, values, gates],
        scratch=[
            pltpu.VMEM((heads, n, n), F32),
            pltpu.VMEM((rows, tiles, heads, LANES), F32),
            pltpu.VMEM((rows, tiles, n, heads * LANES), BF16),
            pltpu.VMEM((rows, width, n), BF16),
        ]
        + [pltpu.VMEM((rows, n, chan), BF16)] * fused,
    )
    if fused:
        to_rows, mirror = result
    else:
        update = lax.psum(result[0], "head").astype(F32)
        new = (x_cols.astype(F32) + update).astype(BF16)
        logits = jnp.einsum("cb,jic->jbi", w_dist, new, preferred_element_type=F32)
        mirror = (logits + dist_bias[None, :, None]).astype(BF16)
        to_rows = new.reshape(rows, peers, rows, chan).transpose(1, 0, 2, 3).reshape(peers, base, chan)
    arrived = all_to_all(to_rows)
    new_rows, dist = call(
        finish_kernel,
        [((rows, n, chan), BF16), ((rows, bins, n), BF16)],
        [arrived, mirror, wd_t, db_col],
        scratch=[
            pltpu.VMEM((rows, n, chan), BF16),
            pltpu.VMEM((rows, bins, n), BF16),
            pltpu.SemaphoreType.DMA((1 + rows // 2,)),
        ],
        hbm_outs=True,
    )
    return new_rows, dist.transpose(0, 2, 1)


def solution(mesh):
    in_specs = (
        P(("dp", "row"), None, None),
        P("dp"),
        P("dp"),
        P(),
        P(None, "head", None),
        P(None, "head"),
        P(None, "head"),
        P("head", None, None),
        P(),
        P(),
    )
    out_specs = (P(("dp", "row"), None, None), P(("dp", "row"), None, None))
    return jax.shard_map(shards, mesh=mesh, in_specs=in_specs, out_specs=out_specs, check_vma=False)
```

```python
import functools

import jax
import jax.numpy as jnp
from jax import lax
from jax.experimental import pallas as pl
from jax.experimental.pallas import tpu as pltpu
from jax.sharding import PartitionSpec as P

LANES = 128
F32 = jnp.float32
BF16 = jnp.bfloat16
LOG2E = 1.4426950408889634


def dot_nt(a, b):
    return lax.dot_general(a, b, (((1,), (1,)), ((), ())), preferred_element_type=F32)


def dot_tn(a, b):
    return lax.dot_general(a, b, (((0,), (0,)), ((), ())), preferred_element_type=F32)


def dot_nn(a, b):
    return jnp.dot(a, b, preferred_element_type=F32)


def centring(chan):
    row = lax.broadcasted_iota(jnp.int32, (2 * chan, 2 * chan), 0)
    col = lax.broadcasted_iota(jnp.int32, (2 * chan, 2 * chan), 1)
    inside = (row // chan) == (col // chan)
    return (jnp.where(row == col, 1.0, 0.0) - jnp.where(inside, 1.0 / chan, 0.0)).astype(BF16)


def layer_norm(values, centre, gain):
    chan = gain.shape[1]
    centered = dot_nn(values, centre)
    halves = []
    for part in (centered[:, :chan], centered[:, chan:]):
        variance = jnp.mean(part * part, -1, keepdims=True)
        halves.append((part * lax.rsqrt(variance + 1e-05) * gain).astype(BF16))
    return halves


def swap_matrix(rows):
    size = 2 * rows * rows
    out = lax.broadcasted_iota(jnp.int32, (size, size), 0)
    col = lax.broadcasted_iota(jnp.int32, (size, size), 1)
    b, rest = out // (2 * rows), out % (2 * rows)
    wanted = (rest // rows) * (rows * rows) + (rest % rows) * rows + b
    return jnp.where(col == wanted, 1.0, 0.0).astype(BF16)


def pack_kernel(
    x_hbm, gain_hbm, wb_hbm, out_hbm, bias_hbm,
    x_ref, gain_ref, wb_ref, n_ref, out_ref, bias_ref, sems, out_sems,
):
    rows, n, chan = x_ref.shape
    peers = n // rows
    heads = wb_ref.shape[0]
    fetch_gain = pltpu.make_async_copy(gain_hbm, gain_ref, sems.at[rows])
    fetch_wb = pltpu.make_async_copy(wb_hbm, wb_ref, sems.at[rows + 1])
    fetches = [pltpu.make_async_copy(x_hbm.at[k], x_ref.at[k], sems.at[k]) for k in range(rows)]
    for copy in (fetch_gain, fetch_wb, *fetches):
        copy.start()
    for copy in (fetch_gain, fetch_wb, *fetches):
        copy.wait()
    for pair in range(rows // 2):
        both = [x_ref[k].astype(F32).reshape(peers, rows, chan) for k in (2 * pair, 2 * pair + 1)]
        out_ref[:, 2 * rows * pair : 2 * rows * (pair + 1), :] = jnp.concatenate(both, 1).astype(BF16)
    stores = [pltpu.make_async_copy(out_ref, out_hbm, out_sems.at[0])]
    stores[0].start()
    centre = centring(chan)
    gain = gain_ref[...]
    wb = wb_ref[...].astype(F32)
    wb = jnp.concatenate([jnp.broadcast_to(wb[h : h + 1], (rows, chan)) for h in range(heads)], 0)
    owner = lax.broadcasted_iota(jnp.int32, wb.shape, 0) % rows
    bias = jnp.zeros((wb.shape[0], n), F32)
    for pair in range(rows // 2):
        two = jnp.concatenate([x_ref[2 * pair], x_ref[2 * pair + 1]], 1)
        n_ref[pair] = jnp.concatenate(layer_norm(two, centre, gain), 1)
    for pair in range(rows // 2):
        mine = [jnp.where(owner == k, wb, 0.0).astype(BF16) for k in (2 * pair, 2 * pair + 1)]
        bias = bias + dot_nt(jnp.concatenate(mine, 1), n_ref[pair])
    step = wb.shape[0]
    for t in range(n // LANES):
        bias_ref[t * step : (t + 1) * step] = bias[:, t * LANES : (t + 1) * LANES].astype(BF16)
    stores.append(pltpu.make_async_copy(bias_ref, bias_hbm, out_sems.at[1]))
    stores[1].start()
    for copy in stores:
        copy.wait()


def prepare_kernel(
    heads,
    chain_ref, mask_ref, cb_ref, w_ref, db_ref, gain_ref, wo_ref, wd_ref,
    term_ref, wt_ref, wk_out, dbc_ref, gain_out, wo_out, wd_out,
):
    gain_out[...] = gain_ref[...]
    chan = w_ref.shape[0]
    width = wo_ref.shape[0]
    wk_out[...] = jnp.zeros_like(wk_out)
    wo_out[...] = jnp.zeros_like(wo_out)
    for side in range(2):
        wo_out[side * width : (side + 1) * width, side * chan : (side + 1) * chan] = wo_ref[...]
    wd_out[...] = wd_ref[...]
    n = chain_ref.shape[1]
    tiles = n // LANES
    dim = w_ref.shape[2] // 4

    def column_of(row):
        return jnp.transpose(jnp.broadcast_to(row, (LANES, LANES)))

    for kt in range(tiles):
        ks = slice(kt * LANES, (kt + 1) * LANES)
        chain_k = column_of(chain_ref[:, ks].astype(F32))
        mask_k = (column_of(mask_ref[:, ks].astype(F32)) - 1.0) * 1000000000.0
        for it in range(tiles):
            cs = slice(it * LANES, (it + 1) * LANES)
            same = chain_k == chain_ref[:, cs].astype(F32)
            for h in range(heads):
                term_ref[h, ks, cs] = (jnp.where(same, cb_ref[1, h], cb_ref[0, h]) + mask_k) * LOG2E
    for h in range(heads):
        turned = jnp.transpose(w_ref[:, h, :].astype(F32)).astype(BF16)
        for place, kind in enumerate((0, 2, 3)):
            start = place * width + h * dim
            wt_ref[start : start + dim] = turned[kind * dim : (kind + 1) * dim]
        for side in range(2):
            start = side * width + h * dim
            wk_out[start : start + dim, side * chan : (side + 1) * chan] = turned[dim : 2 * dim]
    bins = dbc_ref.shape[0]
    db_rows = jnp.broadcast_to(jnp.concatenate([db_ref[...], db_ref[...]], 1)[:, :LANES], (LANES, LANES))
    dbc_ref[...] = jnp.transpose(db_rows)[:bins]


def permuted(blocks, swap):
    left, right = jnp.concatenate(blocks[:2], 0), jnp.concatenate(blocks[2:], 0)
    return dot_nn(swap, jnp.concatenate([left, right], 1)).astype(BF16)


def project_kernel(heads, recv_ref, gain_ref, w_ref, wk_ref, x_s, spread_s, k_s, v_s, g_s, n_s):
    peers = recv_ref.shape[0]
    rows, n, chan = x_s.shape
    tiles = n // LANES
    dim = w_ref.shape[0] // (3 * heads)
    width = heads * dim
    base = rows * rows
    gain = gain_ref[...]
    swap = swap_matrix(rows)
    centre = centring(chan)
    group = 2 * rows
    w_k = wk_ref[...]

    quads = range(peers // 4)
    x = [permuted([recv_ref[4 * quad + s, :base] for s in range(4)], swap) for quad in quads]
    normed = [layer_norm(two, centre, gain) for two in x]
    keys = [dot_nt(jnp.concatenate(two, 1), w_k).astype(BF16) for two in normed]
    for quad in quads:
        for side in range(2):
            at = slice((2 * quad + side) * group, (2 * quad + side + 1) * group)
            x_s[:, at, :] = x[quad][:, side * chan : (side + 1) * chan].reshape(rows, group, chan)
            n_s[:, at, :] = normed[quad][side].reshape(rows, group, chan)
            k_s[:, at, :] = keys[quad][:, side * width : (side + 1) * width].reshape(rows, group, width)

    w_qvg = w_ref[...]
    zero = jnp.zeros((dim, LANES), BF16)

    def project(pair):
        both = dot_nt(w_qvg, n_s[pl.ds(2 * pair, 2)].reshape(2 * n, chan)).astype(BF16)
        for side in range(2):
            j = 2 * pair + side
            qvg = both[:, side * n : (side + 1) * n]
            v_s[j] = qvg[width : 2 * width]
            g_s[j] = jax.nn.sigmoid(qvg[2 * width :].astype(F32))
            for t in range(tiles):
                for h in range(heads):
                    for other in range(heads):
                        block = qvg[h * dim : (h + 1) * dim, t * LANES : (t + 1) * LANES] if h == other else zero
                        spread_s[j, t, other * dim : (other + 1) * dim, h * LANES : (h + 1) * LANES] = block

    if tiles == 1:
        for pair in range(rows // 2):
            project(pair)
    else:
        pl.loop(0, rows // 2)(project)


def attend_kernel(
    heads, fused,
    gathered_ref, term_ref, wo_ref, wd_ref, db_ref, x_s, spread_s, k_s, v_s, g_s,
    out_ref, *refs,
):
    if fused:
        second_ref, bias_s, inv_s, e_s, gated_s, new_s = refs
    else:
        bias_s, inv_s, e_s, gated_s = refs
    peers = gathered_ref.shape[0]
    rows, n, chan = x_s.shape
    tiles = n // LANES
    dim = wo_ref.shape[0] // (2 * heads)
    for s in range(peers):
        at = slice(s * rows, (s + 1) * rows)
        extra = gathered_ref[s].astype(F32) * LOG2E
        for t in range(tiles):
            cs = slice(t * LANES, (t + 1) * LANES)
            for h in range(heads):
                start = (t * heads + h) * rows
                bias_s[h, at, cs] = extra[start : start + rows] + term_ref[h, at, cs]

    scaling = dim ** (-0.5) * LOG2E
    w_out = wo_ref[...]

    def soften(j, t):
        cs = slice(t * LANES, (t + 1) * LANES)
        scores = dot_nn(k_s[j], spread_s[j, t])
        for h in range(heads):
            s = scores[:, h * LANES : (h + 1) * LANES] * scaling + bias_s[h, :, cs]
            e = jnp.exp2(s - jnp.max(s, 0, keepdims=True))
            inv_s[j, t, h : h + 1] = 1.0 / jnp.sum(e, 0, keepdims=True)
            e_s[j, t, :, h * LANES : (h + 1) * LANES] = e.astype(BF16)

    def combine(j, t):
        cs = slice(t * LANES, (t + 1) * LANES)
        for first in range(0, heads, 2):
            o = dot_nn(v_s[j, first * dim : (first + 2) * dim], e_s[j, t, :, first * LANES : (first + 2) * LANES])
            for side in range(2):
                h = first + side
                part = o[side * dim : (side + 1) * dim, side * LANES : (side + 1) * LANES]
                mine = slice(h * dim, (h + 1) * dim)
                gated_s[j, mine, cs] = (g_s[j, mine, cs] * (part * inv_s[j, t, h : h + 1])).astype(BF16)

    def updated(pair):
        both = gated_s[pl.ds(2 * pair, 2)].reshape(2 * heads * dim, n)
        return dot_tn(both, w_out).astype(BF16)

    if not fused:

        @pl.loop(0, rows // 2)
        def _(pair):
            for j in (2 * pair, 2 * pair + 1):
                for t in range(tiles):
                    soften(j, t)
                    combine(j, t)
            update = updated(pair)
            for side in range(2):
                out_ref[2 * pair + side] = update[:, side * chan : (side + 1) * chan]

        return

    for stage in (soften, combine):
        for j in range(rows):
            for t in range(tiles):
                stage(j, t)
    for j in range(0, rows, 2):
        update = updated(j // 2).astype(F32)
        both = []
        for side in range(2):
            new = (x_s[j + side].astype(F32) + update[:, side * chan : (side + 1) * chan]).astype(BF16)
            new_s[j + side] = new
            both.append(new.astype(F32).reshape(peers, rows, chan))
        out_ref[:, j * rows : (j + 2) * rows, :] = jnp.concatenate(both, 1).astype(BF16)
    logits_of(new_s, wd_ref[...], db_ref[:, :1], second_ref)


def logits_of(new_ref, w_dist, d_bias, out_ref):
    rows, n, chan = new_ref.shape
    logits = dot_nt(w_dist, new_ref[...].reshape(rows * n, chan)) + d_bias
    for j in range(rows):
        out_ref[j] = logits[:, j * n : (j + 1) * n].astype(BF16)


def finish_kernel(recv_ref, mirror_ref, wd_ref, db_ref, new_hbm, dist_hbm, new_ref, dist_ref, sems):
    peers, _, chan = recv_ref.shape
    rows = new_ref.shape[0]
    group = 2 * rows
    swap = swap_matrix(rows)
    for quad in range(peers // 4):
        new = permuted([recv_ref[4 * quad + s] for s in range(4)], swap)
        for side in range(2):
            at = slice((2 * quad + side) * group, (2 * quad + side + 1) * group)
            new_ref[:, at, :] = new[:, side * chan : (side + 1) * chan].reshape(rows, group, chan)
    copies = [pltpu.make_async_copy(new_ref, new_hbm, sems.at[0])]
    copies[0].start()
    logits_of(new_ref, wd_ref[...], db_ref[:, :1], dist_ref)
    for i in range(rows):
        dist_ref[i] = (dist_ref[i].astype(F32) + mirror_ref[i].astype(F32)).astype(BF16)
        if i % 2:
            at = pl.ds(i - 1, 2)
            copies.append(pltpu.make_async_copy(dist_ref.at[at], dist_hbm.at[at], sems.at[1 + i // 2]))
            copies[-1].start()
    for copy in copies:
        copy.wait()


def call(kernel, outs, args, scratch=(), smem=(), hbm=(), hbm_outs=False, limit=48):
    spaces = [pltpu.SMEM if i in smem else pl.ANY if i in hbm else pltpu.VMEM for i in range(len(args))]
    return pl.pallas_call(
        kernel,
        out_shape=[jax.ShapeDtypeStruct(s, d) for s, d in outs],
        in_specs=[pl.BlockSpec(memory_space=space) for space in spaces],
        out_specs=[pl.BlockSpec(memory_space=pl.ANY if hbm_outs else pltpu.VMEM)] * len(outs),
        scratch_shapes=list(scratch),
        compiler_params=pltpu.CompilerParams(vmem_limit_bytes=limit * 1024 * 1024),
    )(*args)


def all_to_all(blocks):
    return lax.all_to_all(blocks, "row", split_axis=0, concat_axis=0, tiled=True)


def shards(
    pair_act, chain_id, residue_mask, norm_gain, w_proj, w_bias, chain_bias, w_out, w_dist, dist_bias,
):
    rows, n, chan = pair_act.shape
    peers = n // rows
    heads, dim = w_out.shape[0], w_out.shape[1]
    bins = w_dist.shape[1]
    tiles = n // LANES
    width = heads * dim
    fused = lax.axis_size("head") == 1
    gain = norm_gain[None, :]
    base = rows * rows
    length = tiles * heads * rows

    packed, bias = call(
        pack_kernel,
        [((peers, base, chan), BF16), ((length, LANES), BF16)],
        [pair_act, gain, w_bias.T],
        scratch=[
            pltpu.VMEM(pair_act.shape, BF16),
            pltpu.VMEM(gain.shape, F32),
            pltpu.VMEM((heads, chan), BF16),
            pltpu.VMEM((rows // 2, n, 2 * chan), BF16),
            pltpu.VMEM((peers, base, chan), BF16),
            pltpu.VMEM((length, LANES), BF16),
            pltpu.SemaphoreType.DMA((rows + 2,)),
            pltpu.SemaphoreType.DMA((2,)),
        ],
        hbm=(0, 1, 2),
        hbm_outs=True,
        limit=60,
    )
    bias = lax.all_gather(bias, "row", axis=0, tiled=True)
    received = all_to_all(packed)
    term, w_types, w_keys, db_col, gain, w_out, wd_t = call(
        functools.partial(prepare_kernel, heads),
        [
            ((heads, n, n), F32), ((3 * width, chan), BF16), ((2 * width, 2 * chan), BF16), ((bins, LANES), F32),
            ((1, chan), F32), ((2 * width, 2 * chan), BF16), ((bins, chan), BF16),
        ],
        [
            chain_id[None, :], residue_mask[None, :], chain_bias, w_proj, dist_bias[None, :],
            gain, w_out.reshape(width, chan), w_dist.T,
        ],
        smem=(2,),
    )
    received, term, w_types, w_keys, db_col, gain, w_out, wd_t = lax.optimization_barrier(
        (received, term, w_types, w_keys, db_col, gain, w_out, wd_t)
    )
    x_cols, spread, keys, values, gates = call(
        functools.partial(project_kernel, heads),
        [
            ((rows, n, chan), BF16),
            ((rows, tiles, width, heads * LANES), BF16),
            ((rows, n, width), BF16),
            ((rows, width, n), BF16),
            ((rows, width, n), F32),
        ],
        [received, gain, w_types, w_keys],
        scratch=[pltpu.VMEM((rows, n, chan), BF16)],
    )
    if fused:
        outs = [((peers, base, chan), BF16), ((rows, bins, n), BF16)]
    else:
        outs = [((rows, n, chan), BF16)]
    result = call(
        functools.partial(attend_kernel, heads, fused),
        outs,
        [bias.reshape(peers, length, LANES), term, w_out, wd_t, db_col, x_cols, spread, keys, values, gates],
        scratch=[
            pltpu.VMEM((heads, n, n), F32),
            pltpu.VMEM((rows, tiles, heads, LANES), F32),
            pltpu.VMEM((rows, tiles, n, heads * LANES), BF16),
            pltpu.VMEM((rows, width, n), BF16),
        ]
        + [pltpu.VMEM((rows, n, chan), BF16)] * fused,
    )
    if fused:
        to_rows, mirror = result
    else:
        update = lax.psum(result[0], "head").astype(F32)
        new = (x_cols.astype(F32) + update).astype(BF16)
        logits = jnp.einsum("cb,jic->jbi", w_dist, new, preferred_element_type=F32)
        mirror = (logits + dist_bias[None, :, None]).astype(BF16)
        to_rows = new.reshape(rows, peers, rows, chan).transpose(1, 0, 2, 3).reshape(peers, base, chan)
    arrived = all_to_all(to_rows)
    new_rows, dist = call(
        finish_kernel,
        [((rows, n, chan), BF16), ((rows, bins, n), BF16)],
        [arrived, mirror, wd_t, db_col],
        scratch=[
            pltpu.VMEM((rows, n, chan), BF16),
            pltpu.VMEM((rows, bins, n), BF16),
            pltpu.SemaphoreType.DMA((1 + rows // 2,)),
        ],
        hbm_outs=True,
    )
    return new_rows, dist.transpose(0, 2, 1)


def solution(mesh):
    in_specs = (
        P(("dp", "row"), None, None),
        P("dp"),
        P("dp"),
        P(),
        P(None, "head", None),
        P(None, "head"),
        P(None, "head"),
        P("head", None, None),
        P(),
        P(),
    )
    out_specs = (P(("dp", "row"), None, None), P(("dp", "row"), None, None))
    return jax.shard_map(shards, mesh=mesh, in_specs=in_specs, out_specs=out_specs, check_vma=False)
```

```python
import functools

import jax
import jax.numpy as jnp
from jax import lax
from jax.experimental import pallas as pl
from jax.experimental.pallas import tpu as pltpu
from jax.sharding import PartitionSpec as P

LANES = 128
F32 = jnp.float32
BF16 = jnp.bfloat16
LOG2E = 1.4426950408889634


def dot_nt(a, b):
    return lax.dot_general(a, b, (((1,), (1,)), ((), ())), preferred_element_type=F32)


def dot_tn(a, b):
    return lax.dot_general(a, b, (((0,), (0,)), ((), ())), preferred_element_type=F32)


def dot_nn(a, b):
    return jnp.dot(a, b, preferred_element_type=F32)


def centring(chan):
    row = lax.broadcasted_iota(jnp.int32, (2 * chan, 2 * chan), 0)
    col = lax.broadcasted_iota(jnp.int32, (2 * chan, 2 * chan), 1)
    inside = (row // chan) == (col // chan)
    return (jnp.where(row == col, 1.0, 0.0) - jnp.where(inside, 1.0 / chan, 0.0)).astype(BF16)


def layer_norm(values, centre, gain):
    chan = gain.shape[1]
    centered = dot_nn(values, centre)
    halves = []
    for part in (centered[:, :chan], centered[:, chan:]):
        variance = jnp.mean(part * part, -1, keepdims=True)
        halves.append((part * lax.rsqrt(variance + 1e-05) * gain).astype(BF16))
    return halves


def swap_matrix(rows):
    size = 2 * rows * rows
    out = lax.broadcasted_iota(jnp.int32, (size, size), 0)
    col = lax.broadcasted_iota(jnp.int32, (size, size), 1)
    b, rest = out // (2 * rows), out % (2 * rows)
    wanted = (rest // rows) * (rows * rows) + (rest % rows) * rows + b
    return jnp.where(col == wanted, 1.0, 0.0).astype(BF16)


def pack_kernel(x_hbm, gain_hbm, wb_hbm, out_hbm, x_ref, gain_ref, wb_ref, out_ref, sems, out_sems):
    rows, n, chan = x_ref.shape
    peers = n // rows
    heads = wb_ref.shape[0]
    half = heads * rows // 2
    base = rows * rows
    fetch_gain = pltpu.make_async_copy(gain_hbm, gain_ref, sems.at[rows])
    fetch_wb = pltpu.make_async_copy(wb_hbm, wb_ref, sems.at[rows + 1])
    fetches = [pltpu.make_async_copy(x_hbm.at[k], x_ref.at[k], sems.at[k]) for k in range(rows)]
    for copy in (fetch_gain, fetch_wb, *fetches):
        copy.start()
    stores = []

    def store(first, count):
        at = pl.ds(first, count)
        copy = pltpu.make_async_copy(out_ref.at[:, at, :], out_hbm.at[:, at, :], out_sems.at[len(stores)])
        copy.start()
        stores.append(copy)

    centre = centring(chan)
    owner = lax.broadcasted_iota(jnp.int32, (heads * rows, chan), 0) % rows
    bias = jnp.zeros((heads * rows, n), F32)
    fetch_gain.wait()
    fetch_wb.wait()
    gain = gain_ref[...]
    wb = wb_ref[...].astype(F32)
    wb = jnp.concatenate([jnp.broadcast_to(wb[h : h + 1], (rows, chan)) for h in range(heads)], 0)
    mine = [jnp.where(owner == k, wb, 0.0).astype(BF16) for k in range(rows)]
    mine = [jnp.concatenate(mine[k : k + 2], 1) for k in range(0, rows, 2)]
    for copy in fetches:
        copy.wait()
    for pair in range(rows // 2):
        both = [x_ref[k].astype(F32).reshape(peers, rows, chan) for k in (2 * pair, 2 * pair + 1)]
        out_ref[:, 2 * rows * pair : 2 * rows * (pair + 1), :] = jnp.concatenate(both, 1).astype(BF16)
    store(0, base)
    two = [jnp.concatenate([x_ref[k], x_ref[k + 1]], 1) for k in range(0, rows, 2)]
    normed = [layer_norm(values, centre, gain) for values in two]
    for pair in range(rows // 2):
        bias = bias + dot_nt(mine[pair], jnp.concatenate(normed[pair], 1))
    bias = bias.astype(BF16)
    for t in range(n // LANES):
        block = bias[:, t * LANES : (t + 1) * LANES]
        for d in range(peers):
            part = block[(d % 2) * half : (d % 2 + 1) * half]
            out_ref[d, base + t * half : base + (t + 1) * half] = part
    store(base, (n // LANES) * half)
    for copy in stores:
        copy.wait()


def prepare_kernel(
    heads, rows,
    chain_ref, mask_ref, cb_ref, w_ref, db_ref, gain_ref, wo_ref, wd_ref,
    term_ref, wt_ref, wk_out, dbc_ref, gain_out, wo_out, wd_out, swap_ref, centre_ref,
):
    gain_out[...] = gain_ref[...]
    swap_ref[...] = swap_matrix(rows)
    centre_ref[...] = centring(w_ref.shape[0])
    chan = w_ref.shape[0]
    width = wo_ref.shape[0]
    wk_out[...] = jnp.zeros_like(wk_out)
    wo_out[...] = jnp.zeros_like(wo_out)
    for side in range(2):
        wo_out[side * width : (side + 1) * width, side * chan : (side + 1) * chan] = wo_ref[...]
    wd_out[...] = wd_ref[...]
    n = chain_ref.shape[1]
    tiles = n // LANES
    dim = w_ref.shape[2] // 4

    def column_of(row):
        return jnp.transpose(jnp.broadcast_to(row, (LANES, LANES)))

    for kt in range(tiles):
        ks = slice(kt * LANES, (kt + 1) * LANES)
        chain_k = column_of(chain_ref[:, ks].astype(F32))
        mask_k = (column_of(mask_ref[:, ks].astype(F32)) - 1.0) * 1000000000.0
        for it in range(tiles):
            cs = slice(it * LANES, (it + 1) * LANES)
            same = chain_k == chain_ref[:, cs].astype(F32)
            for h in range(heads):
                term_ref[h, ks, cs] = (jnp.where(same, cb_ref[1, h], cb_ref[0, h]) + mask_k) * LOG2E
    for h in range(heads):
        turned = jnp.transpose(w_ref[:, h, :].astype(F32)).astype(BF16)
        for place, kind in enumerate((0, 2, 3)):
            start = place * width + h * dim
            wt_ref[start : start + dim] = turned[kind * dim : (kind + 1) * dim]
        for side in range(2):
            start = side * width + h * dim
            wk_out[start : start + dim, side * chan : (side + 1) * chan] = turned[dim : 2 * dim]
    bins = dbc_ref.shape[0]
    db_rows = jnp.broadcast_to(jnp.concatenate([db_ref[...], db_ref[...]], 1)[:, :LANES], (LANES, LANES))
    dbc_ref[...] = jnp.transpose(db_rows)[:bins]


def permuted(blocks, swap):
    left, right = jnp.concatenate(blocks[:2], 0), jnp.concatenate(blocks[2:], 0)
    return dot_nn(swap, jnp.concatenate([left, right], 1)).astype(BF16)


def project_kernel(heads, recv_ref, gain_ref, w_ref, wk_ref, swap_ref, centre_ref, x_s, spread_s, k_s, v_s, g_s, n_s):
    peers = recv_ref.shape[0]
    rows, n, chan = x_s.shape
    tiles = n // LANES
    dim = w_ref.shape[0] // (3 * heads)
    width = heads * dim
    base = rows * rows
    gain = gain_ref[...]
    swap = swap_ref[...]
    centre = centre_ref[...]
    group = 2 * rows
    w_k = wk_ref[...]

    quads = range(peers // 4)
    x = [permuted([recv_ref[4 * quad + s, :base] for s in range(4)], swap) for quad in quads]
    normed = [layer_norm(two, centre, gain) for two in x]
    keys = [dot_nt(jnp.concatenate(two, 1), w_k).astype(BF16) for two in normed]
    for quad in quads:
        for side in range(2):
            at = slice((2 * quad + side) * group, (2 * quad + side + 1) * group)
            x_s[:, at, :] = x[quad][:, side * chan : (side + 1) * chan].reshape(rows, group, chan)
            n_s[:, at, :] = normed[quad][side].reshape(rows, group, chan)
            k_s[:, at, :] = keys[quad][:, side * width : (side + 1) * width].reshape(rows, group, width)

    w_qvg = w_ref[...]
    zero = jnp.zeros((dim, LANES), BF16)

    def project(pair):
        both = dot_nt(w_qvg, n_s[pl.ds(2 * pair, 2)].reshape(2 * n, chan)).astype(BF16)
        for side in range(2):
            j = 2 * pair + side
            qvg = both[:, side * n : (side + 1) * n]
            v_s[j] = qvg[width : 2 * width]
            g_s[j] = jax.nn.sigmoid(qvg[2 * width :].astype(F32))
            for t in range(tiles):
                for h in range(heads):
                    for other in range(heads):
                        block = qvg[h * dim : (h + 1) * dim, t * LANES : (t + 1) * LANES] if h == other else zero
                        spread_s[j, t, other * dim : (other + 1) * dim, h * LANES : (h + 1) * LANES] = block

    if tiles == 1:
        for pair in range(rows // 2):
            project(pair)
    else:
        pl.loop(0, rows // 2)(project)


def attend_kernel(
    heads, fused,
    recv_ref, other_ref, term_ref, wo_ref, wd_ref, db_ref, x_s, spread_s, k_s, v_s, g_s,
    out_ref, *refs,
):
    if fused:
        second_ref, bias_s, inv_s, e_s, gated_s, new_s = refs
    else:
        bias_s, inv_s, e_s, gated_s = refs
    peers = recv_ref.shape[0]
    rows, n, chan = x_s.shape
    tiles = n // LANES
    dim = wo_ref.shape[0] // (2 * heads)
    half = heads // 2
    base = rows * rows
    core = lax.axis_index("row") % 2

    for s in range(peers):
        at = slice(s * rows, (s + 1) * rows)
        for block, owner in ((recv_ref[s, base:], core), (other_ref[s], 1 - core)):
            extra = block.astype(F32) * LOG2E
            for t in range(tiles):
                cs = slice(t * LANES, (t + 1) * LANES)
                for h in range(half):
                    start = (t * half + h) * rows
                    head = owner * half + h
                    bias_s[head, at, cs] = extra[start : start + rows] + term_ref[head, at, cs]

    scaling = dim ** (-0.5) * LOG2E
    w_out = wo_ref[...]

    def soften(j, t):
        cs = slice(t * LANES, (t + 1) * LANES)
        scores = dot_nn(k_s[j], spread_s[j, t])
        for h in range(heads):
            s = scores[:, h * LANES : (h + 1) * LANES] * scaling + bias_s[h, :, cs]
            e = jnp.exp2(s - jnp.max(s, 0, keepdims=True))
            inv_s[j, t, h : h + 1] = 1.0 / jnp.sum(e, 0, keepdims=True)
            e_s[j, t, :, h * LANES : (h + 1) * LANES] = e.astype(BF16)

    def combine(j, t):
        cs = slice(t * LANES, (t + 1) * LANES)
        for first in range(0, heads, 2):
            o = dot_nn(v_s[j, first * dim : (first + 2) * dim], e_s[j, t, :, first * LANES : (first + 2) * LANES])
            for side in range(2):
                h = first + side
                part = o[side * dim : (side + 1) * dim, side * LANES : (side + 1) * LANES]
                mine = slice(h * dim, (h + 1) * dim)
                gated_s[j, mine, cs] = (g_s[j, mine, cs] * (part * inv_s[j, t, h : h + 1])).astype(BF16)

    def updated(pair):
        both = gated_s[pl.ds(2 * pair, 2)].reshape(2 * heads * dim, n)
        return dot_tn(both, w_out).astype(BF16)

    if not fused:

        @pl.loop(0, rows // 2)
        def _(pair):
            for j in (2 * pair, 2 * pair + 1):
                for t in range(tiles):
                    soften(j, t)
                    combine(j, t)
            update = updated(pair)
            for side in range(2):
                out_ref[2 * pair + side] = update[:, side * chan : (side + 1) * chan]

        return

    for stage in (soften, combine):
        for j in range(rows):
            for t in range(tiles):
                stage(j, t)
    for j in range(0, rows, 2):
        update = updated(j // 2).astype(F32)
        both = []
        for side in range(2):
            new = (x_s[j + side].astype(F32) + update[:, side * chan : (side + 1) * chan]).astype(BF16)
            new_s[j + side] = new
            both.append(new.astype(F32).reshape(peers, rows, chan))
        out_ref[:, j * rows : (j + 2) * rows, :] = jnp.concatenate(both, 1).astype(BF16)
    logits_of(new_s, wd_ref[...], db_ref[:, :1], second_ref)


def logits_of(new_ref, w_dist, d_bias, out_ref):
    rows, n, chan = new_ref.shape
    logits = dot_nt(w_dist, new_ref[...].reshape(rows * n, chan)) + d_bias
    for j in range(rows):
        out_ref[j] = logits[:, j * n : (j + 1) * n].astype(BF16)


def finish_kernel(recv_ref, mirror_ref, wd_ref, db_ref, swap_ref, new_hbm, dist_hbm, new_ref, dist_ref, sems):
    peers, _, chan = recv_ref.shape
    rows = new_ref.shape[0]
    group = 2 * rows
    swap = swap_ref[...]
    for quad in range(peers // 4):
        new = permuted([recv_ref[4 * quad + s] for s in range(4)], swap)
        for side in range(2):
            at = slice((2 * quad + side) * group, (2 * quad + side + 1) * group)
            new_ref[:, at, :] = new[:, side * chan : (side + 1) * chan].reshape(rows, group, chan)
    copies = [pltpu.make_async_copy(new_ref, new_hbm, sems.at[0])]
    copies[0].start()
    logits_of(new_ref, wd_ref[...], db_ref[:, :1], dist_ref)
    for i in range(rows):
        dist_ref[i] = (dist_ref[i].astype(F32) + mirror_ref[i].astype(F32)).astype(BF16)
        if i % 2:
            at = pl.ds(i - 1, 2)
            copies.append(pltpu.make_async_copy(dist_ref.at[at], dist_hbm.at[at], sems.at[1 + i // 2]))
            copies[-1].start()
    for copy in copies:
        copy.wait()


def call(kernel, outs, args, scratch=(), smem=(), hbm=(), hbm_outs=False, limit=48):
    spaces = [pltpu.SMEM if i in smem else pl.ANY if i in hbm else pltpu.VMEM for i in range(len(args))]
    return pl.pallas_call(
        kernel,
        out_shape=[jax.ShapeDtypeStruct(s, d) for s, d in outs],
        in_specs=[pl.BlockSpec(memory_space=space) for space in spaces],
        out_specs=[pl.BlockSpec(memory_space=pl.ANY if hbm_outs else pltpu.VMEM)] * len(outs),
        scratch_shapes=list(scratch),
        compiler_params=pltpu.CompilerParams(vmem_limit_bytes=limit * 1024 * 1024),
    )(*args)


def swap_cores(values):
    peers = lax.axis_size("row")
    return lax.ppermute(values, "row", [(i, i ^ 1) for i in range(peers)])


def all_to_all(blocks):
    return lax.all_to_all(blocks, "row", split_axis=0, concat_axis=0, tiled=True)


def shards(
    pair_act, chain_id, residue_mask, norm_gain, w_proj, w_bias, chain_bias, w_out, w_dist, dist_bias,
):
    rows, n, chan = pair_act.shape
    peers = n // rows
    heads, dim = w_out.shape[0], w_out.shape[1]
    bins = w_dist.shape[1]
    tiles = n // LANES
    width = heads * dim
    fused = lax.axis_size("head") == 1
    gain = norm_gain[None, :]
    base = rows * rows
    length = base + tiles * heads * rows // 2

    (packed,) = call(
        pack_kernel,
        [((peers, length, chan), BF16)],
        [pair_act, gain, w_bias.T],
        scratch=[
            pltpu.VMEM(pair_act.shape, BF16),
            pltpu.VMEM(gain.shape, F32),
            pltpu.VMEM((heads, chan), BF16),
            pltpu.VMEM((peers, length, chan), BF16),
            pltpu.SemaphoreType.DMA((rows + 2,)),
            pltpu.SemaphoreType.DMA((2,)),
        ],
        hbm=(0, 1, 2),
        hbm_outs=True,
        limit=60,
    )
    received = all_to_all(packed)
    prepared = call(
        functools.partial(prepare_kernel, heads, rows),
        [
            ((heads, n, n), F32), ((3 * width, chan), BF16), ((2 * width, 2 * chan), BF16), ((bins, LANES), F32),
            ((1, chan), F32), ((2 * width, 2 * chan), BF16), ((bins, chan), BF16),
            ((2 * base, 2 * base), BF16), ((2 * chan, 2 * chan), BF16),
        ],
        [
            chain_id[None, :], residue_mask[None, :], chain_bias, w_proj, dist_bias[None, :],
            gain, w_out.reshape(width, chan), w_dist.T,
        ],
        smem=(2,),
    )
    received, *prepared = lax.optimization_barrier((received, *prepared))
    term, w_types, w_keys, db_col, gain, w_out, wd_t, swap, centre = prepared
    other_bias = swap_cores(received[:, base:])
    x_cols, spread, keys, values, gates = call(
        functools.partial(project_kernel, heads),
        [
            ((rows, n, chan), BF16),
            ((rows, tiles, width, heads * LANES), BF16),
            ((rows, n, width), BF16),
            ((rows, width, n), BF16),
            ((rows, width, n), F32),
        ],
        [received, gain, w_types, w_keys, swap, centre],
        scratch=[pltpu.VMEM((rows, n, chan), BF16)],
    )
    if fused:
        outs = [((peers, base, chan), BF16), ((rows, bins, n), BF16)]
    else:
        outs = [((rows, n, chan), BF16)]
    result = call(
        functools.partial(attend_kernel, heads, fused),
        outs,
        [received, other_bias, term, w_out, wd_t, db_col, x_cols, spread, keys, values, gates],
        scratch=[
            pltpu.VMEM((heads, n, n), F32),
            pltpu.VMEM((rows, tiles, heads, LANES), F32),
            pltpu.VMEM((rows, tiles, n, heads * LANES), BF16),
            pltpu.VMEM((rows, width, n), BF16),
        ]
        + [pltpu.VMEM((rows, n, chan), BF16)] * fused,
    )
    if fused:
        to_rows, mirror = result
    else:
        update = lax.psum(result[0], "head").astype(F32)
        new = (x_cols.astype(F32) + update).astype(BF16)
        logits = jnp.einsum("cb,jic->jbi", w_dist, new, preferred_element_type=F32)
        mirror = (logits + dist_bias[None, :, None]).astype(BF16)
        to_rows = new.reshape(rows, peers, rows, chan).transpose(1, 0, 2, 3).reshape(peers, base, chan)
    arrived = all_to_all(to_rows)
    new_rows, dist = call(
        finish_kernel,
        [((rows, n, chan), BF16), ((rows, bins, n), BF16)],
        [arrived, mirror, wd_t, db_col, swap],
        scratch=[
            pltpu.VMEM((rows, n, chan), BF16),
            pltpu.VMEM((rows, bins, n), BF16),
            pltpu.SemaphoreType.DMA((1 + rows // 2,)),
        ],
        hbm_outs=True,
    )
    return new_rows, dist.transpose(0, 2, 1)


def solution(mesh):
    in_specs = (
        P(("dp", "row"), None, None),
        P("dp"),
        P("dp"),
        P(),
        P(None, "head", None),
        P(None, "head"),
        P(None, "head"),
        P("head", None, None),
        P(),
        P(),
    )
    out_specs = (P(("dp", "row"), None, None), P(("dp", "row"), None, None))
    return jax.shard_map(shards, mesh=mesh, in_specs=in_specs, out_specs=out_specs, check_vma=False)
```

```python
import functools

import jax
import jax.numpy as jnp
from jax import lax
from jax.experimental import pallas as pl
from jax.experimental.pallas import tpu as pltpu
from jax.sharding import PartitionSpec as P

LANES = 128
F32 = jnp.float32
BF16 = jnp.bfloat16
LOG2E = 1.4426950408889634


def dot_nt(a, b):
    return lax.dot_general(a, b, (((1,), (1,)), ((), ())), preferred_element_type=F32)


def dot_tn(a, b):
    return lax.dot_general(a, b, (((0,), (0,)), ((), ())), preferred_element_type=F32)


def dot_nn(a, b):
    return jnp.dot(a, b, preferred_element_type=F32)


def centring(chan):
    row = lax.broadcasted_iota(jnp.int32, (2 * chan, 2 * chan), 0)
    col = lax.broadcasted_iota(jnp.int32, (2 * chan, 2 * chan), 1)
    inside = (row // chan) == (col // chan)
    return (jnp.where(row == col, 1.0, 0.0) - jnp.where(inside, 1.0 / chan, 0.0)).astype(BF16)


def layer_norm(values, centre, gain):
    chan = gain.shape[1]
    centered = dot_nn(values, centre)
    halves = []
    for part in (centered[:, :chan], centered[:, chan:]):
        variance = jnp.mean(part * part, -1, keepdims=True)
        halves.append((part * lax.rsqrt(variance + 1e-05) * gain).astype(BF16))
    return halves


def swap_matrix(rows):
    size = 2 * rows * rows
    out = lax.broadcasted_iota(jnp.int32, (size, size), 0)
    col = lax.broadcasted_iota(jnp.int32, (size, size), 1)
    b, rest = out // (2 * rows), out % (2 * rows)
    wanted = (rest // rows) * (rows * rows) + (rest % rows) * rows + b
    return jnp.where(col == wanted, 1.0, 0.0).astype(BF16)


def pack_kernel(x_hbm, gain_hbm, wb_hbm, out_hbm, x_ref, gain_ref, wb_ref, out_ref, sems, out_sems):
    rows, n, chan = x_ref.shape
    peers = n // rows
    heads = wb_ref.shape[0]
    half = heads * rows // 2
    base = rows * rows
    fetch_gain = pltpu.make_async_copy(gain_hbm, gain_ref, sems.at[rows])
    fetch_wb = pltpu.make_async_copy(wb_hbm, wb_ref, sems.at[rows + 1])
    fetches = [pltpu.make_async_copy(x_hbm.at[k], x_ref.at[k], sems.at[k]) for k in range(rows)]
    for copy in (fetch_gain, fetch_wb, *fetches):
        copy.start()
    stores = []

    def store(*at):
        copy = pltpu.make_async_copy(out_ref.at[at], out_hbm.at[at], out_sems.at[len(stores)])
        copy.start()
        stores.append(copy)

    centre = centring(chan)
    owner = lax.broadcasted_iota(jnp.int32, (heads * rows, chan), 0) % rows
    bias = jnp.zeros((heads * rows, n), F32)
    fetch_gain.wait()
    fetch_wb.wait()
    gain = gain_ref[...]
    wb = wb_ref[...].astype(F32)
    wb = jnp.concatenate([jnp.broadcast_to(wb[h : h + 1], (rows, chan)) for h in range(heads)], 0)
    mine = [jnp.where(owner == k, wb, 0.0).astype(BF16) for k in range(rows)]
    mine = [jnp.concatenate(mine[k : k + 2], 1) for k in range(0, rows, 2)]
    for copy in fetches:
        copy.wait()
    share = peers // 4
    for first in range(0, peers, share):
        for pair in range(rows // 2):
            at = pl.ds(first * rows, share * rows)
            both = [x_ref[k, at, :].astype(F32).reshape(share, rows, chan) for k in (2 * pair, 2 * pair + 1)]
            joined = jnp.concatenate(both, 1).astype(BF16)
            out_ref[first : first + share, 2 * rows * pair : 2 * rows * (pair + 1), :] = joined
        store(pl.ds(first, share), pl.ds(0, base), slice(None))
    two = [jnp.concatenate([x_ref[k], x_ref[k + 1]], 1) for k in range(0, rows, 2)]
    normed = [layer_norm(values, centre, gain) for values in two]
    for pair in range(rows // 2):
        bias = bias + dot_nt(mine[pair], jnp.concatenate(normed[pair], 1))
    bias = bias.astype(BF16)
    for t in range(n // LANES):
        block = bias[:, t * LANES : (t + 1) * LANES]
        for d in range(peers):
            part = block[(d % 2) * half : (d % 2 + 1) * half]
            out_ref[d, base + t * half : base + (t + 1) * half] = part
    store(slice(None), pl.ds(base, (n // LANES) * half), slice(None))
    for copy in stores:
        copy.wait()


def prepare_kernel(
    heads, rows,
    chain_ref, mask_ref, cb_ref, w_ref, db_ref, gain_ref, wo_ref, wd_ref,
    term_ref, wt_ref, wk_out, dbc_ref, gain_out, wo_out, wd_out, swap_ref, centre_ref,
):
    gain_out[...] = gain_ref[...]
    swap_ref[...] = swap_matrix(rows)
    centre_ref[...] = centring(w_ref.shape[0])
    chan = w_ref.shape[0]
    width = wo_ref.shape[0]
    wk_out[...] = jnp.zeros_like(wk_out)
    wo_out[...] = jnp.zeros_like(wo_out)
    for side in range(2):
        wo_out[side * width : (side + 1) * width, side * chan : (side + 1) * chan] = wo_ref[...]
    wd_out[...] = wd_ref[...]
    n = chain_ref.shape[1]
    tiles = n // LANES
    dim = w_ref.shape[2] // 4

    def column_of(row):
        return jnp.transpose(jnp.broadcast_to(row, (LANES, LANES)))

    for kt in range(tiles):
        ks = slice(kt * LANES, (kt + 1) * LANES)
        chain_k = column_of(chain_ref[:, ks].astype(F32))
        mask_k = (column_of(mask_ref[:, ks].astype(F32)) - 1.0) * 1000000000.0
        for it in range(tiles):
            cs = slice(it * LANES, (it + 1) * LANES)
            same = chain_k == chain_ref[:, cs].astype(F32)
            for h in range(heads):
                term_ref[h, ks, cs] = (jnp.where(same, cb_ref[1, h], cb_ref[0, h]) + mask_k) * LOG2E
    for h in range(heads):
        turned = jnp.transpose(w_ref[:, h, :].astype(F32)).astype(BF16)
        for place, kind in enumerate((0, 2, 3)):
            start = place * width + h * dim
            wt_ref[start : start + dim] = turned[kind * dim : (kind + 1) * dim]
        for side in range(2):
            start = side * width + h * dim
            wk_out[start : start + dim, side * chan : (side + 1) * chan] = turned[dim : 2 * dim]
    bins = dbc_ref.shape[0]
    db_rows = jnp.broadcast_to(jnp.concatenate([db_ref[...], db_ref[...]], 1)[:, :LANES], (LANES, LANES))
    dbc_ref[...] = jnp.transpose(db_rows)[:bins]


def permuted(blocks, swap):
    left, right = jnp.concatenate(blocks[:2], 0), jnp.concatenate(blocks[2:], 0)
    return dot_nn(swap, jnp.concatenate([left, right], 1)).astype(BF16)


def unpack_bias(blocks, term_ref, owner, bias_ref):
    half, n = bias_ref.shape[0], bias_ref.shape[1]
    rows = n // len(blocks)
    for s, block in enumerate(blocks):
        at = slice(s * rows, (s + 1) * rows)
        extra = block.astype(F32) * LOG2E
        for t in range(n // LANES):
            cs = slice(t * LANES, (t + 1) * LANES)
            for h in range(half):
                start = (t * half + h) * rows
                bias_ref[h, at, cs] = extra[start : start + rows] + term_ref[owner * half + h, at, cs]


def project_kernel(
    heads, recv_ref, gain_ref, w_ref, wk_ref, swap_ref, centre_ref, term_ref,
    x_s, spread_s, k_s, v_s, g_s, own_s, n_s,
):
    peers = recv_ref.shape[0]
    rows, n, chan = x_s.shape
    tiles = n // LANES
    dim = w_ref.shape[0] // (3 * heads)
    width = heads * dim
    base = rows * rows
    gain = gain_ref[...]
    swap = swap_ref[...]
    centre = centre_ref[...]
    group = 2 * rows
    w_k = wk_ref[...]

    quads = range(peers // 4)
    x = [permuted([recv_ref[4 * quad + s, :base] for s in range(4)], swap) for quad in quads]
    normed = [layer_norm(two, centre, gain) for two in x]
    keys = [dot_nt(jnp.concatenate(two, 1), w_k).astype(BF16) for two in normed]
    for quad in quads:
        for side in range(2):
            at = slice((2 * quad + side) * group, (2 * quad + side + 1) * group)
            x_s[:, at, :] = x[quad][:, side * chan : (side + 1) * chan].reshape(rows, group, chan)
            n_s[:, at, :] = normed[quad][side].reshape(rows, group, chan)
            k_s[:, at, :] = keys[quad][:, side * width : (side + 1) * width].reshape(rows, group, width)

    w_qvg = w_ref[...]
    zero = jnp.zeros((dim, LANES), BF16)

    def project(pair):
        both = dot_nt(w_qvg, n_s[pl.ds(2 * pair, 2)].reshape(2 * n, chan)).astype(BF16)
        for side in range(2):
            j = 2 * pair + side
            qvg = both[:, side * n : (side + 1) * n]
            v_s[j] = qvg[width : 2 * width]
            g_s[j] = jax.nn.sigmoid(qvg[2 * width :].astype(F32))
            for t in range(tiles):
                for h in range(heads):
                    for other in range(heads):
                        block = qvg[h * dim : (h + 1) * dim, t * LANES : (t + 1) * LANES] if h == other else zero
                        spread_s[j, t, other * dim : (other + 1) * dim, h * LANES : (h + 1) * LANES] = block

    if tiles == 1:
        for pair in range(rows // 2):
            project(pair)
    else:
        pl.loop(0, rows // 2)(project)
    unpack_bias([recv_ref[s, base:] for s in range(peers)], term_ref, lax.axis_index("row") % 2, own_s)


def attend_kernel(
    heads, fused,
    other_ref, own_s, term_ref, wo_ref, wd_ref, db_ref, x_s, spread_s, k_s, v_s, g_s,
    out_ref, *refs,
):
    if fused:
        second_ref, bias_s, inv_s, e_s, gated_s, new_s = refs
    else:
        bias_s, inv_s, e_s, gated_s = refs
    peers = other_ref.shape[0]
    rows, n, chan = x_s.shape
    tiles = n // LANES
    dim = wo_ref.shape[0] // (2 * heads)
    half = heads // 2
    core = lax.axis_index("row") % 2

    bias_s[pl.ds(core * half, half)] = own_s[...]
    other_half = bias_s.at[pl.ds((1 - core) * half, half)]
    unpack_bias([other_ref[s] for s in range(peers)], term_ref, 1 - core, other_half)

    scaling = dim ** (-0.5) * LOG2E
    w_out = wo_ref[...]

    def soften(j, t):
        cs = slice(t * LANES, (t + 1) * LANES)
        scores = dot_nn(k_s[j], spread_s[j, t])
        for h in range(heads):
            s = scores[:, h * LANES : (h + 1) * LANES] * scaling + bias_s[h, :, cs]
            e = jnp.exp2(s - jnp.max(s, 0, keepdims=True))
            inv_s[j, t, h : h + 1] = 1.0 / jnp.sum(e, 0, keepdims=True)
            e_s[j, t, :, h * LANES : (h + 1) * LANES] = e.astype(BF16)

    def combine(j, t):
        cs = slice(t * LANES, (t + 1) * LANES)
        for first in range(0, heads, 2):
            o = dot_nn(v_s[j, first * dim : (first + 2) * dim], e_s[j, t, :, first * LANES : (first + 2) * LANES])
            for side in range(2):
                h = first + side
                part = o[side * dim : (side + 1) * dim, side * LANES : (side + 1) * LANES]
                mine = slice(h * dim, (h + 1) * dim)
                gated_s[j, mine, cs] = (g_s[j, mine, cs] * (part * inv_s[j, t, h : h + 1])).astype(BF16)

    def updated(pair):
        both = gated_s[pl.ds(2 * pair, 2)].reshape(2 * heads * dim, n)
        return dot_tn(both, w_out).astype(BF16)

    if not fused:

        @pl.loop(0, rows // 2)
        def _(pair):
            for j in (2 * pair, 2 * pair + 1):
                for t in range(tiles):
                    soften(j, t)
                    combine(j, t)
            update = updated(pair)
            for side in range(2):
                out_ref[2 * pair + side] = update[:, side * chan : (side + 1) * chan]

        return

    for stage in (soften, combine):
        for j in range(rows):
            for t in range(tiles):
                stage(j, t)
    for j in range(0, rows, 2):
        update = updated(j // 2).astype(F32)
        both = []
        for side in range(2):
            new = (x_s[j + side].astype(F32) + update[:, side * chan : (side + 1) * chan]).astype(BF16)
            new_s[j + side] = new
            both.append(new.astype(F32).reshape(peers, rows, chan))
        out_ref[:, j * rows : (j + 2) * rows, :] = jnp.concatenate(both, 1).astype(BF16)
    logits_of(new_s, wd_ref[...], db_ref[:, :1], second_ref)


def logits_of(new_ref, w_dist, d_bias, out_ref):
    rows, n, chan = new_ref.shape
    logits = dot_nt(w_dist, new_ref[...].reshape(rows * n, chan)) + d_bias
    for j in range(rows):
        out_ref[j] = logits[:, j * n : (j + 1) * n].astype(BF16)


def finish_kernel(recv_ref, mirror_ref, wd_ref, db_ref, swap_ref, new_hbm, dist_hbm, new_ref, dist_ref, sems):
    peers, _, chan = recv_ref.shape
    rows = new_ref.shape[0]
    group = 2 * rows
    swap = swap_ref[...]
    copies = []
    for quad in range(peers // 4):
        new = permuted([recv_ref[4 * quad + s] for s in range(4)], swap)
        for side in range(2):
            at = slice((2 * quad + side) * group, (2 * quad + side + 1) * group)
            new_ref[:, at, :] = new[:, side * chan : (side + 1) * chan].reshape(rows, group, chan)
        at = pl.ds(2 * quad * group, 2 * group)
        copies.append(pltpu.make_async_copy(new_ref.at[:, at, :], new_hbm.at[:, at, :], sems.at[quad]))
        copies[-1].start()
    logits_of(new_ref, wd_ref[...], db_ref[:, :1], dist_ref)
    for i in range(rows):
        dist_ref[i] = (dist_ref[i].astype(F32) + mirror_ref[i].astype(F32)).astype(BF16)
        if i % 2:
            at = pl.ds(i - 1, 2)
            copies.append(pltpu.make_async_copy(dist_ref.at[at], dist_hbm.at[at], sems.at[peers // 4 + i // 2]))
            copies[-1].start()
    for copy in copies:
        copy.wait()


def call(kernel, outs, args, scratch=(), smem=(), hbm=(), hbm_outs=False, limit=48):
    spaces = [pltpu.SMEM if i in smem else pl.ANY if i in hbm else pltpu.VMEM for i in range(len(args))]
    return pl.pallas_call(
        kernel,
        out_shape=[jax.ShapeDtypeStruct(s, d) for s, d in outs],
        in_specs=[pl.BlockSpec(memory_space=space) for space in spaces],
        out_specs=[pl.BlockSpec(memory_space=pl.ANY if hbm_outs else pltpu.VMEM)] * len(outs),
        scratch_shapes=list(scratch),
        compiler_params=pltpu.CompilerParams(vmem_limit_bytes=limit * 1024 * 1024),
    )(*args)


def swap_cores(values):
    peers = lax.axis_size("row")
    return lax.ppermute(values, "row", [(i, i ^ 1) for i in range(peers)])


def all_to_all(blocks):
    return lax.all_to_all(blocks, "row", split_axis=0, concat_axis=0, tiled=True)


def shards(
    pair_act, chain_id, residue_mask, norm_gain, w_proj, w_bias, chain_bias, w_out, w_dist, dist_bias,
):
    rows, n, chan = pair_act.shape
    peers = n // rows
    heads, dim = w_out.shape[0], w_out.shape[1]
    bins = w_dist.shape[1]
    tiles = n // LANES
    width = heads * dim
    fused = lax.axis_size("head") == 1
    gain = norm_gain[None, :]
    base = rows * rows
    length = base + tiles * heads * rows // 2

    (packed,) = call(
        pack_kernel,
        [((peers, length, chan), BF16)],
        [pair_act, gain, w_bias.T],
        scratch=[
            pltpu.VMEM(pair_act.shape, BF16),
            pltpu.VMEM(gain.shape, F32),
            pltpu.VMEM((heads, chan), BF16),
            pltpu.VMEM((peers, length, chan), BF16),
            pltpu.SemaphoreType.DMA((rows + 2,)),
            pltpu.SemaphoreType.DMA((5,)),
        ],
        hbm=(0, 1, 2),
        hbm_outs=True,
        limit=60,
    )
    received = all_to_all(packed)
    prepared = call(
        functools.partial(prepare_kernel, heads, rows),
        [
            ((heads, n, n), F32), ((3 * width, chan), BF16), ((2 * width, 2 * chan), BF16), ((bins, LANES), F32),
            ((1, chan), F32), ((2 * width, 2 * chan), BF16), ((bins, chan), BF16),
            ((2 * base, 2 * base), BF16), ((2 * chan, 2 * chan), BF16),
        ],
        [
            chain_id[None, :], residue_mask[None, :], chain_bias, w_proj, dist_bias[None, :],
            gain, w_out.reshape(width, chan), w_dist.T,
        ],
        smem=(2,),
    )
    received, *prepared = lax.optimization_barrier((received, *prepared))
    term, w_types, w_keys, db_col, gain, w_out, wd_t, swap, centre = prepared
    other_bias = swap_cores(received[:, base:])
    x_cols, spread, keys, values, gates, own_bias = call(
        functools.partial(project_kernel, heads),
        [
            ((rows, n, chan), BF16),
            ((rows, tiles, width, heads * LANES), BF16),
            ((rows, n, width), BF16),
            ((rows, width, n), BF16),
            ((rows, width, n), F32),
            ((heads // 2, n, n), F32),
        ],
        [received, gain, w_types, w_keys, swap, centre, term],
        scratch=[pltpu.VMEM((rows, n, chan), BF16)],
    )
    if fused:
        outs = [((peers, base, chan), BF16), ((rows, bins, n), BF16)]
    else:
        outs = [((rows, n, chan), BF16)]
    result = call(
        functools.partial(attend_kernel, heads, fused),
        outs,
        [other_bias, own_bias, term, w_out, wd_t, db_col, x_cols, spread, keys, values, gates],
        scratch=[
            pltpu.VMEM((heads, n, n), F32),
            pltpu.VMEM((rows, tiles, heads, LANES), F32),
            pltpu.VMEM((rows, tiles, n, heads * LANES), BF16),
            pltpu.VMEM((rows, width, n), BF16),
        ]
        + [pltpu.VMEM((rows, n, chan), BF16)] * fused,
    )
    if fused:
        to_rows, mirror = result
    else:
        update = lax.psum(result[0], "head").astype(F32)
        new = (x_cols.astype(F32) + update).astype(BF16)
        logits = jnp.einsum("cb,jic->jbi", w_dist, new, preferred_element_type=F32)
        mirror = (logits + dist_bias[None, :, None]).astype(BF16)
        to_rows = new.reshape(rows, peers, rows, chan).transpose(1, 0, 2, 3).reshape(peers, base, chan)
    arrived = all_to_all(to_rows)
    new_rows, dist = call(
        finish_kernel,
        [((rows, n, chan), BF16), ((rows, bins, n), BF16)],
        [arrived, mirror, wd_t, db_col, swap],
        scratch=[
            pltpu.VMEM((rows, n, chan), BF16),
            pltpu.VMEM((rows, bins, n), BF16),
            pltpu.SemaphoreType.DMA((peers // 4 + rows // 2,)),
        ],
        hbm_outs=True,
    )
    return new_rows, dist.transpose(0, 2, 1)


def solution(mesh):
    in_specs = (
        P(("dp", "row"), None, None),
        P("dp"),
        P("dp"),
        P(),
        P(None, "head", None),
        P(None, "head"),
        P(None, "head"),
        P("head", None, None),
        P(),
        P(),
    )
    out_specs = (P(("dp", "row"), None, None), P(("dp", "row"), None, None))
    return jax.shard_map(shards, mesh=mesh, in_specs=in_specs, out_specs=out_specs, check_vma=False)
```

```python
import functools

import jax
import jax.numpy as jnp
from jax import lax
from jax.experimental import pallas as pl
from jax.experimental.pallas import tpu as pltpu
from jax.sharding import PartitionSpec as P

LANES = 128
F32 = jnp.float32
BF16 = jnp.bfloat16
LOG2E = 1.4426950408889634


def dot_nt(a, b):
    return lax.dot_general(a, b, (((1,), (1,)), ((), ())), preferred_element_type=F32)


def dot_tn(a, b):
    return lax.dot_general(a, b, (((0,), (0,)), ((), ())), preferred_element_type=F32)


def dot_nn(a, b):
    return jnp.dot(a, b, preferred_element_type=F32)


def centring(chan):
    row = lax.broadcasted_iota(jnp.int32, (2 * chan, 2 * chan), 0)
    col = lax.broadcasted_iota(jnp.int32, (2 * chan, 2 * chan), 1)
    inside = (row // chan) == (col // chan)
    return (jnp.where(row == col, 1.0, 0.0) - jnp.where(inside, 1.0 / chan, 0.0)).astype(BF16)


def layer_norm(values, centre, gain):
    chan = gain.shape[1]
    centered = dot_nn(values, centre)
    average = jnp.full((2 * chan, chan), 1.0 / chan, BF16)
    halves = []
    for part in (centered[:, :chan], centered[:, chan:]):
        square = part * part
        high = square.astype(BF16)
        low = (square - high.astype(F32)).astype(BF16)
        variance = dot_nn(jnp.concatenate([high, low], 1), average)
        halves.append((part * lax.rsqrt(variance + 1e-05) * gain).astype(BF16))
    return halves


def swap_matrix(rows):
    size = 2 * rows * rows
    out = lax.broadcasted_iota(jnp.int32, (size, size), 0)
    col = lax.broadcasted_iota(jnp.int32, (size, size), 1)
    b, rest = out // (2 * rows), out % (2 * rows)
    wanted = (rest // rows) * (rows * rows) + (rest % rows) * rows + b
    return jnp.where(col == wanted, 1.0, 0.0).astype(BF16)


def pack_kernel(x_hbm, gain_hbm, wb_hbm, out_hbm, x_ref, gain_ref, wb_ref, out_ref, sems, out_sems):
    rows, n, chan = x_ref.shape
    peers = n // rows
    heads = wb_ref.shape[0]
    half = heads * rows // 2
    base = rows * rows
    fetch_gain = pltpu.make_async_copy(gain_hbm, gain_ref, sems.at[rows])
    fetch_wb = pltpu.make_async_copy(wb_hbm, wb_ref, sems.at[rows + 1])
    fetches = [pltpu.make_async_copy(x_hbm.at[k], x_ref.at[k], sems.at[k]) for k in range(rows)]
    for copy in (fetch_gain, fetch_wb, *fetches):
        copy.start()
    stores = []

    def store(first, count):
        at = pl.ds(first, count)
        copy = pltpu.make_async_copy(out_ref.at[:, at, :], out_hbm.at[:, at, :], out_sems.at[len(stores)])
        copy.start()
        stores.append(copy)

    centre = centring(chan)
    owner = lax.broadcasted_iota(jnp.int32, (heads * rows, chan), 0) % rows
    turned = jnp.zeros((n, chan), F32)
    rest = jnp.zeros((chan - heads * rows, 2 * chan), BF16)
    fetch_gain.wait()
    fetch_wb.wait()
    gain = gain_ref[...]
    wb = wb_ref[...].astype(F32)
    wb = jnp.concatenate([jnp.broadcast_to(wb[h : h + 1], (rows, chan)) for h in range(heads)], 0)
    mine = [jnp.where(owner == k, wb, 0.0).astype(BF16) for k in range(rows)]
    mine = [jnp.concatenate([jnp.concatenate(mine[k : k + 2], 1), rest], 0) for k in range(0, rows, 2)]
    for copy in fetches:
        copy.wait()
    for pair in range(rows // 2):
        both = [x_ref[k].astype(F32).reshape(peers, rows, chan) for k in (2 * pair, 2 * pair + 1)]
        out_ref[:, 2 * rows * pair : 2 * rows * (pair + 1), :] = jnp.concatenate(both, 1).astype(BF16)
    store(0, base)
    two = [jnp.concatenate([x_ref[k], x_ref[k + 1]], 1) for k in range(0, rows, 2)]
    normed = [layer_norm(values, centre, gain) for values in two]
    for pair in range(rows // 2):
        turned = turned + dot_nt(jnp.concatenate(normed[pair], 1), mine[pair])
    for t in range(n // LANES):
        block = jnp.transpose(turned[t * LANES : (t + 1) * LANES])[: heads * rows].astype(BF16)
        for d in range(peers):
            part = block[(d % 2) * half : (d % 2 + 1) * half]
            out_ref[d, base + t * half : base + (t + 1) * half] = part
    store(base, (n // LANES) * half)
    for copy in stores:
        copy.wait()


def prepare_kernel(
    heads, rows,
    chain_ref, mask_ref, cb_ref, w_ref, db_ref, gain_ref, wo_ref, wd_ref,
    term_ref, wt_ref, wk_out, dbc_ref, gain_out, wo_out, wd_out, swap_ref, centre_ref,
):
    gain_out[...] = gain_ref[...]
    swap_ref[...] = swap_matrix(rows)
    centre_ref[...] = centring(w_ref.shape[0])
    chan = w_ref.shape[0]
    width = wo_ref.shape[0]
    half = heads // 2
    core = lax.axis_index("row") % 2
    w_out = wo_ref[...].astype(F32)
    other_first = jnp.concatenate([w_out[width // 2 :], w_out[: width // 2]], 0)
    w_out = jnp.where(core == 0, w_out, other_first).astype(BF16)
    wk_out[...] = jnp.zeros_like(wk_out)
    wo_out[...] = jnp.zeros_like(wo_out)
    for side in range(2):
        wo_out[side * width : (side + 1) * width, side * chan : (side + 1) * chan] = w_out
    wd_out[...] = wd_ref[...]
    n = chain_ref.shape[1]
    tiles = n // LANES
    dim = w_ref.shape[2] // 4

    def column_of(row):
        return jnp.transpose(jnp.broadcast_to(row, (LANES, LANES)))

    for kt in range(tiles):
        ks = slice(kt * LANES, (kt + 1) * LANES)
        chain_k = column_of(chain_ref[:, ks].astype(F32))
        mask_k = (column_of(mask_ref[:, ks].astype(F32)) - 1.0) * 1000000000.0
        for it in range(tiles):
            cs = slice(it * LANES, (it + 1) * LANES)
            same = chain_k == chain_ref[:, cs].astype(F32)
            for h in range(heads):
                inside, outside = [jnp.where(core == 0, cb_ref[r, h], cb_ref[r, (h + half) % heads]) for r in (1, 0)]
                term_ref[h, ks, cs] = (jnp.where(same, inside, outside) + mask_k) * LOG2E
    for h in range(heads):
        mine = jnp.where(core == 0, w_ref[:, h, :].astype(F32), w_ref[:, (h + half) % heads, :].astype(F32))
        turned = jnp.transpose(mine).astype(BF16)
        for place, kind in enumerate((0, 2, 3)):
            start = place * width + h * dim
            wt_ref[start : start + dim] = turned[kind * dim : (kind + 1) * dim]
        for side in range(2):
            start = side * width + h * dim
            wk_out[start : start + dim, side * chan : (side + 1) * chan] = turned[dim : 2 * dim]
    bins = dbc_ref.shape[0]
    db_rows = jnp.broadcast_to(jnp.concatenate([db_ref[...], db_ref[...]], 1)[:, :LANES], (LANES, LANES))
    dbc_ref[...] = jnp.transpose(db_rows)[:bins]


def unpack_bias(blocks, term_ref, first, bias_ref):
    half, n = bias_ref.shape[0], bias_ref.shape[1]
    rows = n // len(blocks)
    for s, block in enumerate(blocks):
        at = slice(s * rows, (s + 1) * rows)
        extra = block.astype(F32) * LOG2E
        for t in range(n // LANES):
            cs = slice(t * LANES, (t + 1) * LANES)
            for h in range(half):
                start = (t * half + h) * rows
                bias_ref[h, at, cs] = extra[start : start + rows] + term_ref[first + h, at, cs]


def soften(j, t, keys, spread, bias_ref, scaling, inv_s, e_s):
    scores = dot_nn(keys, spread)
    for h in range(bias_ref.shape[0]):
        cs = slice(h * LANES, (h + 1) * LANES)
        s = scores[:, cs] * scaling + bias_ref[h, :, t * LANES : (t + 1) * LANES]
        e = jnp.exp2(s - jnp.max(s, 0, keepdims=True))
        inv_s[j, t, h : h + 1] = 1.0 / jnp.sum(e, 0, keepdims=True)
        e_s[j, t, :, cs] = e.astype(BF16)


def combine(j, t, values, gates, inv_s, e_s, gated_ref):
    half = inv_s.shape[2]
    dim = values.shape[0] // half
    cs = slice(t * LANES, (t + 1) * LANES)
    o = dot_nn(values, e_s[j, t])
    for h in range(half):
        mine = slice(h * dim, (h + 1) * dim)
        part = o[mine, h * LANES : (h + 1) * LANES] * inv_s[j, t, h : h + 1]
        gated_ref[j, mine, cs] = (gates[mine, cs] * part).astype(BF16)


def for_each(count, tiles, body):
    if tiles == 1:
        for i in range(count):
            body(i)
    else:

        @pl.loop(0, count)
        def _(i):
            body(i)


def permuted(blocks, swap):
    left, right = jnp.concatenate(blocks[:2], 0), jnp.concatenate(blocks[2:], 0)
    return dot_nn(swap, jnp.concatenate([left, right], 1)).astype(BF16)


def project_kernel(
    heads,
    recv_ref, gain_ref, w_ref, wk_ref, swap_ref, centre_ref, term_ref,
    x_s, spread_s, k_s, v_s, g_s, gated_ref,
    n_s, own_spread, own_v, own_g, bias_s, inv_s, e_s,
):
    peers = recv_ref.shape[0]
    rows, n, chan = x_s.shape
    tiles = n // LANES
    dim = w_ref.shape[0] // (3 * heads)
    width = heads * dim
    base = rows * rows
    gain = gain_ref[...]
    swap = swap_ref[...]
    centre = centre_ref[...]
    group = 2 * rows
    w_k = wk_ref[...]

    quads = range(peers // 4)
    x = [permuted([recv_ref[4 * quad + s, :base] for s in range(4)], swap) for quad in quads]
    normed = [layer_norm(two, centre, gain) for two in x]
    keys = [dot_nt(jnp.concatenate(two, 1), w_k).astype(BF16) for two in normed]
    for quad in quads:
        for side in range(2):
            at = slice((2 * quad + side) * group, (2 * quad + side + 1) * group)
            x_s[:, at, :] = x[quad][:, side * chan : (side + 1) * chan].reshape(rows, group, chan)
            n_s[:, at, :] = normed[quad][side].reshape(rows, group, chan)
            k_s[:, at, :] = keys[quad][:, side * width : (side + 1) * width].reshape(rows, group, width)

    half, part = heads // 2, width // 2
    unpack_bias([recv_ref[s, base:] for s in range(peers)], term_ref, 0, bias_s)
    w_qvg = w_ref[...]
    zero = jnp.zeros((dim, LANES), BF16)

    def project(pair):
        both = dot_nt(w_qvg, n_s[pl.ds(2 * pair, 2)].reshape(2 * n, chan)).astype(BF16)
        for side in range(2):
            j = 2 * pair + side
            qvg = both[:, side * n : (side + 1) * n]
            gate = jax.nn.sigmoid(qvg[2 * width :].astype(F32))
            own_v[j], v_s[j] = qvg[width : width + part], qvg[width + part : 2 * width]
            own_g[j], g_s[j] = gate[:part], gate[part:]
            for t in range(tiles):
                for h in range(heads):
                    target = (own_spread, spread_s)[h // half]
                    cs = slice(h % half * LANES, (h % half + 1) * LANES)
                    for other in range(heads):
                        block = qvg[h * dim : (h + 1) * dim, t * LANES : (t + 1) * LANES] if h == other else zero
                        target[j, t, other * dim : (other + 1) * dim, cs] = block

    scaling = dim ** (-0.5) * LOG2E
    for_each(rows // 2, tiles, project)
    for_each(rows, tiles, lambda j: [soften(j, t, k_s[j], own_spread[j, t], bias_s, scaling, inv_s, e_s) for t in range(tiles)])
    for_each(rows, tiles, lambda j: [combine(j, t, own_v[j], own_g[j], inv_s, e_s, gated_ref) for t in range(tiles)])


def attend_kernel(
    fused,
    other_ref, term_ref, wo_ref, wd_ref, db_ref, x_s, spread_s, k_s, v_s, g_s, gated_ref,
    out_ref, *refs,
):
    if fused:
        second_ref, bias_s, inv_s, e_s, gated_s, new_s = refs
    else:
        bias_s, inv_s, e_s, gated_s = refs
    peers = other_ref.shape[0]
    rows, n, chan = x_s.shape
    tiles = n // LANES
    half, part = bias_s.shape[0], v_s.shape[1]
    scaling = (part // half) ** (-0.5) * LOG2E
    w_out = wo_ref[...]

    unpack_bias([other_ref[s] for s in range(peers)], term_ref, half, bias_s)
    for_each(rows, tiles, lambda j: [soften(j, t, k_s[j], spread_s[j, t], bias_s, scaling, inv_s, e_s) for t in range(tiles)])
    for_each(rows, tiles, lambda j: [combine(j, t, v_s[j], g_s[j], inv_s, e_s, gated_s) for t in range(tiles)])

    def updated(pair):
        both = [ref[2 * pair + side] for side in range(2) for ref in (gated_ref, gated_s)]
        return dot_tn(jnp.concatenate(both, 0), w_out).astype(BF16)

    def store_update(pair):
        update = updated(pair)
        for side in range(2):
            out_ref[2 * pair + side] = update[:, side * chan : (side + 1) * chan]

    if not fused:
        for_each(rows // 2, tiles, store_update)
        return

    for j in range(0, rows, 2):
        update = updated(j // 2).astype(F32)
        both = []
        for side in range(2):
            new = (x_s[j + side].astype(F32) + update[:, side * chan : (side + 1) * chan]).astype(BF16)
            new_s[j + side] = new
            both.append(new.astype(F32).reshape(peers, rows, chan))
        out_ref[:, j * rows : (j + 2) * rows, :] = jnp.concatenate(both, 1).astype(BF16)
    logits_of(new_s, wd_ref[...], db_ref[:, :1], second_ref)


def logits_of(new_ref, w_dist, d_bias, out_ref):
    rows, n, chan = new_ref.shape
    logits = dot_nt(w_dist, new_ref[...].reshape(rows * n, chan)) + d_bias
    for j in range(rows):
        out_ref[j] = logits[:, j * n : (j + 1) * n].astype(BF16)


def finish_kernel(recv_ref, mirror_ref, wd_ref, db_ref, swap_ref, new_hbm, dist_hbm, new_ref, dist_ref, sems):
    peers, _, chan = recv_ref.shape
    rows = new_ref.shape[0]
    group = 2 * rows
    swap = swap_ref[...]
    for quad in range(peers // 4):
        new = permuted([recv_ref[4 * quad + s] for s in range(4)], swap)
        for side in range(2):
            at = slice((2 * quad + side) * group, (2 * quad + side + 1) * group)
            new_ref[:, at, :] = new[:, side * chan : (side + 1) * chan].reshape(rows, group, chan)
    copies = [pltpu.make_async_copy(new_ref, new_hbm, sems.at[0])]
    copies[0].start()
    logits_of(new_ref, wd_ref[...], db_ref[:, :1], dist_ref)
    for i in range(rows):
        dist_ref[i] = (dist_ref[i].astype(F32) + mirror_ref[i].astype(F32)).astype(BF16)
        if i % 2:
            at = pl.ds(i - 1, 2)
            copies.append(pltpu.make_async_copy(dist_ref.at[at], dist_hbm.at[at], sems.at[1 + i // 2]))
            copies[-1].start()
    for copy in copies:
        copy.wait()


def call(kernel, outs, args, scratch=(), smem=(), hbm=(), hbm_outs=False, limit=48):
    spaces = [pltpu.SMEM if i in smem else pl.ANY if i in hbm else pltpu.VMEM for i in range(len(args))]
    return pl.pallas_call(
        kernel,
        out_shape=[jax.ShapeDtypeStruct(s, d) for s, d in outs],
        in_specs=[pl.BlockSpec(memory_space=space) for space in spaces],
        out_specs=[pl.BlockSpec(memory_space=pl.ANY if hbm_outs else pltpu.VMEM)] * len(outs),
        scratch_shapes=list(scratch),
        compiler_params=pltpu.CompilerParams(vmem_limit_bytes=limit * 1024 * 1024),
    )(*args)


def swap_cores(values):
    peers = lax.axis_size("row")
    return lax.ppermute(values, "row", [(i, i ^ 1) for i in range(peers)])


def all_to_all(blocks):
    return lax.all_to_all(blocks, "row", split_axis=0, concat_axis=0, tiled=True)


def shards(
    pair_act, chain_id, residue_mask, norm_gain, w_proj, w_bias, chain_bias, w_out, w_dist, dist_bias,
):
    rows, n, chan = pair_act.shape
    peers = n // rows
    heads, dim = w_out.shape[0], w_out.shape[1]
    bins = w_dist.shape[1]
    tiles = n // LANES
    width = heads * dim
    fused = lax.axis_size("head") == 1
    gain = norm_gain[None, :]
    base = rows * rows
    length = base + tiles * heads * rows // 2

    (packed,) = call(
        pack_kernel,
        [((peers, length, chan), BF16)],
        [pair_act, gain, w_bias.T],
        scratch=[
            pltpu.VMEM(pair_act.shape, BF16),
            pltpu.VMEM(gain.shape, F32),
            pltpu.VMEM((heads, chan), BF16),
            pltpu.VMEM((peers, length, chan), BF16),
            pltpu.SemaphoreType.DMA((rows + 2,)),
            pltpu.SemaphoreType.DMA((2,)),
        ],
        hbm=(0, 1, 2),
        hbm_outs=True,
        limit=60,
    )
    received = all_to_all(packed)
    prepared = call(
        functools.partial(prepare_kernel, heads, rows),
        [
            ((heads, n, n), F32), ((3 * width, chan), BF16), ((2 * width, 2 * chan), BF16), ((bins, LANES), F32),
            ((1, chan), F32), ((2 * width, 2 * chan), BF16), ((bins, chan), BF16),
            ((2 * base, 2 * base), BF16), ((2 * chan, 2 * chan), BF16),
        ],
        [
            chain_id[None, :], residue_mask[None, :], chain_bias, w_proj, dist_bias[None, :],
            gain, w_out.reshape(width, chan), w_dist.T,
        ],
        smem=(2,),
    )
    received, *prepared = lax.optimization_barrier((received, *prepared))
    term, w_types, w_keys, db_col, gain, w_out, wd_t, swap, centre = prepared
    other_bias = swap_cores(received[:, base:])
    spread_shape = ((rows, tiles, width, heads // 2 * LANES), BF16)
    values_shape, gates_shape = ((rows, width // 2, n), BF16), ((rows, width // 2, n), F32)
    softmax_scratch = [
        pltpu.VMEM((heads // 2, n, n), F32),
        pltpu.VMEM((rows, tiles, heads // 2, LANES), F32),
        pltpu.VMEM((rows, tiles, n, heads // 2 * LANES), BF16),
    ]
    x_cols, spread, keys, values, gates, gated = call(
        functools.partial(project_kernel, heads),
        [
            ((rows, n, chan), BF16),
            spread_shape,
            ((rows, n, width), BF16),
            values_shape,
            gates_shape,
            values_shape,
        ],
        [received, gain, w_types, w_keys, swap, centre, term],
        scratch=[
            pltpu.VMEM((rows, n, chan), BF16),
            *(pltpu.VMEM(*shape) for shape in (spread_shape, values_shape, gates_shape)),
            *softmax_scratch,
        ],
    )
    if fused:
        outs = [((peers, base, chan), BF16), ((rows, bins, n), BF16)]
    else:
        outs = [((rows, n, chan), BF16)]
    result = call(
        functools.partial(attend_kernel, fused),
        outs,
        [other_bias, term, w_out, wd_t, db_col, x_cols, spread, keys, values, gates, gated],
        scratch=softmax_scratch + [pltpu.VMEM(*values_shape)] + [pltpu.VMEM((rows, n, chan), BF16)] * fused,
    )
    if fused:
        to_rows, mirror = result
    else:
        update = lax.psum(result[0], "head").astype(F32)
        new = (x_cols.astype(F32) + update).astype(BF16)
        logits = jnp.einsum("cb,jic->jbi", w_dist, new, preferred_element_type=F32)
        mirror = (logits + dist_bias[None, :, None]).astype(BF16)
        to_rows = new.reshape(rows, peers, rows, chan).transpose(1, 0, 2, 3).reshape(peers, base, chan)
    arrived = all_to_all(to_rows)
    new_rows, dist = call(
        finish_kernel,
        [((rows, n, chan), BF16), ((rows, bins, n), BF16)],
        [arrived, mirror, wd_t, db_col, swap],
        scratch=[
            pltpu.VMEM((rows, n, chan), BF16),
            pltpu.VMEM((rows, bins, n), BF16),
            pltpu.SemaphoreType.DMA((1 + rows // 2,)),
        ],
        hbm_outs=True,
    )
    return new_rows, dist.transpose(0, 2, 1)


def solution(mesh):
    in_specs = (
        P(("dp", "row"), None, None),
        P("dp"),
        P("dp"),
        P(),
        P(None, "head", None),
        P(None, "head"),
        P(None, "head"),
        P("head", None, None),
        P(),
        P(),
    )
    out_specs = (P(("dp", "row"), None, None), P(("dp", "row"), None, None))
    return jax.shard_map(shards, mesh=mesh, in_specs=in_specs, out_specs=out_specs, check_vma=False)
```

```python
import functools

import jax
import jax.numpy as jnp
from jax import lax
from jax.experimental import pallas as pl
from jax.experimental.pallas import tpu as pltpu
from jax.sharding import PartitionSpec as P

LANES = 128
F32 = jnp.float32
BF16 = jnp.bfloat16
LOG2E = 1.4426950408889634


def dot_nt(a, b):
    return lax.dot_general(a, b, (((1,), (1,)), ((), ())), preferred_element_type=F32)


def dot_tn(a, b):
    return lax.dot_general(a, b, (((0,), (0,)), ((), ())), preferred_element_type=F32)


def dot_nn(a, b):
    return jnp.dot(a, b, preferred_element_type=F32)


def layer_norm(values, gain):
    center = jnp.mean(values, -1, keepdims=True)
    centered = values - center
    variance = jnp.mean(centered * centered, -1, keepdims=True)
    return (centered * lax.rsqrt(variance + 1e-05) * gain).astype(BF16)


def swap_matrix(rows):
    size = 2 * rows * rows
    out = lax.broadcasted_iota(jnp.int32, (size, size), 0)
    col = lax.broadcasted_iota(jnp.int32, (size, size), 1)
    b, rest = out // (2 * rows), out % (2 * rows)
    wanted = (rest // rows) * (rows * rows) + (rest % rows) * rows + b
    return jnp.where(col == wanted, 1.0, 0.0).astype(BF16)


def pack_kernel(x_hbm, gain_hbm, wb_hbm, out_hbm, x_ref, gain_ref, wb_ref, out_ref, sems, out_sems):
    rows, n, chan = x_ref.shape
    peers = n // rows
    heads = wb_ref.shape[0]
    half = heads * rows // 2
    base = rows * rows
    fetch_gain = pltpu.make_async_copy(gain_hbm, gain_ref, sems.at[rows])
    fetch_wb = pltpu.make_async_copy(wb_hbm, wb_ref, sems.at[rows + 1])
    fetches = [pltpu.make_async_copy(x_hbm.at[k], x_ref.at[k], sems.at[k]) for k in range(rows)]
    for copy in (fetch_gain, fetch_wb, *fetches):
        copy.start()
    stores = []

    def store(first, count):
        at = pl.ds(first, count)
        copy = pltpu.make_async_copy(out_ref.at[:, at, :], out_hbm.at[:, at, :], out_sems.at[len(stores)])
        copy.start()
        stores.append(copy)

    owner = lax.broadcasted_iota(jnp.int32, (heads * rows, chan), 0) % rows
    bias = jnp.zeros((heads * rows, n), F32)
    fetch_gain.wait()
    fetch_wb.wait()
    gain = gain_ref[...]
    wb = wb_ref[...].astype(F32)
    wb = jnp.concatenate([jnp.broadcast_to(wb[h : h + 1], (rows, chan)) for h in range(heads)], 0)
    mine = [jnp.where(owner == k, wb, 0.0).astype(BF16) for k in range(rows)]
    mine = [jnp.concatenate(mine[k : k + 2], 1) for k in range(0, rows, 2)]
    for copy in fetches:
        copy.wait()
    for pair in range(rows // 2):
        both = [x_ref[k].astype(F32).reshape(peers, rows, chan) for k in (2 * pair, 2 * pair + 1)]
        out_ref[:, 2 * rows * pair : 2 * rows * (pair + 1), :] = jnp.concatenate(both, 1).astype(BF16)
    store(0, base)
    normed = [layer_norm(x_ref[k].astype(F32), gain) for k in range(rows)]
    for pair in range(rows // 2):
        bias = bias + dot_nt(mine[pair], jnp.concatenate(normed[2 * pair : 2 * pair + 2], 1))
    bias = bias.astype(BF16)
    for t in range(n // LANES):
        block = bias[:, t * LANES : (t + 1) * LANES]
        for d in range(peers):
            part = block[(d % 2) * half : (d % 2 + 1) * half]
            out_ref[d, base + t * half : base + (t + 1) * half] = part
    store(base, (n // LANES) * half)
    for copy in stores:
        copy.wait()


def prepare_kernel(
    heads, rows,
    chain_ref, mask_ref, cb_ref, w_ref, db_ref, gain_ref, wo_ref, wd_ref,
    term_ref, wt_ref, wk_out, dbc_ref, gain_out, wo_out, wd_out, swap_ref,
):
    gain_out[...] = gain_ref[...]
    swap_ref[...] = swap_matrix(rows)
    chan = w_ref.shape[0]
    width = wo_ref.shape[0]
    half = heads // 2
    core = lax.axis_index("row") % 2
    w_out = wo_ref[...].astype(F32)
    other_first = jnp.concatenate([w_out[width // 2 :], w_out[: width // 2]], 0)
    w_out = jnp.where(core == 0, w_out, other_first).astype(BF16)
    wk_out[...] = jnp.zeros_like(wk_out)
    wo_out[...] = jnp.zeros_like(wo_out)
    for side in range(2):
        wo_out[side * width : (side + 1) * width, side * chan : (side + 1) * chan] = w_out
    wd_out[...] = wd_ref[...]
    n = chain_ref.shape[1]
    tiles = n // LANES
    dim = w_ref.shape[2] // 4

    def column_of(row):
        return jnp.transpose(jnp.broadcast_to(row, (LANES, LANES)))

    for kt in range(tiles):
        ks = slice(kt * LANES, (kt + 1) * LANES)
        chain_k = column_of(chain_ref[:, ks].astype(F32))
        mask_k = (column_of(mask_ref[:, ks].astype(F32)) - 1.0) * 1000000000.0
        for it in range(tiles):
            cs = slice(it * LANES, (it + 1) * LANES)
            same = chain_k == chain_ref[:, cs].astype(F32)
            for h in range(heads):
                inside, outside = [jnp.where(core == 0, cb_ref[r, h], cb_ref[r, (h + half) % heads]) for r in (1, 0)]
                term_ref[h, ks, cs] = (jnp.where(same, inside, outside) + mask_k) * LOG2E
    for h in range(heads):
        mine = jnp.where(core == 0, w_ref[:, h, :].astype(F32), w_ref[:, (h + half) % heads, :].astype(F32))
        turned = jnp.transpose(mine).astype(BF16)
        for place, kind in enumerate((0, 2, 3)):
            start = place * width + h * dim
            wt_ref[start : start + dim] = turned[kind * dim : (kind + 1) * dim]
        for side in range(2):
            start = side * width + h * dim
            wk_out[start : start + dim, side * chan : (side + 1) * chan] = turned[dim : 2 * dim]
    bins = dbc_ref.shape[0]
    db_rows = jnp.broadcast_to(jnp.concatenate([db_ref[...], db_ref[...]], 1)[:, :LANES], (LANES, LANES))
    dbc_ref[...] = jnp.transpose(db_rows)[:bins]


def unpack_bias(blocks, term_ref, first, bias_ref):
    half, n = bias_ref.shape[0], bias_ref.shape[1]
    rows = n // len(blocks)
    for s, block in enumerate(blocks):
        at = slice(s * rows, (s + 1) * rows)
        extra = block.astype(F32) * LOG2E
        for t in range(n // LANES):
            cs = slice(t * LANES, (t + 1) * LANES)
            for h in range(half):
                start = (t * half + h) * rows
                bias_ref[h, at, cs] = extra[start : start + rows] + term_ref[first + h, at, cs]


def soften(j, t, keys, spread, bias_ref, scaling, inv_s, e_s):
    scores = dot_nn(keys, spread)
    for h in range(bias_ref.shape[0]):
        cs = slice(h * LANES, (h + 1) * LANES)
        s = scores[:, cs] * scaling + bias_ref[h, :, t * LANES : (t + 1) * LANES]
        e = jnp.exp2(s - jnp.max(s, 0, keepdims=True))
        inv_s[j, t, h : h + 1] = 1.0 / jnp.sum(e, 0, keepdims=True)
        e_s[j, t, :, cs] = e.astype(BF16)


def combine(j, t, values, gates, inv_s, e_s, gated_ref):
    half = inv_s.shape[2]
    dim = values.shape[0] // half
    cs = slice(t * LANES, (t + 1) * LANES)
    o = dot_nn(values, e_s[j, t])
    for h in range(half):
        mine = slice(h * dim, (h + 1) * dim)
        part = o[mine, h * LANES : (h + 1) * LANES] * inv_s[j, t, h : h + 1]
        gated_ref[j, mine, cs] = (gates[mine, cs] * part).astype(BF16)


def for_each(count, tiles, body):
    if tiles == 1:
        for i in range(count):
            body(i)
    else:

        @pl.loop(0, count)
        def _(i):
            body(i)


def permuted(blocks, swap):
    left, right = jnp.concatenate(blocks[:2], 0), jnp.concatenate(blocks[2:], 0)
    return dot_nn(swap, jnp.concatenate([left, right], 1))


def project_kernel(
    heads,
    recv_ref, gain_ref, w_ref, wk_ref, swap_ref, term_ref,
    x_s, spread_s, k_s, v_s, g_s, gated_ref,
    n_s, own_spread, own_v, own_g, bias_s, inv_s, e_s,
):
    peers = recv_ref.shape[0]
    rows, n, chan = x_s.shape
    tiles = n // LANES
    dim = w_ref.shape[0] // (3 * heads)
    width = heads * dim
    base = rows * rows
    gain = gain_ref[...]
    swap = swap_ref[...]
    group = 2 * rows
    w_k = wk_ref[...]

    quads = range(peers // 4)
    x = [permuted([recv_ref[4 * quad + s, :base] for s in range(4)], swap) for quad in quads]
    normed = [[layer_norm(two[:, :chan], gain), layer_norm(two[:, chan:], gain)] for two in x]
    keys = [dot_nt(jnp.concatenate(two, 1), w_k).astype(BF16) for two in normed]
    for quad in quads:
        for side in range(2):
            at = slice((2 * quad + side) * group, (2 * quad + side + 1) * group)
            x_s[:, at, :] = x[quad][:, side * chan : (side + 1) * chan].astype(BF16).reshape(rows, group, chan)
            n_s[:, at, :] = normed[quad][side].reshape(rows, group, chan)
            k_s[:, at, :] = keys[quad][:, side * width : (side + 1) * width].reshape(rows, group, width)

    half, part = heads // 2, width // 2
    unpack_bias([recv_ref[s, base:] for s in range(peers)], term_ref, 0, bias_s)
    w_qvg = w_ref[...]
    zero = jnp.zeros((dim, LANES), BF16)

    def project(pair):
        both = dot_nt(w_qvg, n_s[pl.ds(2 * pair, 2)].reshape(2 * n, chan)).astype(BF16)
        for side in range(2):
            j = 2 * pair + side
            qvg = both[:, side * n : (side + 1) * n]
            gate = jax.nn.sigmoid(qvg[2 * width :].astype(F32))
            own_v[j], v_s[j] = qvg[width : width + part], qvg[width + part : 2 * width]
            own_g[j], g_s[j] = gate[:part], gate[part:]
            for t in range(tiles):
                for h in range(heads):
                    target = (own_spread, spread_s)[h // half]
                    cs = slice(h % half * LANES, (h % half + 1) * LANES)
                    for other in range(heads):
                        block = qvg[h * dim : (h + 1) * dim, t * LANES : (t + 1) * LANES] if h == other else zero
                        target[j, t, other * dim : (other + 1) * dim, cs] = block

    scaling = dim ** (-0.5) * LOG2E
    for_each(rows // 2, tiles, project)
    for_each(rows, tiles, lambda j: [soften(j, t, k_s[j], own_spread[j, t], bias_s, scaling, inv_s, e_s) for t in range(tiles)])
    for_each(rows, tiles, lambda j: [combine(j, t, own_v[j], own_g[j], inv_s, e_s, gated_ref) for t in range(tiles)])


def attend_kernel(
    fused,
    other_ref, term_ref, wo_ref, wd_ref, db_ref, x_s, spread_s, k_s, v_s, g_s, gated_ref,
    out_ref, *refs,
):
    if fused:
        second_ref, bias_s, inv_s, e_s, gated_s, new_s = refs
    else:
        bias_s, inv_s, e_s, gated_s = refs
    peers = other_ref.shape[0]
    rows, n, chan = x_s.shape
    tiles = n // LANES
    half, part = bias_s.shape[0], v_s.shape[1]
    scaling = (part // half) ** (-0.5) * LOG2E
    w_out = wo_ref[...]

    unpack_bias([other_ref[s] for s in range(peers)], term_ref, half, bias_s)
    for_each(rows, tiles, lambda j: [soften(j, t, k_s[j], spread_s[j, t], bias_s, scaling, inv_s, e_s) for t in range(tiles)])
    for_each(rows, tiles, lambda j: [combine(j, t, v_s[j], g_s[j], inv_s, e_s, gated_s) for t in range(tiles)])

    def updated(pair):
        both = [ref[2 * pair + side] for side in range(2) for ref in (gated_ref, gated_s)]
        return dot_tn(jnp.concatenate(both, 0), w_out).astype(BF16)

    def store_update(pair):
        update = updated(pair)
        for side in range(2):
            out_ref[2 * pair + side] = update[:, side * chan : (side + 1) * chan]

    if not fused:
        for_each(rows // 2, tiles, store_update)
        return

    for j in range(0, rows, 2):
        update = updated(j // 2).astype(F32)
        both = []
        for side in range(2):
            new = (x_s[j + side].astype(F32) + update[:, side * chan : (side + 1) * chan]).astype(BF16)
            new_s[j + side] = new
            both.append(new.astype(F32).reshape(peers, rows, chan))
        out_ref[:, j * rows : (j + 2) * rows, :] = jnp.concatenate(both, 1).astype(BF16)
    logits_of(new_s, wd_ref[...], db_ref[:, :1], second_ref)


def logits_of(new_ref, w_dist, d_bias, out_ref):
    rows, n, chan = new_ref.shape
    logits = dot_nt(w_dist, new_ref[...].reshape(rows * n, chan)) + d_bias
    for j in range(rows):
        out_ref[j] = logits[:, j * n : (j + 1) * n].astype(BF16)


def finish_kernel(recv_ref, mirror_ref, wd_ref, db_ref, swap_ref, new_hbm, dist_hbm, new_ref, dist_ref, sems):
    peers, _, chan = recv_ref.shape
    rows = new_ref.shape[0]
    group = 2 * rows
    swap = swap_ref[...]
    for quad in range(peers // 4):
        new = permuted([recv_ref[4 * quad + s] for s in range(4)], swap).astype(BF16)
        for side in range(2):
            at = slice((2 * quad + side) * group, (2 * quad + side + 1) * group)
            new_ref[:, at, :] = new[:, side * chan : (side + 1) * chan].reshape(rows, group, chan)
    copies = [pltpu.make_async_copy(new_ref, new_hbm, sems.at[0])]
    copies[0].start()
    logits_of(new_ref, wd_ref[...], db_ref[:, :1], dist_ref)
    for i in range(rows):
        dist_ref[i] = (dist_ref[i].astype(F32) + mirror_ref[i].astype(F32)).astype(BF16)
        if i % 2:
            at = pl.ds(i - 1, 2)
            copies.append(pltpu.make_async_copy(dist_ref.at[at], dist_hbm.at[at], sems.at[1 + i // 2]))
            copies[-1].start()
    for copy in copies:
        copy.wait()


def call(kernel, outs, args, scratch=(), smem=(), hbm=(), hbm_outs=False, limit=48):
    spaces = [pltpu.SMEM if i in smem else pl.ANY if i in hbm else pltpu.VMEM for i in range(len(args))]
    return pl.pallas_call(
        kernel,
        out_shape=[jax.ShapeDtypeStruct(s, d) for s, d in outs],
        in_specs=[pl.BlockSpec(memory_space=space) for space in spaces],
        out_specs=[pl.BlockSpec(memory_space=pl.ANY if hbm_outs else pltpu.VMEM)] * len(outs),
        scratch_shapes=list(scratch),
        compiler_params=pltpu.CompilerParams(vmem_limit_bytes=limit * 1024 * 1024),
    )(*args)


def swap_cores(values):
    peers = lax.axis_size("row")
    return lax.ppermute(values, "row", [(i, i ^ 1) for i in range(peers)])


def all_to_all(blocks):
    return lax.all_to_all(blocks, "row", split_axis=0, concat_axis=0, tiled=True)


def shards(
    pair_act, chain_id, residue_mask, norm_gain, w_proj, w_bias, chain_bias, w_out, w_dist, dist_bias,
):
    rows, n, chan = pair_act.shape
    peers = n // rows
    heads, dim = w_out.shape[0], w_out.shape[1]
    bins = w_dist.shape[1]
    tiles = n // LANES
    width = heads * dim
    fused = lax.axis_size("head") == 1
    gain = norm_gain[None, :]
    base = rows * rows
    length = base + tiles * heads * rows // 2

    (packed,) = call(
        pack_kernel,
        [((peers, length, chan), BF16)],
        [pair_act, gain, w_bias.T],
        scratch=[
            pltpu.VMEM(pair_act.shape, BF16),
            pltpu.VMEM(gain.shape, F32),
            pltpu.VMEM((heads, chan), BF16),
            pltpu.VMEM((peers, length, chan), BF16),
            pltpu.SemaphoreType.DMA((rows + 2,)),
            pltpu.SemaphoreType.DMA((2,)),
        ],
        hbm=(0, 1, 2),
        hbm_outs=True,
        limit=60,
    )
    received = all_to_all(packed)
    prepared = call(
        functools.partial(prepare_kernel, heads, rows),
        [
            ((heads, n, n), F32), ((3 * width, chan), BF16), ((2 * width, 2 * chan), BF16), ((bins, LANES), F32),
            ((1, chan), F32), ((2 * width, 2 * chan), BF16), ((bins, chan), BF16),
            ((2 * base, 2 * base), BF16),
        ],
        [
            chain_id[None, :], residue_mask[None, :], chain_bias, w_proj, dist_bias[None, :],
            gain, w_out.reshape(width, chan), w_dist.T,
        ],
        smem=(2,),
    )
    received, *prepared = lax.optimization_barrier((received, *prepared))
    term, w_types, w_keys, db_col, gain, w_out, wd_t, swap = prepared
    other_bias = swap_cores(received[:, base:])
    spread_shape = ((rows, tiles, width, heads // 2 * LANES), BF16)
    values_shape, gates_shape = ((rows, width // 2, n), BF16), ((rows, width // 2, n), F32)
    softmax_scratch = [
        pltpu.VMEM((heads // 2, n, n), F32),
        pltpu.VMEM((rows, tiles, heads // 2, LANES), F32),
        pltpu.VMEM((rows, tiles, n, heads // 2 * LANES), BF16),
    ]
    x_cols, spread, keys, values, gates, gated = call(
        functools.partial(project_kernel, heads),
        [
            ((rows, n, chan), BF16),
            spread_shape,
            ((rows, n, width), BF16),
            values_shape,
            gates_shape,
            values_shape,
        ],
        [received, gain, w_types, w_keys, swap, term],
        scratch=[
            pltpu.VMEM((rows, n, chan), BF16),
            *(pltpu.VMEM(*shape) for shape in (spread_shape, values_shape, gates_shape)),
            *softmax_scratch,
        ],
    )
    if fused:
        outs = [((peers, base, chan), BF16), ((rows, bins, n), BF16)]
    else:
        outs = [((rows, n, chan), BF16)]
    result = call(
        functools.partial(attend_kernel, fused),
        outs,
        [other_bias, term, w_out, wd_t, db_col, x_cols, spread, keys, values, gates, gated],
        scratch=softmax_scratch + [pltpu.VMEM(*values_shape)] + [pltpu.VMEM((rows, n, chan), BF16)] * fused,
    )
    if fused:
        to_rows, mirror = result
    else:
        update = lax.psum(result[0], "head").astype(F32)
        new = (x_cols.astype(F32) + update).astype(BF16)
        logits = jnp.einsum("cb,jic->jbi", w_dist, new, preferred_element_type=F32)
        mirror = (logits + dist_bias[None, :, None]).astype(BF16)
        to_rows = new.reshape(rows, peers, rows, chan).transpose(1, 0, 2, 3).reshape(peers, base, chan)
    arrived = all_to_all(to_rows)
    new_rows, dist = call(
        finish_kernel,
        [((rows, n, chan), BF16), ((rows, bins, n), BF16)],
        [arrived, mirror, wd_t, db_col, swap],
        scratch=[
            pltpu.VMEM((rows, n, chan), BF16),
            pltpu.VMEM((rows, bins, n), BF16),
            pltpu.SemaphoreType.DMA((1 + rows // 2,)),
        ],
        hbm_outs=True,
    )
    return new_rows, dist.transpose(0, 2, 1)


def solution(mesh):
    in_specs = (
        P(("dp", "row"), None, None),
        P("dp"),
        P("dp"),
        P(),
        P(None, "head", None),
        P(None, "head"),
        P(None, "head"),
        P("head", None, None),
        P(),
        P(),
    )
    out_specs = (P(("dp", "row"), None, None), P(("dp", "row"), None, None))
    return jax.shard_map(shards, mesh=mesh, in_specs=in_specs, out_specs=out_specs, check_vma=False)
```

```python
import functools

import jax
import jax.numpy as jnp
from jax import lax
from jax.experimental import pallas as pl
from jax.experimental.pallas import tpu as pltpu
from jax.sharding import PartitionSpec as P

LANES = 128
F32 = jnp.float32
BF16 = jnp.bfloat16
LOG2E = 1.4426950408889634


def dot_nt(a, b):
    return lax.dot_general(a, b, (((1,), (1,)), ((), ())), preferred_element_type=F32)


def dot_tn(a, b):
    return lax.dot_general(a, b, (((0,), (0,)), ((), ())), preferred_element_type=F32)


def dot_nn(a, b):
    return jnp.dot(a, b, preferred_element_type=F32)


def layer_norm(values, gain):
    center = jnp.mean(values, -1, keepdims=True)
    centered = values - center
    variance = jnp.mean(centered * centered, -1, keepdims=True)
    return (centered * lax.rsqrt(variance + 1e-05) * gain).astype(BF16)


def pack_kernel(x_hbm, gain_hbm, wb_hbm, out_hbm, x_ref, gain_ref, wb_ref, wide, out_ref, sems, out_sems):
    rows, n, chan = x_ref.shape
    peers = n // rows
    heads = wb_ref.shape[0]
    half = heads * rows // 2
    base = rows * rows
    fetch_gain = pltpu.make_async_copy(gain_hbm, gain_ref, sems.at[rows])
    fetch_wb = pltpu.make_async_copy(wb_hbm, wb_ref, sems.at[rows + 1])
    fetches = [pltpu.make_async_copy(x_hbm.at[k], x_ref.at[k], sems.at[k]) for k in range(rows)]
    for copy in (fetch_gain, fetch_wb, *fetches):
        copy.start()
    stores = []

    def store(first, count):
        at = pl.ds(first, count)
        copy = pltpu.make_async_copy(out_ref.at[:, at, :], out_hbm.at[:, at, :], out_sems.at[len(stores)])
        copy.start()
        stores.append(copy)

    owner = lax.broadcasted_iota(jnp.int32, (heads * rows, chan), 0) % rows
    bias = jnp.zeros((heads * rows, n), F32)
    fetch_gain.wait()
    fetch_wb.wait()
    gain = gain_ref[...]
    wb = wb_ref[...].astype(F32)
    wb = jnp.concatenate([jnp.broadcast_to(wb[h : h + 1], (rows, chan)) for h in range(heads)], 0)
    mine = [jnp.where(owner == k, wb, 0.0).astype(BF16) for k in range(rows)]
    mine = [jnp.concatenate(mine[k : k + 2], 1) for k in range(0, rows, 2)]
    for copy in fetches:
        copy.wait()
    for k in range(rows):
        wide[:, pl.ds(k, rows, stride=rows), :] = x_ref[k].astype(F32).reshape(peers, rows, chan)
    out_ref[:, :base, :] = wide[...].astype(BF16)
    store(0, base)
    normed = [layer_norm(x_ref[k].astype(F32), gain) for k in range(rows)]
    for pair in range(rows // 2):
        bias = bias + dot_nt(mine[pair], jnp.concatenate(normed[2 * pair : 2 * pair + 2], 1))
    bias = bias.astype(BF16)
    for t in range(n // LANES):
        block = bias[:, t * LANES : (t + 1) * LANES]
        for d in range(peers):
            part = block[(d % 2) * half : (d % 2 + 1) * half]
            out_ref[d, base + t * half : base + (t + 1) * half] = part
    store(base, (n // LANES) * half)
    for copy in stores:
        copy.wait()


def prepare_kernel(
    heads,
    chain_ref, mask_ref, cb_ref, w_ref, db_ref, gain_ref, wo_ref, wd_ref,
    term_ref, wt_ref, wk_out, dbc_ref, gain_out, wo_out, wd_out,
):
    gain_out[...] = gain_ref[...]
    chan = w_ref.shape[0]
    width = wo_ref.shape[0]
    half = heads // 2
    core = lax.axis_index("row") % 2
    w_out = wo_ref[...].astype(F32)
    other_first = jnp.concatenate([w_out[width // 2 :], w_out[: width // 2]], 0)
    w_out = jnp.where(core == 0, w_out, other_first).astype(BF16)
    wk_out[...] = jnp.zeros_like(wk_out)
    wo_out[...] = jnp.zeros_like(wo_out)
    for side in range(2):
        wo_out[side * width : (side + 1) * width, side * chan : (side + 1) * chan] = w_out
    wd_out[...] = wd_ref[...]
    n = chain_ref.shape[1]
    tiles = n // LANES
    dim = w_ref.shape[2] // 4

    def column_of(row):
        return jnp.transpose(jnp.broadcast_to(row, (LANES, LANES)))

    for kt in range(tiles):
        ks = slice(kt * LANES, (kt + 1) * LANES)
        chain_k = column_of(chain_ref[:, ks].astype(F32))
        mask_k = (column_of(mask_ref[:, ks].astype(F32)) - 1.0) * 1000000000.0
        for it in range(tiles):
            cs = slice(it * LANES, (it + 1) * LANES)
            same = chain_k == chain_ref[:, cs].astype(F32)
            for h in range(heads):
                inside, outside = [jnp.where(core == 0, cb_ref[r, h], cb_ref[r, (h + half) % heads]) for r in (1, 0)]
                term_ref[h, ks, cs] = (jnp.where(same, inside, outside) + mask_k) * LOG2E
    for h in range(heads):
        mine = jnp.where(core == 0, w_ref[:, h, :].astype(F32), w_ref[:, (h + half) % heads, :].astype(F32))
        turned = jnp.transpose(mine).astype(BF16)
        for place, kind in enumerate((0, 2, 3)):
            start = place * width + h * dim
            wt_ref[start : start + dim] = turned[kind * dim : (kind + 1) * dim]
        for side in range(2):
            start = side * width + h * dim
            wk_out[start : start + dim, side * chan : (side + 1) * chan] = turned[dim : 2 * dim]
    bins = dbc_ref.shape[0]
    db_rows = jnp.broadcast_to(jnp.concatenate([db_ref[...], db_ref[...]], 1)[:, :LANES], (LANES, LANES))
    dbc_ref[...] = jnp.transpose(db_rows)[:bins]


def unpack_bias(blocks, term_ref, first, bias_ref):
    half, n = bias_ref.shape[0], bias_ref.shape[1]
    rows = n // len(blocks)
    for s, block in enumerate(blocks):
        at = slice(s * rows, (s + 1) * rows)
        extra = block.astype(F32) * LOG2E
        for t in range(n // LANES):
            cs = slice(t * LANES, (t + 1) * LANES)
            for h in range(half):
                start = (t * half + h) * rows
                bias_ref[h, at, cs] = extra[start : start + rows] + term_ref[first + h, at, cs]


def soften(j, t, keys, spread, bias_ref, scaling, inv_s, e_s):
    scores = dot_nn(keys, spread)
    for h in range(bias_ref.shape[0]):
        cs = slice(h * LANES, (h + 1) * LANES)
        s = scores[:, cs] * scaling + bias_ref[h, :, t * LANES : (t + 1) * LANES]
        e = jnp.exp2(s - jnp.max(s, 0, keepdims=True))
        inv_s[j, t, h : h + 1] = 1.0 / jnp.sum(e, 0, keepdims=True)
        e_s[j, t, :, cs] = e.astype(BF16)


def combine(j, t, values, gates, inv_s, e_s, gated_ref):
    half = inv_s.shape[2]
    dim = values.shape[0] // half
    cs = slice(t * LANES, (t + 1) * LANES)
    o = dot_nn(values, e_s[j, t])
    for h in range(half):
        mine = slice(h * dim, (h + 1) * dim)
        part = o[mine, h * LANES : (h + 1) * LANES] * inv_s[j, t, h : h + 1]
        gated_ref[j, mine, cs] = (gates[mine, cs] * part).astype(BF16)


def for_each(count, tiles, body):
    if tiles == 1:
        for i in range(count):
            body(i)
    else:

        @pl.loop(0, count)
        def _(i):
            body(i)


def regrouped(left, right, rows):
    both = [block.astype(F32).reshape(rows, rows, LANES) for block in (left, right)]
    return jnp.concatenate(both, 1).reshape(2 * rows * rows, LANES)


def project_kernel(
    heads,
    recv_ref, gain_ref, w_ref, wk_ref, term_ref,
    x_s, spread_s, k_s, v_s, g_s, gated_ref,
    n_s, own_spread, own_v, own_g, bias_s, inv_s, e_s,
):
    peers = recv_ref.shape[0]
    rows, n, chan = x_s.shape
    tiles = n // LANES
    dim = w_ref.shape[0] // (3 * heads)
    width = heads * dim
    base = rows * rows
    gain = gain_ref[...]
    group = 2 * rows
    w_k = wk_ref[...]

    quads = range(peers // 4)
    x = [[regrouped(recv_ref[s, :base], recv_ref[s + 1, :base], rows) for s in (4 * q, 4 * q + 2)] for q in quads]
    normed = [[layer_norm(part, gain) for part in two] for two in x]
    keys = [dot_nt(jnp.concatenate(two, 1), w_k).astype(BF16) for two in normed]
    for quad in quads:
        for side in range(2):
            at = slice((2 * quad + side) * group, (2 * quad + side + 1) * group)
            x_s[:, at, :] = x[quad][side].astype(BF16).reshape(rows, group, chan)
            n_s[:, at, :] = normed[quad][side].reshape(rows, group, chan)
            k_s[:, at, :] = keys[quad][:, side * width : (side + 1) * width].reshape(rows, group, width)

    half, part = heads // 2, width // 2
    unpack_bias([recv_ref[s, base:] for s in range(peers)], term_ref, 0, bias_s)
    w_qvg = w_ref[...]
    zero = jnp.zeros((dim, LANES), BF16)

    def project(pair):
        both = dot_nt(w_qvg, n_s[pl.ds(2 * pair, 2)].reshape(2 * n, chan)).astype(BF16)
        for side in range(2):
            j = 2 * pair + side
            qvg = both[:, side * n : (side + 1) * n]
            gate = jax.nn.sigmoid(qvg[2 * width :].astype(F32))
            own_v[j], v_s[j] = qvg[width : width + part], qvg[width + part : 2 * width]
            own_g[j], g_s[j] = gate[:part], gate[part:]
            for t in range(tiles):
                for h in range(heads):
                    target = (own_spread, spread_s)[h // half]
                    cs = slice(h % half * LANES, (h % half + 1) * LANES)
                    for other in range(heads):
                        block = qvg[h * dim : (h + 1) * dim, t * LANES : (t + 1) * LANES] if h == other else zero
                        target[j, t, other * dim : (other + 1) * dim, cs] = block

    scaling = dim ** (-0.5) * LOG2E
    for_each(rows // 2, tiles, project)
    for_each(rows, tiles, lambda j: [soften(j, t, k_s[j], own_spread[j, t], bias_s, scaling, inv_s, e_s) for t in range(tiles)])
    for_each(rows, tiles, lambda j: [combine(j, t, own_v[j], own_g[j], inv_s, e_s, gated_ref) for t in range(tiles)])


def attend_kernel(
    fused,
    other_ref, term_ref, wo_ref, wd_ref, db_ref, x_s, spread_s, k_s, v_s, g_s, gated_ref,
    out_ref, *refs,
):
    if fused:
        second_ref, bias_s, inv_s, e_s, gated_s, new_s, wide = refs
    else:
        bias_s, inv_s, e_s, gated_s = refs
    peers = other_ref.shape[0]
    rows, n, chan = x_s.shape
    tiles = n // LANES
    half, part = bias_s.shape[0], v_s.shape[1]
    scaling = (part // half) ** (-0.5) * LOG2E
    w_out = wo_ref[...]

    unpack_bias([other_ref[s] for s in range(peers)], term_ref, half, bias_s)
    for_each(rows, tiles, lambda j: [soften(j, t, k_s[j], spread_s[j, t], bias_s, scaling, inv_s, e_s) for t in range(tiles)])
    for_each(rows, tiles, lambda j: [combine(j, t, v_s[j], g_s[j], inv_s, e_s, gated_s) for t in range(tiles)])

    def updated(pair):
        both = [ref[2 * pair + side] for side in range(2) for ref in (gated_ref, gated_s)]
        return dot_tn(jnp.concatenate(both, 0), w_out).astype(BF16)

    def store_update(pair):
        update = updated(pair)
        for side in range(2):
            out_ref[2 * pair + side] = update[:, side * chan : (side + 1) * chan]

    if not fused:
        for_each(rows // 2, tiles, store_update)
        return

    for j in range(0, rows, 2):
        update = updated(j // 2).astype(F32)
        for side in range(2):
            new = (x_s[j + side].astype(F32) + update[:, side * chan : (side + 1) * chan]).astype(BF16)
            new_s[j + side] = new
            wide[:, pl.ds(j + side, rows, stride=rows), :] = new.astype(F32).reshape(peers, rows, chan)
    out_ref[...] = wide[...].astype(BF16)
    logits_of(new_s, wd_ref[...], db_ref[:, :1], second_ref)


def logits_of(new_ref, w_dist, d_bias, out_ref):
    rows, n, chan = new_ref.shape
    logits = dot_nt(w_dist, new_ref[...].reshape(rows * n, chan)) + d_bias
    for j in range(rows):
        out_ref[j] = logits[:, j * n : (j + 1) * n].astype(BF16)


def finish_kernel(recv_ref, mirror_ref, wd_ref, db_ref, new_hbm, dist_hbm, new_ref, dist_ref, sems):
    peers, _, chan = recv_ref.shape
    rows = new_ref.shape[0]
    group = 2 * rows
    for pair in range(peers // 2):
        at = slice(pair * group, (pair + 1) * group)
        block = regrouped(recv_ref[2 * pair], recv_ref[2 * pair + 1], rows)
        new_ref[:, at, :] = block.astype(BF16).reshape(rows, group, chan)
    copies = [pltpu.make_async_copy(new_ref, new_hbm, sems.at[0])]
    copies[0].start()
    logits_of(new_ref, wd_ref[...], db_ref[:, :1], dist_ref)
    for i in range(rows):
        dist_ref[i] = (dist_ref[i].astype(F32) + mirror_ref[i].astype(F32)).astype(BF16)
        if i % 2:
            at = pl.ds(i - 1, 2)
            copies.append(pltpu.make_async_copy(dist_ref.at[at], dist_hbm.at[at], sems.at[1 + i // 2]))
            copies[-1].start()
    for copy in copies:
        copy.wait()


def call(kernel, outs, args, scratch=(), smem=(), hbm=(), hbm_outs=False, limit=48):
    spaces = [pltpu.SMEM if i in smem else pl.ANY if i in hbm else pltpu.VMEM for i in range(len(args))]
    return pl.pallas_call(
        kernel,
        out_shape=[jax.ShapeDtypeStruct(s, d) for s, d in outs],
        in_specs=[pl.BlockSpec(memory_space=space) for space in spaces],
        out_specs=[pl.BlockSpec(memory_space=pl.ANY if hbm_outs else pltpu.VMEM)] * len(outs),
        scratch_shapes=list(scratch),
        compiler_params=pltpu.CompilerParams(vmem_limit_bytes=limit * 1024 * 1024),
    )(*args)


def swap_cores(values):
    peers = lax.axis_size("row")
    return lax.ppermute(values, "row", [(i, i ^ 1) for i in range(peers)])


def all_to_all(blocks):
    return lax.all_to_all(blocks, "row", split_axis=0, concat_axis=0, tiled=True)


def shards(
    pair_act, chain_id, residue_mask, norm_gain, w_proj, w_bias, chain_bias, w_out, w_dist, dist_bias,
):
    rows, n, chan = pair_act.shape
    peers = n // rows
    heads, dim = w_out.shape[0], w_out.shape[1]
    bins = w_dist.shape[1]
    tiles = n // LANES
    width = heads * dim
    fused = lax.axis_size("head") == 1
    gain = norm_gain[None, :]
    base = rows * rows
    length = base + tiles * heads * rows // 2

    (packed,) = call(
        pack_kernel,
        [((peers, length, chan), BF16)],
        [pair_act, gain, w_bias.T],
        scratch=[
            pltpu.VMEM(pair_act.shape, BF16),
            pltpu.VMEM(gain.shape, F32),
            pltpu.VMEM((heads, chan), BF16),
            pltpu.VMEM((peers, base, chan), F32),
            pltpu.VMEM((peers, length, chan), BF16),
            pltpu.SemaphoreType.DMA((rows + 2,)),
            pltpu.SemaphoreType.DMA((2,)),
        ],
        hbm=(0, 1, 2),
        hbm_outs=True,
        limit=60,
    )
    received = all_to_all(packed)
    prepared = call(
        functools.partial(prepare_kernel, heads),
        [
            ((heads, n, n), F32), ((3 * width, chan), BF16), ((2 * width, 2 * chan), BF16), ((bins, LANES), F32),
            ((1, chan), F32), ((2 * width, 2 * chan), BF16), ((bins, chan), BF16),
        ],
        [
            chain_id[None, :], residue_mask[None, :], chain_bias, w_proj, dist_bias[None, :],
            gain, w_out.reshape(width, chan), w_dist.T,
        ],
        smem=(2,),
    )
    received, *prepared = lax.optimization_barrier((received, *prepared))
    term, w_types, w_keys, db_col, gain, w_out, wd_t = prepared
    other_bias = swap_cores(received[:, base:])
    spread_shape = ((rows, tiles, width, heads // 2 * LANES), BF16)
    values_shape, gates_shape = ((rows, width // 2, n), BF16), ((rows, width // 2, n), F32)
    softmax_scratch = [
        pltpu.VMEM((heads // 2, n, n), F32),
        pltpu.VMEM((rows, tiles, heads // 2, LANES), F32),
        pltpu.VMEM((rows, tiles, n, heads // 2 * LANES), BF16),
    ]
    x_cols, spread, keys, values, gates, gated = call(
        functools.partial(project_kernel, heads),
        [
            ((rows, n, chan), BF16),
            spread_shape,
            ((rows, n, width), BF16),
            values_shape,
            gates_shape,
            values_shape,
        ],
        [received, gain, w_types, w_keys, term],
        scratch=[
            pltpu.VMEM((rows, n, chan), BF16),
            *(pltpu.VMEM(*shape) for shape in (spread_shape, values_shape, gates_shape)),
            *softmax_scratch,
        ],
    )
    if fused:
        outs = [((peers, base, chan), BF16), ((rows, bins, n), BF16)]
    else:
        outs = [((rows, n, chan), BF16)]
    result = call(
        functools.partial(attend_kernel, fused),
        outs,
        [other_bias, term, w_out, wd_t, db_col, x_cols, spread, keys, values, gates, gated],
        scratch=softmax_scratch + [pltpu.VMEM(*values_shape)] + [pltpu.VMEM((rows, n, chan), BF16), pltpu.VMEM((peers, base, chan), F32)] * fused,
    )
    if fused:
        to_rows, mirror = result
    else:
        update = lax.psum(result[0], "head").astype(F32)
        new = (x_cols.astype(F32) + update).astype(BF16)
        logits = jnp.einsum("cb,jic->jbi", w_dist, new, preferred_element_type=F32)
        mirror = (logits + dist_bias[None, :, None]).astype(BF16)
        to_rows = new.reshape(rows, peers, rows, chan).transpose(1, 2, 0, 3).reshape(peers, base, chan)
    arrived = all_to_all(to_rows)
    new_rows, dist = call(
        finish_kernel,
        [((rows, n, chan), BF16), ((rows, bins, n), BF16)],
        [arrived, mirror, wd_t, db_col],
        scratch=[
            pltpu.VMEM((rows, n, chan), BF16),
            pltpu.VMEM((rows, bins, n), BF16),
            pltpu.SemaphoreType.DMA((1 + rows // 2,)),
        ],
        hbm_outs=True,
    )
    return new_rows, dist.transpose(0, 2, 1)


def solution(mesh):
    in_specs = (
        P(("dp", "row"), None, None),
        P("dp"),
        P("dp"),
        P(),
        P(None, "head", None),
        P(None, "head"),
        P(None, "head"),
        P("head", None, None),
        P(),
        P(),
    )
    out_specs = (P(("dp", "row"), None, None), P(("dp", "row"), None, None))
    return jax.shard_map(shards, mesh=mesh, in_specs=in_specs, out_specs=out_specs, check_vma=False)
```

```python
import functools

import jax
import jax.numpy as jnp
from jax import lax
from jax.experimental import pallas as pl
from jax.experimental.pallas import tpu as pltpu
from jax.sharding import PartitionSpec as P

LANES = 128
F32 = jnp.float32
BF16 = jnp.bfloat16
LOG2E = 1.4426950408889634


def dot_nt(a, b):
    return lax.dot_general(a, b, (((1,), (1,)), ((), ())), preferred_element_type=F32)


def dot_tn(a, b):
    return lax.dot_general(a, b, (((0,), (0,)), ((), ())), preferred_element_type=F32)


def dot_nn(a, b):
    return jnp.dot(a, b, preferred_element_type=F32)


def layer_norm(values, gain):
    center = jnp.mean(values, -1, keepdims=True)
    centered = values - center
    variance = jnp.mean(centered * centered, -1, keepdims=True)
    return (centered * lax.rsqrt(variance + 1e-05) * gain).astype(BF16)


def pack_kernel(x_hbm, gain_hbm, wb_hbm, out_hbm, x_ref, gain_ref, wb_ref, wide, out_ref, sems, out_sems):
    rows, n, chan = x_ref.shape
    peers = n // rows
    heads = wb_ref.shape[0]
    half = heads * rows // 2
    base = rows * rows
    fetch_gain = pltpu.make_async_copy(gain_hbm, gain_ref, sems.at[rows])
    fetch_wb = pltpu.make_async_copy(wb_hbm, wb_ref, sems.at[rows + 1])
    fetches = [pltpu.make_async_copy(x_hbm.at[k], x_ref.at[k], sems.at[k]) for k in range(rows)]
    for copy in (fetch_gain, fetch_wb, *fetches):
        copy.start()
    stores = []

    def store(first, count):
        at = pl.ds(first, count)
        copy = pltpu.make_async_copy(out_ref.at[:, at, :], out_hbm.at[:, at, :], out_sems.at[len(stores)])
        copy.start()
        stores.append(copy)

    owner = lax.broadcasted_iota(jnp.int32, (heads * rows, chan), 0) % rows
    bias = jnp.zeros((heads * rows, n), F32)
    fetch_gain.wait()
    fetch_wb.wait()
    gain = gain_ref[...]
    wb = wb_ref[...].astype(F32)
    wb = jnp.concatenate([jnp.broadcast_to(wb[h : h + 1], (rows, chan)) for h in range(heads)], 0)
    mine = [jnp.where(owner == k, wb, 0.0).astype(BF16) for k in range(rows)]
    mine = [jnp.concatenate(mine[k : k + 2], 1) for k in range(0, rows, 2)]
    for copy in fetches:
        copy.wait()
    normed = [layer_norm(x_ref[k].astype(F32), gain) for k in range(rows)]
    for k in range(rows):
        wide[:, pl.ds(k, rows, stride=rows), :] = x_ref[k].astype(F32).reshape(peers, rows, chan)
    out_ref[:, :base, :] = wide[...].astype(BF16)
    store(0, base)
    for pair in range(rows // 2):
        bias = bias + dot_nt(mine[pair], jnp.concatenate(normed[2 * pair : 2 * pair + 2], 1))
    bias = bias.astype(BF16)
    for t in range(n // LANES):
        block = bias[:, t * LANES : (t + 1) * LANES]
        for d in range(peers):
            part = block[(d % 2) * half : (d % 2 + 1) * half]
            out_ref[d, base + t * half : base + (t + 1) * half] = part
    store(base, (n // LANES) * half)
    for copy in stores:
        copy.wait()


def prepare_kernel(
    heads,
    chain_ref, mask_ref, cb_ref, w_ref, db_ref, gain_ref, wo_ref, wd_ref,
    term_ref, wt_ref, wk_out, dbc_ref, gain_out, wo_out, wd_out,
):
    gain_out[...] = gain_ref[...]
    chan = w_ref.shape[0]
    width = wo_ref.shape[0]
    half = heads // 2
    core = lax.axis_index("row") % 2
    w_out = wo_ref[...].astype(F32)
    other_first = jnp.concatenate([w_out[width // 2 :], w_out[: width // 2]], 0)
    w_out = jnp.where(core == 0, w_out, other_first).astype(BF16)
    wk_out[...] = jnp.zeros_like(wk_out)
    wo_out[...] = jnp.zeros_like(wo_out)
    for side in range(2):
        wo_out[side * width : (side + 1) * width, side * chan : (side + 1) * chan] = w_out
    wd_out[...] = wd_ref[...]
    n = chain_ref.shape[1]
    tiles = n // LANES
    dim = w_ref.shape[2] // 4

    def column_of(row):
        return jnp.transpose(jnp.broadcast_to(row, (LANES, LANES)))

    for kt in range(tiles):
        ks = slice(kt * LANES, (kt + 1) * LANES)
        chain_k = column_of(chain_ref[:, ks].astype(F32))
        mask_k = (column_of(mask_ref[:, ks].astype(F32)) - 1.0) * 1000000000.0
        for it in range(tiles):
            cs = slice(it * LANES, (it + 1) * LANES)
            same = chain_k == chain_ref[:, cs].astype(F32)
            for h in range(heads):
                inside, outside = [jnp.where(core == 0, cb_ref[r, h], cb_ref[r, (h + half) % heads]) for r in (1, 0)]
                term_ref[h, ks, cs] = (jnp.where(same, inside, outside) + mask_k) * LOG2E
    for h in range(heads):
        mine = jnp.where(core == 0, w_ref[:, h, :].astype(F32), w_ref[:, (h + half) % heads, :].astype(F32))
        turned = jnp.transpose(mine).astype(BF16)
        for place, kind in enumerate((0, 2, 3)):
            start = place * width + h * dim
            wt_ref[start : start + dim] = turned[kind * dim : (kind + 1) * dim]
        for side in range(2):
            start = side * width + h * dim
            wk_out[start : start + dim, side * chan : (side + 1) * chan] = turned[dim : 2 * dim]
    bins = dbc_ref.shape[0]
    db_rows = jnp.broadcast_to(jnp.concatenate([db_ref[...], db_ref[...]], 1)[:, :LANES], (LANES, LANES))
    dbc_ref[...] = jnp.transpose(db_rows)[:bins]


def unpack_bias(blocks, term_ref, first, bias_ref):
    half, n = bias_ref.shape[0], bias_ref.shape[1]
    rows = n // len(blocks)
    for s, block in enumerate(blocks):
        at = slice(s * rows, (s + 1) * rows)
        extra = block.astype(F32) * LOG2E
        for t in range(n // LANES):
            cs = slice(t * LANES, (t + 1) * LANES)
            for h in range(half):
                start = (t * half + h) * rows
                bias_ref[h, at, cs] = extra[start : start + rows] + term_ref[first + h, at, cs]


def soften(j, t, keys, spread, bias_ref, scaling, inv_s, e_s):
    scores = dot_nn(keys, spread)
    for h in range(bias_ref.shape[0]):
        cs = slice(h * LANES, (h + 1) * LANES)
        s = scores[:, cs] * scaling + bias_ref[h, :, t * LANES : (t + 1) * LANES]
        e = jnp.exp2(s - jnp.max(s, 0, keepdims=True))
        inv_s[j, t, h : h + 1] = 1.0 / jnp.sum(e, 0, keepdims=True)
        e_s[j, t, :, cs] = e.astype(BF16)


def combine(j, t, values, gates, inv_s, e_s, gated_ref):
    half = inv_s.shape[2]
    dim = values.shape[0] // half
    cs = slice(t * LANES, (t + 1) * LANES)
    o = dot_nn(values, e_s[j, t])
    for h in range(half):
        mine = slice(h * dim, (h + 1) * dim)
        part = o[mine, h * LANES : (h + 1) * LANES] * inv_s[j, t, h : h + 1]
        gated_ref[j, mine, cs] = (gates[mine, cs] * part).astype(BF16)


def for_each(count, tiles, body):
    if tiles == 1:
        for i in range(count):
            body(i)
    else:

        @pl.loop(0, count)
        def _(i):
            body(i)


def regrouped(left, right, rows):
    both = [block.astype(F32).reshape(rows, rows, LANES) for block in (left, right)]
    return jnp.concatenate(both, 1).reshape(2 * rows * rows, LANES)


def project_kernel(
    heads,
    recv_ref, gain_ref, w_ref, wk_ref, term_ref,
    x_s, spread_s, k_s, v_s, g_s, gated_ref,
    n_s, own_spread, own_v, own_g, bias_s, inv_s, e_s,
):
    peers = recv_ref.shape[0]
    rows, n, chan = x_s.shape
    tiles = n // LANES
    dim = w_ref.shape[0] // (3 * heads)
    width = heads * dim
    base = rows * rows
    gain = gain_ref[...]
    group = 2 * rows
    w_k = wk_ref[...]

    quads = range(peers // 4)
    x = [[regrouped(recv_ref[s, :base], recv_ref[s + 1, :base], rows) for s in (4 * q, 4 * q + 2)] for q in quads]
    normed = [[layer_norm(part, gain) for part in two] for two in x]
    keys = [dot_nt(jnp.concatenate(two, 1), w_k).astype(BF16) for two in normed]
    for quad in quads:
        for side in range(2):
            at = slice((2 * quad + side) * group, (2 * quad + side + 1) * group)
            x_s[:, at, :] = x[quad][side].astype(BF16).reshape(rows, group, chan)
            n_s[:, at, :] = normed[quad][side].reshape(rows, group, chan)
            k_s[:, at, :] = keys[quad][:, side * width : (side + 1) * width].reshape(rows, group, width)

    half, part = heads // 2, width // 2
    unpack_bias([recv_ref[s, base:] for s in range(peers)], term_ref, 0, bias_s)
    w_qvg = w_ref[...]
    zero = jnp.zeros((dim, LANES), BF16)

    def project(pair):
        both = dot_nt(w_qvg, n_s[pl.ds(2 * pair, 2)].reshape(2 * n, chan)).astype(BF16)
        for side in range(2):
            j = 2 * pair + side
            qvg = both[:, side * n : (side + 1) * n]
            gate = jax.nn.sigmoid(qvg[2 * width :].astype(F32))
            own_v[j], v_s[j] = qvg[width : width + part], qvg[width + part : 2 * width]
            own_g[j], g_s[j] = gate[:part], gate[part:]
            for t in range(tiles):
                for h in range(heads):
                    target = (own_spread, spread_s)[h // half]
                    cs = slice(h % half * LANES, (h % half + 1) * LANES)
                    for other in range(heads):
                        block = qvg[h * dim : (h + 1) * dim, t * LANES : (t + 1) * LANES] if h == other else zero
                        target[j, t, other * dim : (other + 1) * dim, cs] = block

    scaling = dim ** (-0.5) * LOG2E
    for_each(rows // 2, tiles, project)
    for_each(rows, tiles, lambda j: [soften(j, t, k_s[j], own_spread[j, t], bias_s, scaling, inv_s, e_s) for t in range(tiles)])
    for_each(rows, tiles, lambda j: [combine(j, t, own_v[j], own_g[j], inv_s, e_s, gated_ref) for t in range(tiles)])


def attend_kernel(
    fused,
    other_ref, term_ref, wo_ref, wd_ref, db_ref, x_s, spread_s, k_s, v_s, g_s, gated_ref,
    out_ref, *refs,
):
    if fused:
        second_ref, bias_s, inv_s, e_s, gated_s, new_s, wide = refs
    else:
        bias_s, inv_s, e_s, gated_s = refs
    peers = other_ref.shape[0]
    rows, n, chan = x_s.shape
    tiles = n // LANES
    half, part = bias_s.shape[0], v_s.shape[1]
    scaling = (part // half) ** (-0.5) * LOG2E
    w_out = wo_ref[...]

    unpack_bias([other_ref[s] for s in range(peers)], term_ref, half, bias_s)
    for_each(rows, tiles, lambda j: [soften(j, t, k_s[j], spread_s[j, t], bias_s, scaling, inv_s, e_s) for t in range(tiles)])
    for_each(rows, tiles, lambda j: [combine(j, t, v_s[j], g_s[j], inv_s, e_s, gated_s) for t in range(tiles)])

    def updated(pair):
        both = [ref[2 * pair + side] for side in range(2) for ref in (gated_ref, gated_s)]
        return dot_tn(jnp.concatenate(both, 0), w_out).astype(BF16)

    def store_update(pair):
        update = updated(pair)
        for side in range(2):
            out_ref[2 * pair + side] = update[:, side * chan : (side + 1) * chan]

    if not fused:
        for_each(rows // 2, tiles, store_update)
        return

    for j in range(0, rows, 2):
        update = updated(j // 2).astype(F32)
        for side in range(2):
            new = (x_s[j + side].astype(F32) + update[:, side * chan : (side + 1) * chan]).astype(BF16)
            new_s[j + side] = new
            wide[:, pl.ds(j + side, rows, stride=rows), :] = new.astype(F32).reshape(peers, rows, chan)
    out_ref[...] = wide[...].astype(BF16)
    logits_of(new_s, wd_ref[...], db_ref[:, :1], second_ref)


def logits_of(new_ref, w_dist, d_bias, out_ref):
    rows, n, chan = new_ref.shape
    logits = dot_nt(w_dist, new_ref[...].reshape(rows * n, chan)) + d_bias
    for j in range(rows):
        out_ref[j] = logits[:, j * n : (j + 1) * n].astype(BF16)


def finish_kernel(recv_ref, mirror_ref, wd_ref, db_ref, new_hbm, dist_hbm, new_ref, dist_ref, sems):
    peers, _, chan = recv_ref.shape
    rows = new_ref.shape[0]
    group = 2 * rows
    share = peers // 4
    copies = []
    for pair in range(peers // 2):
        at = slice(pair * group, (pair + 1) * group)
        block = regrouped(recv_ref[2 * pair], recv_ref[2 * pair + 1], rows)
        new_ref[:, at, :] = block.astype(BF16).reshape(rows, group, chan)
        if (pair + 1) % share == 0:
            at = pl.ds((pair + 1 - share) * group, share * group)
            copies.append(pltpu.make_async_copy(new_ref.at[:, at, :], new_hbm.at[:, at, :], sems.at[len(copies)]))
            copies[-1].start()
    logits_of(new_ref, wd_ref[...], db_ref[:, :1], dist_ref)
    for i in range(rows):
        dist_ref[i] = (dist_ref[i].astype(F32) + mirror_ref[i].astype(F32)).astype(BF16)
        if i % 2:
            at = pl.ds(i - 1, 2)
            copies.append(pltpu.make_async_copy(dist_ref.at[at], dist_hbm.at[at], sems.at[len(copies)]))
            copies[-1].start()
    for copy in copies:
        copy.wait()


def call(kernel, outs, args, scratch=(), smem=(), hbm=(), hbm_outs=False, limit=48):
    spaces = [pltpu.SMEM if i in smem else pl.ANY if i in hbm else pltpu.VMEM for i in range(len(args))]
    return pl.pallas_call(
        kernel,
        out_shape=[jax.ShapeDtypeStruct(s, d) for s, d in outs],
        in_specs=[pl.BlockSpec(memory_space=space) for space in spaces],
        out_specs=[pl.BlockSpec(memory_space=pl.ANY if hbm_outs else pltpu.VMEM)] * len(outs),
        scratch_shapes=list(scratch),
        compiler_params=pltpu.CompilerParams(vmem_limit_bytes=limit * 1024 * 1024),
    )(*args)


def swap_cores(values):
    peers = lax.axis_size("row")
    return lax.ppermute(values, "row", [(i, i ^ 1) for i in range(peers)])


def all_to_all(blocks):
    return lax.all_to_all(blocks, "row", split_axis=0, concat_axis=0, tiled=True)


def shards(
    pair_act, chain_id, residue_mask, norm_gain, w_proj, w_bias, chain_bias, w_out, w_dist, dist_bias,
):
    rows, n, chan = pair_act.shape
    peers = n // rows
    heads, dim = w_out.shape[0], w_out.shape[1]
    bins = w_dist.shape[1]
    tiles = n // LANES
    width = heads * dim
    fused = lax.axis_size("head") == 1
    gain = norm_gain[None, :]
    base = rows * rows
    length = base + tiles * heads * rows // 2

    (packed,) = call(
        pack_kernel,
        [((peers, length, chan), BF16)],
        [pair_act, gain, w_bias.T],
        scratch=[
            pltpu.VMEM(pair_act.shape, BF16),
            pltpu.VMEM(gain.shape, F32),
            pltpu.VMEM((heads, chan), BF16),
            pltpu.VMEM((peers, base, chan), F32),
            pltpu.VMEM((peers, length, chan), BF16),
            pltpu.SemaphoreType.DMA((rows + 2,)),
            pltpu.SemaphoreType.DMA((2,)),
        ],
        hbm=(0, 1, 2),
        hbm_outs=True,
        limit=60,
    )
    received = all_to_all(packed)
    prepared = call(
        functools.partial(prepare_kernel, heads),
        [
            ((heads, n, n), F32), ((3 * width, chan), BF16), ((2 * width, 2 * chan), BF16), ((bins, LANES), F32),
            ((1, chan), F32), ((2 * width, 2 * chan), BF16), ((bins, chan), BF16),
        ],
        [
            chain_id[None, :], residue_mask[None, :], chain_bias, w_proj, dist_bias[None, :],
            gain, w_out.reshape(width, chan), w_dist.T,
        ],
        smem=(2,),
    )
    received, *prepared = lax.optimization_barrier((received, *prepared))
    term, w_types, w_keys, db_col, gain, w_out, wd_t = prepared
    other_bias = swap_cores(received[:, base:])
    spread_shape = ((rows, tiles, width, heads // 2 * LANES), BF16)
    values_shape, gates_shape = ((rows, width // 2, n), BF16), ((rows, width // 2, n), F32)
    softmax_scratch = [
        pltpu.VMEM((heads // 2, n, n), F32),
        pltpu.VMEM((rows, tiles, heads // 2, LANES), F32),
        pltpu.VMEM((rows, tiles, n, heads // 2 * LANES), BF16),
    ]
    x_cols, spread, keys, values, gates, gated = call(
        functools.partial(project_kernel, heads),
        [
            ((rows, n, chan), BF16),
            spread_shape,
            ((rows, n, width), BF16),
            values_shape,
            gates_shape,
            values_shape,
        ],
        [received, gain, w_types, w_keys, term],
        scratch=[
            pltpu.VMEM((rows, n, chan), BF16),
            *(pltpu.VMEM(*shape) for shape in (spread_shape, values_shape, gates_shape)),
            *softmax_scratch,
        ],
    )
    if fused:
        outs = [((peers, base, chan), BF16), ((rows, bins, n), BF16)]
    else:
        outs = [((rows, n, chan), BF16)]
    result = call(
        functools.partial(attend_kernel, fused),
        outs,
        [other_bias, term, w_out, wd_t, db_col, x_cols, spread, keys, values, gates, gated],
        scratch=softmax_scratch + [pltpu.VMEM(*values_shape)] + [pltpu.VMEM((rows, n, chan), BF16), pltpu.VMEM((peers, base, chan), F32)] * fused,
    )
    if fused:
        to_rows, mirror = result
    else:
        update = lax.psum(result[0], "head").astype(F32)
        new = (x_cols.astype(F32) + update).astype(BF16)
        logits = jnp.einsum("cb,jic->jbi", w_dist, new, preferred_element_type=F32)
        mirror = (logits + dist_bias[None, :, None]).astype(BF16)
        to_rows = new.reshape(rows, peers, rows, chan).transpose(1, 2, 0, 3).reshape(peers, base, chan)
    arrived = all_to_all(to_rows)
    new_rows, dist = call(
        finish_kernel,
        [((rows, n, chan), BF16), ((rows, bins, n), BF16)],
        [arrived, mirror, wd_t, db_col],
        scratch=[
            pltpu.VMEM((rows, n, chan), BF16),
            pltpu.VMEM((rows, bins, n), BF16),
            pltpu.SemaphoreType.DMA((2 + rows // 2,)),
        ],
        hbm_outs=True,
    )
    return new_rows, dist.transpose(0, 2, 1)


def solution(mesh):
    in_specs = (
        P(("dp", "row"), None, None),
        P("dp"),
        P("dp"),
        P(),
        P(None, "head", None),
        P(None, "head"),
        P(None, "head"),
        P("head", None, None),
        P(),
        P(),
    )
    out_specs = (P(("dp", "row"), None, None), P(("dp", "row"), None, None))
    return jax.shard_map(shards, mesh=mesh, in_specs=in_specs, out_specs=out_specs, check_vma=False)
```

```python
import functools

import jax
import jax.numpy as jnp
from jax import lax
from jax.experimental import pallas as pl
from jax.experimental.pallas import tpu as pltpu
from jax.sharding import PartitionSpec as P

LANES = 128
F32 = jnp.float32
BF16 = jnp.bfloat16
LOG2E = 1.4426950408889634


def dot_nt(a, b):
    return lax.dot_general(a, b, (((1,), (1,)), ((), ())), preferred_element_type=F32)


def dot_tn(a, b):
    return lax.dot_general(a, b, (((0,), (0,)), ((), ())), preferred_element_type=F32)


def dot_nn(a, b):
    return jnp.dot(a, b, preferred_element_type=F32)


def layer_norm(values, gain):
    center = jnp.mean(values, -1, keepdims=True)
    centered = values - center
    variance = jnp.mean(centered * centered, -1, keepdims=True)
    return (centered * lax.rsqrt(variance + 1e-05) * gain).astype(BF16)


def pack_kernel(x_hbm, gain_hbm, wb_hbm, out_hbm, x_ref, gain_ref, wb_ref, wide, out_ref, sems, out_sems):
    rows, n, chan = x_ref.shape
    peers = n // rows
    heads = wb_ref.shape[0]
    half = heads * rows // 2
    base = rows * rows
    fetch_gain = pltpu.make_async_copy(gain_hbm, gain_ref, sems.at[2])
    fetch_wb = pltpu.make_async_copy(wb_hbm, wb_ref, sems.at[3])
    parts = [pl.ds(part * rows // 2, rows // 2) for part in range(2)]
    fetches = [pltpu.make_async_copy(x_hbm.at[at], x_ref.at[at], sems.at[i]) for i, at in enumerate(parts)]
    for copy in (*fetches, fetch_gain, fetch_wb):
        copy.start()
    stores = []

    def store(first, count):
        at = pl.ds(first, count)
        copy = pltpu.make_async_copy(out_ref.at[:, at, :], out_hbm.at[:, at, :], out_sems.at[len(stores)])
        copy.start()
        stores.append(copy)

    owner = lax.broadcasted_iota(jnp.int32, (heads * rows, chan), 0) % rows
    bias = jnp.zeros((heads * rows, n), F32)
    fetch_gain.wait()
    fetch_wb.wait()
    gain = gain_ref[...]
    wb = wb_ref[...].astype(F32)
    wb = jnp.concatenate([jnp.broadcast_to(wb[h : h + 1], (rows, chan)) for h in range(heads)], 0)
    mine = [jnp.where(owner == k, wb, 0.0).astype(BF16) for k in range(rows)]
    mine = [jnp.concatenate(mine[k : k + 2], 1) for k in range(0, rows, 2)]
    for copy in fetches:
        copy.wait()
    normed = [layer_norm(x_ref[k].astype(F32), gain) for k in range(rows)]
    for k in range(rows):
        wide[:, pl.ds(k, rows, stride=rows), :] = x_ref[k].astype(F32).reshape(peers, rows, chan)
    out_ref[:, :base, :] = wide[...].astype(BF16)
    store(0, base)
    for pair in range(rows // 2):
        bias = bias + dot_nt(mine[pair], jnp.concatenate(normed[2 * pair : 2 * pair + 2], 1))
    bias = bias.astype(BF16)
    for t in range(n // LANES):
        block = bias[:, t * LANES : (t + 1) * LANES]
        for d in range(peers):
            part = block[(d % 2) * half : (d % 2 + 1) * half]
            out_ref[d, base + t * half : base + (t + 1) * half] = part
    store(base, (n // LANES) * half)
    for copy in stores:
        copy.wait()


def prepare_kernel(
    heads,
    chain_ref, mask_ref, cb_ref, w_ref, db_ref, gain_ref, wo_ref, wd_ref,
    term_ref, wt_ref, wk_out, dbc_ref, gain_out, wo_out, wd_out,
):
    gain_out[...] = gain_ref[...]
    chan = w_ref.shape[0]
    width = wo_ref.shape[0]
    half = heads // 2
    core = lax.axis_index("row") % 2
    w_out = wo_ref[...].astype(F32)
    other_first = jnp.concatenate([w_out[width // 2 :], w_out[: width // 2]], 0)
    w_out = jnp.where(core == 0, w_out, other_first).astype(BF16)
    wk_out[...] = jnp.zeros_like(wk_out)
    wo_out[...] = jnp.zeros_like(wo_out)
    for side in range(2):
        wo_out[side * width : (side + 1) * width, side * chan : (side + 1) * chan] = w_out
    wd_out[...] = wd_ref[...]
    n = chain_ref.shape[1]
    tiles = n // LANES
    dim = w_ref.shape[2] // 4

    def column_of(row):
        return jnp.transpose(jnp.broadcast_to(row, (LANES, LANES)))

    for kt in range(tiles):
        ks = slice(kt * LANES, (kt + 1) * LANES)
        chain_k = column_of(chain_ref[:, ks].astype(F32))
        mask_k = (column_of(mask_ref[:, ks].astype(F32)) - 1.0) * 1000000000.0
        for it in range(tiles):
            cs = slice(it * LANES, (it + 1) * LANES)
            same = chain_k == chain_ref[:, cs].astype(F32)
            for h in range(heads):
                inside, outside = [jnp.where(core == 0, cb_ref[r, h], cb_ref[r, (h + half) % heads]) for r in (1, 0)]
                term_ref[h, ks, cs] = (jnp.where(same, inside, outside) + mask_k) * LOG2E
    for h in range(heads):
        mine = jnp.where(core == 0, w_ref[:, h, :].astype(F32), w_ref[:, (h + half) % heads, :].astype(F32))
        turned = jnp.transpose(mine).astype(BF16)
        for place, kind in enumerate((0, 2, 3)):
            start = place * width + h * dim
            wt_ref[start : start + dim] = turned[kind * dim : (kind + 1) * dim]
        for side in range(2):
            start = side * width + h * dim
            wk_out[start : start + dim, side * chan : (side + 1) * chan] = turned[dim : 2 * dim]
    bins = dbc_ref.shape[0]
    db_rows = jnp.broadcast_to(jnp.concatenate([db_ref[...], db_ref[...]], 1)[:, :LANES], (LANES, LANES))
    dbc_ref[...] = jnp.transpose(db_rows)[:bins]


def unpack_bias(blocks, term_ref, first, bias_ref):
    half, n = bias_ref.shape[0], bias_ref.shape[1]
    rows = n // len(blocks)
    for s, block in enumerate(blocks):
        at = slice(s * rows, (s + 1) * rows)
        extra = block.astype(F32) * LOG2E
        for t in range(n // LANES):
            cs = slice(t * LANES, (t + 1) * LANES)
            for h in range(half):
                start = (t * half + h) * rows
                bias_ref[h, at, cs] = extra[start : start + rows] + term_ref[first + h, at, cs]


def soften(j, t, keys, spread, bias_ref, scaling, inv_s, e_s):
    scores = dot_nn(keys, spread)
    for h in range(bias_ref.shape[0]):
        cs = slice(h * LANES, (h + 1) * LANES)
        s = scores[:, cs] * scaling + bias_ref[h, :, t * LANES : (t + 1) * LANES]
        e = jnp.exp2(s - jnp.max(s, 0, keepdims=True))
        inv_s[j, t, h : h + 1] = 1.0 / jnp.sum(e, 0, keepdims=True)
        e_s[j, t, :, cs] = e.astype(BF16)


def combine(j, t, values, gates, inv_s, e_s, gated_ref):
    half = inv_s.shape[2]
    dim = values.shape[0] // half
    cs = slice(t * LANES, (t + 1) * LANES)
    o = dot_nn(values, e_s[j, t])
    for h in range(half):
        mine = slice(h * dim, (h + 1) * dim)
        part = o[mine, h * LANES : (h + 1) * LANES] * inv_s[j, t, h : h + 1]
        gated_ref[j, mine, cs] = (gates[mine, cs] * part).astype(BF16)


def for_each(count, tiles, body):
    if tiles == 1:
        for i in range(count):
            body(i)
    else:

        @pl.loop(0, count)
        def _(i):
            body(i)


def regrouped(left, right, rows):
    both = [block.astype(F32).reshape(rows, rows, LANES) for block in (left, right)]
    return jnp.concatenate(both, 1).reshape(2 * rows * rows, LANES)


def project_kernel(
    heads,
    recv_ref, gain_ref, w_ref, wk_ref, term_ref,
    x_s, spread_s, k_s, v_s, g_s, gated_ref,
    n_s, own_spread, own_v, own_g, bias_s, inv_s, e_s,
):
    peers = recv_ref.shape[0]
    rows, n, chan = x_s.shape
    tiles = n // LANES
    dim = w_ref.shape[0] // (3 * heads)
    width = heads * dim
    base = rows * rows
    gain = gain_ref[...]
    group = 2 * rows
    w_k = wk_ref[...]

    quads = range(peers // 4)
    x = [[regrouped(recv_ref[s, :base], recv_ref[s + 1, :base], rows) for s in (4 * q, 4 * q + 2)] for q in quads]
    normed = [[layer_norm(part, gain) for part in two] for two in x]
    keys = [dot_nt(jnp.concatenate(two, 1), w_k).astype(BF16) for two in normed]
    for quad in quads:
        for side in range(2):
            at = slice((2 * quad + side) * group, (2 * quad + side + 1) * group)
            x_s[:, at, :] = x[quad][side].astype(BF16).reshape(rows, group, chan)
            n_s[:, at, :] = normed[quad][side].reshape(rows, group, chan)
            k_s[:, at, :] = keys[quad][:, side * width : (side + 1) * width].reshape(rows, group, width)

    half, part = heads // 2, width // 2
    unpack_bias([recv_ref[s, base:] for s in range(peers)], term_ref, 0, bias_s)
    w_qvg = w_ref[...]
    zero = jnp.zeros((dim, LANES), BF16)

    def project(pair):
        both = dot_nt(w_qvg, n_s[pl.ds(2 * pair, 2)].reshape(2 * n, chan)).astype(BF16)
        for side in range(2):
            j = 2 * pair + side
            qvg = both[:, side * n : (side + 1) * n]
            gate = jax.nn.sigmoid(qvg[2 * width :].astype(F32))
            own_v[j], v_s[j] = qvg[width : width + part], qvg[width + part : 2 * width]
            own_g[j], g_s[j] = gate[:part], gate[part:]
            for t in range(tiles):
                for h in range(heads):
                    target = (own_spread, spread_s)[h // half]
                    cs = slice(h % half * LANES, (h % half + 1) * LANES)
                    for other in range(heads):
                        block = qvg[h * dim : (h + 1) * dim, t * LANES : (t + 1) * LANES] if h == other else zero
                        target[j, t, other * dim : (other + 1) * dim, cs] = block

    scaling = dim ** (-0.5) * LOG2E
    for_each(rows // 2, tiles, project)
    for_each(rows, tiles, lambda j: [soften(j, t, k_s[j], own_spread[j, t], bias_s, scaling, inv_s, e_s) for t in range(tiles)])
    for_each(rows, tiles, lambda j: [combine(j, t, own_v[j], own_g[j], inv_s, e_s, gated_ref) for t in range(tiles)])


def attend_kernel(
    fused,
    other_ref, term_ref, wo_ref, wd_ref, db_ref, x_s, spread_s, k_s, v_s, g_s, gated_ref,
    out_ref, *refs,
):
    if fused:
        second_ref, bias_s, inv_s, e_s, gated_s, new_s, wide = refs
    else:
        bias_s, inv_s, e_s, gated_s = refs
    peers = other_ref.shape[0]
    rows, n, chan = x_s.shape
    tiles = n // LANES
    half, part = bias_s.shape[0], v_s.shape[1]
    scaling = (part // half) ** (-0.5) * LOG2E
    w_out = wo_ref[...]

    unpack_bias([other_ref[s] for s in range(peers)], term_ref, half, bias_s)
    for_each(rows, tiles, lambda j: [soften(j, t, k_s[j], spread_s[j, t], bias_s, scaling, inv_s, e_s) for t in range(tiles)])
    for_each(rows, tiles, lambda j: [combine(j, t, v_s[j], g_s[j], inv_s, e_s, gated_s) for t in range(tiles)])

    def updated(pair):
        both = [ref[2 * pair + side] for side in range(2) for ref in (gated_ref, gated_s)]
        return dot_tn(jnp.concatenate(both, 0), w_out).astype(BF16)

    def store_update(pair):
        update = updated(pair)
        for side in range(2):
            out_ref[2 * pair + side] = update[:, side * chan : (side + 1) * chan]

    if not fused:
        for_each(rows // 2, tiles, store_update)
        return

    for j in range(0, rows, 2):
        update = updated(j // 2).astype(F32)
        for side in range(2):
            new = (x_s[j + side].astype(F32) + update[:, side * chan : (side + 1) * chan]).astype(BF16)
            new_s[j + side] = new
            wide[:, pl.ds(j + side, rows, stride=rows), :] = new.astype(F32).reshape(peers, rows, chan)
    out_ref[...] = wide[...].astype(BF16)
    logits_of(new_s, wd_ref[...], db_ref[:, :1], second_ref)


def logits_of(new_ref, w_dist, d_bias, out_ref):
    rows, n, chan = new_ref.shape
    logits = dot_nt(w_dist, new_ref[...].reshape(rows * n, chan)) + d_bias
    for j in range(rows):
        out_ref[j] = logits[:, j * n : (j + 1) * n].astype(BF16)


def finish_kernel(recv_ref, mirror_ref, wd_ref, db_ref, new_hbm, dist_hbm, new_ref, dist_ref, sems):
    peers, _, chan = recv_ref.shape
    rows = new_ref.shape[0]
    group = 2 * rows
    share = peers // 4
    copies = []
    for pair in range(peers // 2):
        at = slice(pair * group, (pair + 1) * group)
        block = regrouped(recv_ref[2 * pair], recv_ref[2 * pair + 1], rows)
        new_ref[:, at, :] = block.astype(BF16).reshape(rows, group, chan)
        if (pair + 1) % share == 0:
            at = pl.ds((pair + 1 - share) * group, share * group)
            copies.append(pltpu.make_async_copy(new_ref.at[:, at, :], new_hbm.at[:, at, :], sems.at[len(copies)]))
            copies[-1].start()
    logits_of(new_ref, wd_ref[...], db_ref[:, :1], dist_ref)
    for i in range(rows):
        dist_ref[i] = (dist_ref[i].astype(F32) + mirror_ref[i].astype(F32)).astype(BF16)
        if i % 2:
            at = pl.ds(i - 1, 2)
            copies.append(pltpu.make_async_copy(dist_ref.at[at], dist_hbm.at[at], sems.at[len(copies)]))
            copies[-1].start()
    for copy in copies:
        copy.wait()


def call(kernel, outs, args, scratch=(), smem=(), hbm=(), hbm_outs=False, limit=48):
    spaces = [pltpu.SMEM if i in smem else pl.ANY if i in hbm else pltpu.VMEM for i in range(len(args))]
    return pl.pallas_call(
        kernel,
        out_shape=[jax.ShapeDtypeStruct(s, d) for s, d in outs],
        in_specs=[pl.BlockSpec(memory_space=space) for space in spaces],
        out_specs=[pl.BlockSpec(memory_space=pl.ANY if hbm_outs else pltpu.VMEM)] * len(outs),
        scratch_shapes=list(scratch),
        compiler_params=pltpu.CompilerParams(vmem_limit_bytes=limit * 1024 * 1024),
    )(*args)


def swap_cores(values):
    peers = lax.axis_size("row")
    return lax.ppermute(values, "row", [(i, i ^ 1) for i in range(peers)])


def all_to_all(blocks):
    return lax.all_to_all(blocks, "row", split_axis=0, concat_axis=0, tiled=True)


def shards(
    pair_act, chain_id, residue_mask, norm_gain, w_proj, w_bias, chain_bias, w_out, w_dist, dist_bias,
):
    rows, n, chan = pair_act.shape
    peers = n // rows
    heads, dim = w_out.shape[0], w_out.shape[1]
    bins = w_dist.shape[1]
    tiles = n // LANES
    width = heads * dim
    fused = lax.axis_size("head") == 1
    gain = norm_gain[None, :]
    base = rows * rows
    length = base + tiles * heads * rows // 2

    (packed,) = call(
        pack_kernel,
        [((peers, length, chan), BF16)],
        [pair_act, gain, w_bias.T],
        scratch=[
            pltpu.VMEM(pair_act.shape, BF16),
            pltpu.VMEM(gain.shape, F32),
            pltpu.VMEM((heads, chan), BF16),
            pltpu.VMEM((peers, base, chan), F32),
            pltpu.VMEM((peers, length, chan), BF16),
            pltpu.SemaphoreType.DMA((4,)),
            pltpu.SemaphoreType.DMA((2,)),
        ],
        hbm=(0, 1, 2),
        hbm_outs=True,
        limit=60,
    )
    received = all_to_all(packed)
    prepared = call(
        functools.partial(prepare_kernel, heads),
        [
            ((heads, n, n), F32), ((3 * width, chan), BF16), ((2 * width, 2 * chan), BF16), ((bins, LANES), F32),
            ((1, chan), F32), ((2 * width, 2 * chan), BF16), ((bins, chan), BF16),
        ],
        [
            chain_id[None, :], residue_mask[None, :], chain_bias, w_proj, dist_bias[None, :],
            gain, w_out.reshape(width, chan), w_dist.T,
        ],
        smem=(2,),
    )
    received, *prepared = lax.optimization_barrier((received, *prepared))
    term, w_types, w_keys, db_col, gain, w_out, wd_t = prepared
    other_bias = swap_cores(received[:, base:])
    spread_shape = ((rows, tiles, width, heads // 2 * LANES), BF16)
    values_shape, gates_shape = ((rows, width // 2, n), BF16), ((rows, width // 2, n), F32)
    softmax_scratch = [
        pltpu.VMEM((heads // 2, n, n), F32),
        pltpu.VMEM((rows, tiles, heads // 2, LANES), F32),
        pltpu.VMEM((rows, tiles, n, heads // 2 * LANES), BF16),
    ]
    x_cols, spread, keys, values, gates, gated = call(
        functools.partial(project_kernel, heads),
        [
            ((rows, n, chan), BF16),
            spread_shape,
            ((rows, n, width), BF16),
            values_shape,
            gates_shape,
            values_shape,
        ],
        [received, gain, w_types, w_keys, term],
        scratch=[
            pltpu.VMEM((rows, n, chan), BF16),
            *(pltpu.VMEM(*shape) for shape in (spread_shape, values_shape, gates_shape)),
            *softmax_scratch,
        ],
    )
    if fused:
        outs = [((peers, base, chan), BF16), ((rows, bins, n), BF16)]
    else:
        outs = [((rows, n, chan), BF16)]
    result = call(
        functools.partial(attend_kernel, fused),
        outs,
        [other_bias, term, w_out, wd_t, db_col, x_cols, spread, keys, values, gates, gated],
        scratch=softmax_scratch + [pltpu.VMEM(*values_shape)] + [pltpu.VMEM((rows, n, chan), BF16), pltpu.VMEM((peers, base, chan), F32)] * fused,
    )
    if fused:
        to_rows, mirror = result
    else:
        update = lax.psum(result[0], "head").astype(F32)
        new = (x_cols.astype(F32) + update).astype(BF16)
        logits = jnp.einsum("cb,jic->jbi", w_dist, new, preferred_element_type=F32)
        mirror = (logits + dist_bias[None, :, None]).astype(BF16)
        to_rows = new.reshape(rows, peers, rows, chan).transpose(1, 2, 0, 3).reshape(peers, base, chan)
    arrived = all_to_all(to_rows)
    new_rows, dist = call(
        finish_kernel,
        [((rows, n, chan), BF16), ((rows, bins, n), BF16)],
        [arrived, mirror, wd_t, db_col],
        scratch=[
            pltpu.VMEM((rows, n, chan), BF16),
            pltpu.VMEM((rows, bins, n), BF16),
            pltpu.SemaphoreType.DMA((2 + rows // 2,)),
        ],
        hbm_outs=True,
    )
    return new_rows, dist.transpose(0, 2, 1)


def solution(mesh):
    in_specs = (
        P(("dp", "row"), None, None),
        P("dp"),
        P("dp"),
        P(),
        P(None, "head", None),
        P(None, "head"),
        P(None, "head"),
        P("head", None, None),
        P(),
        P(),
    )
    out_specs = (P(("dp", "row"), None, None), P(("dp", "row"), None, None))
    return jax.shard_map(shards, mesh=mesh, in_specs=in_specs, out_specs=out_specs, check_vma=False)
```

```python
import functools

import jax
import jax.numpy as jnp
from jax import lax
from jax.experimental import pallas as pl
from jax.experimental.pallas import tpu as pltpu
from jax.sharding import PartitionSpec as P

LANES = 128
F32 = jnp.float32
BF16 = jnp.bfloat16
LOG2E = 1.4426950408889634


def dot_nt(a, b):
    return lax.dot_general(a, b, (((1,), (1,)), ((), ())), preferred_element_type=F32)


def dot_tn(a, b):
    return lax.dot_general(a, b, (((0,), (0,)), ((), ())), preferred_element_type=F32)


def dot_nn(a, b):
    return jnp.dot(a, b, preferred_element_type=F32)


def layer_norm(values, gain):
    center = jnp.mean(values, -1, keepdims=True)
    centered = values - center
    variance = jnp.mean(centered * centered, -1, keepdims=True)
    return (centered * lax.rsqrt(variance + 1e-05) * gain).astype(BF16)


def pack_kernel(x_hbm, gain_hbm, wb_hbm, out_hbm, x_ref, gain_ref, wb_ref, wide, out_ref, sems, out_sems):
    rows, n, chan = x_ref.shape
    peers = n // rows
    heads = wb_ref.shape[0]
    half = heads * rows // 2
    base = rows * rows
    fetch_gain = pltpu.make_async_copy(gain_hbm, gain_ref, sems.at[rows])
    fetch_wb = pltpu.make_async_copy(wb_hbm, wb_ref, sems.at[rows + 1])
    fetches = [pltpu.make_async_copy(x_hbm.at[k], x_ref.at[k], sems.at[k]) for k in range(rows)]
    for copy in (fetch_gain, fetch_wb, *fetches):
        copy.start()
    stores = []

    def store(first, count):
        at = pl.ds(first, count)
        copy = pltpu.make_async_copy(out_ref.at[:, at, :], out_hbm.at[:, at, :], out_sems.at[len(stores)])
        copy.start()
        stores.append(copy)

    owner = lax.broadcasted_iota(jnp.int32, (heads * rows, chan), 0) % rows
    bias = jnp.zeros((heads * rows, n), F32)
    fetch_gain.wait()
    fetch_wb.wait()
    gain = gain_ref[...]
    wb = wb_ref[...].astype(F32)
    wb = jnp.concatenate([jnp.broadcast_to(wb[h : h + 1], (rows, chan)) for h in range(heads)], 0)
    mine = [jnp.where(owner == k, wb, 0.0).astype(BF16) for k in range(rows)]
    mine = [jnp.concatenate(mine[k : k + 2], 1) for k in range(0, rows, 2)]
    for copy in fetches:
        copy.wait()
    normed = [layer_norm(x_ref[k].astype(F32), gain) for k in range(rows)]
    for k in range(rows):
        wide[:, pl.ds(k, rows, stride=rows), :] = x_ref[k].astype(F32).reshape(peers, rows, chan)
    out_ref[:, :base, :] = wide[...].astype(BF16)
    store(0, base)
    for pair in range(rows // 2):
        bias = bias + dot_nt(mine[pair], jnp.concatenate(normed[2 * pair : 2 * pair + 2], 1))
    bias = bias.astype(BF16)
    for t in range(n // LANES):
        block = bias[:, t * LANES : (t + 1) * LANES]
        for d in range(peers):
            part = block[(d % 2) * half : (d % 2 + 1) * half]
            out_ref[d, base + t * half : base + (t + 1) * half] = part
    store(base, (n // LANES) * half)
    for copy in stores:
        copy.wait()


def prepare_kernel(
    heads,
    chain_ref, mask_ref, cb_ref, w_ref, db_ref, gain_ref, wo_ref, wd_ref,
    term_ref, wt_ref, wk_out, dbc_ref, gain_out, wo_out, wd_out,
):
    gain_out[...] = gain_ref[...]
    chan = w_ref.shape[0]
    width = wo_ref.shape[0]
    half = heads // 2
    core = lax.axis_index("row") % 2
    w_out = wo_ref[...].astype(F32)
    other_first = jnp.concatenate([w_out[width // 2 :], w_out[: width // 2]], 0)
    w_out = jnp.where(core == 0, w_out, other_first).astype(BF16)
    wk_out[...] = jnp.zeros_like(wk_out)
    wo_out[...] = jnp.zeros_like(wo_out)
    for side in range(2):
        wo_out[side * width : (side + 1) * width, side * chan : (side + 1) * chan] = w_out
    wd_out[...] = wd_ref[...]
    n = chain_ref.shape[1]
    tiles = n // LANES
    dim = w_ref.shape[2] // 4

    def column_of(row):
        return jnp.transpose(jnp.broadcast_to(row, (LANES, LANES)))

    for kt in range(tiles):
        ks = slice(kt * LANES, (kt + 1) * LANES)
        chain_k = column_of(chain_ref[:, ks].astype(F32))
        mask_k = (column_of(mask_ref[:, ks].astype(F32)) - 1.0) * 1000000000.0
        for it in range(tiles):
            cs = slice(it * LANES, (it + 1) * LANES)
            same = chain_k == chain_ref[:, cs].astype(F32)
            for h in range(heads):
                inside, outside = [jnp.where(core == 0, cb_ref[r, h], cb_ref[r, (h + half) % heads]) for r in (1, 0)]
                term_ref[h, ks, cs] = (jnp.where(same, inside, outside) + mask_k) * LOG2E
    for h in range(heads):
        mine = jnp.where(core == 0, w_ref[:, h, :].astype(F32), w_ref[:, (h + half) % heads, :].astype(F32))
        turned = jnp.transpose(mine).astype(BF16)
        for place, kind in enumerate((0, 2, 3)):
            start = place * width + h * dim
            wt_ref[start : start + dim] = turned[kind * dim : (kind + 1) * dim]
        for side in range(2):
            start = side * width + h * dim
            wk_out[start : start + dim, side * chan : (side + 1) * chan] = turned[dim : 2 * dim]
    bins = dbc_ref.shape[0]
    db_rows = jnp.broadcast_to(jnp.concatenate([db_ref[...], db_ref[...]], 1)[:, :LANES], (LANES, LANES))
    dbc_ref[...] = jnp.transpose(db_rows)[:bins]


def unpack_bias(blocks, term_ref, first, bias_ref):
    half, n = bias_ref.shape[0], bias_ref.shape[1]
    rows = n // len(blocks)
    for s, block in enumerate(blocks):
        at = slice(s * rows, (s + 1) * rows)
        extra = block.astype(F32) * LOG2E
        for t in range(n // LANES):
            cs = slice(t * LANES, (t + 1) * LANES)
            for h in range(half):
                start = (t * half + h) * rows
                bias_ref[h, at, cs] = extra[start : start + rows] + term_ref[first + h, at, cs]


def soften(j, t, keys, spread, bias_ref, scaling, inv_s, e_s):
    scores = dot_nn(keys, spread)
    for h in range(bias_ref.shape[0]):
        cs = slice(h * LANES, (h + 1) * LANES)
        s = scores[:, cs] * scaling + bias_ref[h, :, t * LANES : (t + 1) * LANES]
        e = jnp.exp2(s - jnp.max(s, 0, keepdims=True))
        inv_s[j, t, h : h + 1] = 1.0 / jnp.sum(e, 0, keepdims=True)
        e_s[j, t, :, cs] = e.astype(BF16)


def combine(j, t, values, gates, inv_s, e_s, gated_ref):
    half = inv_s.shape[2]
    dim = values.shape[0] // half
    cs = slice(t * LANES, (t + 1) * LANES)
    o = dot_nn(values, e_s[j, t])
    for h in range(half):
        mine = slice(h * dim, (h + 1) * dim)
        part = o[mine, h * LANES : (h + 1) * LANES] * inv_s[j, t, h : h + 1]
        gated_ref[j, mine, cs] = (gates[mine, cs] * part).astype(BF16)


def for_each(count, tiles, body):
    if tiles == 1:
        for i in range(count):
            body(i)
    else:

        @pl.loop(0, count)
        def _(i):
            body(i)


def regrouped(left, right, rows):
    both = [block.astype(F32).reshape(rows, rows, LANES) for block in (left, right)]
    return jnp.concatenate(both, 1).reshape(2 * rows * rows, LANES)


def project_kernel(
    heads,
    recv_ref, gain_ref, w_ref, wk_ref, term_ref,
    x_s, spread_s, k_s, v_s, g_s, gated_ref,
    n_s, own_spread, own_v, own_g, bias_s, inv_s, e_s,
):
    peers = recv_ref.shape[0]
    rows, n, chan = x_s.shape
    tiles = n // LANES
    dim = w_ref.shape[0] // (3 * heads)
    width = heads * dim
    base = rows * rows
    gain = gain_ref[...]
    group = 2 * rows
    w_k = wk_ref[...]

    quads = range(peers // 4)
    x = [[regrouped(recv_ref[s, :base], recv_ref[s + 1, :base], rows) for s in (4 * q, 4 * q + 2)] for q in quads]
    normed = [[layer_norm(part, gain) for part in two] for two in x]
    keys = [dot_nt(jnp.concatenate(two, 1), w_k).astype(BF16) for two in normed]
    for quad in quads:
        for side in range(2):
            at = slice((2 * quad + side) * group, (2 * quad + side + 1) * group)
            x_s[:, at, :] = x[quad][side].astype(BF16).reshape(rows, group, chan)
            n_s[:, at, :] = normed[quad][side].reshape(rows, group, chan)
            k_s[:, at, :] = keys[quad][:, side * width : (side + 1) * width].reshape(rows, group, width)

    half, part = heads // 2, width // 2
    unpack_bias([recv_ref[s, base:] for s in range(peers)], term_ref, 0, bias_s)
    w_qvg = w_ref[...]
    zero = jnp.zeros((dim, LANES), BF16)

    def project(pair):
        both = dot_nt(w_qvg, n_s[pl.ds(2 * pair, 2)].reshape(2 * n, chan)).astype(BF16)
        for side in range(2):
            j = 2 * pair + side
            qvg = both[:, side * n : (side + 1) * n]
            gate = jax.nn.sigmoid(qvg[2 * width :].astype(F32))
            own_v[j], v_s[j] = qvg[width : width + part], qvg[width + part : 2 * width]
            own_g[j], g_s[j] = gate[:part], gate[part:]
            for t in range(tiles):
                for h in range(heads):
                    target = (own_spread, spread_s)[h // half]
                    cs = slice(h % half * LANES, (h % half + 1) * LANES)
                    for other in range(heads):
                        block = qvg[h * dim : (h + 1) * dim, t * LANES : (t + 1) * LANES] if h == other else zero
                        target[j, t, other * dim : (other + 1) * dim, cs] = block

    scaling = dim ** (-0.5) * LOG2E
    for_each(rows // 2, tiles, project)
    for_each(rows, tiles, lambda j: [soften(j, t, k_s[j], own_spread[j, t], bias_s, scaling, inv_s, e_s) for t in range(tiles)])
    for_each(rows, tiles, lambda j: [combine(j, t, own_v[j], own_g[j], inv_s, e_s, gated_ref) for t in range(tiles)])


def attend_kernel(
    fused,
    other_ref, term_ref, wo_ref, x_s, spread_s, k_s, v_s, g_s, gated_ref,
    out_ref, *refs,
):
    if fused:
        new_s, bias_s, inv_s, e_s, gated_s, wide = refs
    else:
        bias_s, inv_s, e_s, gated_s = refs
    peers = other_ref.shape[0]
    rows, n, chan = x_s.shape
    tiles = n // LANES
    half, part = bias_s.shape[0], v_s.shape[1]
    scaling = (part // half) ** (-0.5) * LOG2E
    w_out = wo_ref[...]

    unpack_bias([other_ref[s] for s in range(peers)], term_ref, half, bias_s)
    for_each(rows, tiles, lambda j: [soften(j, t, k_s[j], spread_s[j, t], bias_s, scaling, inv_s, e_s) for t in range(tiles)])
    for_each(rows, tiles, lambda j: [combine(j, t, v_s[j], g_s[j], inv_s, e_s, gated_s) for t in range(tiles)])

    def updated(pair):
        both = [ref[2 * pair + side] for side in range(2) for ref in (gated_ref, gated_s)]
        return dot_tn(jnp.concatenate(both, 0), w_out).astype(BF16)

    def store_update(pair):
        update = updated(pair)
        for side in range(2):
            out_ref[2 * pair + side] = update[:, side * chan : (side + 1) * chan]

    if not fused:
        for_each(rows // 2, tiles, store_update)
        return

    for j in range(0, rows, 2):
        update = updated(j // 2).astype(F32)
        for side in range(2):
            new = (x_s[j + side].astype(F32) + update[:, side * chan : (side + 1) * chan]).astype(BF16)
            new_s[j + side] = new
            wide[:, pl.ds(j + side, rows, stride=rows), :] = new.astype(F32).reshape(peers, rows, chan)
    out_ref[...] = wide[...].astype(BF16)


def mirror_kernel(new_ref, wd_ref, db_ref, out_ref):
    logits_of(new_ref, wd_ref[...], db_ref[:, :1], out_ref)


def logits_of(new_ref, w_dist, d_bias, out_ref):
    rows, n, chan = new_ref.shape
    logits = dot_nt(w_dist, new_ref[...].reshape(rows * n, chan)) + d_bias
    for j in range(rows):
        out_ref[j] = logits[:, j * n : (j + 1) * n].astype(BF16)


def finish_kernel(recv_ref, mirror_ref, wd_ref, db_ref, new_hbm, dist_hbm, new_ref, dist_ref, sems):
    peers, _, chan = recv_ref.shape
    rows = new_ref.shape[0]
    group = 2 * rows
    share = peers // 4
    copies = []
    for pair in range(peers // 2):
        at = slice(pair * group, (pair + 1) * group)
        block = regrouped(recv_ref[2 * pair], recv_ref[2 * pair + 1], rows)
        new_ref[:, at, :] = block.astype(BF16).reshape(rows, group, chan)
        if (pair + 1) % share == 0:
            at = pl.ds((pair + 1 - share) * group, share * group)
            copies.append(pltpu.make_async_copy(new_ref.at[:, at, :], new_hbm.at[:, at, :], sems.at[len(copies)]))
            copies[-1].start()
    logits_of(new_ref, wd_ref[...], db_ref[:, :1], dist_ref)
    for i in range(rows):
        dist_ref[i] = (dist_ref[i].astype(F32) + mirror_ref[i].astype(F32)).astype(BF16)
        if i % 2:
            at = pl.ds(i - 1, 2)
            copies.append(pltpu.make_async_copy(dist_ref.at[at], dist_hbm.at[at], sems.at[len(copies)]))
            copies[-1].start()
    for copy in copies:
        copy.wait()


def call(kernel, outs, args, scratch=(), smem=(), hbm=(), hbm_outs=False, limit=48):
    spaces = [pltpu.SMEM if i in smem else pl.ANY if i in hbm else pltpu.VMEM for i in range(len(args))]
    return pl.pallas_call(
        kernel,
        out_shape=[jax.ShapeDtypeStruct(s, d) for s, d in outs],
        in_specs=[pl.BlockSpec(memory_space=space) for space in spaces],
        out_specs=[pl.BlockSpec(memory_space=pl.ANY if hbm_outs else pltpu.VMEM)] * len(outs),
        scratch_shapes=list(scratch),
        compiler_params=pltpu.CompilerParams(vmem_limit_bytes=limit * 1024 * 1024),
    )(*args)


def swap_cores(values):
    peers = lax.axis_size("row")
    return lax.ppermute(values, "row", [(i, i ^ 1) for i in range(peers)])


def all_to_all(blocks):
    return lax.all_to_all(blocks, "row", split_axis=0, concat_axis=0, tiled=True)


def shards(
    pair_act, chain_id, residue_mask, norm_gain, w_proj, w_bias, chain_bias, w_out, w_dist, dist_bias,
):
    rows, n, chan = pair_act.shape
    peers = n // rows
    heads, dim = w_out.shape[0], w_out.shape[1]
    bins = w_dist.shape[1]
    tiles = n // LANES
    width = heads * dim
    fused = lax.axis_size("head") == 1
    gain = norm_gain[None, :]
    base = rows * rows
    length = base + tiles * heads * rows // 2

    (packed,) = call(
        pack_kernel,
        [((peers, length, chan), BF16)],
        [pair_act, gain, w_bias.T],
        scratch=[
            pltpu.VMEM(pair_act.shape, BF16),
            pltpu.VMEM(gain.shape, F32),
            pltpu.VMEM((heads, chan), BF16),
            pltpu.VMEM((peers, base, chan), F32),
            pltpu.VMEM((peers, length, chan), BF16),
            pltpu.SemaphoreType.DMA((rows + 2,)),
            pltpu.SemaphoreType.DMA((2,)),
        ],
        hbm=(0, 1, 2),
        hbm_outs=True,
        limit=60,
    )
    received = all_to_all(packed)
    prepared = call(
        functools.partial(prepare_kernel, heads),
        [
            ((heads, n, n), F32), ((3 * width, chan), BF16), ((2 * width, 2 * chan), BF16), ((bins, LANES), F32),
            ((1, chan), F32), ((2 * width, 2 * chan), BF16), ((bins, chan), BF16),
        ],
        [
            chain_id[None, :], residue_mask[None, :], chain_bias, w_proj, dist_bias[None, :],
            gain, w_out.reshape(width, chan), w_dist.T,
        ],
        smem=(2,),
    )
    received, *prepared = lax.optimization_barrier((received, *prepared))
    term, w_types, w_keys, db_col, gain, w_out, wd_t = prepared
    other_bias = swap_cores(received[:, base:])
    spread_shape = ((rows, tiles, width, heads // 2 * LANES), BF16)
    values_shape, gates_shape = ((rows, width // 2, n), BF16), ((rows, width // 2, n), F32)
    softmax_scratch = [
        pltpu.VMEM((heads // 2, n, n), F32),
        pltpu.VMEM((rows, tiles, heads // 2, LANES), F32),
        pltpu.VMEM((rows, tiles, n, heads // 2 * LANES), BF16),
    ]
    x_cols, spread, keys, values, gates, gated = call(
        functools.partial(project_kernel, heads),
        [
            ((rows, n, chan), BF16),
            spread_shape,
            ((rows, n, width), BF16),
            values_shape,
            gates_shape,
            values_shape,
        ],
        [received, gain, w_types, w_keys, term],
        scratch=[
            pltpu.VMEM((rows, n, chan), BF16),
            *(pltpu.VMEM(*shape) for shape in (spread_shape, values_shape, gates_shape)),
            *softmax_scratch,
        ],
    )
    if fused:
        outs = [((peers, base, chan), BF16), ((rows, n, chan), BF16)]
    else:
        outs = [((rows, n, chan), BF16)]
    result = call(
        functools.partial(attend_kernel, fused),
        outs,
        [other_bias, term, w_out, x_cols, spread, keys, values, gates, gated],
        scratch=softmax_scratch + [pltpu.VMEM(*values_shape)] + [pltpu.VMEM((peers, base, chan), F32)] * fused,
    )
    if fused:
        to_rows, new = result
    else:
        update = lax.psum(result[0], "head").astype(F32)
        new = (x_cols.astype(F32) + update).astype(BF16)
        to_rows = new.reshape(rows, peers, rows, chan).transpose(1, 2, 0, 3).reshape(peers, base, chan)
    arrived = all_to_all(to_rows)
    (mirror,) = call(mirror_kernel, [((rows, bins, n), BF16)], [new, wd_t, db_col])
    arrived, mirror = lax.optimization_barrier((arrived, mirror))
    new_rows, dist = call(
        finish_kernel,
        [((rows, n, chan), BF16), ((rows, bins, n), BF16)],
        [arrived, mirror, wd_t, db_col],
        scratch=[
            pltpu.VMEM((rows, n, chan), BF16),
            pltpu.VMEM((rows, bins, n), BF16),
            pltpu.SemaphoreType.DMA((2 + rows // 2,)),
        ],
        hbm_outs=True,
    )
    return new_rows, dist.transpose(0, 2, 1)


def solution(mesh):
    in_specs = (
        P(("dp", "row"), None, None),
        P("dp"),
        P("dp"),
        P(),
        P(None, "head", None),
        P(None, "head"),
        P(None, "head"),
        P("head", None, None),
        P(),
        P(),
    )
    out_specs = (P(("dp", "row"), None, None), P(("dp", "row"), None, None))
    return jax.shard_map(shards, mesh=mesh, in_specs=in_specs, out_specs=out_specs, check_vma=False)
```

```python
import functools

import jax
import jax.numpy as jnp
from jax import lax
from jax.experimental import pallas as pl
from jax.experimental.pallas import tpu as pltpu
from jax.sharding import PartitionSpec as P

LANES = 128
F32 = jnp.float32
BF16 = jnp.bfloat16
LOG2E = 1.4426950408889634


def dot_nt(a, b):
    return lax.dot_general(a, b, (((1,), (1,)), ((), ())), preferred_element_type=F32)


def dot_tn(a, b):
    return lax.dot_general(a, b, (((0,), (0,)), ((), ())), preferred_element_type=F32)


def dot_nn(a, b):
    return jnp.dot(a, b, preferred_element_type=F32)


def layer_norm(values, gain):
    center = jnp.mean(values, -1, keepdims=True)
    centered = values - center
    variance = jnp.mean(centered * centered, -1, keepdims=True)
    return (centered * lax.rsqrt(variance + 1e-05) * gain).astype(BF16)


def pack_kernel(x_hbm, gain_hbm, wb_hbm, out_hbm, x_ref, gain_ref, wb_ref, wide, out_ref, sems, out_sems):
    rows, n, chan = x_ref.shape
    peers = n // rows
    heads = wb_ref.shape[0]
    half = heads * rows // 2
    base = rows * rows
    fetch_gain = pltpu.make_async_copy(gain_hbm, gain_ref, sems.at[rows])
    fetch_wb = pltpu.make_async_copy(wb_hbm, wb_ref, sems.at[rows + 1])
    fetches = [pltpu.make_async_copy(x_hbm.at[k], x_ref.at[k], sems.at[k]) for k in range(rows)]
    for copy in (fetch_gain, fetch_wb, *fetches):
        copy.start()
    stores = []

    def store(first, count):
        at = pl.ds(first, count)
        copy = pltpu.make_async_copy(out_ref.at[:, at, :], out_hbm.at[:, at, :], out_sems.at[len(stores)])
        copy.start()
        stores.append(copy)

    owner = lax.broadcasted_iota(jnp.int32, (heads * rows, chan), 0) % rows
    bias = jnp.zeros((heads * rows, n), F32)
    fetch_gain.wait()
    fetch_wb.wait()
    gain = gain_ref[...]
    wb = wb_ref[...].astype(F32)
    wb = jnp.concatenate([jnp.broadcast_to(wb[h : h + 1], (rows, chan)) for h in range(heads)], 0)
    mine = [jnp.where(owner == k, wb, 0.0).astype(BF16) for k in range(rows)]
    mine = [jnp.concatenate(mine[k : k + 2], 1) for k in range(0, rows, 2)]
    for copy in fetches:
        copy.wait()
    normed = [layer_norm(x_ref[k].astype(F32), gain) for k in range(rows)]
    for k in range(rows):
        wide[:, pl.ds(k, rows, stride=rows), :] = x_ref[k].astype(F32).reshape(peers, rows, chan)
    out_ref[:, :base, :] = wide[...].astype(BF16)
    store(0, base)
    for pair in range(rows // 2):
        bias = bias + dot_nt(mine[pair], jnp.concatenate(normed[2 * pair : 2 * pair + 2], 1))
    bias = bias.astype(BF16)
    for t in range(n // LANES):
        block = bias[:, t * LANES : (t + 1) * LANES]
        for d in range(peers):
            part = block[(d % 2) * half : (d % 2 + 1) * half]
            out_ref[d, base + t * half : base + (t + 1) * half] = part
    store(base, (n // LANES) * half)
    for copy in stores:
        copy.wait()


def prepare_kernel(
    heads,
    chain_ref, mask_ref, cb_ref, w_ref, db_ref, gain_ref, wo_ref, wd_ref,
    term_ref, wt_ref, wk_out, dbc_ref, gain_out, wo_out, wd_out,
):
    gain_out[...] = gain_ref[...]
    chan = w_ref.shape[0]
    width = wo_ref.shape[0]
    half = heads // 2
    core = lax.axis_index("row") % 2
    w_out = wo_ref[...].astype(F32)
    other_first = jnp.concatenate([w_out[width // 2 :], w_out[: width // 2]], 0)
    w_out = jnp.where(core == 0, w_out, other_first).astype(BF16)
    wk_out[...] = jnp.zeros_like(wk_out)
    wo_out[...] = jnp.zeros_like(wo_out)
    for side in range(2):
        wo_out[side * width : (side + 1) * width, side * chan : (side + 1) * chan] = w_out
    wd_out[...] = wd_ref[...]
    n = chain_ref.shape[1]
    tiles = n // LANES
    dim = w_ref.shape[2] // 4

    def column_of(row):
        return jnp.transpose(jnp.broadcast_to(row, (LANES, LANES)))

    for kt in range(tiles):
        ks = slice(kt * LANES, (kt + 1) * LANES)
        chain_k = column_of(chain_ref[:, ks].astype(F32))
        mask_k = (column_of(mask_ref[:, ks].astype(F32)) - 1.0) * 1000000000.0
        for it in range(tiles):
            cs = slice(it * LANES, (it + 1) * LANES)
            same = chain_k == chain_ref[:, cs].astype(F32)
            for h in range(heads):
                inside, outside = [jnp.where(core == 0, cb_ref[r, h], cb_ref[r, (h + half) % heads]) for r in (1, 0)]
                term_ref[h, ks, cs] = (jnp.where(same, inside, outside) + mask_k) * LOG2E
    for h in range(heads):
        mine = jnp.where(core == 0, w_ref[:, h, :].astype(F32), w_ref[:, (h + half) % heads, :].astype(F32))
        turned = jnp.transpose(mine).astype(BF16)
        for place, kind in enumerate((0, 2, 3)):
            start = place * width + h * dim
            wt_ref[start : start + dim] = turned[kind * dim : (kind + 1) * dim]
        for side in range(2):
            start = side * width + h * dim
            wk_out[start : start + dim, side * chan : (side + 1) * chan] = turned[dim : 2 * dim]
    bins = dbc_ref.shape[0]
    db_rows = jnp.broadcast_to(jnp.concatenate([db_ref[...], db_ref[...]], 1)[:, :LANES], (LANES, LANES))
    dbc_ref[...] = jnp.transpose(db_rows)[:bins]


def unpack_bias(blocks, term_ref, first, bias_ref):
    half, n = bias_ref.shape[0], bias_ref.shape[1]
    rows = n // len(blocks)
    for s, block in enumerate(blocks):
        at = slice(s * rows, (s + 1) * rows)
        extra = block.astype(F32) * LOG2E
        for t in range(n // LANES):
            cs = slice(t * LANES, (t + 1) * LANES)
            for h in range(half):
                start = (t * half + h) * rows
                bias_ref[h, at, cs] = extra[start : start + rows] + term_ref[first + h, at, cs]


def soften(j, t, keys, spread, bias_ref, inv_s, e_s):
    scores = dot_nn(keys, spread)
    for h in range(bias_ref.shape[0]):
        cs = slice(h * LANES, (h + 1) * LANES)
        s = scores[:, cs] + bias_ref[h, :, t * LANES : (t + 1) * LANES]
        e = jnp.exp2(s - jnp.max(s, 0, keepdims=True))
        inv_s[j, t, h : h + 1] = 1.0 / jnp.sum(e, 0, keepdims=True)
        e_s[j, t, :, cs] = e.astype(BF16)


def combine(j, t, values, gates, inv_s, e_s, gated_ref):
    half = inv_s.shape[2]
    dim = values.shape[0] // half
    cs = slice(t * LANES, (t + 1) * LANES)
    o = dot_nn(values, e_s[j, t])
    for h in range(half):
        mine = slice(h * dim, (h + 1) * dim)
        part = o[mine, h * LANES : (h + 1) * LANES] * inv_s[j, t, h : h + 1]
        gated_ref[j, mine, cs] = (gates[mine, cs] * part).astype(BF16)


def for_each(count, tiles, body):
    if tiles == 1:
        for i in range(count):
            body(i)
    else:

        @pl.loop(0, count)
        def _(i):
            body(i)


def regrouped(left, right, rows):
    both = [block.astype(F32).reshape(rows, rows, LANES) for block in (left, right)]
    return jnp.concatenate(both, 1).reshape(2 * rows * rows, LANES)


def project_kernel(
    heads,
    recv_ref, gain_ref, w_ref, wk_ref, term_ref,
    x_s, spread_s, k_s, v_s, g_s, gated_ref,
    n_s, own_spread, own_v, own_g, bias_s, inv_s, e_s,
):
    peers = recv_ref.shape[0]
    rows, n, chan = x_s.shape
    tiles = n // LANES
    dim = w_ref.shape[0] // (3 * heads)
    width = heads * dim
    base = rows * rows
    gain = gain_ref[...]
    group = 2 * rows
    w_k = wk_ref[...]

    quads = range(peers // 4)
    x = [[regrouped(recv_ref[s, :base], recv_ref[s + 1, :base], rows) for s in (4 * q, 4 * q + 2)] for q in quads]
    normed = [[layer_norm(part, gain) for part in two] for two in x]
    keys = [dot_nt(jnp.concatenate(two, 1), w_k).astype(BF16) for two in normed]
    for quad in quads:
        for side in range(2):
            at = slice((2 * quad + side) * group, (2 * quad + side + 1) * group)
            x_s[:, at, :] = x[quad][side].astype(BF16).reshape(rows, group, chan)
            n_s[:, at, :] = normed[quad][side].reshape(rows, group, chan)
            k_s[:, at, :] = keys[quad][:, side * width : (side + 1) * width].reshape(rows, group, width)

    half, part = heads // 2, width // 2
    unpack_bias([recv_ref[s, base:] for s in range(peers)], term_ref, 0, bias_s)
    w_qvg = w_ref[...]
    zero = jnp.zeros((dim, LANES), BF16)
    scaling = dim ** (-0.5) * LOG2E

    def project(pair):
        both = dot_nt(w_qvg, n_s[pl.ds(2 * pair, 2)].reshape(2 * n, chan))
        both = jnp.concatenate([both[:width] * scaling, both[width:]], 0).astype(BF16)
        for side in range(2):
            j = 2 * pair + side
            qvg = both[:, side * n : (side + 1) * n]
            gate = jax.nn.sigmoid(qvg[2 * width :].astype(F32))
            own_v[j], v_s[j] = qvg[width : width + part], qvg[width + part : 2 * width]
            own_g[j], g_s[j] = gate[:part], gate[part:]
            for t in range(tiles):
                for h in range(heads):
                    target = (own_spread, spread_s)[h // half]
                    cs = slice(h % half * LANES, (h % half + 1) * LANES)
                    for other in range(half if h < half else heads):
                        block = qvg[h * dim : (h + 1) * dim, t * LANES : (t + 1) * LANES] if h == other else zero
                        target[j, t, other * dim : (other + 1) * dim, cs] = block

    for_each(rows // 2, tiles, project)
    for_each(rows, tiles, lambda j: [soften(j, t, k_s[j, :, :part], own_spread[j, t], bias_s, inv_s, e_s) for t in range(tiles)])
    for_each(rows, tiles, lambda j: [combine(j, t, own_v[j], own_g[j], inv_s, e_s, gated_ref) for t in range(tiles)])


def attend_kernel(
    fused,
    other_ref, term_ref, wo_ref, wd_ref, db_ref, x_s, spread_s, k_s, v_s, g_s, gated_ref,
    out_ref, *refs,
):
    if fused:
        second_ref, bias_s, inv_s, e_s, gated_s, new_s, wide = refs
    else:
        bias_s, inv_s, e_s, gated_s = refs
    peers = other_ref.shape[0]
    rows, n, chan = x_s.shape
    tiles = n // LANES
    half = bias_s.shape[0]
    w_out = wo_ref[...]

    unpack_bias([other_ref[s] for s in range(peers)], term_ref, half, bias_s)
    for_each(rows, tiles, lambda j: [soften(j, t, k_s[j], spread_s[j, t], bias_s, inv_s, e_s) for t in range(tiles)])
    for_each(rows, tiles, lambda j: [combine(j, t, v_s[j], g_s[j], inv_s, e_s, gated_s) for t in range(tiles)])

    def updated(pair):
        both = [ref[2 * pair + side] for side in range(2) for ref in (gated_ref, gated_s)]
        return dot_tn(jnp.concatenate(both, 0), w_out).astype(BF16)

    def store_update(pair):
        update = updated(pair)
        for side in range(2):
            out_ref[2 * pair + side] = update[:, side * chan : (side + 1) * chan]

    if not fused:
        for_each(rows // 2, tiles, store_update)
        return

    for j in range(0, rows, 2):
        update = updated(j // 2).astype(F32)
        for side in range(2):
            new = (x_s[j + side].astype(F32) + update[:, side * chan : (side + 1) * chan]).astype(BF16)
            new_s[j + side] = new
            wide[:, pl.ds(j + side, rows, stride=rows), :] = new.astype(F32).reshape(peers, rows, chan)
    out_ref[...] = wide[...].astype(BF16)
    logits_of(new_s, wd_ref[...], db_ref[:, :1], second_ref)


def logits_of(new_ref, w_dist, d_bias, out_ref):
    rows, n, chan = new_ref.shape
    logits = dot_nt(w_dist, new_ref[...].reshape(rows * n, chan)) + d_bias
    for j in range(rows):
        out_ref[j] = logits[:, j * n : (j + 1) * n].astype(BF16)


def finish_kernel(recv_ref, mirror_ref, wd_ref, db_ref, new_hbm, dist_hbm, new_ref, dist_ref, sems):
    peers, _, chan = recv_ref.shape
    rows = new_ref.shape[0]
    group = 2 * rows
    share = peers // 4
    copies = []
    for pair in range(peers // 2):
        at = slice(pair * group, (pair + 1) * group)
        block = regrouped(recv_ref[2 * pair], recv_ref[2 * pair + 1], rows)
        new_ref[:, at, :] = block.astype(BF16).reshape(rows, group, chan)
        if (pair + 1) % share == 0:
            at = pl.ds((pair + 1 - share) * group, share * group)
            copies.append(pltpu.make_async_copy(new_ref.at[:, at, :], new_hbm.at[:, at, :], sems.at[len(copies)]))
            copies[-1].start()
    logits_of(new_ref, wd_ref[...], db_ref[:, :1], dist_ref)
    for i in range(rows):
        dist_ref[i] = (dist_ref[i].astype(F32) + mirror_ref[i].astype(F32)).astype(BF16)
        if i % 2:
            at = pl.ds(i - 1, 2)
            copies.append(pltpu.make_async_copy(dist_ref.at[at], dist_hbm.at[at], sems.at[len(copies)]))
            copies[-1].start()
    for copy in copies:
        copy.wait()


def call(kernel, outs, args, scratch=(), smem=(), hbm=(), hbm_outs=False, limit=48):
    spaces = [pltpu.SMEM if i in smem else pl.ANY if i in hbm else pltpu.VMEM for i in range(len(args))]
    return pl.pallas_call(
        kernel,
        out_shape=[jax.ShapeDtypeStruct(s, d) for s, d in outs],
        in_specs=[pl.BlockSpec(memory_space=space) for space in spaces],
        out_specs=[pl.BlockSpec(memory_space=pl.ANY if hbm_outs else pltpu.VMEM)] * len(outs),
        scratch_shapes=list(scratch),
        compiler_params=pltpu.CompilerParams(vmem_limit_bytes=limit * 1024 * 1024),
    )(*args)


def swap_cores(values):
    peers = lax.axis_size("row")
    return lax.ppermute(values, "row", [(i, i ^ 1) for i in range(peers)])


def all_to_all(blocks):
    return lax.all_to_all(blocks, "row", split_axis=0, concat_axis=0, tiled=True)


def shards(
    pair_act, chain_id, residue_mask, norm_gain, w_proj, w_bias, chain_bias, w_out, w_dist, dist_bias,
):
    rows, n, chan = pair_act.shape
    peers = n // rows
    heads, dim = w_out.shape[0], w_out.shape[1]
    bins = w_dist.shape[1]
    tiles = n // LANES
    width = heads * dim
    fused = lax.axis_size("head") == 1
    gain = norm_gain[None, :]
    base = rows * rows
    length = base + tiles * heads * rows // 2

    (packed,) = call(
        pack_kernel,
        [((peers, length, chan), BF16)],
        [pair_act, gain, w_bias.T],
        scratch=[
            pltpu.VMEM(pair_act.shape, BF16),
            pltpu.VMEM(gain.shape, F32),
            pltpu.VMEM((heads, chan), BF16),
            pltpu.VMEM((peers, base, chan), F32),
            pltpu.VMEM((peers, length, chan), BF16),
            pltpu.SemaphoreType.DMA((rows + 2,)),
            pltpu.SemaphoreType.DMA((2,)),
        ],
        hbm=(0, 1, 2),
        hbm_outs=True,
        limit=60,
    )
    received = all_to_all(packed)
    prepared = call(
        functools.partial(prepare_kernel, heads),
        [
            ((heads, n, n), F32), ((3 * width, chan), BF16), ((2 * width, 2 * chan), BF16), ((bins, LANES), F32),
            ((1, chan), F32), ((2 * width, 2 * chan), BF16), ((bins, chan), BF16),
        ],
        [
            chain_id[None, :], residue_mask[None, :], chain_bias, w_proj, dist_bias[None, :],
            gain, w_out.reshape(width, chan), w_dist.T,
        ],
        smem=(2,),
    )
    received, *prepared = lax.optimization_barrier((received, *prepared))
    term, w_types, w_keys, db_col, gain, w_out, wd_t = prepared
    other_bias = swap_cores(received[:, base:])
    spread_shape = ((rows, tiles, width, heads // 2 * LANES), BF16)
    values_shape, gates_shape = ((rows, width // 2, n), BF16), ((rows, width // 2, n), F32)
    softmax_scratch = [
        pltpu.VMEM((heads // 2, n, n), F32),
        pltpu.VMEM((rows, tiles, heads // 2, LANES), F32),
        pltpu.VMEM((rows, tiles, n, heads // 2 * LANES), BF16),
    ]
    x_cols, spread, keys, values, gates, gated = call(
        functools.partial(project_kernel, heads),
        [
            ((rows, n, chan), BF16),
            spread_shape,
            ((rows, n, width), BF16),
            values_shape,
            gates_shape,
            values_shape,
        ],
        [received, gain, w_types, w_keys, term],
        scratch=[
            pltpu.VMEM((rows, n, chan), BF16),
            pltpu.VMEM((rows, tiles, width // 2, heads // 2 * LANES), BF16),
            *(pltpu.VMEM(*shape) for shape in (values_shape, gates_shape)),
            *softmax_scratch,
        ],
    )
    if fused:
        outs = [((peers, base, chan), BF16), ((rows, bins, n), BF16)]
    else:
        outs = [((rows, n, chan), BF16)]
    result = call(
        functools.partial(attend_kernel, fused),
        outs,
        [other_bias, term, w_out, wd_t, db_col, x_cols, spread, keys, values, gates, gated],
        scratch=softmax_scratch + [pltpu.VMEM(*values_shape)] + [pltpu.VMEM((rows, n, chan), BF16), pltpu.VMEM((peers, base, chan), F32)] * fused,
    )
    if fused:
        to_rows, mirror = result
    else:
        update = lax.psum(result[0], "head").astype(F32)
        new = (x_cols.astype(F32) + update).astype(BF16)
        logits = jnp.einsum("cb,jic->jbi", w_dist, new, preferred_element_type=F32)
        mirror = (logits + dist_bias[None, :, None]).astype(BF16)
        to_rows = new.reshape(rows, peers, rows, chan).transpose(1, 2, 0, 3).reshape(peers, base, chan)
    arrived = all_to_all(to_rows)
    new_rows, dist = call(
        finish_kernel,
        [((rows, n, chan), BF16), ((rows, bins, n), BF16)],
        [arrived, mirror, wd_t, db_col],
        scratch=[
            pltpu.VMEM((rows, n, chan), BF16),
            pltpu.VMEM((rows, bins, n), BF16),
            pltpu.SemaphoreType.DMA((2 + rows // 2,)),
        ],
        hbm_outs=True,
    )
    return new_rows, dist.transpose(0, 2, 1)


def solution(mesh):
    in_specs = (
        P(("dp", "row"), None, None),
        P("dp"),
        P("dp"),
        P(),
        P(None, "head", None),
        P(None, "head"),
        P(None, "head"),
        P("head", None, None),
        P(),
        P(),
    )
    out_specs = (P(("dp", "row"), None, None), P(("dp", "row"), None, None))
    return jax.shard_map(shards, mesh=mesh, in_specs=in_specs, out_specs=out_specs, check_vma=False)
```

```python
import functools

import jax
import jax.numpy as jnp
from jax import lax
from jax.experimental import pallas as pl
from jax.experimental.pallas import tpu as pltpu
from jax.sharding import PartitionSpec as P

LANES = 128
F32 = jnp.float32
BF16 = jnp.bfloat16
LOG2E = 1.4426950408889634


def dot_nt(a, b):
    return lax.dot_general(a, b, (((1,), (1,)), ((), ())), preferred_element_type=F32)


def dot_tn(a, b):
    return lax.dot_general(a, b, (((0,), (0,)), ((), ())), preferred_element_type=F32)


def dot_nn(a, b):
    return jnp.dot(a, b, preferred_element_type=F32)


def layer_norm(values, gain):
    center = jnp.mean(values, -1, keepdims=True)
    centered = values - center
    variance = jnp.mean(centered * centered, -1, keepdims=True)
    return (centered * lax.rsqrt(variance + 1e-05) * gain).astype(BF16)


def pack_kernel(x_hbm, gain_hbm, wb_hbm, out_hbm, x_ref, gain_ref, wb_ref, wide, out_ref, sems, out_sems):
    rows, n, chan = x_ref.shape
    peers = n // rows
    heads = wb_ref.shape[0]
    half = heads * rows // 2
    base = rows * rows
    fetch_gain = pltpu.make_async_copy(gain_hbm, gain_ref, sems.at[rows])
    fetch_wb = pltpu.make_async_copy(wb_hbm, wb_ref, sems.at[rows + 1])
    fetches = [pltpu.make_async_copy(x_hbm.at[k], x_ref.at[k], sems.at[k]) for k in range(rows)]
    for copy in (fetch_gain, fetch_wb, *fetches):
        copy.start()
    stores = []

    def store(first, count):
        at = pl.ds(first, count)
        copy = pltpu.make_async_copy(out_ref.at[:, at, :], out_hbm.at[:, at, :], out_sems.at[len(stores)])
        copy.start()
        stores.append(copy)

    owner = lax.broadcasted_iota(jnp.int32, (heads * rows, chan), 0) % rows
    bias = jnp.zeros((heads * rows, n), F32)
    fetch_gain.wait()
    fetch_wb.wait()
    gain = gain_ref[...]
    wb = wb_ref[...].astype(F32)
    wb = jnp.concatenate([jnp.broadcast_to(wb[h : h + 1], (rows, chan)) for h in range(heads)], 0)
    mine = [jnp.where(owner == k, wb, 0.0).astype(BF16) for k in range(rows)]
    mine = [jnp.concatenate(mine[k : k + 2], 1) for k in range(0, rows, 2)]
    for copy in fetches:
        copy.wait()
    normed = [layer_norm(x_ref[k].astype(F32), gain) for k in range(rows)]
    for k in range(rows):
        wide[:, pl.ds(k, rows, stride=rows), :] = x_ref[k].astype(F32).reshape(peers, rows, chan)
    out_ref[:, :base, :] = wide[...].astype(BF16)
    store(0, base)
    for pair in range(rows // 2):
        bias = bias + dot_nt(mine[pair], jnp.concatenate(normed[2 * pair : 2 * pair + 2], 1))
    bias = bias.astype(BF16)
    for t in range(n // LANES):
        block = bias[:, t * LANES : (t + 1) * LANES]
        for d in range(peers):
            part = block[(d % 2) * half : (d % 2 + 1) * half]
            out_ref[d, base + t * half : base + (t + 1) * half] = part
    store(base, (n // LANES) * half)
    for copy in stores:
        copy.wait()


def prepare_kernel(
    heads,
    chain_ref, mask_ref, cb_ref, w_ref, db_ref, gain_ref, wo_ref, wd_ref,
    term_ref, wt_ref, wk_out, dbc_ref, gain_out, wo_out, wd_out,
):
    gain_out[...] = gain_ref[...]
    chan = w_ref.shape[0]
    width = wo_ref.shape[0]
    half = heads // 2
    core = lax.axis_index("row") % 2
    w_out = wo_ref[...].astype(F32)
    other_first = jnp.concatenate([w_out[width // 2 :], w_out[: width // 2]], 0)
    w_out = jnp.where(core == 0, w_out, other_first).astype(BF16)
    wk_out[...] = jnp.zeros_like(wk_out)
    wo_out[...] = jnp.zeros_like(wo_out)
    for side in range(2):
        wo_out[side * width : (side + 1) * width, side * chan : (side + 1) * chan] = w_out
    wd_out[...] = wd_ref[...]
    n = chain_ref.shape[1]
    tiles = n // LANES
    dim = w_ref.shape[2] // 4

    def column_of(row):
        return jnp.transpose(jnp.broadcast_to(row, (LANES, LANES)))

    for kt in range(tiles):
        ks = slice(kt * LANES, (kt + 1) * LANES)
        chain_k = column_of(chain_ref[:, ks].astype(F32))
        mask_k = (column_of(mask_ref[:, ks].astype(F32)) - 1.0) * 1000000000.0
        for it in range(tiles):
            cs = slice(it * LANES, (it + 1) * LANES)
            same = chain_k == chain_ref[:, cs].astype(F32)
            for h in range(heads):
                inside, outside = [jnp.where(core == 0, cb_ref[r, h], cb_ref[r, (h + half) % heads]) for r in (1, 0)]
                term_ref[h, ks, cs] = (jnp.where(same, inside, outside) + mask_k) * LOG2E
    for h in range(heads):
        mine = jnp.where(core == 0, w_ref[:, h, :].astype(F32), w_ref[:, (h + half) % heads, :].astype(F32))
        turned = jnp.transpose(mine).astype(BF16)
        for place, kind in enumerate((0, 2, 3)):
            start = place * width + h * dim
            wt_ref[start : start + dim] = turned[kind * dim : (kind + 1) * dim]
        for side in range(2):
            start = side * width + h * dim
            wk_out[start : start + dim, side * chan : (side + 1) * chan] = turned[dim : 2 * dim]
    bins = dbc_ref.shape[0]
    db_rows = jnp.broadcast_to(jnp.concatenate([db_ref[...], db_ref[...]], 1)[:, :LANES], (LANES, LANES))
    dbc_ref[...] = jnp.transpose(db_rows)[:bins]


def unpack_bias(blocks, term_ref, first, bias_ref):
    half, n = bias_ref.shape[0], bias_ref.shape[1]
    rows = n // len(blocks)
    for s, block in enumerate(blocks):
        at = slice(s * rows, (s + 1) * rows)
        extra = block.astype(F32) * LOG2E
        for t in range(n // LANES):
            cs = slice(t * LANES, (t + 1) * LANES)
            for h in range(half):
                start = (t * half + h) * rows
                bias_ref[h, at, cs] = extra[start : start + rows] + term_ref[first + h, at, cs]


def soften(j, t, keys, spread, bias_ref, scaling, inv_s, e_s):
    scores = dot_nn(keys, spread)
    for h in range(bias_ref.shape[0]):
        cs = slice(h * LANES, (h + 1) * LANES)
        s = scores[:, cs] * scaling + bias_ref[h, :, t * LANES : (t + 1) * LANES]
        e = jnp.exp2(s - jnp.max(s, 0, keepdims=True))
        inv_s[j, t, h : h + 1] = 1.0 / jnp.sum(e, 0, keepdims=True)
        e_s[j, t, :, cs] = e.astype(BF16)


def combine(j, t, values, gates, inv_s, e_s, gated_ref):
    half = inv_s.shape[2]
    dim = values.shape[0] // half
    cs = slice(t * LANES, (t + 1) * LANES)
    o = dot_nn(values, e_s[j, t])
    for h in range(half):
        mine = slice(h * dim, (h + 1) * dim)
        part = o[mine, h * LANES : (h + 1) * LANES] * inv_s[j, t, h : h + 1]
        gated_ref[j, mine, cs] = (gates[mine, cs] * part).astype(BF16)


def for_each(count, tiles, body):
    if tiles == 1:
        for i in range(count):
            body(i)
    else:

        @pl.loop(0, count)
        def _(i):
            body(i)


def regrouped(left, right, rows):
    both = [block.astype(F32).reshape(rows, rows, LANES) for block in (left, right)]
    return jnp.concatenate(both, 1).reshape(2 * rows * rows, LANES)


def project_kernel(
    heads,
    recv_ref, gain_ref, w_ref, wk_ref, term_ref,
    x_s, spread_s, k_s, v_s, g_s, gated_ref,
    n_s, own_spread, own_v, own_g, bias_s, inv_s, e_s,
):
    peers = recv_ref.shape[0]
    rows, n, chan = x_s.shape
    tiles = n // LANES
    dim = w_ref.shape[0] // (3 * heads)
    width = heads * dim
    base = rows * rows
    gain = gain_ref[...]
    group = 2 * rows
    w_k = wk_ref[...]

    quads = range(peers // 4)
    x = [[regrouped(recv_ref[s, :base], recv_ref[s + 1, :base], rows) for s in (4 * q, 4 * q + 2)] for q in quads]
    normed = [[layer_norm(part, gain) for part in two] for two in x]
    keys = [dot_nt(jnp.concatenate(two, 1), w_k).astype(BF16) for two in normed]
    for quad in quads:
        for side in range(2):
            at = slice((2 * quad + side) * group, (2 * quad + side + 1) * group)
            x_s[:, at, :] = x[quad][side].astype(BF16).reshape(rows, group, chan)
            n_s[:, at, :] = normed[quad][side].reshape(rows, group, chan)
            k_s[:, at, :] = keys[quad][:, side * width : (side + 1) * width].reshape(rows, group, width)

    half, part = heads // 2, width // 2
    unpack_bias([recv_ref[s, base:] for s in range(peers)], term_ref, 0, bias_s)
    w_qvg = w_ref[...]
    zero = jnp.zeros((dim, LANES), BF16)

    def product(pair):
        return dot_nt(w_qvg, n_s[pl.ds(2 * pair, 2)].reshape(2 * n, chan)).astype(BF16)

    def spread_out(pair, both):
        for side in range(2):
            j = 2 * pair + side
            qvg = both[:, side * n : (side + 1) * n]
            gate = jax.nn.sigmoid(qvg[2 * width :].astype(F32))
            own_v[j], v_s[j] = qvg[width : width + part], qvg[width + part : 2 * width]
            own_g[j], g_s[j] = gate[:part], gate[part:]
            for t in range(tiles):
                for h in range(heads):
                    target = (own_spread, spread_s)[h // half]
                    cs = slice(h % half * LANES, (h % half + 1) * LANES)
                    for other in range(heads):
                        block = qvg[h * dim : (h + 1) * dim, t * LANES : (t + 1) * LANES] if h == other else zero
                        target[j, t, other * dim : (other + 1) * dim, cs] = block

    scaling = dim ** (-0.5) * LOG2E
    if tiles == 1:
        products = [product(pair) for pair in range(rows // 2)]
        for pair in range(rows // 2):
            spread_out(pair, products[pair])
    else:
        pl.loop(0, rows // 2)(lambda pair: spread_out(pair, product(pair)))
    for_each(rows, tiles, lambda j: [soften(j, t, k_s[j], own_spread[j, t], bias_s, scaling, inv_s, e_s) for t in range(tiles)])
    for_each(rows, tiles, lambda j: [combine(j, t, own_v[j], own_g[j], inv_s, e_s, gated_ref) for t in range(tiles)])


def attend_kernel(
    fused,
    other_ref, term_ref, wo_ref, wd_ref, db_ref, x_s, spread_s, k_s, v_s, g_s, gated_ref,
    out_ref, *refs,
):
    if fused:
        second_ref, bias_s, inv_s, e_s, gated_s, new_s, wide = refs
    else:
        bias_s, inv_s, e_s, gated_s = refs
    peers = other_ref.shape[0]
    rows, n, chan = x_s.shape
    tiles = n // LANES
    half, part = bias_s.shape[0], v_s.shape[1]
    scaling = (part // half) ** (-0.5) * LOG2E
    w_out = wo_ref[...]

    unpack_bias([other_ref[s] for s in range(peers)], term_ref, half, bias_s)
    for_each(rows, tiles, lambda j: [soften(j, t, k_s[j], spread_s[j, t], bias_s, scaling, inv_s, e_s) for t in range(tiles)])
    for_each(rows, tiles, lambda j: [combine(j, t, v_s[j], g_s[j], inv_s, e_s, gated_s) for t in range(tiles)])

    def updated(pair):
        both = [ref[2 * pair + side] for side in range(2) for ref in (gated_ref, gated_s)]
        return dot_tn(jnp.concatenate(both, 0), w_out).astype(BF16)

    def store_update(pair):
        update = updated(pair)
        for side in range(2):
            out_ref[2 * pair + side] = update[:, side * chan : (side + 1) * chan]

    if not fused:
        for_each(rows // 2, tiles, store_update)
        return

    updates = [updated(pair) for pair in range(rows // 2)]
    for j in range(0, rows, 2):
        update = updates[j // 2].astype(F32)
        for side in range(2):
            new = (x_s[j + side].astype(F32) + update[:, side * chan : (side + 1) * chan]).astype(BF16)
            new_s[j + side] = new
            wide[:, pl.ds(j + side, rows, stride=rows), :] = new.astype(F32).reshape(peers, rows, chan)
    out_ref[...] = wide[...].astype(BF16)
    logits_of(new_s, wd_ref[...], db_ref[:, :1], second_ref)


def logits_of(new_ref, w_dist, d_bias, out_ref):
    rows, n, chan = new_ref.shape
    logits = dot_nt(w_dist, new_ref[...].reshape(rows * n, chan)) + d_bias
    for j in range(rows):
        out_ref[j] = logits[:, j * n : (j + 1) * n].astype(BF16)


def finish_kernel(recv_ref, mirror_ref, wd_ref, db_ref, new_hbm, dist_hbm, new_ref, dist_ref, sems):
    peers, _, chan = recv_ref.shape
    rows = new_ref.shape[0]
    group = 2 * rows
    share = peers // 4
    copies = []
    for pair in range(peers // 2):
        at = slice(pair * group, (pair + 1) * group)
        block = regrouped(recv_ref[2 * pair], recv_ref[2 * pair + 1], rows)
        new_ref[:, at, :] = block.astype(BF16).reshape(rows, group, chan)
        if (pair + 1) % share == 0:
            at = pl.ds((pair + 1 - share) * group, share * group)
            copies.append(pltpu.make_async_copy(new_ref.at[:, at, :], new_hbm.at[:, at, :], sems.at[len(copies)]))
            copies[-1].start()
    logits_of(new_ref, wd_ref[...], db_ref[:, :1], dist_ref)
    for i in range(rows):
        dist_ref[i] = (dist_ref[i].astype(F32) + mirror_ref[i].astype(F32)).astype(BF16)
        if i % 2:
            at = pl.ds(i - 1, 2)
            copies.append(pltpu.make_async_copy(dist_ref.at[at], dist_hbm.at[at], sems.at[len(copies)]))
            copies[-1].start()
    for copy in copies:
        copy.wait()


def call(kernel, outs, args, scratch=(), smem=(), hbm=(), hbm_outs=False, limit=48):
    spaces = [pltpu.SMEM if i in smem else pl.ANY if i in hbm else pltpu.VMEM for i in range(len(args))]
    return pl.pallas_call(
        kernel,
        out_shape=[jax.ShapeDtypeStruct(s, d) for s, d in outs],
        in_specs=[pl.BlockSpec(memory_space=space) for space in spaces],
        out_specs=[pl.BlockSpec(memory_space=pl.ANY if hbm_outs else pltpu.VMEM)] * len(outs),
        scratch_shapes=list(scratch),
        compiler_params=pltpu.CompilerParams(vmem_limit_bytes=limit * 1024 * 1024),
    )(*args)


def swap_cores(values):
    peers = lax.axis_size("row")
    return lax.ppermute(values, "row", [(i, i ^ 1) for i in range(peers)])


def all_to_all(blocks):
    return lax.all_to_all(blocks, "row", split_axis=0, concat_axis=0, tiled=True)


def shards(
    pair_act, chain_id, residue_mask, norm_gain, w_proj, w_bias, chain_bias, w_out, w_dist, dist_bias,
):
    rows, n, chan = pair_act.shape
    peers = n // rows
    heads, dim = w_out.shape[0], w_out.shape[1]
    bins = w_dist.shape[1]
    tiles = n // LANES
    width = heads * dim
    fused = lax.axis_size("head") == 1
    gain = norm_gain[None, :]
    base = rows * rows
    length = base + tiles * heads * rows // 2

    (packed,) = call(
        pack_kernel,
        [((peers, length, chan), BF16)],
        [pair_act, gain, w_bias.T],
        scratch=[
            pltpu.VMEM(pair_act.shape, BF16),
            pltpu.VMEM(gain.shape, F32),
            pltpu.VMEM((heads, chan), BF16),
            pltpu.VMEM((peers, base, chan), F32),
            pltpu.VMEM((peers, length, chan), BF16),
            pltpu.SemaphoreType.DMA((rows + 2,)),
            pltpu.SemaphoreType.DMA((2,)),
        ],
        hbm=(0, 1, 2),
        hbm_outs=True,
        limit=60,
    )
    received = all_to_all(packed)
    prepared = call(
        functools.partial(prepare_kernel, heads),
        [
            ((heads, n, n), F32), ((3 * width, chan), BF16), ((2 * width, 2 * chan), BF16), ((bins, LANES), F32),
            ((1, chan), F32), ((2 * width, 2 * chan), BF16), ((bins, chan), BF16),
        ],
        [
            chain_id[None, :], residue_mask[None, :], chain_bias, w_proj, dist_bias[None, :],
            gain, w_out.reshape(width, chan), w_dist.T,
        ],
        smem=(2,),
    )
    received, *prepared = lax.optimization_barrier((received, *prepared))
    term, w_types, w_keys, db_col, gain, w_out, wd_t = prepared
    other_bias = swap_cores(received[:, base:])
    spread_shape = ((rows, tiles, width, heads // 2 * LANES), BF16)
    values_shape, gates_shape = ((rows, width // 2, n), BF16), ((rows, width // 2, n), F32)
    softmax_scratch = [
        pltpu.VMEM((heads // 2, n, n), F32),
        pltpu.VMEM((rows, tiles, heads // 2, LANES), F32),
        pltpu.VMEM((rows, tiles, n, heads // 2 * LANES), BF16),
    ]
    x_cols, spread, keys, values, gates, gated = call(
        functools.partial(project_kernel, heads),
        [
            ((rows, n, chan), BF16),
            spread_shape,
            ((rows, n, width), BF16),
            values_shape,
            gates_shape,
            values_shape,
        ],
        [received, gain, w_types, w_keys, term],
        scratch=[
            pltpu.VMEM((rows, n, chan), BF16),
            *(pltpu.VMEM(*shape) for shape in (spread_shape, values_shape, gates_shape)),
            *softmax_scratch,
        ],
    )
    if fused:
        outs = [((peers, base, chan), BF16), ((rows, bins, n), BF16)]
    else:
        outs = [((rows, n, chan), BF16)]
    result = call(
        functools.partial(attend_kernel, fused),
        outs,
        [other_bias, term, w_out, wd_t, db_col, x_cols, spread, keys, values, gates, gated],
        scratch=softmax_scratch + [pltpu.VMEM(*values_shape)] + [pltpu.VMEM((rows, n, chan), BF16), pltpu.VMEM((peers, base, chan), F32)] * fused,
    )
    if fused:
        to_rows, mirror = result
    else:
        update = lax.psum(result[0], "head").astype(F32)
        new = (x_cols.astype(F32) + update).astype(BF16)
        logits = jnp.einsum("cb,jic->jbi", w_dist, new, preferred_element_type=F32)
        mirror = (logits + dist_bias[None, :, None]).astype(BF16)
        to_rows = new.reshape(rows, peers, rows, chan).transpose(1, 2, 0, 3).reshape(peers, base, chan)
    arrived = all_to_all(to_rows)
    new_rows, dist = call(
        finish_kernel,
        [((rows, n, chan), BF16), ((rows, bins, n), BF16)],
        [arrived, mirror, wd_t, db_col],
        scratch=[
            pltpu.VMEM((rows, n, chan), BF16),
            pltpu.VMEM((rows, bins, n), BF16),
            pltpu.SemaphoreType.DMA((2 + rows // 2,)),
        ],
        hbm_outs=True,
    )
    return new_rows, dist.transpose(0, 2, 1)


def solution(mesh):
    in_specs = (
        P(("dp", "row"), None, None),
        P("dp"),
        P("dp"),
        P(),
        P(None, "head", None),
        P(None, "head"),
        P(None, "head"),
        P("head", None, None),
        P(),
        P(),
    )
    out_specs = (P(("dp", "row"), None, None), P(("dp", "row"), None, None))
    return jax.shard_map(shards, mesh=mesh, in_specs=in_specs, out_specs=out_specs, check_vma=False)
```

```python
import functools

import jax
import jax.numpy as jnp
from jax import lax
from jax.experimental import pallas as pl
from jax.experimental.pallas import tpu as pltpu
from jax.sharding import PartitionSpec as P

LANES = 128
F32 = jnp.float32
BF16 = jnp.bfloat16
LOG2E = 1.4426950408889634


def dot_nt(a, b):
    return lax.dot_general(a, b, (((1,), (1,)), ((), ())), preferred_element_type=F32)


def dot_tn(a, b):
    return lax.dot_general(a, b, (((0,), (0,)), ((), ())), preferred_element_type=F32)


def dot_nn(a, b):
    return jnp.dot(a, b, preferred_element_type=F32)


def layer_norm(values, gain):
    center = jnp.mean(values, -1, keepdims=True)
    centered = values - center
    variance = jnp.mean(centered * centered, -1, keepdims=True)
    return (centered * lax.rsqrt(variance + 1e-05) * gain).astype(BF16)


def pack_kernel(x_hbm, gain_hbm, wb_hbm, out_hbm, x_ref, gain_ref, wb_ref, wide, out_ref, sems, out_sems):
    rows, n, chan = x_ref.shape
    peers = n // rows
    heads = wb_ref.shape[0]
    half = heads * rows // 2
    base = rows * rows
    fetch_gain = pltpu.make_async_copy(gain_hbm, gain_ref, sems.at[rows])
    fetch_wb = pltpu.make_async_copy(wb_hbm, wb_ref, sems.at[rows + 1])
    fetches = [pltpu.make_async_copy(x_hbm.at[k], x_ref.at[k], sems.at[k]) for k in range(rows)]
    for copy in (fetch_gain, fetch_wb, *fetches):
        copy.start()
    stores = []

    def store(first, count):
        at = pl.ds(first, count)
        copy = pltpu.make_async_copy(out_ref.at[:, at, :], out_hbm.at[:, at, :], out_sems.at[len(stores)])
        copy.start()
        stores.append(copy)

    owner = lax.broadcasted_iota(jnp.int32, (heads * rows, chan), 0) % rows
    bias = jnp.zeros((heads * rows, n), F32)
    fetch_gain.wait()
    fetch_wb.wait()
    gain = gain_ref[...]
    wb = wb_ref[...].astype(F32)
    wb = jnp.concatenate([jnp.broadcast_to(wb[h : h + 1], (rows, chan)) for h in range(heads)], 0)
    mine = [jnp.where(owner == k, wb, 0.0).astype(BF16) for k in range(rows)]
    mine = [jnp.concatenate(mine[k : k + 2], 1) for k in range(0, rows, 2)]
    for copy in fetches:
        copy.wait()
    normed = [layer_norm(x_ref[k].astype(F32), gain) for k in range(rows)]
    for k in range(rows):
        wide[:, pl.ds(k, rows, stride=rows), :] = x_ref[k].astype(F32).reshape(peers, rows, chan)
    out_ref[:, :base, :] = wide[...].astype(BF16)
    store(0, base)
    for pair in range(rows // 2):
        bias = bias + dot_nt(mine[pair], jnp.concatenate(normed[2 * pair : 2 * pair + 2], 1))
    bias = bias.astype(BF16)
    for t in range(n // LANES):
        block = bias[:, t * LANES : (t + 1) * LANES]
        for d in range(peers):
            part = block[(d % 2) * half : (d % 2 + 1) * half]
            out_ref[d, base + t * half : base + (t + 1) * half] = part
    store(base, (n // LANES) * half)
    for copy in stores:
        copy.wait()


def prepare_kernel(
    heads,
    chain_ref, mask_ref, cb_ref, w_ref, db_ref, gain_ref, wo_ref, wd_ref,
    term_ref, wt_ref, wk_out, dbc_ref, gain_out, wo_out, wd_out,
):
    gain_out[...] = gain_ref[...]
    chan = w_ref.shape[0]
    width = wo_ref.shape[0]
    half = heads // 2
    core = lax.axis_index("row") % 2
    w_out = wo_ref[...].astype(F32)
    other_first = jnp.concatenate([w_out[width // 2 :], w_out[: width // 2]], 0)
    w_out = jnp.where(core == 0, w_out, other_first).astype(BF16)
    wk_out[...] = jnp.zeros_like(wk_out)
    wo_out[...] = jnp.zeros_like(wo_out)
    for side in range(2):
        wo_out[side * width : (side + 1) * width, side * chan : (side + 1) * chan] = w_out
    wd_out[...] = wd_ref[...]
    n = chain_ref.shape[1]
    tiles = n // LANES
    dim = w_ref.shape[2] // 4

    def column_of(row):
        return jnp.transpose(jnp.broadcast_to(row, (LANES, LANES)))

    for kt in range(tiles):
        ks = slice(kt * LANES, (kt + 1) * LANES)
        chain_k = column_of(chain_ref[:, ks].astype(F32))
        mask_k = (column_of(mask_ref[:, ks].astype(F32)) - 1.0) * 1000000000.0
        for it in range(tiles):
            cs = slice(it * LANES, (it + 1) * LANES)
            same = chain_k == chain_ref[:, cs].astype(F32)
            for h in range(heads):
                inside, outside = [jnp.where(core == 0, cb_ref[r, h], cb_ref[r, (h + half) % heads]) for r in (1, 0)]
                term_ref[h, ks, cs] = (jnp.where(same, inside, outside) + mask_k) * LOG2E
    for h in range(heads):
        mine = jnp.where(core == 0, w_ref[:, h, :].astype(F32), w_ref[:, (h + half) % heads, :].astype(F32))
        turned = jnp.transpose(mine).astype(BF16)
        for place, kind in enumerate((0, 2, 3)):
            start = place * width + h * dim
            wt_ref[start : start + dim] = turned[kind * dim : (kind + 1) * dim]
        for side in range(2):
            start = side * width + h * dim
            wk_out[start : start + dim, side * chan : (side + 1) * chan] = turned[dim : 2 * dim]
    bins = dbc_ref.shape[0]
    db_rows = jnp.broadcast_to(jnp.concatenate([db_ref[...], db_ref[...]], 1)[:, :LANES], (LANES, LANES))
    dbc_ref[...] = jnp.transpose(db_rows)[:bins]


def unpack_bias(blocks, term_ref, first, bias_ref):
    half, n = bias_ref.shape[0], bias_ref.shape[1]
    rows = n // len(blocks)
    for s, block in enumerate(blocks):
        at = slice(s * rows, (s + 1) * rows)
        extra = block.astype(F32) * LOG2E
        for t in range(n // LANES):
            cs = slice(t * LANES, (t + 1) * LANES)
            for h in range(half):
                start = (t * half + h) * rows
                bias_ref[h, at, cs] = extra[start : start + rows] + term_ref[first + h, at, cs]


def soften(j, t, keys, spread, bias_ref, scaling, inv_s, e_s):
    scores = dot_nn(keys, spread)
    for h in range(bias_ref.shape[0]):
        cs = slice(h * LANES, (h + 1) * LANES)
        s = scores[:, cs] * scaling + bias_ref[h, :, t * LANES : (t + 1) * LANES]
        e = jnp.exp2(s - jnp.max(s, 0, keepdims=True))
        inv_s[j, t, h : h + 1] = 1.0 / jnp.sum(e, 0, keepdims=True)
        e_s[j, t, :, cs] = e.astype(BF16)


def combine(j, t, values, gates, inv_s, e_s, gated_ref):
    half = inv_s.shape[2]
    dim = values.shape[0] // half
    cs = slice(t * LANES, (t + 1) * LANES)
    o = dot_nn(values, e_s[j, t])
    for h in range(half):
        mine = slice(h * dim, (h + 1) * dim)
        part = o[mine, h * LANES : (h + 1) * LANES] * inv_s[j, t, h : h + 1]
        gated_ref[j, mine, cs] = (gates[mine, cs] * part).astype(BF16)


def for_each(count, tiles, body):
    if tiles == 1:
        for i in range(count):
            body(i)
    else:

        @pl.loop(0, count)
        def _(i):
            body(i)


def regrouped(left, right, rows):
    both = [block.astype(F32).reshape(rows, rows, LANES) for block in (left, right)]
    return jnp.concatenate(both, 1).reshape(2 * rows * rows, LANES)


def project_kernel(
    heads,
    recv_ref, gain_ref, w_ref, wk_ref, term_ref,
    x_s, spread_s, k_s, v_s, g_s, gated_ref,
    n_s, own_spread, own_v, own_g, bias_s, inv_s, e_s,
):
    peers = recv_ref.shape[0]
    rows, n, chan = x_s.shape
    tiles = n // LANES
    dim = w_ref.shape[0] // (3 * heads)
    width = heads * dim
    base = rows * rows
    gain = gain_ref[...]
    group = 2 * rows
    w_k = wk_ref[...]

    quads = range(peers // 4)
    x = [[regrouped(recv_ref[s, :base], recv_ref[s + 1, :base], rows) for s in (4 * q, 4 * q + 2)] for q in quads]
    normed = [[layer_norm(part, gain) for part in two] for two in x]
    keys = [dot_nt(jnp.concatenate(two, 1), w_k).astype(BF16) for two in normed]
    for quad in quads:
        for side in range(2):
            at = slice((2 * quad + side) * group, (2 * quad + side + 1) * group)
            x_s[:, at, :] = x[quad][side].astype(BF16).reshape(rows, group, chan)
            n_s[:, at, :] = normed[quad][side].reshape(rows, group, chan)
            k_s[:, at, :] = keys[quad][:, side * width : (side + 1) * width].reshape(rows, group, width)

    half, part = heads // 2, width // 2
    unpack_bias([recv_ref[s, base:] for s in range(peers)], term_ref, 0, bias_s)
    w_qvg = w_ref[...]
    zero = jnp.zeros((dim, LANES), BF16)

    def project(pair):
        both = dot_nt(w_qvg, n_s[pl.ds(2 * pair, 2)].reshape(2 * n, chan)).astype(BF16)
        for side in range(2):
            j = 2 * pair + side
            qvg = both[:, side * n : (side + 1) * n]
            gate = jax.nn.sigmoid(qvg[2 * width :].astype(F32))
            own_v[j], v_s[j] = qvg[width : width + part], qvg[width + part : 2 * width]
            own_g[j], g_s[j] = gate[:part], gate[part:]
            for t in range(tiles):
                for h in range(heads):
                    target = (own_spread, spread_s)[h // half]
                    cs = slice(h % half * LANES, (h % half + 1) * LANES)
                    for other in range(heads):
                        block = qvg[h * dim : (h + 1) * dim, t * LANES : (t + 1) * LANES] if h == other else zero
                        target[j, t, other * dim : (other + 1) * dim, cs] = block

    scaling = dim ** (-0.5) * LOG2E
    for_each(rows // 2, tiles, project)
    for_each(rows, tiles, lambda j: [soften(j, t, k_s[j], own_spread[j, t], bias_s, scaling, inv_s, e_s) for t in range(tiles)])
    for_each(rows, tiles, lambda j: [combine(j, t, own_v[j], own_g[j], inv_s, e_s, gated_ref) for t in range(tiles)])


def attend_kernel(
    fused,
    other_ref, term_ref, wo_ref, wd_ref, db_ref, x_s, spread_s, k_s, v_s, g_s, gated_ref,
    out_ref, *refs,
):
    if fused:
        second_ref, bias_s, inv_s, e_s, gated_s, new_s, wide = refs
    else:
        bias_s, inv_s, e_s, gated_s = refs
    peers = other_ref.shape[0]
    rows, n, chan = x_s.shape
    tiles = n // LANES
    half, part = bias_s.shape[0], v_s.shape[1]
    scaling = (part // half) ** (-0.5) * LOG2E
    w_out = wo_ref[...]

    unpack_bias([other_ref[s] for s in range(peers)], term_ref, half, bias_s)
    for_each(rows, tiles, lambda j: [soften(j, t, k_s[j], spread_s[j, t], bias_s, scaling, inv_s, e_s) for t in range(tiles)])
    for_each(rows, tiles, lambda j: [combine(j, t, v_s[j], g_s[j], inv_s, e_s, gated_s) for t in range(tiles)])

    def updated(pair):
        both = [ref[2 * pair + side] for side in range(2) for ref in (gated_ref, gated_s)]
        return dot_tn(jnp.concatenate(both, 0), w_out).astype(BF16)

    def store_update(pair):
        update = updated(pair)
        for side in range(2):
            out_ref[2 * pair + side] = update[:, side * chan : (side + 1) * chan]

    if not fused:
        for_each(rows // 2, tiles, store_update)
        return

    for j in range(0, rows, 2):
        update = updated(j // 2).astype(F32)
        for side in range(2):
            new = (x_s[j + side].astype(F32) + update[:, side * chan : (side + 1) * chan]).astype(BF16)
            new_s[j + side] = new
            wide[:, pl.ds(j + side, rows, stride=rows), :] = new.astype(F32).reshape(peers, rows, chan)
    out_ref[...] = wide[...].astype(BF16)
    logits_of(new_s, wd_ref[...], db_ref[:, :1], second_ref)


def logits_of(new_ref, w_dist, d_bias, out_ref):
    rows, n, chan = new_ref.shape
    logits = dot_nt(w_dist, new_ref[...].reshape(rows * n, chan)) + d_bias
    for j in range(rows):
        out_ref[j] = logits[:, j * n : (j + 1) * n].astype(BF16)


def finish_kernel(recv_ref, mirror_ref, wd_ref, db_ref, new_hbm, dist_hbm, new_ref, dist_ref, sems):
    peers, _, chan = recv_ref.shape
    rows = new_ref.shape[0]
    group = 2 * rows
    share = peers // 4
    copies = []
    for pair in range(peers // 2):
        at = slice(pair * group, (pair + 1) * group)
        block = regrouped(recv_ref[2 * pair], recv_ref[2 * pair + 1], rows)
        new_ref[:, at, :] = block.astype(BF16).reshape(rows, group, chan)
        if (pair + 1) % share == 0:
            at = pl.ds((pair + 1 - share) * group, share * group)
            copies.append(pltpu.make_async_copy(new_ref.at[:, at, :], new_hbm.at[:, at, :], sems.at[len(copies)]))
            copies[-1].start()
    n, half = new_ref.shape[1], rows // 2
    for first in range(0, rows, half):
        block = new_ref[first : first + half].reshape(half * n, chan)
        logits = dot_nt(wd_ref[...], block) + db_ref[:, :1]
        for i in range(half):
            own = logits[:, i * n : (i + 1) * n].astype(BF16).astype(F32)
            dist_ref[first + i] = (own + mirror_ref[first + i].astype(F32)).astype(BF16)
        at = pl.ds(first, half)
        copies.append(pltpu.make_async_copy(dist_ref.at[at], dist_hbm.at[at], sems.at[len(copies)]))
        copies[-1].start()
    for copy in copies:
        copy.wait()


def call(kernel, outs, args, scratch=(), smem=(), hbm=(), hbm_outs=False, limit=48):
    spaces = [pltpu.SMEM if i in smem else pl.ANY if i in hbm else pltpu.VMEM for i in range(len(args))]
    return pl.pallas_call(
        kernel,
        out_shape=[jax.ShapeDtypeStruct(s, d) for s, d in outs],
        in_specs=[pl.BlockSpec(memory_space=space) for space in spaces],
        out_specs=[pl.BlockSpec(memory_space=pl.ANY if hbm_outs else pltpu.VMEM)] * len(outs),
        scratch_shapes=list(scratch),
        compiler_params=pltpu.CompilerParams(vmem_limit_bytes=limit * 1024 * 1024),
    )(*args)


def swap_cores(values):
    peers = lax.axis_size("row")
    return lax.ppermute(values, "row", [(i, i ^ 1) for i in range(peers)])


def all_to_all(blocks):
    return lax.all_to_all(blocks, "row", split_axis=0, concat_axis=0, tiled=True)


def shards(
    pair_act, chain_id, residue_mask, norm_gain, w_proj, w_bias, chain_bias, w_out, w_dist, dist_bias,
):
    rows, n, chan = pair_act.shape
    peers = n // rows
    heads, dim = w_out.shape[0], w_out.shape[1]
    bins = w_dist.shape[1]
    tiles = n // LANES
    width = heads * dim
    fused = lax.axis_size("head") == 1
    gain = norm_gain[None, :]
    base = rows * rows
    length = base + tiles * heads * rows // 2

    (packed,) = call(
        pack_kernel,
        [((peers, length, chan), BF16)],
        [pair_act, gain, w_bias.T],
        scratch=[
            pltpu.VMEM(pair_act.shape, BF16),
            pltpu.VMEM(gain.shape, F32),
            pltpu.VMEM((heads, chan), BF16),
            pltpu.VMEM((peers, base, chan), F32),
            pltpu.VMEM((peers, length, chan), BF16),
            pltpu.SemaphoreType.DMA((rows + 2,)),
            pltpu.SemaphoreType.DMA((2,)),
        ],
        hbm=(0, 1, 2),
        hbm_outs=True,
        limit=60,
    )
    received = all_to_all(packed)
    prepared = call(
        functools.partial(prepare_kernel, heads),
        [
            ((heads, n, n), F32), ((3 * width, chan), BF16), ((2 * width, 2 * chan), BF16), ((bins, LANES), F32),
            ((1, chan), F32), ((2 * width, 2 * chan), BF16), ((bins, chan), BF16),
        ],
        [
            chain_id[None, :], residue_mask[None, :], chain_bias, w_proj, dist_bias[None, :],
            gain, w_out.reshape(width, chan), w_dist.T,
        ],
        smem=(2,),
    )
    received, *prepared = lax.optimization_barrier((received, *prepared))
    term, w_types, w_keys, db_col, gain, w_out, wd_t = prepared
    other_bias = swap_cores(received[:, base:])
    spread_shape = ((rows, tiles, width, heads // 2 * LANES), BF16)
    values_shape, gates_shape = ((rows, width // 2, n), BF16), ((rows, width // 2, n), F32)
    softmax_scratch = [
        pltpu.VMEM((heads // 2, n, n), F32),
        pltpu.VMEM((rows, tiles, heads // 2, LANES), F32),
        pltpu.VMEM((rows, tiles, n, heads // 2 * LANES), BF16),
    ]
    x_cols, spread, keys, values, gates, gated = call(
        functools.partial(project_kernel, heads),
        [
            ((rows, n, chan), BF16),
            spread_shape,
            ((rows, n, width), BF16),
            values_shape,
            gates_shape,
            values_shape,
        ],
        [received, gain, w_types, w_keys, term],
        scratch=[
            pltpu.VMEM((rows, n, chan), BF16),
            *(pltpu.VMEM(*shape) for shape in (spread_shape, values_shape, gates_shape)),
            *softmax_scratch,
        ],
    )
    if fused:
        outs = [((peers, base, chan), BF16), ((rows, bins, n), BF16)]
    else:
        outs = [((rows, n, chan), BF16)]
    result = call(
        functools.partial(attend_kernel, fused),
        outs,
        [other_bias, term, w_out, wd_t, db_col, x_cols, spread, keys, values, gates, gated],
        scratch=softmax_scratch + [pltpu.VMEM(*values_shape)] + [pltpu.VMEM((rows, n, chan), BF16), pltpu.VMEM((peers, base, chan), F32)] * fused,
    )
    if fused:
        to_rows, mirror = result
    else:
        update = lax.psum(result[0], "head").astype(F32)
        new = (x_cols.astype(F32) + update).astype(BF16)
        logits = jnp.einsum("cb,jic->jbi", w_dist, new, preferred_element_type=F32)
        mirror = (logits + dist_bias[None, :, None]).astype(BF16)
        to_rows = new.reshape(rows, peers, rows, chan).transpose(1, 2, 0, 3).reshape(peers, base, chan)
    arrived = all_to_all(to_rows)
    new_rows, dist = call(
        finish_kernel,
        [((rows, n, chan), BF16), ((rows, bins, n), BF16)],
        [arrived, mirror, wd_t, db_col],
        scratch=[
            pltpu.VMEM((rows, n, chan), BF16),
            pltpu.VMEM((rows, bins, n), BF16),
            pltpu.SemaphoreType.DMA((4,)),
        ],
        hbm_outs=True,
    )
    return new_rows, dist.transpose(0, 2, 1)


def solution(mesh):
    in_specs = (
        P(("dp", "row"), None, None),
        P("dp"),
        P("dp"),
        P(),
        P(None, "head", None),
        P(None, "head"),
        P(None, "head"),
        P("head", None, None),
        P(),
        P(),
    )
    out_specs = (P(("dp", "row"), None, None), P(("dp", "row"), None, None))
    return jax.shard_map(shards, mesh=mesh, in_specs=in_specs, out_specs=out_specs, check_vma=False)
```

```python
import functools

import jax
import jax.numpy as jnp
from jax import lax
from jax.experimental import pallas as pl
from jax.experimental.pallas import tpu as pltpu
from jax.sharding import PartitionSpec as P

LANES = 128
F32 = jnp.float32
BF16 = jnp.bfloat16
LOG2E = 1.4426950408889634


def dot_nt(a, b):
    return lax.dot_general(a, b, (((1,), (1,)), ((), ())), preferred_element_type=F32)


def dot_tn(a, b):
    return lax.dot_general(a, b, (((0,), (0,)), ((), ())), preferred_element_type=F32)


def dot_nn(a, b):
    return jnp.dot(a, b, preferred_element_type=F32)


def layer_norm(values, gain):
    center = jnp.mean(values, -1, keepdims=True)
    centered = values - center
    variance = jnp.mean(centered * centered, -1, keepdims=True)
    return (centered * lax.rsqrt(variance + 1e-05) * gain).astype(BF16)


def pack_kernel(x_hbm, gain_hbm, wb_hbm, out_hbm, x_ref, gain_ref, wb_ref, wide, out_ref, sems, out_sems):
    rows, n, chan = x_ref.shape
    peers = n // rows
    heads = wb_ref.shape[0]
    half = heads * rows // 2
    base = rows * rows
    fetch_gain = pltpu.make_async_copy(gain_hbm, gain_ref, sems.at[rows])
    fetch_wb = pltpu.make_async_copy(wb_hbm, wb_ref, sems.at[rows + 1])
    fetches = [pltpu.make_async_copy(x_hbm.at[k], x_ref.at[k], sems.at[k]) for k in range(rows)]
    for copy in (fetch_gain, fetch_wb, *fetches):
        copy.start()
    stores = []

    def store(first, count):
        at = pl.ds(first, count)
        copy = pltpu.make_async_copy(out_ref.at[:, at, :], out_hbm.at[:, at, :], out_sems.at[len(stores)])
        copy.start()
        stores.append(copy)

    owner = lax.broadcasted_iota(jnp.int32, (heads * rows, chan), 0) % rows
    bias = jnp.zeros((heads * rows, n), F32)
    fetch_gain.wait()
    fetch_wb.wait()
    gain = gain_ref[...]
    wb = wb_ref[...].astype(F32)
    wb = jnp.concatenate([jnp.broadcast_to(wb[h : h + 1], (rows, chan)) for h in range(heads)], 0)
    mine = [jnp.where(owner == k, wb, 0.0).astype(BF16) for k in range(rows)]
    mine = [jnp.concatenate(mine[k : k + 2], 1) for k in range(0, rows, 2)]
    for copy in fetches:
        copy.wait()
    normed = [layer_norm(x_ref[k].astype(F32), gain) for k in range(rows)]
    for k in range(rows):
        wide[:, pl.ds(k, rows, stride=rows), :] = x_ref[k].astype(F32).reshape(peers, rows, chan)
    out_ref[:, :base, :] = wide[...].astype(BF16)
    store(0, base)
    for pair in range(rows // 2):
        bias = bias + dot_nt(mine[pair], jnp.concatenate(normed[2 * pair : 2 * pair + 2], 1))
    bias = bias.astype(BF16)
    for t in range(n // LANES):
        block = bias[:, t * LANES : (t + 1) * LANES]
        for d in range(peers):
            part = block[(d % 2) * half : (d % 2 + 1) * half]
            out_ref[d, base + t * half : base + (t + 1) * half] = part
    store(base, (n // LANES) * half)
    for copy in stores:
        copy.wait()


def prepare_kernel(
    heads,
    chain_ref, mask_ref, cb_ref, w_ref, db_ref, gain_ref, wo_ref, wd_ref,
    term_ref, wt_ref, wk_out, dbc_ref, gain_out, wo_out, wd_out,
):
    gain_out[...] = gain_ref[...]
    chan = w_ref.shape[0]
    width = wo_ref.shape[0]
    half = heads // 2
    core = lax.axis_index("row") % 2
    w_out = wo_ref[...].astype(F32)
    other_first = jnp.concatenate([w_out[width // 2 :], w_out[: width // 2]], 0)
    w_out = jnp.where(core == 0, w_out, other_first).astype(BF16)
    wk_out[...] = jnp.zeros_like(wk_out)
    wo_out[...] = jnp.zeros_like(wo_out)
    for side in range(2):
        wo_out[side * width : (side + 1) * width, side * chan : (side + 1) * chan] = w_out
    wd_out[...] = wd_ref[...]
    n = chain_ref.shape[1]
    tiles = n // LANES
    dim = w_ref.shape[2] // 4

    def column_of(row):
        return jnp.transpose(jnp.broadcast_to(row, (LANES, LANES)))

    for kt in range(tiles):
        ks = slice(kt * LANES, (kt + 1) * LANES)
        chain_k = column_of(chain_ref[:, ks].astype(F32))
        mask_k = (column_of(mask_ref[:, ks].astype(F32)) - 1.0) * 1000000000.0
        for it in range(tiles):
            cs = slice(it * LANES, (it + 1) * LANES)
            same = chain_k == chain_ref[:, cs].astype(F32)
            for h in range(heads):
                inside, outside = [jnp.where(core == 0, cb_ref[r, h], cb_ref[r, (h + half) % heads]) for r in (1, 0)]
                term_ref[h, ks, cs] = (jnp.where(same, inside, outside) + mask_k) * LOG2E
    for h in range(heads):
        mine = jnp.where(core == 0, w_ref[:, h, :].astype(F32), w_ref[:, (h + half) % heads, :].astype(F32))
        turned = jnp.transpose(mine).astype(BF16)
        for place, kind in enumerate((0, 2, 3)):
            start = place * width + h * dim
            wt_ref[start : start + dim] = turned[kind * dim : (kind + 1) * dim]
        for side in range(2):
            start = side * width + h * dim
            wk_out[start : start + dim, side * chan : (side + 1) * chan] = turned[dim : 2 * dim]
    bins = dbc_ref.shape[0]
    db_rows = jnp.broadcast_to(jnp.concatenate([db_ref[...], db_ref[...]], 1)[:, :LANES], (LANES, LANES))
    dbc_ref[...] = jnp.transpose(db_rows)[:bins]


def unpack_bias(blocks, term_ref, first, bias_ref):
    half, n = bias_ref.shape[0], bias_ref.shape[1]
    rows = n // len(blocks)
    for s, block in enumerate(blocks):
        at = slice(s * rows, (s + 1) * rows)
        extra = block.astype(F32) * LOG2E
        for t in range(n // LANES):
            cs = slice(t * LANES, (t + 1) * LANES)
            for h in range(half):
                start = (t * half + h) * rows
                bias_ref[h, at, cs] = extra[start : start + rows] + term_ref[first + h, at, cs]


def soften(j, t, keys, spread, bias_ref, inv_s, e_s):
    scores = dot_nn(keys, spread)
    for h in range(bias_ref.shape[0]):
        cs = slice(h * LANES, (h + 1) * LANES)
        s = scores[:, cs] + bias_ref[h, :, t * LANES : (t + 1) * LANES]
        e = jnp.exp2(s - jnp.max(s, 0, keepdims=True))
        inv_s[j, t, h : h + 1] = 1.0 / jnp.sum(e, 0, keepdims=True)
        e_s[j, t, :, cs] = e.astype(BF16)


def combine(j, t, values, gates, inv_s, e_s, gated_ref):
    half = inv_s.shape[2]
    dim = values.shape[0] // half
    cs = slice(t * LANES, (t + 1) * LANES)
    o = dot_nn(values, e_s[j, t])
    for h in range(half):
        mine = slice(h * dim, (h + 1) * dim)
        part = o[mine, h * LANES : (h + 1) * LANES] * inv_s[j, t, h : h + 1]
        gated_ref[j, mine, cs] = (gates[mine, cs] * part).astype(BF16)


def for_each(count, tiles, body):
    if tiles == 1:
        for i in range(count):
            body(i)
    else:

        @pl.loop(0, count)
        def _(i):
            body(i)


def regrouped(left, right, rows):
    both = [block.astype(F32).reshape(rows, rows, LANES) for block in (left, right)]
    return jnp.concatenate(both, 1).reshape(2 * rows * rows, LANES)


def project_kernel(
    heads,
    recv_ref, gain_ref, w_ref, wk_ref, term_ref,
    x_s, spread_s, k_s, v_s, g_s, gated_ref,
    n_s, own_spread, own_v, own_g, bias_s, inv_s, e_s,
):
    peers = recv_ref.shape[0]
    rows, n, chan = x_s.shape
    tiles = n // LANES
    dim = w_ref.shape[0] // (3 * heads)
    width = heads * dim
    base = rows * rows
    gain = gain_ref[...]
    group = 2 * rows
    w_k = wk_ref[...]

    quads = range(peers // 4)
    x = [[regrouped(recv_ref[s, :base], recv_ref[s + 1, :base], rows) for s in (4 * q, 4 * q + 2)] for q in quads]
    normed = [[layer_norm(part, gain) for part in two] for two in x]
    keys = [dot_nt(jnp.concatenate(two, 1), w_k).astype(BF16) for two in normed]
    for quad in quads:
        for side in range(2):
            at = slice((2 * quad + side) * group, (2 * quad + side + 1) * group)
            x_s[:, at, :] = x[quad][side].astype(BF16).reshape(rows, group, chan)
            n_s[:, at, :] = normed[quad][side].reshape(rows, group, chan)
            k_s[:, at, :] = keys[quad][:, side * width : (side + 1) * width].reshape(rows, group, width)

    half, part = heads // 2, width // 2
    unpack_bias([recv_ref[s, base:] for s in range(peers)], term_ref, 0, bias_s)
    w_qvg = w_ref[...]
    zero = jnp.zeros((dim, LANES), BF16)
    scaling = dim ** (-0.5) * LOG2E

    def project(pair):
        both = dot_nt(w_qvg, n_s[pl.ds(2 * pair, 2)].reshape(2 * n, chan))
        both = jnp.concatenate([both[:width] * scaling, both[width:]], 0).astype(BF16)
        for side in range(2):
            j = 2 * pair + side
            qvg = both[:, side * n : (side + 1) * n]
            gate = jax.nn.sigmoid(qvg[2 * width :].astype(F32))
            own_v[j], v_s[j] = qvg[width : width + part], qvg[width + part : 2 * width]
            own_g[j], g_s[j] = gate[:part], gate[part:]
            for t in range(tiles):
                for h in range(heads):
                    target = (own_spread, spread_s)[h // half]
                    cs = slice(h % half * LANES, (h % half + 1) * LANES)
                    for other in range(half if h < half else heads):
                        block = qvg[h * dim : (h + 1) * dim, t * LANES : (t + 1) * LANES] if h == other else zero
                        target[j, t, other * dim : (other + 1) * dim, cs] = block

    for_each(rows // 2, tiles, project)
    for_each(rows, tiles, lambda j: [soften(j, t, k_s[j, :, :part], own_spread[j, t], bias_s, inv_s, e_s) for t in range(tiles)])
    for_each(rows, tiles, lambda j: [combine(j, t, own_v[j], own_g[j], inv_s, e_s, gated_ref) for t in range(tiles)])


def attend_kernel(
    fused,
    other_ref, term_ref, wo_ref, wd_ref, db_ref, x_s, spread_s, k_s, v_s, g_s, gated_ref,
    out_ref, *refs,
):
    if fused:
        second_ref, bias_s, inv_s, e_s, gated_s, new_s, wide = refs
    else:
        bias_s, inv_s, e_s, gated_s = refs
    peers = other_ref.shape[0]
    rows, n, chan = x_s.shape
    tiles = n // LANES
    half = bias_s.shape[0]
    w_out = wo_ref[...]

    unpack_bias([other_ref[s] for s in range(peers)], term_ref, half, bias_s)
    for_each(rows, tiles, lambda j: [soften(j, t, k_s[j], spread_s[j, t], bias_s, inv_s, e_s) for t in range(tiles)])
    for_each(rows, tiles, lambda j: [combine(j, t, v_s[j], g_s[j], inv_s, e_s, gated_s) for t in range(tiles)])

    def updated(pair):
        both = [ref[2 * pair + side] for side in range(2) for ref in (gated_ref, gated_s)]
        return dot_tn(jnp.concatenate(both, 0), w_out).astype(BF16)

    def store_update(pair):
        update = updated(pair)
        for side in range(2):
            out_ref[2 * pair + side] = update[:, side * chan : (side + 1) * chan]

    if not fused:
        for_each(rows // 2, tiles, store_update)
        return

    for j in range(0, rows, 2):
        update = updated(j // 2).astype(F32)
        for side in range(2):
            new = (x_s[j + side].astype(F32) + update[:, side * chan : (side + 1) * chan]).astype(BF16)
            new_s[j + side] = new
            wide[:, pl.ds(j + side, rows, stride=rows), :] = new.astype(F32).reshape(peers, rows, chan)
    out_ref[...] = wide[...].astype(BF16)
    logits_of(new_s, wd_ref[...], db_ref[:, :1], second_ref)


def logits_of(new_ref, w_dist, d_bias, out_ref):
    rows, n, chan = new_ref.shape
    logits = dot_nt(w_dist, new_ref[...].reshape(rows * n, chan)) + d_bias
    for j in range(rows):
        out_ref[j] = logits[:, j * n : (j + 1) * n].astype(BF16)


def finish_kernel(recv_ref, mirror_ref, wd_ref, db_ref, new_hbm, dist_hbm, new_ref, dist_ref, sems):
    peers, _, chan = recv_ref.shape
    rows = new_ref.shape[0]
    group = 2 * rows
    share = peers // 4
    copies = []
    for pair in range(peers // 2):
        at = slice(pair * group, (pair + 1) * group)
        block = regrouped(recv_ref[2 * pair], recv_ref[2 * pair + 1], rows)
        new_ref[:, at, :] = block.astype(BF16).reshape(rows, group, chan)
        if (pair + 1) % share == 0:
            at = pl.ds((pair + 1 - share) * group, share * group)
            copies.append(pltpu.make_async_copy(new_ref.at[:, at, :], new_hbm.at[:, at, :], sems.at[len(copies)]))
            copies[-1].start()
    n, half = new_ref.shape[1], rows // 2
    for first in range(0, rows, half):
        block = new_ref[first : first + half].reshape(half * n, chan)
        logits = dot_nt(wd_ref[...], block) + db_ref[:, :1]
        for i in range(half):
            own = logits[:, i * n : (i + 1) * n].astype(BF16).astype(F32)
            dist_ref[first + i] = (own + mirror_ref[first + i].astype(F32)).astype(BF16)
        at = pl.ds(first, half)
        copies.append(pltpu.make_async_copy(dist_ref.at[at], dist_hbm.at[at], sems.at[len(copies)]))
        copies[-1].start()
    for copy in copies:
        copy.wait()


def call(kernel, outs, args, scratch=(), smem=(), hbm=(), hbm_outs=False, limit=48):
    spaces = [pltpu.SMEM if i in smem else pl.ANY if i in hbm else pltpu.VMEM for i in range(len(args))]
    return pl.pallas_call(
        kernel,
        out_shape=[jax.ShapeDtypeStruct(s, d) for s, d in outs],
        in_specs=[pl.BlockSpec(memory_space=space) for space in spaces],
        out_specs=[pl.BlockSpec(memory_space=pl.ANY if hbm_outs else pltpu.VMEM)] * len(outs),
        scratch_shapes=list(scratch),
        compiler_params=pltpu.CompilerParams(vmem_limit_bytes=limit * 1024 * 1024),
    )(*args)


def swap_cores(values):
    peers = lax.axis_size("row")
    return lax.ppermute(values, "row", [(i, i ^ 1) for i in range(peers)])


def all_to_all(blocks):
    return lax.all_to_all(blocks, "row", split_axis=0, concat_axis=0, tiled=True)


def shards(
    pair_act, chain_id, residue_mask, norm_gain, w_proj, w_bias, chain_bias, w_out, w_dist, dist_bias,
):
    rows, n, chan = pair_act.shape
    peers = n // rows
    heads, dim = w_out.shape[0], w_out.shape[1]
    bins = w_dist.shape[1]
    tiles = n // LANES
    width = heads * dim
    fused = lax.axis_size("head") == 1
    gain = norm_gain[None, :]
    base = rows * rows
    length = base + tiles * heads * rows // 2

    (packed,) = call(
        pack_kernel,
        [((peers, length, chan), BF16)],
        [pair_act, gain, w_bias.T],
        scratch=[
            pltpu.VMEM(pair_act.shape, BF16),
            pltpu.VMEM(gain.shape, F32),
            pltpu.VMEM((heads, chan), BF16),
            pltpu.VMEM((peers, base, chan), F32),
            pltpu.VMEM((peers, length, chan), BF16),
            pltpu.SemaphoreType.DMA((rows + 2,)),
            pltpu.SemaphoreType.DMA((2,)),
        ],
        hbm=(0, 1, 2),
        hbm_outs=True,
        limit=60,
    )
    received = all_to_all(packed)
    prepared = call(
        functools.partial(prepare_kernel, heads),
        [
            ((heads, n, n), F32), ((3 * width, chan), BF16), ((2 * width, 2 * chan), BF16), ((bins, LANES), F32),
            ((1, chan), F32), ((2 * width, 2 * chan), BF16), ((bins, chan), BF16),
        ],
        [
            chain_id[None, :], residue_mask[None, :], chain_bias, w_proj, dist_bias[None, :],
            gain, w_out.reshape(width, chan), w_dist.T,
        ],
        smem=(2,),
    )
    received, *prepared = lax.optimization_barrier((received, *prepared))
    term, w_types, w_keys, db_col, gain, w_out, wd_t = prepared
    other_bias = swap_cores(received[:, base:])
    spread_shape = ((rows, tiles, width, heads // 2 * LANES), BF16)
    values_shape, gates_shape = ((rows, width // 2, n), BF16), ((rows, width // 2, n), F32)
    softmax_scratch = [
        pltpu.VMEM((heads // 2, n, n), F32),
        pltpu.VMEM((rows, tiles, heads // 2, LANES), F32),
        pltpu.VMEM((rows, tiles, n, heads // 2 * LANES), BF16),
    ]
    x_cols, spread, keys, values, gates, gated = call(
        functools.partial(project_kernel, heads),
        [
            ((rows, n, chan), BF16),
            spread_shape,
            ((rows, n, width), BF16),
            values_shape,
            gates_shape,
            values_shape,
        ],
        [received, gain, w_types, w_keys, term],
        scratch=[
            pltpu.VMEM((rows, n, chan), BF16),
            pltpu.VMEM((rows, tiles, width // 2, heads // 2 * LANES), BF16),
            *(pltpu.VMEM(*shape) for shape in (values_shape, gates_shape)),
            *softmax_scratch,
        ],
    )
    if fused:
        outs = [((peers, base, chan), BF16), ((rows, bins, n), BF16)]
    else:
        outs = [((rows, n, chan), BF16)]
    result = call(
        functools.partial(attend_kernel, fused),
        outs,
        [other_bias, term, w_out, wd_t, db_col, x_cols, spread, keys, values, gates, gated],
        scratch=softmax_scratch + [pltpu.VMEM(*values_shape)] + [pltpu.VMEM((rows, n, chan), BF16), pltpu.VMEM((peers, base, chan), F32)] * fused,
    )
    if fused:
        to_rows, mirror = result
    else:
        update = lax.psum(result[0], "head").astype(F32)
        new = (x_cols.astype(F32) + update).astype(BF16)
        logits = jnp.einsum("cb,jic->jbi", w_dist, new, preferred_element_type=F32)
        mirror = (logits + dist_bias[None, :, None]).astype(BF16)
        to_rows = new.reshape(rows, peers, rows, chan).transpose(1, 2, 0, 3).reshape(peers, base, chan)
    arrived = all_to_all(to_rows)
    new_rows, dist = call(
        finish_kernel,
        [((rows, n, chan), BF16), ((rows, bins, n), BF16)],
        [arrived, mirror, wd_t, db_col],
        scratch=[
            pltpu.VMEM((rows, n, chan), BF16),
            pltpu.VMEM((rows, bins, n), BF16),
            pltpu.SemaphoreType.DMA((4,)),
        ],
        hbm_outs=True,
    )
    return new_rows, dist.transpose(0, 2, 1)


def solution(mesh):
    in_specs = (
        P(("dp", "row"), None, None),
        P("dp"),
        P("dp"),
        P(),
        P(None, "head", None),
        P(None, "head"),
        P(None, "head"),
        P("head", None, None),
        P(),
        P(),
    )
    out_specs = (P(("dp", "row"), None, None), P(("dp", "row"), None, None))
    return jax.shard_map(shards, mesh=mesh, in_specs=in_specs, out_specs=out_specs, check_vma=False)
```
